32 devices in a mesh: section: 4 (over y, x), rows: 8 (over z, core).
Axes of the slice: x: 2, y: 2, z: 4, core: 2. Of those that a mesh axis runs over, the one named last changes fastest.
Arguments:
- activations: bfloat16 [32, 16, 64, 128], P('section', 'rows'), may hold values from -48 to 48
- first_cache: bfloat16 [2, 16, 64, 128], P(None, 'rows'), may hold values from -4 to 4
- second_cache: bfloat16 [2, 16, 64, 128], P(None, 'rows'), may hold values from -4 to 4
- norm1_scale: float32 [128], replicated, may hold values from 0.1 to 1.9
- norm1_shift: float32 [128], replicated, may hold values from -3 to 3
- conv1_weight: bfloat16 [3, 3, 3, 128, 128], replicated, may hold values from -0.109375 to 0.109375
- conv1_bias: float32 [128], replicated, may hold values from -5 to 5
- norm2_scale: float32 [128], replicated, may hold values from 0.1 to 1.9
- norm2_shift: float32 [128], replicated, may hold values from -3 to 3
- conv2_weight: bfloat16 [3, 3, 3, 128, 128], replicated, may hold values from -0.109375 to 0.109375
- conv2_bias: float32 [128], replicated, may hold values from -3 to 3
Outputs:
- block_output: bfloat16 [32, 16, 64, 128], P('section', 'rows')
The draws below stay inside these ranges and needn't reach their ends.
All inputs are finite; a program needn't handle non-finite values.
Results may differ from the reference program's by a relative error of at most 0.007.
Values may be sent and summed in bfloat16 or wider, within the bound.
No kernel may reach another device: no remote copies, remote signals or barrier semaphores. Data moves between devices by JAX's collectives and lax.ppermute only.
A program may use at most 64 MiB of HBM per device.

```python
import math
import jax
import jax.numpy as jnp
from jax import lax

C = 128
GROUPS = 32
SPAN = 8
ROWS_DEV = 2
COLS = 64
FRAMES = 32
ROWS = 16
N_SECTION = 4


def draw_activations(key, part):
    key_base = jax.random.fold_in(key, 11)
    key_values, key_rows, key_cols, key_device, key_flip, key_frames = jax.random.split(key_base, 6)
    shape_full = (FRAMES, ROWS, COLS, C)
    row_scale = jnp.exp(jax.random.uniform(key_rows, (ROWS,), jnp.float32) * math.log(1.78))
    col_scale = jnp.exp(jax.random.uniform(key_cols, (COLS,), jnp.float32) * math.log(3.16))
    device_count = ROWS // ROWS_DEV
    flip_bit = jax.random.randint(key_flip, (), 0, 2)
    parity = ((jnp.arange(device_count, dtype=jnp.int32) + flip_bit) % 2).astype(jnp.float32)
    device_level = jnp.exp(0.5 * math.log(10.0) * (jax.random.uniform(key_device, (device_count,), jnp.float32) + parity))
    device_scale = jnp.repeat(device_level, ROWS_DEV)
    frame_level = jnp.exp(jax.random.uniform(key_frames, (FRAMES,), jnp.float32, math.log(0.5), math.log(2.0)))
    base = jax.random.truncated_normal(key_values, -4.0, 4.0, shape_full, jnp.float32)
    factor = row_scale * device_scale
    return (0.06 * base * factor[None, :, None, None] * col_scale[None, None, :, None] * frame_level[:, None, None, None]).astype(jnp.bfloat16)


def block_levels(own_key, dims, cuts, least, largest):
    level = 1.0
    for axis_at, blocks in cuts:
        steps = jax.random.uniform(jax.random.fold_in(jax.random.fold_in(own_key, 6), axis_at), (blocks,), jnp.float32, least / len(cuts), largest / len(cuts))
        level = level * jnp.repeat(jnp.exp(steps), dims[axis_at] // blocks).reshape((-1,) + (1,) * (len(dims) - 1 - axis_at))
    return level


def scatter_about(rng, extent, scale, reach, shards=(), kind=jnp.bfloat16):
    array = scale * jax.random.normal(rng, extent, jnp.float32)
    if shards:
        array = array * block_levels(rng, extent, shards, -0.22, 0.18)
    return jnp.clip(array, -reach, reach).astype(kind)


def setup_inputs(seed: int = 0) -> dict:
    keys = jax.random.split(jax.random.key(seed), 12)
    return {
        "activations": draw_activations(jax.random.fold_in(keys[11], 71), 0),
        "first_cache": scatter_about(keys[1], (2, ROWS, COLS, C), 0.7, 4.0, ((1, 8),)),
        "second_cache": scatter_about(keys[2], (2, ROWS, COLS, C), 0.7, 4.0, ((1, 8),)),
        "norm1_scale": jnp.clip(1.0 + 0.18 * jax.random.normal(keys[3], (C,), jnp.float32), 0.1, 1.9),
        "norm1_shift": scatter_about(keys[4], (C,), 0.5, 3.0, (), jnp.float32),
        "conv1_weight": scatter_about(keys[5], (3, 3, 3, C, C), (27 * C) ** -0.5, 0.109375),
        "conv1_bias": scatter_about(keys[6], (C,), 1.0, 5.0, (), jnp.float32),
        "norm2_scale": jnp.clip(1.0 + 0.18 * jax.random.normal(keys[7], (C,), jnp.float32), 0.1, 1.9),
        "norm2_shift": scatter_about(keys[8], (C,), 0.5, 3.0, (), jnp.float32),
        "conv2_weight": scatter_about(keys[9], (3, 3, 3, C, C), (27 * C) ** -0.5, 0.109375),
        "conv2_bias": scatter_about(keys[10], (C,), 0.5, 3.0, (), jnp.float32),
    }


epsilon = 1e-06

def norm_silu(values, scale, shift):
    spans = values.reshape(N_SECTION, SPAN, ROWS, COLS, C)

    def per_span(span_block):
        grouped = span_block.astype(jnp.float32).reshape(SPAN, ROWS, COLS, GROUPS, C // GROUPS)
        average = lax.optimization_barrier(jnp.mean(grouped, axis=(0, 1, 2, 4), keepdims=True))
        centred = grouped - average
        spread = lax.optimization_barrier(jnp.mean(centred * centred, axis=(0, 1, 2, 4), keepdims=True))
        normal = (centred / jnp.sqrt(spread + epsilon)).reshape(SPAN, ROWS, COLS, C)
        return jax.nn.silu(normal * scale + shift).astype(jnp.bfloat16)
    return lax.map(per_span, spans).reshape(FRAMES, ROWS, COLS, C)

def causal_conv(source, weight, bias):
    padded = jnp.pad(source, ((0, 0), (1, 1), (1, 1), (0, 0)))

    def per_frame(frame_index):
        window = lax.dynamic_slice_in_dim(padded, frame_index, 3, 0)
        totals = jnp.zeros((ROWS * COLS, C), jnp.float32)
        for frame_tap in range(3):
            for row_tap in range(3):
                for col_tap in range(3):
                    piece = window[frame_tap, row_tap:row_tap + ROWS, col_tap:col_tap + COLS].reshape(ROWS * COLS, C)
                    totals = totals + jnp.dot(piece, weight[frame_tap, row_tap, col_tap], preferred_element_type=jnp.float32)
        return totals.reshape(ROWS, COLS, C)
    return lax.map(per_frame, jnp.arange(FRAMES, dtype=jnp.int32)) + bias

def reference(activations, first_cache, second_cache, norm1_scale, norm1_shift, conv1_weight, conv1_bias, norm2_scale, norm2_shift, conv2_weight, conv2_bias):
    entry_block = norm_silu(activations, norm1_scale, norm1_shift)
    middle = causal_conv(jnp.concatenate([first_cache, entry_block], 0), conv1_weight, conv1_bias).astype(jnp.bfloat16)
    second = norm_silu(middle, norm2_scale, norm2_shift)
    final = causal_conv(jnp.concatenate([second_cache, second], 0), conv2_weight, conv2_bias)
    return (activations.astype(jnp.float32) + final).astype(jnp.bfloat16)
```

```python
import jax
import jax.numpy as jnp
from jax import lax
from jax.sharding import PartitionSpec as P

GROUPS = 32


epsilon = 1e-06


def from_behind(block, axis, distance):
    devices = range(lax.axis_size(axis))
    route = [(i - distance, i) for i in devices if i - distance in devices]
    return lax.ppermute(block, axis, route)


def extended(block, sides, width):
    for axis, dim in sides:
        count = lax.axis_size(axis)
        forward = [(i, i + 1) for i in range(count - 1)]
        backward = [(target, source) for source, target in forward]
        low = lax.ppermute(
            lax.slice_in_dim(block, block.shape[dim] - width, None, axis=dim), axis, forward
        )
        high = lax.ppermute(lax.slice_in_dim(block, 0, width, axis=dim), axis, backward)
        block = jnp.concatenate([low, block, high], axis=dim)
    return block


def group_moments(values):
    frames, row_count, columns, channels = values.shape
    grouped = values.reshape(frames * row_count * columns, GROUPS, channels // GROUPS)
    cells_total = frames * row_count * columns * (channels // GROUPS) * lax.axis_size("rows")
    partial = jnp.concatenate(
        [jnp.sum(grouped, axis=(0, 2)), jnp.sum(grouped * grouped, axis=(0, 2))]
    )
    everyone = jnp.broadcast_to(partial, (lax.axis_size("rows"), 2 * GROUPS))
    received = lax.all_to_all(everyone, "rows", 0, 0, tiled=True)
    totals, squares = jnp.split(jnp.sum(received, axis=0), 2)
    average = totals / cells_total
    spread = squares / cells_total - average * average
    return (average, spread)


def apply_norm(values, average, spread, scale, shift):
    frames, row_count, columns, channels = values.shape
    grouped = values.reshape(frames, row_count, columns, GROUPS, channels // GROUPS)
    normal = (grouped - average[:, None]) / jnp.sqrt(spread[:, None] + epsilon)
    normal = normal.reshape(frames, row_count, columns, channels)
    return jax.nn.silu(normal * scale + shift).astype(jnp.bfloat16)


def causal_conv(source, weight, bias):
    frames = source.shape[0] - 2
    row_count = source.shape[1] - 2
    columns = source.shape[2]
    padded = jnp.pad(source, ((0, 0), (0, 0), (1, 1), (0, 0)))
    totals = jnp.zeros((frames, row_count, columns, weight.shape[-1]), jnp.float32)
    for frame_tap in range(3):
        for row_tap in range(3):
            for col_tap in range(3):
                piece = padded[
                    frame_tap : frame_tap + frames,
                    row_tap : row_tap + row_count,
                    col_tap : col_tap + columns,
                ]
                totals = totals + jnp.einsum(
                    "fhwc,cd->fhwd",
                    piece,
                    weight[frame_tap, row_tap, col_tap],
                    preferred_element_type=jnp.float32,
                )
    return totals + bias


def on_device(
    activations,
    first_cache,
    second_cache,
    norm1_scale,
    norm1_shift,
    conv1_weight,
    conv1_bias,
    norm2_scale,
    norm2_shift,
    conv2_weight,
    conv2_bias,
):
    at_start = lax.axis_index("section") == 0
    own_rows = activations.astype(jnp.float32)
    average, spread = group_moments(own_rows)
    entry_block = apply_norm(own_rows, average, spread, norm1_scale, norm1_shift)
    received = from_behind(entry_block[-2:], "section", 1)
    joined = jnp.concatenate([jnp.where(at_start, first_cache, received), entry_block], 0)
    padded = extended(joined, (("rows", 1),), 1)
    middle = causal_conv(padded, conv1_weight, conv1_bias).astype(jnp.bfloat16)
    middle_full = middle.astype(jnp.float32)
    average_two, spread_two = group_moments(middle_full)
    second = apply_norm(middle_full, average_two, spread_two, norm2_scale, norm2_shift)
    received_two = from_behind(second[-2:], "section", 1)
    joined_two = jnp.concatenate([jnp.where(at_start, second_cache, received_two), second], 0)
    padded_two = extended(joined_two, (("rows", 1),), 1)
    final = causal_conv(padded_two, conv2_weight, conv2_bias)
    return (own_rows + final).astype(jnp.bfloat16)


def solution(mesh):
    in_specs = (
        P("section", "rows", None, None),
        P(None, "rows", None, None),
        P(None, "rows", None, None),
        P(),
        P(),
        P(),
        P(),
        P(),
        P(),
        P(),
        P(),
    )
    out_specs = P("section", "rows", None, None)
    return jax.shard_map(
        on_device, mesh=mesh, in_specs=in_specs, out_specs=out_specs, check_vma=False
    )
```

```python
import jax
import jax.numpy as jnp
from jax import lax
from jax.sharding import PartitionSpec as P

GROUPS = 32


epsilon = 1e-06


def from_behind(block, axis, distance):
    devices = range(lax.axis_size(axis))
    route = [(i - distance, i) for i in devices if i - distance in devices]
    return lax.ppermute(block, axis, route)


def extended(block, sides, width):
    for axis, dim in sides:
        count = lax.axis_size(axis)
        forward = [(i, i + 1) for i in range(count - 1)]
        backward = [(target, source) for source, target in forward]
        low = lax.ppermute(
            lax.slice_in_dim(block, block.shape[dim] - width, None, axis=dim), axis, forward
        )
        high = lax.ppermute(lax.slice_in_dim(block, 0, width, axis=dim), axis, backward)
        block = jnp.concatenate([low, block, high], axis=dim)
    return block


def group_moments(values):
    frames, row_count, columns, channels = values.shape
    grouped = values.reshape(frames * row_count * columns, GROUPS, channels // GROUPS)
    cells_total = frames * row_count * columns * (channels // GROUPS) * lax.axis_size("rows")
    partial = jnp.concatenate(
        [jnp.sum(grouped, axis=(0, 2)), jnp.sum(grouped * grouped, axis=(0, 2))]
    )
    count = lax.axis_size("rows")
    step = 1
    while step < count:
        partial = partial + lax.ppermute(partial, "rows", [(i, i ^ step) for i in range(count)])
        step *= 2
    totals, squares = jnp.split(partial, 2)
    average = totals / cells_total
    spread = squares / cells_total - average * average
    return (average, spread)


def apply_norm(values, average, spread, scale, shift):
    frames, row_count, columns, channels = values.shape
    grouped = values.reshape(frames, row_count, columns, GROUPS, channels // GROUPS)
    normal = (grouped - average[:, None]) / jnp.sqrt(spread[:, None] + epsilon)
    normal = normal.reshape(frames, row_count, columns, channels)
    return jax.nn.silu(normal * scale + shift).astype(jnp.bfloat16)


def causal_conv(source, weight, bias):
    frames = source.shape[0] - 2
    row_count = source.shape[1] - 2
    columns = source.shape[2]
    padded = jnp.pad(source, ((0, 0), (0, 0), (1, 1), (0, 0)))
    totals = jnp.zeros((frames, row_count, columns, weight.shape[-1]), jnp.float32)
    for frame_tap in range(3):
        for row_tap in range(3):
            for col_tap in range(3):
                piece = padded[
                    frame_tap : frame_tap + frames,
                    row_tap : row_tap + row_count,
                    col_tap : col_tap + columns,
                ]
                totals = totals + jnp.einsum(
                    "fhwc,cd->fhwd",
                    piece,
                    weight[frame_tap, row_tap, col_tap],
                    preferred_element_type=jnp.float32,
                )
    return totals + bias


def on_device(
    activations,
    first_cache,
    second_cache,
    norm1_scale,
    norm1_shift,
    conv1_weight,
    conv1_bias,
    norm2_scale,
    norm2_shift,
    conv2_weight,
    conv2_bias,
):
    at_start = lax.axis_index("section") == 0
    own_rows = activations.astype(jnp.float32)
    average, spread = group_moments(own_rows)
    entry_block = apply_norm(own_rows, average, spread, norm1_scale, norm1_shift)
    received = from_behind(entry_block[-2:], "section", 1)
    joined = jnp.concatenate([jnp.where(at_start, first_cache, received), entry_block], 0)
    padded = extended(joined, (("rows", 1),), 1)
    middle = causal_conv(padded, conv1_weight, conv1_bias).astype(jnp.bfloat16)
    middle_full = middle.astype(jnp.float32)
    average_two, spread_two = group_moments(middle_full)
    second = apply_norm(middle_full, average_two, spread_two, norm2_scale, norm2_shift)
    received_two = from_behind(second[-2:], "section", 1)
    joined_two = jnp.concatenate([jnp.where(at_start, second_cache, received_two), second], 0)
    padded_two = extended(joined_two, (("rows", 1),), 1)
    final = causal_conv(padded_two, conv2_weight, conv2_bias)
    return (own_rows + final).astype(jnp.bfloat16)


def solution(mesh):
    in_specs = (
        P("section", "rows", None, None),
        P(None, "rows", None, None),
        P(None, "rows", None, None),
        P(),
        P(),
        P(),
        P(),
        P(),
        P(),
        P(),
        P(),
    )
    out_specs = P("section", "rows", None, None)
    return jax.shard_map(
        on_device, mesh=mesh, in_specs=in_specs, out_specs=out_specs, check_vma=False
    )
```

```python
import jax
import jax.numpy as jnp
from jax import lax
from jax.sharding import PartitionSpec as P

GROUPS = 32


epsilon = 1e-06


def from_behind(block, axis, distance):
    devices = range(lax.axis_size(axis))
    route = [(i - distance, i) for i in devices if i - distance in devices]
    return lax.ppermute(block, axis, route)


def extended(block, sides, width):
    for axis, dim in sides:
        count = lax.axis_size(axis)
        forward = [(i, i + 1) for i in range(count - 1)]
        backward = [(target, source) for source, target in forward]
        low = lax.ppermute(
            lax.slice_in_dim(block, block.shape[dim] - width, None, axis=dim), axis, forward
        )
        high = lax.ppermute(lax.slice_in_dim(block, 0, width, axis=dim), axis, backward)
        block = jnp.concatenate([low, block, high], axis=dim)
    return block


def group_moments(values):
    frames, row_count, columns, channels = values.shape
    grouped = values.reshape(frames * row_count * columns, GROUPS, channels // GROUPS)
    cells_total = frames * row_count * columns * (channels // GROUPS) * lax.axis_size("rows")
    partial = jnp.concatenate(
        [jnp.sum(grouped, axis=(0, 2)), jnp.sum(grouped * grouped, axis=(0, 2))]
    )
    received = lax.all_gather(partial, "rows")
    totals, squares = jnp.split(jnp.sum(received, axis=0), 2)
    average = totals / cells_total
    spread = squares / cells_total - average * average
    return (average, spread)


def apply_norm(values, average, spread, scale, shift):
    frames, row_count, columns, channels = values.shape
    grouped = values.reshape(frames, row_count, columns, GROUPS, channels // GROUPS)
    normal = (grouped - average[:, None]) / jnp.sqrt(spread[:, None] + epsilon)
    normal = normal.reshape(frames, row_count, columns, channels)
    return jax.nn.silu(normal * scale + shift).astype(jnp.bfloat16)


def causal_conv(source, weight, bias):
    frames = source.shape[0] - 2
    row_count = source.shape[1] - 2
    columns = source.shape[2]
    padded = jnp.pad(source, ((0, 0), (0, 0), (1, 1), (0, 0)))
    totals = jnp.zeros((frames, row_count, columns, weight.shape[-1]), jnp.float32)
    for frame_tap in range(3):
        for row_tap in range(3):
            for col_tap in range(3):
                piece = padded[
                    frame_tap : frame_tap + frames,
                    row_tap : row_tap + row_count,
                    col_tap : col_tap + columns,
                ]
                totals = totals + jnp.einsum(
                    "fhwc,cd->fhwd",
                    piece,
                    weight[frame_tap, row_tap, col_tap],
                    preferred_element_type=jnp.float32,
                )
    return totals + bias


def on_device(
    activations,
    first_cache,
    second_cache,
    norm1_scale,
    norm1_shift,
    conv1_weight,
    conv1_bias,
    norm2_scale,
    norm2_shift,
    conv2_weight,
    conv2_bias,
):
    at_start = lax.axis_index("section") == 0
    own_rows = activations.astype(jnp.float32)
    average, spread = group_moments(own_rows)
    entry_block = apply_norm(own_rows, average, spread, norm1_scale, norm1_shift)
    received = from_behind(entry_block[-2:], "section", 1)
    joined = jnp.concatenate([jnp.where(at_start, first_cache, received), entry_block], 0)
    padded = extended(joined, (("rows", 1),), 1)
    middle = causal_conv(padded, conv1_weight, conv1_bias).astype(jnp.bfloat16)
    middle_full = middle.astype(jnp.float32)
    average_two, spread_two = group_moments(middle_full)
    second = apply_norm(middle_full, average_two, spread_two, norm2_scale, norm2_shift)
    received_two = from_behind(second[-2:], "section", 1)
    joined_two = jnp.concatenate([jnp.where(at_start, second_cache, received_two), second], 0)
    padded_two = extended(joined_two, (("rows", 1),), 1)
    final = causal_conv(padded_two, conv2_weight, conv2_bias)
    return (own_rows + final).astype(jnp.bfloat16)


def solution(mesh):
    in_specs = (
        P("section", "rows", None, None),
        P(None, "rows", None, None),
        P(None, "rows", None, None),
        P(),
        P(),
        P(),
        P(),
        P(),
        P(),
        P(),
        P(),
    )
    out_specs = P("section", "rows", None, None)
    return jax.shard_map(
        on_device, mesh=mesh, in_specs=in_specs, out_specs=out_specs, check_vma=False
    )
```

```python
import functools

import functools

import jax
import jax.numpy as jnp
from jax import lax
from jax.experimental import pallas as pl
from jax.experimental.pallas import tpu as pltpu
from jax.sharding import PartitionSpec as P

GROUPS = 32
SPAN_HALO = 4

epsilon = 1e-06


def moments(blocks):
    cells = sum(block.shape[0] for block in blocks)
    total = sum(jnp.sum(block, axis=0, keepdims=True) for block in blocks)
    mean = total * (1.0 / cells)
    centred = sum(
        jnp.sum((block - mean) * (block - mean), axis=0, keepdims=True) for block in blocks
    )
    return jnp.concatenate([total, centred], axis=1)


def group_sum(values, width):
    lanes = values.shape[-1]
    lane = lax.broadcasted_iota(jnp.int32, values.shape, values.ndim - 1)
    step = 1
    while step < width:
        up = pltpu.roll(values, lanes - step, values.ndim - 1)
        down = pltpu.roll(values, step, values.ndim - 1)
        values = values + jnp.where((lane // step) % 2 == 0, up, down)
        step *= 2
    return values


def affine(stats, cells, scale, shift):
    channels = scale.shape[-1]
    width = channels // GROUPS
    totals, centred = stats[:, 0, :channels], stats[:, 0, channels:]
    count = cells * width * stats.shape[0]
    average = group_sum(jnp.sum(totals, axis=0, keepdims=True), width) * (1.0 / count)
    away = totals * (1.0 / cells) - average
    inner = jnp.sum(centred + cells * (away * away), axis=0, keepdims=True)
    spread = group_sum(inner, width) * (1.0 / count)
    slope = 0.5 * scale / jnp.sqrt(spread + epsilon)
    return slope, 0.5 * shift - average * slope


def activate(values, slope, offset):
    half = values.astype(jnp.float32) * slope + offset
    return half + half * jnp.tanh(half)


def pair_conv(field, row, frames, weight_ref):
    columns, channels = field.shape[2], field.shape[3]
    pieces, blocks = [], []
    nothing = jnp.zeros((channels, channels), jnp.bfloat16)
    for frame_tap in range(3):
        for line in range(4):
            piece = field[frame_tap : frame_tap + frames, row + line]
            pieces.append(piece.reshape(frames * columns, channels))
            blocks.append(
                jnp.concatenate(
                    [
                        weight_ref[frame_tap, line - out, col_tap]
                        if 0 <= line - out <= 2
                        else nothing
                        for col_tap in range(3)
                        for out in range(2)
                    ],
                    axis=1,
                )
            )
    product = jnp.dot(
        jnp.concatenate(pieces, axis=1),
        jnp.concatenate(blocks, axis=0),
        preferred_element_type=jnp.float32,
    )
    cells = frames * columns
    column = lax.broadcasted_iota(jnp.int32, (cells, channels), 0) % columns
    results = []
    for out in range(2):
        left, centre, right = (
            product[:, (2 * tap + out) * channels : (2 * tap + out + 1) * channels]
            for tap in range(3)
        )
        left = jnp.where(column == 0, 0.0, pltpu.roll(left, 1, 0))
        right = jnp.where(column == columns - 1, 0.0, pltpu.roll(right, cells - 1, 0))
        results.append(left + centre + right)
    return results


def stats_kernel(own_ref, stats_ref):
    own = own_ref[...].astype(jnp.float32)
    packed = moments([own.reshape(-1, own.shape[-1])])
    stats_ref[...] = jnp.broadcast_to(packed[None], stats_ref.shape)


def first_kernel(
    row_count, place, own_ref, near_ref, far_ref, stats_ref, scale_ref, shift_ref, weight_ref, bias_ref,
    middle_ref, sums_ref, field
):
    section, row_at = place[0], place[1]
    frames, lines, columns, channels = own_ref.shape
    inner = frames - SPAN_HALO
    cells = inner * lines * columns
    scale, shift = scale_ref[...], shift_ref[...]
    mine = stats_ref[pl.ds(section * row_count, row_count)]
    before = stats_ref[pl.ds(jnp.maximum(section - 1, 0) * row_count, row_count)]
    slope, offset = affine(mine, cells, scale, shift)
    slope_before, offset_before = affine(before, cells, scale, shift)
    even = row_at % 2 == 0
    at_start = section == 0
    for line in range(3 * lines):
        side, local = divmod(line, lines)
        if side == 1:
            block = own_ref[:, local]
        else:
            near_side = even if side == 2 else jnp.logical_not(even)
            block = jnp.where(near_side, near_ref[:, local], far_ref[:, local])
        halo, body = block[:SPAN_HALO], block[SPAN_HALO:]
        behind = activate(halo, slope_before, offset_before).astype(jnp.bfloat16)
        behind = jnp.where(at_start, halo, behind)
        ahead = activate(body, slope, offset).astype(jnp.bfloat16)
        if side != 1:
            outside = row_at == 0 if side == 0 else row_at == row_count - 1
            behind = jnp.where(outside, jnp.zeros_like(behind), behind)
            ahead = jnp.where(outside, jnp.zeros_like(ahead), ahead)
        field[:SPAN_HALO, line] = behind
        field[SPAN_HALO:, line] = ahead
    bias = bias_ref[...]
    kept = []
    spare = SPAN_HALO - 2
    for pair in range((lines + 2) // 2):
        results = pair_conv(field, 2 * pair, inner + 2, weight_ref)
        for out in range(2):
            line = 2 * pair + out
            rounded = (results[out] + bias).astype(jnp.bfloat16)
            rounded = rounded.reshape(inner + 2, columns, channels)
            middle_ref[:2, line] = jnp.where(at_start, field[:spare, line + lines - 1], rounded[:2])
            middle_ref[2:, line] = rounded[2:]
            if 1 <= line <= lines:
                kept.append(rounded[2:].astype(jnp.float32).reshape(-1, channels))
    sums_ref[...] = jnp.broadcast_to(moments(kept)[None], sums_ref.shape)


def second_kernel(
    row_count, place, middle_ref, stats_ref, scale_ref, shift_ref, weight_ref, bias_ref, own_ref,
    out_ref, field
):
    section, row_at = place[0], place[1]
    frames, lines, columns, channels = own_ref.shape
    cells = frames * lines * columns
    scale, shift = scale_ref[...], shift_ref[...]
    mine = stats_ref[pl.ds(section * row_count, row_count)]
    before = stats_ref[pl.ds(jnp.maximum(section - 1, 0) * row_count, row_count)]
    slope, offset = affine(mine, cells, scale, shift)
    slope_before, offset_before = affine(before, cells, scale, shift)
    at_start = section == 0
    for line in range(lines + 2):
        halo, body = middle_ref[:2, line], middle_ref[2:, line]
        behind = activate(halo, slope_before, offset_before).astype(jnp.bfloat16)
        behind = jnp.where(at_start, halo, behind)
        ahead = activate(body, slope, offset).astype(jnp.bfloat16)
        if line == 0 or line == lines + 1:
            outside = row_at == 0 if line == 0 else row_at == row_count - 1
            behind = jnp.where(outside, jnp.zeros_like(behind), behind)
            ahead = jnp.where(outside, jnp.zeros_like(ahead), ahead)
        field[:2, line] = behind
        field[2:, line] = ahead
    bias = bias_ref[...]
    for pair in range(lines // 2):
        results = pair_conv(field, 2 * pair, frames, weight_ref)
        for out in range(2):
            line = 2 * pair + out
            result = (results[out] + bias).reshape(frames, columns, channels)
            out_ref[:, line] = (result + own_ref[:, line].astype(jnp.float32)).astype(jnp.bfloat16)


def call(kernel, out_shape, scratch, operands, scalars=True, flops=0):
    specs = [pl.BlockSpec(memory_space=pltpu.VMEM)] * len(operands)
    if scalars:
        specs[0] = pl.BlockSpec(memory_space=pltpu.SMEM)
    return pl.pallas_call(
        kernel,
        out_shape=out_shape,
        in_specs=specs,
        out_specs=jax.tree.map(lambda _: pl.BlockSpec(memory_space=pltpu.VMEM), out_shape),
        scratch_shapes=scratch,
        compiler_params=pltpu.CompilerParams(vmem_limit_bytes=40 * 2**20),
        cost_estimate=pl.CostEstimate(flops=flops, bytes_accessed=2**20, transcendentals=0),
    )(*operands)


def on_device(
    activations,
    first_cache,
    second_cache,
    norm1_scale,
    norm1_shift,
    conv1_weight,
    conv1_bias,
    norm2_scale,
    norm2_shift,
    conv2_weight,
    conv2_bias,
):
    frames, lines, columns, channels = activations.shape
    sections, row_count = lax.axis_size("section"), lax.axis_size("rows")
    everyone = sections * row_count
    section, row_at = lax.axis_index("section"), lax.axis_index("rows")
    place = jnp.stack([section, row_at]).astype(jnp.int32)
    stats_shape = jax.ShapeDtypeStruct((everyone, 1, 2 * channels), jnp.float32)

    def flat(vector):
        return vector.reshape(1, channels)

    def exchange(stats):
        return lax.all_to_all(stats, ("section", "rows"), 0, 0, tiled=True)

    ring = [(i, (i + 1) % sections) for i in range(sections)]
    near = [(i, i ^ 1) for i in range(row_count)]
    far = [(0, 0)] + [(i, i + 1 if i % 2 else i - 1) for i in range(1, row_count - 1)]
    far = far + [(row_count - 1, row_count - 1)]

    received = lax.ppermute(activations[-SPAN_HALO:], "section", ring)
    sums = call(stats_kernel, stats_shape, [], (activations,), scalars=False)
    caches = jnp.concatenate([second_cache, first_cache], axis=0)
    halo = jnp.where(section == 0, caches, received)
    own = jnp.concatenate([halo, activations], axis=0)
    own, sums = lax.optimization_barrier((own, sums))
    from_near = lax.ppermute(own, "rows", near)
    from_far = lax.ppermute(own, "rows", far)
    stats = exchange(sums)
    middle, sums_two = call(
        functools.partial(first_kernel, row_count),
        (
            jax.ShapeDtypeStruct((frames + 2, lines + 2, columns, channels), jnp.bfloat16),
            stats_shape,
        ),
        [pltpu.VMEM((frames + SPAN_HALO, 3 * lines, columns, channels), jnp.bfloat16)],
        (
            place, own, from_near, from_far, stats, flat(norm1_scale), flat(norm1_shift),
            conv1_weight, flat(conv1_bias),
        ),
        flops=10**9,
    )
    stats_two = exchange(sums_two)
    return call(
        functools.partial(second_kernel, row_count),
        jax.ShapeDtypeStruct(activations.shape, jnp.bfloat16),
        [pltpu.VMEM((frames + 2, lines + 2, columns, channels), jnp.bfloat16)],
        (
            place, middle, stats_two, flat(norm2_scale), flat(norm2_shift), conv2_weight,
            flat(conv2_bias), activations,
        ),
        flops=10**9,
    )


def solution(mesh):
    in_specs = (
        P("section", "rows", None, None),
        P(None, "rows", None, None),
        P(None, "rows", None, None),
        P(),
        P(),
        P(),
        P(),
        P(),
        P(),
        P(),
        P(),
    )
    out_specs = P("section", "rows", None, None)
    return jax.shard_map(
        on_device, mesh=mesh, in_specs=in_specs, out_specs=out_specs, check_vma=False
    )
```

```python
import functools

import functools

import jax
import jax.numpy as jnp
from jax import lax
from jax.experimental import pallas as pl
from jax.experimental.pallas import tpu as pltpu
from jax.sharding import PartitionSpec as P

GROUPS = 32
SPAN_HALO = 4

epsilon = 1e-06


def group_sum(values, width):
    lanes = values.shape[-1]
    lane = lax.broadcasted_iota(jnp.int32, values.shape, values.ndim - 1)
    step = 1
    while step < width:
        up = pltpu.roll(values, lanes - step, values.ndim - 1)
        down = pltpu.roll(values, step, values.ndim - 1)
        values = values + jnp.where((lane // step) % 2 == 0, up, down)
        step *= 2
    return values


def moments(blocks):
    channels = blocks[0].shape[1]
    width = channels // GROUPS
    cells = sum(block.shape[0] for block in blocks) * width
    total = group_sum(sum(jnp.sum(block, axis=0, keepdims=True) for block in blocks), width)
    mean = total * (1.0 / cells)
    centred = group_sum(
        sum(jnp.sum((block - mean) * (block - mean), axis=0, keepdims=True) for block in blocks),
        width,
    )
    lane = lax.broadcasted_iota(jnp.int32, total.shape, 1)
    return jnp.where(lane % width == 0, total, centred)


def affine(stats, cells, scale, shift):
    devices, _, channels = stats.shape
    width = channels // GROUPS
    stats = stats.reshape(devices, channels)
    lane = lax.broadcasted_iota(jnp.int32, stats.shape, 1) % width
    totals = group_sum(jnp.where(lane == 0, stats, 0.0), width)
    centred = group_sum(jnp.where(lane == 1, stats, 0.0), width)
    cells = cells * width
    average = jnp.sum(totals, axis=0, keepdims=True) * (1.0 / (cells * devices))
    away = totals * (1.0 / cells) - average
    inner = jnp.sum(centred + cells * (away * away), axis=0, keepdims=True)
    slope = 0.5 * scale / jnp.sqrt(inner * (1.0 / (cells * devices)) + epsilon)
    return slope, 0.5 * shift - average * slope


def activate(values, slope, offset):
    half = values.astype(jnp.float32) * slope + offset
    return half + half * jnp.tanh(half)


def pair_conv(field, row, frames, weight_ref):
    columns, channels = field.shape[2], field.shape[3]
    pieces, blocks = [], []
    nothing = jnp.zeros((channels, channels), jnp.bfloat16)
    for frame_tap in range(3):
        for line in range(4):
            piece = field[frame_tap : frame_tap + frames, row + line]
            pieces.append(piece.reshape(frames * columns, channels))
            blocks.append(
                jnp.concatenate(
                    [
                        weight_ref[frame_tap, line - out, col_tap]
                        if 0 <= line - out <= 2
                        else nothing
                        for col_tap in range(3)
                        for out in range(2)
                    ],
                    axis=1,
                )
            )
    product = jnp.dot(
        jnp.concatenate(pieces, axis=1),
        jnp.concatenate(blocks, axis=0),
        preferred_element_type=jnp.float32,
    )
    cells = frames * columns
    column = lax.broadcasted_iota(jnp.int32, (cells, channels), 0) % columns
    results = []
    for out in range(2):
        left, centre, right = (
            product[:, (2 * tap + out) * channels : (2 * tap + out + 1) * channels]
            for tap in range(3)
        )
        left = jnp.where(column == 0, 0.0, pltpu.roll(left, 1, 0))
        right = jnp.where(column == columns - 1, 0.0, pltpu.roll(right, cells - 1, 0))
        results.append(left + centre + right)
    return results


def prepare_kernel(
    place, own_ref, second_cache_ref, first_cache_ref, *rest
):
    *vector_refs, stats_ref, halo_ref, vectors_ref, copied, sems = rest
    last = place[0] == place[2] - 1
    frames = own_ref.shape[0]
    load = pltpu.make_async_copy(own_ref, copied, sems.at[0])
    load.start()
    tail = pltpu.make_async_copy(own_ref.at[frames - SPAN_HALO :], halo_ref, sems.at[1])
    spare = SPAN_HALO - 2
    older = pltpu.make_async_copy(second_cache_ref, halo_ref.at[:spare], sems.at[2])
    newer = pltpu.make_async_copy(first_cache_ref, halo_ref.at[spare:], sems.at[3])

    @pl.when(last)
    def _():
        older.start()
        newer.start()

    @pl.when(jnp.logical_not(last))
    def _():
        tail.start()

    vector_loads = [
        pltpu.make_async_copy(vector_ref, vectors_ref.at[index], sems.at[4 + index])
        for index, vector_ref in enumerate(vector_refs)
    ]
    for vector_load in vector_loads:
        vector_load.start()
    load.wait()
    own = copied[...].astype(jnp.float32)
    packed = moments([own.reshape(-1, own.shape[-1])])
    stats_ref[...] = jnp.broadcast_to(packed[None], stats_ref.shape)

    for vector_load in vector_loads:
        vector_load.wait()

    @pl.when(last)
    def _():
        older.wait()
        newer.wait()

    @pl.when(jnp.logical_not(last))
    def _():
        tail.wait()


def first_kernel(
    row_count, place, own_ref, near_ref, far_ref, halo_ref, halo_near_ref, halo_far_ref,
    stats_ref, vectors_ref, far_weight_ref, middle_ref, sums_ref, field, weight_ref, sem
):
    load = pltpu.make_async_copy(far_weight_ref, weight_ref, sem)
    load.start()
    section, row_at = place[0], place[1]
    inner, lines, columns, channels = own_ref.shape
    cells = inner * lines * columns
    scale, shift = vectors_ref[0], vectors_ref[1]
    mine = stats_ref[pl.ds(section * row_count, row_count)]
    before = stats_ref[pl.ds(jnp.maximum(section - 1, 0) * row_count, row_count)]
    slope, offset = affine(mine, cells, scale, shift)
    slope_before, offset_before = affine(before, cells, scale, shift)
    even = row_at % 2 == 0
    at_start = section == 0
    for line in range(3 * lines):
        side, local = divmod(line, lines)
        if side == 1:
            halo, body = halo_ref[:, local], own_ref[:, local]
        else:
            near_side = even if side == 2 else jnp.logical_not(even)
            halo = jnp.where(near_side, halo_near_ref[:, local], halo_far_ref[:, local])
            body = jnp.where(near_side, near_ref[:, local], far_ref[:, local])
        behind = activate(halo, slope_before, offset_before).astype(jnp.bfloat16)
        behind = jnp.where(at_start, halo, behind)
        ahead = activate(body, slope, offset).astype(jnp.bfloat16)
        if side != 1:
            outside = row_at == 0 if side == 0 else row_at == row_count - 1
            behind = jnp.where(outside, jnp.zeros_like(behind), behind)
            ahead = jnp.where(outside, jnp.zeros_like(ahead), ahead)
        field[:SPAN_HALO, line] = behind
        field[SPAN_HALO:, line] = ahead
    load.wait()
    bias = vectors_ref[2]
    kept = []
    spare = SPAN_HALO - 2
    for pair in range((lines + 2) // 2):
        results = pair_conv(field, 2 * pair, inner + 2, weight_ref)
        for out in range(2):
            line = 2 * pair + out
            rounded = (results[out] + bias).astype(jnp.bfloat16)
            rounded = rounded.reshape(inner + 2, columns, channels)
            middle_ref[:2, line] = jnp.where(at_start, field[:spare, line + lines - 1], rounded[:2])
            middle_ref[2:, line] = rounded[2:]
            if 1 <= line <= lines:
                kept.append(rounded[2:].astype(jnp.float32).reshape(-1, channels))
    sums_ref[...] = jnp.broadcast_to(moments(kept)[None], sums_ref.shape)


def second_kernel(
    row_count, place, middle_ref, stats_ref, vectors_ref, far_weight_ref, own_ref, out_ref,
    field, weight_ref, sem
):
    load = pltpu.make_async_copy(far_weight_ref, weight_ref, sem)
    load.start()
    section, row_at = place[0], place[1]
    frames, lines, columns, channels = own_ref.shape
    cells = frames * lines * columns
    scale, shift = vectors_ref[3], vectors_ref[4]
    mine = stats_ref[pl.ds(section * row_count, row_count)]
    before = stats_ref[pl.ds(jnp.maximum(section - 1, 0) * row_count, row_count)]
    slope, offset = affine(mine, cells, scale, shift)
    slope_before, offset_before = affine(before, cells, scale, shift)
    at_start = section == 0
    for line in range(lines + 2):
        halo, body = middle_ref[:2, line], middle_ref[2:, line]
        behind = activate(halo, slope_before, offset_before).astype(jnp.bfloat16)
        behind = jnp.where(at_start, halo, behind)
        ahead = activate(body, slope, offset).astype(jnp.bfloat16)
        if line == 0 or line == lines + 1:
            outside = row_at == 0 if line == 0 else row_at == row_count - 1
            behind = jnp.where(outside, jnp.zeros_like(behind), behind)
            ahead = jnp.where(outside, jnp.zeros_like(ahead), ahead)
        field[:2, line] = behind
        field[2:, line] = ahead
    load.wait()
    bias = vectors_ref[5]
    for pair in range(lines // 2):
        results = pair_conv(field, 2 * pair, frames, weight_ref)
        for out in range(2):
            line = 2 * pair + out
            result = (results[out] + bias).reshape(frames, columns, channels)
            out_ref[:, line] = (result + own_ref[:, line].astype(jnp.float32)).astype(jnp.bfloat16)


def call(kernel, out_shape, scratch, operands, in_place=(), flops=0):
    vmem = pl.BlockSpec(memory_space=pltpu.VMEM)
    specs = [pl.BlockSpec(memory_space=pltpu.SMEM)] + [vmem] * (len(operands) - 1)
    for index in in_place:
        specs[index] = pl.BlockSpec(memory_space=pltpu.HBM)
    operands = [
        pltpu.with_memory_space_constraint(operand, pltpu.HBM) if index in in_place else operand
        for index, operand in enumerate(operands)
    ]
    return pl.pallas_call(
        kernel,
        out_shape=out_shape,
        in_specs=specs,
        out_specs=jax.tree.map(lambda _: vmem, out_shape),
        scratch_shapes=scratch,
        compiler_params=pltpu.CompilerParams(vmem_limit_bytes=40 * 2**20),
        cost_estimate=pl.CostEstimate(flops=flops, bytes_accessed=2**20, transcendentals=0),
    )(*operands)


def on_device(
    activations,
    first_cache,
    second_cache,
    norm1_scale,
    norm1_shift,
    conv1_weight,
    conv1_bias,
    norm2_scale,
    norm2_shift,
    conv2_weight,
    conv2_bias,
):
    frames, lines, columns, channels = activations.shape
    sections, row_count = lax.axis_size("section"), lax.axis_size("rows")
    everyone = sections * row_count
    section, row_at = lax.axis_index("section"), lax.axis_index("rows")
    place = jnp.stack([section, row_at, jnp.int32(sections)]).astype(jnp.int32)
    stats_shape = jax.ShapeDtypeStruct((everyone, 1, channels), jnp.float32)
    vectors = (norm1_scale, norm1_shift, conv1_bias, norm2_scale, norm2_shift, conv2_bias)

    def exchange(stats):
        return lax.all_to_all(stats, ("section", "rows"), 0, 0, tiled=True)

    weight_scratch = [
        pltpu.VMEM(conv1_weight.shape, jnp.bfloat16), pltpu.SemaphoreType.DMA
    ]
    near = [i ^ 1 for i in range(row_count)]
    far = [0] + [i + 1 if i % 2 else i - 1 for i in range(1, row_count - 1)] + [row_count - 1]

    def across(block, partner):
        return lax.ppermute(block, "rows", list(enumerate(partner)))

    def onward(block, partner):
        route = [
            (at * row_count + row, (at + 1) % sections * row_count + partner[row])
            for at in range(sections)
            for row in range(row_count)
        ]
        return lax.ppermute(block, ("section", "rows"), route)

    sums, halo, packed, own = call(
        prepare_kernel,
        (
            stats_shape,
            jax.ShapeDtypeStruct((SPAN_HALO, lines, columns, channels), jnp.bfloat16),
            jax.ShapeDtypeStruct((len(vectors), 1, channels), jnp.float32),
            jax.ShapeDtypeStruct(activations.shape, jnp.bfloat16),
        ),
        [pltpu.SemaphoreType.DMA((4 + len(vectors),))],
        (place, activations, second_cache, first_cache)
        + tuple(vector.reshape(1, channels) for vector in vectors),
        in_place=range(1, 4 + len(vectors)),
    )
    beside = [across(activations, near), across(activations, far)]
    behind = [onward(halo, partner) for partner in (range(row_count), near, far)]
    stats = exchange(sums)
    middle, sums_two = call(
        functools.partial(first_kernel, row_count),
        (
            jax.ShapeDtypeStruct((frames + 2, lines + 2, columns, channels), jnp.bfloat16),
            stats_shape,
        ),
        [pltpu.VMEM((frames + SPAN_HALO, 3 * lines, columns, channels), jnp.bfloat16)]
        + weight_scratch,
        (place, own, *beside, *behind, stats, packed, conv1_weight),
        in_place=(9,),
        flops=10**9,
    )
    stats_two = exchange(sums_two)
    return call(
        functools.partial(second_kernel, row_count),
        jax.ShapeDtypeStruct(activations.shape, jnp.bfloat16),
        [pltpu.VMEM((frames + 2, lines + 2, columns, channels), jnp.bfloat16)]
        + weight_scratch,
        (place, middle, stats_two, packed, conv2_weight, own),
        in_place=(4,),
        flops=10**9,
    )


def solution(mesh):
    in_specs = (
        P("section", "rows", None, None),
        P(None, "rows", None, None),
        P(None, "rows", None, None),
        P(),
        P(),
        P(),
        P(),
        P(),
        P(),
        P(),
        P(),
    )
    out_specs = P("section", "rows", None, None)
    return jax.shard_map(
        on_device, mesh=mesh, in_specs=in_specs, out_specs=out_specs, check_vma=False
    )
```

```python
import functools
import itertools

import functools
import itertools

import jax
import jax.numpy as jnp
from jax import lax
from jax.experimental import pallas as pl
from jax.experimental.pallas import tpu as pltpu
from jax.sharding import PartitionSpec as P

GROUPS = 32
SPAN_HALO = 4
PARTS = 4

epsilon = 1e-06


def group_sum(values, width):
    lanes = values.shape[-1]
    lane = lax.broadcasted_iota(jnp.int32, values.shape, values.ndim - 1)
    step = 1
    while step < width:
        up = pltpu.roll(values, lanes - step, values.ndim - 1)
        down = pltpu.roll(values, step, values.ndim - 1)
        values = values + jnp.where((lane // step) % 2 == 0, up, down)
        step *= 2
    return values


def moments(blocks):
    first = next(blocks)
    pivot = jnp.sum(first, axis=0, keepdims=True) * (1.0 / first.shape[0])
    cells, total, squares = 0, 0.0, 0.0
    for block in itertools.chain([first], blocks):
        away = block - pivot
        cells += block.shape[0]
        total = total + jnp.sum(away, axis=0, keepdims=True)
        squares = squares + jnp.sum(away * away, axis=0, keepdims=True)
    shift = total * (1.0 / cells)
    return jnp.concatenate([(pivot + shift) * cells, squares - total * shift], axis=1)


def affine(stats, cells, scale, shift):
    devices, channels = stats.shape[0], scale.shape[-1]
    width = channels // GROUPS
    totals, centred = stats[:, :channels], stats[:, channels:]
    count = cells * width * devices
    average = group_sum(jnp.sum(totals, axis=0, keepdims=True), width) * (1.0 / count)
    away = totals * (1.0 / cells) - average
    inner = jnp.sum(centred + cells * (away * away), axis=0, keepdims=True)
    spread = group_sum(inner, width) * (1.0 / count)
    slope = 0.5 * scale / jnp.sqrt(spread + epsilon)
    return slope, 0.5 * shift - average * slope


def activate(values, slope, offset):
    half = values.astype(jnp.float32) * slope + offset
    return half + half * jnp.tanh(half)


def pair_conv(field, row, frames, weight_ref):
    columns, channels = field.shape[2], field.shape[3]
    pieces, blocks = [], []
    nothing = jnp.zeros((channels, channels), jnp.bfloat16)
    for frame_tap in range(3):
        for line in range(4):
            piece = field[frame_tap : frame_tap + frames, row + line]
            pieces.append(piece.reshape(frames * columns, channels))
            blocks.append(
                jnp.concatenate(
                    [
                        weight_ref[frame_tap, line - out, col_tap]
                        if 0 <= line - out <= 2
                        else nothing
                        for col_tap in range(3)
                        for out in range(2)
                    ],
                    axis=1,
                )
            )
    product = jnp.dot(
        jnp.concatenate(pieces, axis=1),
        jnp.concatenate(blocks, axis=0),
        preferred_element_type=jnp.float32,
    )
    cells = frames * columns
    column = lax.broadcasted_iota(jnp.int32, (cells, channels), 0) % columns
    results = []
    for out in range(2):
        left, centre, right = (
            product[:, (2 * tap + out) * channels : (2 * tap + out + 1) * channels]
            for tap in range(3)
        )
        left = jnp.where(column == 0, 0.0, pltpu.roll(left, 1, 0))
        right = jnp.where(column == columns - 1, 0.0, pltpu.roll(right, cells - 1, 0))
        results.append(left + centre + right)
    return results


def prepare_kernel(
    place, own_ref, second_cache_ref, first_cache_ref, weight_ref, *rest
):
    *vector_refs, stats_ref, halo_ref, vectors_ref, copied, weight_copy, sems = rest
    last = place[0] == place[2] - 1
    frames = own_ref.shape[0]
    part = frames // PARTS
    loads = [
        pltpu.make_async_copy(
            own_ref.at[pl.ds(index * part, part)],
            copied.at[pl.ds(index * part, part)],
            sems.at[3 + index],
        )
        for index in range(PARTS)
    ]
    for load in loads:
        load.start()
    tail = pltpu.make_async_copy(own_ref.at[frames - SPAN_HALO :], halo_ref, sems.at[0])
    spare = SPAN_HALO - 2
    older = pltpu.make_async_copy(second_cache_ref, halo_ref.at[:spare], sems.at[1])
    newer = pltpu.make_async_copy(first_cache_ref, halo_ref.at[spare:], sems.at[2])

    @pl.when(last)
    def _():
        older.start()
        newer.start()

    @pl.when(jnp.logical_not(last))
    def _():
        tail.start()

    late_loads = [
        pltpu.make_async_copy(vector_ref, vectors_ref.at[index], sems.at[3 + PARTS + index])
        for index, vector_ref in enumerate(vector_refs)
    ]
    late_loads.append(
        pltpu.make_async_copy(weight_ref, weight_copy, sems.at[3 + PARTS + len(vector_refs)])
    )
    for late_load in late_loads:
        late_load.start()

    def arriving():
        for index, load in enumerate(loads):
            load.wait()
            block = copied[index * part : (index + 1) * part].astype(jnp.float32)
            yield block.reshape(-1, block.shape[-1])

    stats_ref[...] = moments(arriving())
    for late_load in late_loads:
        late_load.wait()

    @pl.when(last)
    def _():
        older.wait()
        newer.wait()

    @pl.when(jnp.logical_not(last))
    def _():
        tail.wait()


def first_kernel(
    row_count, place, own_ref, near_ref, far_ref, halo_ref, halo_near_ref, halo_far_ref,
    stats_ref, vectors_ref, weight_ref, middle_ref, sums_ref, field
):
    section, row_at = place[0], place[1]
    inner, lines, columns, channels = own_ref.shape
    cells = inner * lines * columns
    scale, shift = vectors_ref[0], vectors_ref[1]
    mine, before = stats_ref[:, 0], stats_ref[:, 1]
    slope, offset = affine(mine, cells, scale, shift)
    slope_before, offset_before = affine(before, cells, scale, shift)
    even = row_at % 2 == 0
    at_start = section == 0
    for line in range(3 * lines):
        side, local = divmod(line, lines)
        if side == 1:
            halo, body = halo_ref[:, local], own_ref[:, local]
        else:
            near_side = even if side == 2 else jnp.logical_not(even)
            halo = jnp.where(near_side, halo_near_ref[:, local], halo_far_ref[:, local])
            body = jnp.where(near_side, near_ref[:, local], far_ref[:, local])
        behind = activate(halo, slope_before, offset_before).astype(jnp.bfloat16)
        behind = jnp.where(at_start, halo, behind)
        ahead = activate(body, slope, offset).astype(jnp.bfloat16)
        if side != 1:
            outside = row_at == 0 if side == 0 else row_at == row_count - 1
            behind = jnp.where(outside, jnp.zeros_like(behind), behind)
            ahead = jnp.where(outside, jnp.zeros_like(ahead), ahead)
        field[:SPAN_HALO, line] = behind
        field[SPAN_HALO:, line] = ahead
    bias = vectors_ref[2]
    kept = []
    spare = SPAN_HALO - 2
    for pair in range((lines + 2) // 2):
        results = pair_conv(field, 2 * pair, inner + 2, weight_ref)
        for out in range(2):
            line = 2 * pair + out
            rounded = (results[out] + bias).astype(jnp.bfloat16)
            rounded = rounded.reshape(inner + 2, columns, channels)
            middle_ref[:2, line] = jnp.where(at_start, field[:spare, line + lines - 1], rounded[:2])
            middle_ref[2:, line] = rounded[2:]
            if 1 <= line <= lines:
                kept.append(rounded[2:].astype(jnp.float32).reshape(-1, channels))
    sums_ref[...] = jnp.broadcast_to(moments(iter(kept))[None], sums_ref.shape)


def second_kernel(
    row_count, place, middle_ref, stats_ref, vectors_ref, weight_ref, own_ref, out_ref, field
):
    section, row_at = place[0], place[1]
    frames, lines, columns, channels = own_ref.shape
    cells = frames * lines * columns
    scale, shift = vectors_ref[3], vectors_ref[4]
    mine = stats_ref[pl.ds(section * row_count, row_count), 0]
    before = stats_ref[pl.ds(jnp.maximum(section - 1, 0) * row_count, row_count), 0]
    slope, offset = affine(mine, cells, scale, shift)
    slope_before, offset_before = affine(before, cells, scale, shift)
    at_start = section == 0
    for line in range(lines + 2):
        halo, body = middle_ref[:2, line], middle_ref[2:, line]
        behind = activate(halo, slope_before, offset_before).astype(jnp.bfloat16)
        behind = jnp.where(at_start, halo, behind)
        ahead = activate(body, slope, offset).astype(jnp.bfloat16)
        if line == 0 or line == lines + 1:
            outside = row_at == 0 if line == 0 else row_at == row_count - 1
            behind = jnp.where(outside, jnp.zeros_like(behind), behind)
            ahead = jnp.where(outside, jnp.zeros_like(ahead), ahead)
        field[:2, line] = behind
        field[2:, line] = ahead
    bias = vectors_ref[5]
    for pair in range(lines // 2):
        results = pair_conv(field, 2 * pair, frames, weight_ref)
        for out in range(2):
            line = 2 * pair + out
            result = (results[out] + bias).reshape(frames, columns, channels)
            out_ref[:, line] = (result + own_ref[:, line].astype(jnp.float32)).astype(jnp.bfloat16)


def call(kernel, out_shape, scratch, operands, in_place=(), flops=0):
    vmem = pl.BlockSpec(memory_space=pltpu.VMEM)
    specs = [pl.BlockSpec(memory_space=pltpu.SMEM)] + [vmem] * (len(operands) - 1)
    for index in in_place:
        specs[index] = pl.BlockSpec(memory_space=pltpu.HBM)
    operands = [
        pltpu.with_memory_space_constraint(operand, pltpu.HBM) if index in in_place else operand
        for index, operand in enumerate(operands)
    ]
    return pl.pallas_call(
        kernel,
        out_shape=out_shape,
        in_specs=specs,
        out_specs=jax.tree.map(lambda _: vmem, out_shape),
        scratch_shapes=scratch,
        compiler_params=pltpu.CompilerParams(vmem_limit_bytes=40 * 2**20),
        cost_estimate=pl.CostEstimate(flops=flops, bytes_accessed=2**20, transcendentals=0),
    )(*operands)


def on_device(
    activations,
    first_cache,
    second_cache,
    norm1_scale,
    norm1_shift,
    conv1_weight,
    conv1_bias,
    norm2_scale,
    norm2_shift,
    conv2_weight,
    conv2_bias,
):
    frames, lines, columns, channels = activations.shape
    sections, row_count = lax.axis_size("section"), lax.axis_size("rows")
    everyone = sections * row_count
    section, row_at = lax.axis_index("section"), lax.axis_index("rows")
    place = jnp.stack([section, row_at, jnp.int32(sections)]).astype(jnp.int32)
    stats_shape = jax.ShapeDtypeStruct((everyone, 1, 2 * channels), jnp.float32)
    vectors = (norm1_scale, norm1_shift, conv1_bias, norm2_scale, norm2_shift, conv2_bias)

    near = [i ^ 1 for i in range(row_count)]
    far = [0] + [i + 1 if i % 2 else i - 1 for i in range(1, row_count - 1)] + [row_count - 1]

    def across(block, partner):
        return lax.ppermute(block, "rows", list(enumerate(partner)))

    def onward(block, partner):
        route = [
            (at * row_count + row, (at + 1) % sections * row_count + partner[row])
            for at in range(sections)
            for row in range(row_count)
        ]
        return lax.ppermute(block, ("section", "rows"), route)

    sums, halo, packed, own, weight = call(
        prepare_kernel,
        (
            jax.ShapeDtypeStruct((1, 2 * channels), jnp.float32),
            jax.ShapeDtypeStruct((SPAN_HALO, lines, columns, channels), jnp.bfloat16),
            jax.ShapeDtypeStruct((len(vectors), 1, channels), jnp.float32),
            jax.ShapeDtypeStruct(activations.shape, jnp.bfloat16),
            jax.ShapeDtypeStruct(conv1_weight.shape, jnp.bfloat16),
        ),
        [pltpu.SemaphoreType.DMA((4 + PARTS + len(vectors),))],
        (place, activations, second_cache, first_cache, conv1_weight)
        + tuple(vector.reshape(1, channels) for vector in vectors),
        in_place=range(1, 5 + len(vectors)),
    )
    beside = [across(activations, near), across(activations, far)]
    behind = [onward(halo, partner) for partner in (range(row_count), near, far)]
    ring = [(at, (at + 1) % sections) for at in range(sections)]
    both = jnp.stack([sums, lax.ppermute(sums, "section", ring)], axis=1)
    both = jnp.broadcast_to(both, (row_count,) + both.shape[1:])
    stats = lax.all_to_all(both, "rows", 0, 0, tiled=True)
    middle, sums_two = call(
        functools.partial(first_kernel, row_count),
        (
            jax.ShapeDtypeStruct((frames + 2, lines + 2, columns, channels), jnp.bfloat16),
            stats_shape,
        ),
        [pltpu.VMEM((frames + SPAN_HALO, 3 * lines, columns, channels), jnp.bfloat16)],
        (place, own, *beside, *behind, stats, packed, weight),
        flops=10**9,
    )
    stats_two = lax.all_to_all(sums_two, ("section", "rows"), 0, 0, tiled=True)
    return call(
        functools.partial(second_kernel, row_count),
        jax.ShapeDtypeStruct(activations.shape, jnp.bfloat16),
        [pltpu.VMEM((frames + 2, lines + 2, columns, channels), jnp.bfloat16)],
        (place, middle, stats_two, packed, conv2_weight, own),
        flops=10**9,
    )


def solution(mesh):
    in_specs = (
        P("section", "rows", None, None),
        P(None, "rows", None, None),
        P(None, "rows", None, None),
        P(),
        P(),
        P(),
        P(),
        P(),
        P(),
        P(),
        P(),
    )
    out_specs = P("section", "rows", None, None)
    return jax.shard_map(
        on_device, mesh=mesh, in_specs=in_specs, out_specs=out_specs, check_vma=False
    )
```

```python
import functools
import itertools

import functools
import itertools

import jax
import jax.numpy as jnp
from jax import lax
from jax.experimental import pallas as pl
from jax.experimental.pallas import tpu as pltpu
from jax.sharding import PartitionSpec as P

GROUPS = 32
SPAN_HALO = 4
PARTS = 4

epsilon = 1e-06


def group_sum(values, width):
    lanes = values.shape[-1]
    lane = lax.broadcasted_iota(jnp.int32, values.shape, values.ndim - 1)
    step = 1
    while step < width:
        up = pltpu.roll(values, lanes - step, values.ndim - 1)
        down = pltpu.roll(values, step, values.ndim - 1)
        values = values + jnp.where((lane // step) % 2 == 0, up, down)
        step *= 2
    return values


def moments(blocks):
    first = next(blocks)
    pivot = jnp.sum(first, axis=0, keepdims=True) * (1.0 / first.shape[0])
    cells, total, squares = 0, 0.0, 0.0
    for block in itertools.chain([first], blocks):
        away = block - pivot
        cells += block.shape[0]
        total = total + jnp.sum(away, axis=0, keepdims=True)
        squares = squares + jnp.sum(away * away, axis=0, keepdims=True)
    shift = total * (1.0 / cells)
    return jnp.concatenate([(pivot + shift) * cells, squares - total * shift], axis=1)


def affine(stats, cells, scale, shift):
    devices, channels = stats.shape[0], scale.shape[-1]
    width = channels // GROUPS
    totals, centred = stats[:, :channels], stats[:, channels:]
    count = cells * width * devices
    average = group_sum(jnp.sum(totals, axis=0, keepdims=True), width) * (1.0 / count)
    away = totals * (1.0 / cells) - average
    inner = jnp.sum(centred + cells * (away * away), axis=0, keepdims=True)
    spread = group_sum(inner, width) * (1.0 / count)
    slope = 0.5 * scale / jnp.sqrt(spread + epsilon)
    return slope, 0.5 * shift - average * slope


def activate(values, slope, offset):
    half = values.astype(jnp.float32) * slope + offset
    return half + half * jnp.tanh(half)


def pair_conv(field, row, frames, weight_ref):
    columns, channels = field.shape[2], field.shape[3]
    pieces, blocks = [], []
    nothing = jnp.zeros((channels, channels), jnp.bfloat16)
    for frame_tap in range(3):
        for line in range(4):
            piece = field[frame_tap : frame_tap + frames, row + line]
            pieces.append(piece.reshape(frames * columns, channels))
            blocks.append(
                jnp.concatenate(
                    [
                        weight_ref[frame_tap, line - out, col_tap]
                        if 0 <= line - out <= 2
                        else nothing
                        for col_tap in range(3)
                        for out in range(2)
                    ],
                    axis=1,
                )
            )
    product = jnp.dot(
        jnp.concatenate(pieces, axis=1),
        jnp.concatenate(blocks, axis=0),
        preferred_element_type=jnp.float32,
    )
    cells = frames * columns
    column = lax.broadcasted_iota(jnp.int32, (cells, channels), 0) % columns
    results = []
    for out in range(2):
        left, centre, right = (
            product[:, (2 * tap + out) * channels : (2 * tap + out + 1) * channels]
            for tap in range(3)
        )
        left = jnp.where(column == 0, 0.0, pltpu.roll(left, 1, 0))
        right = jnp.where(column == columns - 1, 0.0, pltpu.roll(right, cells - 1, 0))
        results.append(left + centre + right)
    return results


def prepare_kernel(
    place, own_ref, second_cache_ref, first_cache_ref, weight_ref, *rest
):
    *vector_refs, stats_ref, halo_ref, vectors_ref, copied, weight_copy, sems = rest
    last = place[0] == place[2] - 1
    frames = own_ref.shape[0]
    part = frames // PARTS
    loads = [
        pltpu.make_async_copy(
            own_ref.at[pl.ds(index * part, part)],
            copied.at[pl.ds(index * part, part)],
            sems.at[3 + index],
        )
        for index in range(PARTS)
    ]
    for load in loads:
        load.start()
    tail = pltpu.make_async_copy(own_ref.at[frames - SPAN_HALO :], halo_ref, sems.at[0])
    spare = SPAN_HALO - 2
    older = pltpu.make_async_copy(second_cache_ref, halo_ref.at[:spare], sems.at[1])
    newer = pltpu.make_async_copy(first_cache_ref, halo_ref.at[spare:], sems.at[2])

    @pl.when(last)
    def _():
        older.start()
        newer.start()

    @pl.when(jnp.logical_not(last))
    def _():
        tail.start()

    late_loads = [
        pltpu.make_async_copy(vector_ref, vectors_ref.at[index], sems.at[3 + PARTS + index])
        for index, vector_ref in enumerate(vector_refs)
    ]
    late_loads.append(
        pltpu.make_async_copy(weight_ref, weight_copy, sems.at[3 + PARTS + len(vector_refs)])
    )
    for late_load in late_loads:
        late_load.start()

    def arriving():
        for index, load in enumerate(loads):
            load.wait()
            block = copied[index * part : (index + 1) * part].astype(jnp.float32)
            yield block.reshape(-1, block.shape[-1])

    stats_ref[...] = moments(arriving())
    for late_load in late_loads:
        late_load.wait()

    @pl.when(last)
    def _():
        older.wait()
        newer.wait()

    @pl.when(jnp.logical_not(last))
    def _():
        tail.wait()


def first_kernel(
    row_count, place, own_ref, near_ref, far_ref, halo_ref, halo_near_ref, halo_far_ref,
    stats_ref, vectors_ref, weight_ref, middle_ref, sums_ref, field
):
    section, row_at = place[0], place[1]
    inner, lines, columns, channels = own_ref.shape
    cells = inner * lines * columns
    scale, shift = vectors_ref[0], vectors_ref[1]
    mine, before = stats_ref[:, 0], stats_ref[:, 1]
    slope, offset = affine(mine, cells, scale, shift)
    slope_before, offset_before = affine(before, cells, scale, shift)
    even = row_at % 2 == 0
    at_start = section == 0
    for line in range(3 * lines):
        side, local = divmod(line, lines)
        if side == 1:
            halo, body = halo_ref[:, local], own_ref[:, local]
        else:
            near_side = even if side == 2 else jnp.logical_not(even)
            halo = jnp.where(near_side, halo_near_ref[:, local], halo_far_ref[:, local])
            body = jnp.where(near_side, near_ref[:, local], far_ref[:, local])
        behind = activate(halo, slope_before, offset_before).astype(jnp.bfloat16)
        behind = jnp.where(at_start, halo, behind)
        ahead = activate(body, slope, offset).astype(jnp.bfloat16)
        if side != 1:
            outside = row_at == 0 if side == 0 else row_at == row_count - 1
            behind = jnp.where(outside, jnp.zeros_like(behind), behind)
            ahead = jnp.where(outside, jnp.zeros_like(ahead), ahead)
        field[:SPAN_HALO, line] = behind
        field[SPAN_HALO:, line] = ahead
    bias = vectors_ref[2]
    kept = []
    spare = SPAN_HALO - 2
    for pair in range((lines + 2) // 2):
        results = pair_conv(field, 2 * pair, inner + 2, weight_ref)
        for out in range(2):
            line = 2 * pair + out
            rounded = (results[out] + bias).astype(jnp.bfloat16)
            rounded = rounded.reshape(inner + 2, columns, channels)
            middle_ref[:2, line] = jnp.where(at_start, field[:spare, line + lines - 1], rounded[:2])
            middle_ref[2:, line] = rounded[2:]
            if 1 <= line <= lines:
                kept.append(rounded[2:].astype(jnp.float32).reshape(-1, channels))
    sums_ref[...] = jnp.broadcast_to(moments(iter(kept))[None], sums_ref.shape)


def second_kernel(
    row_count, place, middle_ref, stats_ref, vectors_ref, weight_ref, own_ref, out_ref, field
):
    section, row_at = place[0], place[1]
    frames, lines, columns, channels = own_ref.shape
    cells = frames * lines * columns
    scale, shift = vectors_ref[3], vectors_ref[4]
    mine = stats_ref[pl.ds(section * row_count, row_count), 0]
    before = stats_ref[pl.ds(jnp.maximum(section - 1, 0) * row_count, row_count), 0]
    slope, offset = affine(mine, cells, scale, shift)
    slope_before, offset_before = affine(before, cells, scale, shift)
    at_start = section == 0
    for line in range(lines + 2):
        halo, body = middle_ref[:2, line], middle_ref[2:, line]
        behind = activate(halo, slope_before, offset_before).astype(jnp.bfloat16)
        behind = jnp.where(at_start, halo, behind)
        ahead = activate(body, slope, offset).astype(jnp.bfloat16)
        if line == 0 or line == lines + 1:
            outside = row_at == 0 if line == 0 else row_at == row_count - 1
            behind = jnp.where(outside, jnp.zeros_like(behind), behind)
            ahead = jnp.where(outside, jnp.zeros_like(ahead), ahead)
        field[:2, line] = behind
        field[2:, line] = ahead
    bias = vectors_ref[5]
    for pair in range(lines // 2):
        results = pair_conv(field, 2 * pair, frames, weight_ref)
        for out in range(2):
            line = 2 * pair + out
            result = (results[out] + bias).reshape(frames, columns, channels)
            out_ref[:, line] = (result + own_ref[:, line].astype(jnp.float32)).astype(jnp.bfloat16)


def call(kernel, out_shape, scratch, operands, in_place=(), flops=0):
    vmem = pl.BlockSpec(memory_space=pltpu.VMEM)
    specs = [pl.BlockSpec(memory_space=pltpu.SMEM)] + [vmem] * (len(operands) - 1)
    for index in in_place:
        specs[index] = pl.BlockSpec(memory_space=pltpu.HBM)
    operands = [
        pltpu.with_memory_space_constraint(operand, pltpu.HBM) if index in in_place else operand
        for index, operand in enumerate(operands)
    ]
    return pl.pallas_call(
        kernel,
        out_shape=out_shape,
        in_specs=specs,
        out_specs=jax.tree.map(lambda _: vmem, out_shape),
        scratch_shapes=scratch,
        compiler_params=pltpu.CompilerParams(vmem_limit_bytes=40 * 2**20),
        cost_estimate=pl.CostEstimate(flops=flops, bytes_accessed=2**20, transcendentals=0),
    )(*operands)


def on_device(
    activations,
    first_cache,
    second_cache,
    norm1_scale,
    norm1_shift,
    conv1_weight,
    conv1_bias,
    norm2_scale,
    norm2_shift,
    conv2_weight,
    conv2_bias,
):
    frames, lines, columns, channels = activations.shape
    sections, row_count = lax.axis_size("section"), lax.axis_size("rows")
    everyone = sections * row_count
    section, row_at = lax.axis_index("section"), lax.axis_index("rows")
    place = jnp.stack([section, row_at, jnp.int32(sections)]).astype(jnp.int32)
    stats_shape = jax.ShapeDtypeStruct((everyone, 1, 2 * channels), jnp.float32)
    vectors = (norm1_scale, norm1_shift, conv1_bias, norm2_scale, norm2_shift, conv2_bias)

    near = [i ^ 1 for i in range(row_count)]
    far = [0] + [i + 1 if i % 2 else i - 1 for i in range(1, row_count - 1)] + [row_count - 1]

    def across(block, partner):
        return lax.ppermute(block, "rows", list(enumerate(partner)))

    ring = [(at, (at + 1) % sections) for at in range(sections)]
    sums, halo, packed, own, weight = call(
        prepare_kernel,
        (
            jax.ShapeDtypeStruct((1, 2 * channels), jnp.float32),
            jax.ShapeDtypeStruct((SPAN_HALO, lines, columns, channels), jnp.bfloat16),
            jax.ShapeDtypeStruct((len(vectors), 1, channels), jnp.float32),
            jax.ShapeDtypeStruct(activations.shape, jnp.bfloat16),
            jax.ShapeDtypeStruct(conv1_weight.shape, jnp.bfloat16),
        ),
        [pltpu.SemaphoreType.DMA((4 + PARTS + len(vectors),))],
        (place, activations, second_cache, first_cache, conv1_weight)
        + tuple(vector.reshape(1, channels) for vector in vectors),
        in_place=range(1, 5 + len(vectors)),
    )
    beside = [across(activations, near), across(activations, far)]
    behind = [lax.ppermute(halo, "section", ring)]
    behind += [across(behind[0], near), across(behind[0], far)]
    both = jnp.stack([sums, lax.ppermute(sums, "section", ring)], axis=1)
    both = jnp.broadcast_to(both, (row_count,) + both.shape[1:])
    stats = lax.all_to_all(both, "rows", 0, 0, tiled=True)
    middle, sums_two = call(
        functools.partial(first_kernel, row_count),
        (
            jax.ShapeDtypeStruct((frames + 2, lines + 2, columns, channels), jnp.bfloat16),
            stats_shape,
        ),
        [pltpu.VMEM((frames + SPAN_HALO, 3 * lines, columns, channels), jnp.bfloat16)],
        (place, own, *beside, *behind, stats, packed, weight),
        flops=10**9,
    )
    stats_two = lax.all_to_all(sums_two, ("section", "rows"), 0, 0, tiled=True)
    return call(
        functools.partial(second_kernel, row_count),
        jax.ShapeDtypeStruct(activations.shape, jnp.bfloat16),
        [pltpu.VMEM((frames + 2, lines + 2, columns, channels), jnp.bfloat16)],
        (place, middle, stats_two, packed, conv2_weight, own),
        flops=10**9,
    )


def solution(mesh):
    in_specs = (
        P("section", "rows", None, None),
        P(None, "rows", None, None),
        P(None, "rows", None, None),
        P(),
        P(),
        P(),
        P(),
        P(),
        P(),
        P(),
        P(),
    )
    out_specs = P("section", "rows", None, None)
    return jax.shard_map(
        on_device, mesh=mesh, in_specs=in_specs, out_specs=out_specs, check_vma=False
    )
```

```python
import functools
import itertools

import functools
import itertools

import jax
import jax.numpy as jnp
from jax import lax
from jax.experimental import pallas as pl
from jax.experimental.pallas import tpu as pltpu
from jax.sharding import PartitionSpec as P

GROUPS = 32
SPAN_HALO = 4

epsilon = 1e-06


def group_sum(values, width):
    lanes = values.shape[-1]
    lane = lax.broadcasted_iota(jnp.int32, values.shape, values.ndim - 1)
    step = 1
    while step < width:
        up = pltpu.roll(values, lanes - step, values.ndim - 1)
        down = pltpu.roll(values, step, values.ndim - 1)
        values = values + jnp.where((lane // step) % 2 == 0, up, down)
        step *= 2
    return values


def moments(blocks):
    first = next(blocks)
    pivot = jnp.sum(first, axis=0, keepdims=True) * (1.0 / first.shape[0])
    cells, total, squares = 0, 0.0, 0.0
    for block in itertools.chain([first], blocks):
        away = block - pivot
        cells += block.shape[0]
        total = total + jnp.sum(away, axis=0, keepdims=True)
        squares = squares + jnp.sum(away * away, axis=0, keepdims=True)
    shift = total * (1.0 / cells)
    return jnp.concatenate([(pivot + shift) * cells, squares - total * shift], axis=1)


def affine(stats, cells, scale, shift):
    devices, channels = stats.shape[0], scale.shape[-1]
    width = channels // GROUPS
    totals, centred = stats[:, :channels], stats[:, channels:]
    count = cells * width * devices
    average = group_sum(jnp.sum(totals, axis=0, keepdims=True), width) * (1.0 / count)
    away = totals * (1.0 / cells) - average
    inner = jnp.sum(centred + cells * (away * away), axis=0, keepdims=True)
    spread = group_sum(inner, width) * (1.0 / count)
    slope = 0.5 * scale / jnp.sqrt(spread + epsilon)
    return slope, 0.5 * shift - average * slope


def activate(values, slope, offset):
    half = values.astype(jnp.float32) * slope + offset
    return half + half * jnp.tanh(half)


def pair_conv(field, row, frames, weight_ref):
    columns, channels = field.shape[2], field.shape[3]
    pieces, blocks = [], []
    nothing = jnp.zeros((channels, channels), jnp.bfloat16)
    for frame_tap in range(3):
        for line in range(4):
            piece = field[frame_tap : frame_tap + frames, row + line]
            pieces.append(piece.reshape(frames * columns, channels))
            blocks.append(
                jnp.concatenate(
                    [
                        weight_ref[frame_tap, line - out, col_tap]
                        if 0 <= line - out <= 2
                        else nothing
                        for col_tap in range(3)
                        for out in range(2)
                    ],
                    axis=1,
                )
            )
    product = jnp.dot(
        jnp.concatenate(pieces, axis=1),
        jnp.concatenate(blocks, axis=0),
        preferred_element_type=jnp.float32,
    )
    cells = frames * columns
    column = lax.broadcasted_iota(jnp.int32, (cells, channels), 0) % columns
    results = []
    for out in range(2):
        left, centre, right = (
            product[:, (2 * tap + out) * channels : (2 * tap + out + 1) * channels]
            for tap in range(3)
        )
        left = jnp.where(column == 0, 0.0, pltpu.roll(left, 1, 0))
        right = jnp.where(column == columns - 1, 0.0, pltpu.roll(right, cells - 1, 0))
        results.append(left + centre + right)
    return results


def copy_kernel(sections, own_ref, second_cache_ref, first_cache_ref, copied, halo_ref, sems):
    last = lax.axis_index("section") == sections - 1
    frames = own_ref.shape[0]
    spare = SPAN_HALO - 2
    tail = pltpu.make_async_copy(own_ref.at[frames - SPAN_HALO :], halo_ref, sems.at[0])
    older = pltpu.make_async_copy(second_cache_ref, halo_ref.at[:spare], sems.at[1])
    newer = pltpu.make_async_copy(first_cache_ref, halo_ref.at[spare:], sems.at[2])
    load = pltpu.make_async_copy(own_ref, copied, sems.at[3])

    @pl.when(last)
    def _():
        older.start()
        newer.start()

    @pl.when(jnp.logical_not(last))
    def _():
        tail.start()

    load.start()

    @pl.when(last)
    def _():
        older.wait()
        newer.wait()

    @pl.when(jnp.logical_not(last))
    def _():
        tail.wait()

    load.wait()


def stats_kernel(own_ref, weight_ref, *rest):
    *vector_refs, stats_ref, vectors_ref, weight_copy, sems = rest
    loads = [pltpu.make_async_copy(weight_ref, weight_copy, sems.at[0])]
    loads += [
        pltpu.make_async_copy(vector_ref, vectors_ref.at[index], sems.at[1 + index])
        for index, vector_ref in enumerate(vector_refs)
    ]
    for load in loads:
        load.start()
    channels = own_ref.shape[-1]
    blocks = (own_ref[frame].astype(jnp.float32) for frame in range(own_ref.shape[0]))
    stats_ref[...] = moments(block.reshape(-1, channels) for block in blocks)
    for load in loads:
        load.wait()


def first_kernel(
    row_count, own_ref, near_ref, far_ref, halo_ref, halo_near_ref, halo_far_ref,
    stats_ref, vectors_ref, weight_ref, middle_ref, sums_ref, field
):
    section, row_at = lax.axis_index("section"), lax.axis_index("rows")
    inner, lines, columns, channels = own_ref.shape
    cells = inner * lines * columns
    scale, shift = vectors_ref[0], vectors_ref[1]
    mine, before = stats_ref[:, 0], stats_ref[:, 1]
    slope, offset = affine(mine, cells, scale, shift)
    slope_before, offset_before = affine(before, cells, scale, shift)
    even = row_at % 2 == 0
    at_start = section == 0

    def fill(line):
        side, local = divmod(line, lines)
        if side == 1:
            halo, body = halo_ref[:, local], own_ref[:, local]
        else:
            near_side = even if side == 2 else jnp.logical_not(even)
            halo = jnp.where(near_side, halo_near_ref[:, local], halo_far_ref[:, local])
            body = jnp.where(near_side, near_ref[:, local], far_ref[:, local])
        behind = activate(halo, slope_before, offset_before).astype(jnp.bfloat16)
        behind = jnp.where(at_start, halo, behind)
        ahead = activate(body, slope, offset).astype(jnp.bfloat16)
        if side != 1:
            outside = row_at == 0 if side == 0 else row_at == row_count - 1
            behind = jnp.where(outside, jnp.zeros_like(behind), behind)
            ahead = jnp.where(outside, jnp.zeros_like(ahead), ahead)
        field[:SPAN_HALO, line] = behind
        field[SPAN_HALO:, line] = ahead

    bias = vectors_ref[2]
    kept = []
    spare = SPAN_HALO - 2
    ready = 0
    for pair in range((lines + 2) // 2):
        for line in range(ready, 2 * pair + 4):
            fill(line)
        ready = 2 * pair + 4
        results = pair_conv(field, 2 * pair, inner + 2, weight_ref)
        for out in range(2):
            line = 2 * pair + out
            rounded = (results[out] + bias).astype(jnp.bfloat16)
            rounded = rounded.reshape(inner + 2, columns, channels)
            middle_ref[:2, line] = jnp.where(at_start, field[:spare, line + lines - 1], rounded[:2])
            middle_ref[2:, line] = rounded[2:]
            if 1 <= line <= lines:
                kept.append(rounded[2:].astype(jnp.float32).reshape(-1, channels))
    sums_ref[...] = jnp.broadcast_to(moments(iter(kept))[None], sums_ref.shape)


def second_kernel(
    row_count, middle_ref, stats_ref, vectors_ref, weight_ref, own_ref, out_ref, field
):
    section, row_at = lax.axis_index("section"), lax.axis_index("rows")
    frames, lines, columns, channels = own_ref.shape
    cells = frames * lines * columns
    scale, shift = vectors_ref[3], vectors_ref[4]
    mine = stats_ref[pl.ds(section * row_count, row_count), 0]
    before = stats_ref[pl.ds(jnp.maximum(section - 1, 0) * row_count, row_count), 0]
    slope, offset = affine(mine, cells, scale, shift)
    slope_before, offset_before = affine(before, cells, scale, shift)
    at_start = section == 0
    for line in range(lines + 2):
        halo, body = middle_ref[:2, line], middle_ref[2:, line]
        behind = activate(halo, slope_before, offset_before).astype(jnp.bfloat16)
        behind = jnp.where(at_start, halo, behind)
        ahead = activate(body, slope, offset).astype(jnp.bfloat16)
        if line == 0 or line == lines + 1:
            outside = row_at == 0 if line == 0 else row_at == row_count - 1
            behind = jnp.where(outside, jnp.zeros_like(behind), behind)
            ahead = jnp.where(outside, jnp.zeros_like(ahead), ahead)
        field[:2, line] = behind
        field[2:, line] = ahead
    bias = vectors_ref[5]
    for pair in range(lines // 2):
        results = pair_conv(field, 2 * pair, frames, weight_ref)
        for out in range(2):
            line = 2 * pair + out
            result = (results[out] + bias).reshape(frames, columns, channels)
            out_ref[:, line] = (result + own_ref[:, line].astype(jnp.float32)).astype(jnp.bfloat16)


def call(kernel, out_shape, scratch, operands, in_place=(), flops=0):
    vmem = pl.BlockSpec(memory_space=pltpu.VMEM)
    specs = [vmem] * len(operands)
    for index in in_place:
        specs[index] = pl.BlockSpec(memory_space=pltpu.HBM)
    operands = [
        pltpu.with_memory_space_constraint(operand, pltpu.HBM) if index in in_place else operand
        for index, operand in enumerate(operands)
    ]
    return pl.pallas_call(
        kernel,
        out_shape=out_shape,
        in_specs=specs,
        out_specs=jax.tree.map(lambda _: vmem, out_shape),
        scratch_shapes=scratch,
        compiler_params=pltpu.CompilerParams(vmem_limit_bytes=40 * 2**20),
        cost_estimate=pl.CostEstimate(flops=flops, bytes_accessed=2**20, transcendentals=0),
    )(*operands)


def on_device(
    activations,
    first_cache,
    second_cache,
    norm1_scale,
    norm1_shift,
    conv1_weight,
    conv1_bias,
    norm2_scale,
    norm2_shift,
    conv2_weight,
    conv2_bias,
):
    frames, lines, columns, channels = activations.shape
    sections, row_count = lax.axis_size("section"), lax.axis_size("rows")
    everyone = sections * row_count
    stats_shape = jax.ShapeDtypeStruct((everyone, 1, 2 * channels), jnp.float32)
    vectors = (norm1_scale, norm1_shift, conv1_bias, norm2_scale, norm2_shift, conv2_bias)

    near = [i ^ 1 for i in range(row_count)]
    far = [0] + [i + 1 if i % 2 else i - 1 for i in range(1, row_count - 1)] + [row_count - 1]

    def across(block, partner):
        return lax.ppermute(block, "rows", list(enumerate(partner)))

    ring = [(at, (at + 1) % sections) for at in range(sections)]
    own, halo = call(
        functools.partial(copy_kernel, sections),
        (
            jax.ShapeDtypeStruct(activations.shape, jnp.bfloat16),
            jax.ShapeDtypeStruct((SPAN_HALO, lines, columns, channels), jnp.bfloat16),
        ),
        [pltpu.SemaphoreType.DMA((4,))],
        (activations, second_cache, first_cache),
        in_place=range(3),
    )
    sums, packed, weight = call(
        stats_kernel,
        (
            jax.ShapeDtypeStruct((1, 2 * channels), jnp.float32),
            jax.ShapeDtypeStruct((len(vectors), 1, channels), jnp.float32),
            jax.ShapeDtypeStruct(conv1_weight.shape, jnp.bfloat16),
        ),
        [pltpu.SemaphoreType.DMA((1 + len(vectors),))],
        (own, conv1_weight) + tuple(vector.reshape(1, channels) for vector in vectors),
        in_place=range(1, 2 + len(vectors)),
    )
    beside = [across(own, near), across(own, far)]
    behind = [lax.ppermute(halo, "section", ring)]
    behind += [across(behind[0], near), across(behind[0], far)]
    both = jnp.stack([sums, lax.ppermute(sums, "section", ring)], axis=1)
    both = jnp.broadcast_to(both, (row_count,) + both.shape[1:])
    stats = lax.all_to_all(both, "rows", 0, 0, tiled=True)
    middle, sums_two = call(
        functools.partial(first_kernel, row_count),
        (
            jax.ShapeDtypeStruct((frames + 2, lines + 2, columns, channels), jnp.bfloat16),
            stats_shape,
        ),
        [pltpu.VMEM((frames + SPAN_HALO, 3 * lines, columns, channels), jnp.bfloat16)],
        (own, *beside, *behind, stats, packed, weight),
        flops=10**9,
    )
    stats_two = lax.all_to_all(sums_two, ("section", "rows"), 0, 0, tiled=True)
    return call(
        functools.partial(second_kernel, row_count),
        jax.ShapeDtypeStruct(activations.shape, jnp.bfloat16),
        [pltpu.VMEM((frames + 2, lines + 2, columns, channels), jnp.bfloat16)],
        (middle, stats_two, packed, conv2_weight, own),
        flops=10**9,
    )


def solution(mesh):
    in_specs = (
        P("section", "rows", None, None),
        P(None, "rows", None, None),
        P(None, "rows", None, None),
        P(),
        P(),
        P(),
        P(),
        P(),
        P(),
        P(),
        P(),
    )
    out_specs = P("section", "rows", None, None)
    return jax.shard_map(
        on_device, mesh=mesh, in_specs=in_specs, out_specs=out_specs, check_vma=False
    )
```

```python
import functools
import itertools

import functools
import itertools

import jax
import jax.numpy as jnp
from jax import lax
from jax.experimental import pallas as pl
from jax.experimental.pallas import tpu as pltpu
from jax.sharding import PartitionSpec as P

GROUPS = 32
SPAN_HALO = 4

epsilon = 1e-06


def group_sum(values, width):
    lanes = values.shape[-1]
    lane = lax.broadcasted_iota(jnp.int32, values.shape, values.ndim - 1)
    step = 1
    while step < width:
        up = pltpu.roll(values, lanes - step, values.ndim - 1)
        down = pltpu.roll(values, step, values.ndim - 1)
        values = values + jnp.where((lane // step) % 2 == 0, up, down)
        step *= 2
    return values


def moments(blocks):
    first = next(blocks)
    pivot = jnp.sum(first, axis=0, keepdims=True) * (1.0 / first.shape[0])
    cells, total, squares = 0, 0.0, 0.0
    for block in itertools.chain([first], blocks):
        away = block - pivot
        cells += block.shape[0]
        total = total + jnp.sum(away, axis=0, keepdims=True)
        squares = squares + jnp.sum(away * away, axis=0, keepdims=True)
    shift = total * (1.0 / cells)
    return jnp.concatenate([(pivot + shift) * cells, squares - total * shift], axis=1)


def affine(stats, cells, scale, shift):
    devices, channels = stats.shape[0], scale.shape[-1]
    width = channels // GROUPS
    totals, centred = stats[:, :channels], stats[:, channels:]
    count = cells * width * devices
    average = group_sum(jnp.sum(totals, axis=0, keepdims=True), width) * (1.0 / count)
    away = totals * (1.0 / cells) - average
    inner = jnp.sum(centred + cells * (away * away), axis=0, keepdims=True)
    spread = group_sum(inner, width) * (1.0 / count)
    slope = 0.5 * scale / jnp.sqrt(spread + epsilon)
    return slope, 0.5 * shift - average * slope


def activate(values, slope, offset):
    half = values.astype(jnp.float32) * slope + offset
    return half + half * jnp.tanh(half)


def pair_conv(field, row, frames, weight_ref):
    columns, channels = field.shape[2], field.shape[3]
    pieces, blocks = [], []
    nothing = jnp.zeros((channels, channels), jnp.bfloat16)
    for frame_tap in range(3):
        for line in range(4):
            piece = field[frame_tap : frame_tap + frames, row + line]
            pieces.append(piece.reshape(frames * columns, channels))
            blocks.append(
                jnp.concatenate(
                    [
                        weight_ref[frame_tap, line - out, col_tap]
                        if 0 <= line - out <= 2
                        else nothing
                        for col_tap in range(3)
                        for out in range(2)
                    ],
                    axis=1,
                )
            )
    product = jnp.dot(
        jnp.concatenate(pieces, axis=1),
        jnp.concatenate(blocks, axis=0),
        preferred_element_type=jnp.float32,
    )
    cells = frames * columns
    column = lax.broadcasted_iota(jnp.int32, (cells, channels), 0) % columns
    results = []
    for out in range(2):
        left, centre, right = (
            product[:, (2 * tap + out) * channels : (2 * tap + out + 1) * channels]
            for tap in range(3)
        )
        left = jnp.where(column == 0, 0.0, pltpu.roll(left, 1, 0))
        right = jnp.where(column == columns - 1, 0.0, pltpu.roll(right, cells - 1, 0))
        results.append(left + centre + right)
    return results


def copy_kernel(sections, own_ref, second_cache_ref, first_cache_ref, copied, halo_ref, sems):
    last = lax.axis_index("section") == sections - 1
    frames = own_ref.shape[0]
    spare = SPAN_HALO - 2
    tail = pltpu.make_async_copy(own_ref.at[frames - SPAN_HALO :], halo_ref, sems.at[0])
    older = pltpu.make_async_copy(second_cache_ref, halo_ref.at[:spare], sems.at[1])
    newer = pltpu.make_async_copy(first_cache_ref, halo_ref.at[spare:], sems.at[2])
    load = pltpu.make_async_copy(own_ref, copied, sems.at[3])

    @pl.when(last)
    def _():
        older.start()
        newer.start()

    @pl.when(jnp.logical_not(last))
    def _():
        tail.start()

    load.start()

    @pl.when(last)
    def _():
        older.wait()
        newer.wait()

    @pl.when(jnp.logical_not(last))
    def _():
        tail.wait()

    load.wait()


def stats_kernel(own_ref, weight_ref, *rest):
    *vector_refs, stats_ref, vectors_ref, weight_copy, sems = rest
    loads = [pltpu.make_async_copy(weight_ref, weight_copy, sems.at[0])]
    loads += [
        pltpu.make_async_copy(vector_ref, vectors_ref.at[index], sems.at[1 + index])
        for index, vector_ref in enumerate(vector_refs)
    ]
    for load in loads:
        load.start()
    channels = own_ref.shape[-1]
    blocks = (own_ref[frame].astype(jnp.float32) for frame in range(own_ref.shape[0]))
    stats_ref[...] = moments(block.reshape(-1, channels) for block in blocks)
    for load in loads:
        load.wait()


def first_kernel(
    row_count, own_ref, near_ref, far_ref, stats_ref, vectors_ref, weight_ref, middle_ref,
    sums_ref, field
):
    section, row_at = lax.axis_index("section"), lax.axis_index("rows")
    frames, lines, columns, channels = own_ref.shape
    inner = frames - SPAN_HALO
    cells = inner * lines * columns
    scale, shift = vectors_ref[0], vectors_ref[1]
    mine, before = stats_ref[:, 0], stats_ref[:, 1]
    slope, offset = affine(mine, cells, scale, shift)
    slope_before, offset_before = affine(before, cells, scale, shift)
    even = row_at % 2 == 0
    at_start = section == 0

    def fill(line):
        side, local = divmod(line, lines)
        if side == 1:
            block = own_ref[:, local]
        else:
            near_side = even if side == 2 else jnp.logical_not(even)
            block = jnp.where(near_side, near_ref[:, local], far_ref[:, local])
        halo, body = block[:SPAN_HALO], block[SPAN_HALO:]
        behind = activate(halo, slope_before, offset_before).astype(jnp.bfloat16)
        behind = jnp.where(at_start, halo, behind)
        ahead = activate(body, slope, offset).astype(jnp.bfloat16)
        if side != 1:
            outside = row_at == 0 if side == 0 else row_at == row_count - 1
            behind = jnp.where(outside, jnp.zeros_like(behind), behind)
            ahead = jnp.where(outside, jnp.zeros_like(ahead), ahead)
        field[:SPAN_HALO, line] = behind
        field[SPAN_HALO:, line] = ahead

    bias = vectors_ref[2]
    kept = []
    spare = SPAN_HALO - 2
    ready = 0
    for pair in range((lines + 2) // 2):
        for line in range(ready, 2 * pair + 4):
            fill(line)
        ready = 2 * pair + 4
        results = pair_conv(field, 2 * pair, inner + 2, weight_ref)
        for out in range(2):
            line = 2 * pair + out
            rounded = (results[out] + bias).astype(jnp.bfloat16)
            rounded = rounded.reshape(inner + 2, columns, channels)
            middle_ref[:2, line] = jnp.where(at_start, field[:spare, line + lines - 1], rounded[:2])
            middle_ref[2:, line] = rounded[2:]
            if 1 <= line <= lines:
                kept.append(rounded[2:].astype(jnp.float32).reshape(-1, channels))
    sums_ref[...] = jnp.broadcast_to(moments(iter(kept))[None], sums_ref.shape)


def second_kernel(
    row_count, middle_ref, stats_ref, vectors_ref, weight_ref, own_ref, out_ref, field
):
    section, row_at = lax.axis_index("section"), lax.axis_index("rows")
    frames, lines, columns, channels = own_ref.shape
    cells = frames * lines * columns
    scale, shift = vectors_ref[3], vectors_ref[4]
    mine = stats_ref[pl.ds(section * row_count, row_count), 0]
    before = stats_ref[pl.ds(jnp.maximum(section - 1, 0) * row_count, row_count), 0]
    slope, offset = affine(mine, cells, scale, shift)
    slope_before, offset_before = affine(before, cells, scale, shift)
    at_start = section == 0
    for line in range(lines + 2):
        halo, body = middle_ref[:2, line], middle_ref[2:, line]
        behind = activate(halo, slope_before, offset_before).astype(jnp.bfloat16)
        behind = jnp.where(at_start, halo, behind)
        ahead = activate(body, slope, offset).astype(jnp.bfloat16)
        if line == 0 or line == lines + 1:
            outside = row_at == 0 if line == 0 else row_at == row_count - 1
            behind = jnp.where(outside, jnp.zeros_like(behind), behind)
            ahead = jnp.where(outside, jnp.zeros_like(ahead), ahead)
        field[:2, line] = behind
        field[2:, line] = ahead
    bias = vectors_ref[5]
    for pair in range(lines // 2):
        results = pair_conv(field, 2 * pair, frames, weight_ref)
        for out in range(2):
            line = 2 * pair + out
            result = (results[out] + bias).reshape(frames, columns, channels)
            out_ref[:, line] = (result + own_ref[:, line].astype(jnp.float32)).astype(jnp.bfloat16)


def call(kernel, out_shape, scratch, operands, in_place=(), flops=0):
    vmem = pl.BlockSpec(memory_space=pltpu.VMEM)
    specs = [vmem] * len(operands)
    for index in in_place:
        specs[index] = pl.BlockSpec(memory_space=pltpu.HBM)
    operands = [
        pltpu.with_memory_space_constraint(operand, pltpu.HBM) if index in in_place else operand
        for index, operand in enumerate(operands)
    ]
    return pl.pallas_call(
        kernel,
        out_shape=out_shape,
        in_specs=specs,
        out_specs=jax.tree.map(lambda _: vmem, out_shape),
        scratch_shapes=scratch,
        compiler_params=pltpu.CompilerParams(vmem_limit_bytes=40 * 2**20),
        cost_estimate=pl.CostEstimate(flops=flops, bytes_accessed=2**20, transcendentals=0),
    )(*operands)


def on_device(
    activations,
    first_cache,
    second_cache,
    norm1_scale,
    norm1_shift,
    conv1_weight,
    conv1_bias,
    norm2_scale,
    norm2_shift,
    conv2_weight,
    conv2_bias,
):
    frames, lines, columns, channels = activations.shape
    sections, row_count = lax.axis_size("section"), lax.axis_size("rows")
    everyone = sections * row_count
    stats_shape = jax.ShapeDtypeStruct((everyone, 1, 2 * channels), jnp.float32)
    vectors = (norm1_scale, norm1_shift, conv1_bias, norm2_scale, norm2_shift, conv2_bias)

    near = [i ^ 1 for i in range(row_count)]
    far = [0] + [i + 1 if i % 2 else i - 1 for i in range(1, row_count - 1)] + [row_count - 1]

    def across(block, partner):
        return lax.ppermute(block, "rows", list(enumerate(partner)))

    ring = [(at, (at + 1) % sections) for at in range(sections)]
    own, halo = call(
        functools.partial(copy_kernel, sections),
        (
            jax.ShapeDtypeStruct(activations.shape, jnp.bfloat16),
            jax.ShapeDtypeStruct((SPAN_HALO, lines, columns, channels), jnp.bfloat16),
        ),
        [pltpu.SemaphoreType.DMA((4,))],
        (activations, second_cache, first_cache),
        in_place=range(3),
    )
    sums, packed, weight = call(
        stats_kernel,
        (
            jax.ShapeDtypeStruct((1, 2 * channels), jnp.float32),
            jax.ShapeDtypeStruct((len(vectors), 1, channels), jnp.float32),
            jax.ShapeDtypeStruct(conv1_weight.shape, jnp.bfloat16),
        ),
        [pltpu.SemaphoreType.DMA((1 + len(vectors),))],
        (own, conv1_weight) + tuple(vector.reshape(1, channels) for vector in vectors),
        in_place=range(1, 2 + len(vectors)),
    )
    joined = jnp.concatenate([lax.ppermute(halo, "section", ring), own], axis=0)
    both = jnp.stack([sums, lax.ppermute(sums, "section", ring)], axis=1)
    both = jnp.broadcast_to(both, (row_count,) + both.shape[1:])
    stats = lax.all_to_all(both, "rows", 0, 0, tiled=True)
    middle, sums_two = call(
        functools.partial(first_kernel, row_count),
        (
            jax.ShapeDtypeStruct((frames + 2, lines + 2, columns, channels), jnp.bfloat16),
            stats_shape,
        ),
        [pltpu.VMEM((frames + SPAN_HALO, 3 * lines, columns, channels), jnp.bfloat16)],
        (joined, across(joined, near), across(joined, far), stats, packed, weight),
        flops=10**9,
    )
    stats_two = lax.all_to_all(sums_two, ("section", "rows"), 0, 0, tiled=True)
    return call(
        functools.partial(second_kernel, row_count),
        jax.ShapeDtypeStruct(activations.shape, jnp.bfloat16),
        [pltpu.VMEM((frames + 2, lines + 2, columns, channels), jnp.bfloat16)],
        (middle, stats_two, packed, conv2_weight, own),
        flops=10**9,
    )


def solution(mesh):
    in_specs = (
        P("section", "rows", None, None),
        P(None, "rows", None, None),
        P(None, "rows", None, None),
        P(),
        P(),
        P(),
        P(),
        P(),
        P(),
        P(),
        P(),
    )
    out_specs = P("section", "rows", None, None)
    return jax.shard_map(
        on_device, mesh=mesh, in_specs=in_specs, out_specs=out_specs, check_vma=False
    )
```

```python
import functools
import itertools

import functools
import itertools

import jax
import jax.numpy as jnp
from jax import lax
from jax.experimental import pallas as pl
from jax.experimental.pallas import tpu as pltpu
from jax.sharding import PartitionSpec as P

GROUPS = 32
SPAN_HALO = 4

epsilon = 1e-06


def group_sum(values, width):
    lanes = values.shape[-1]
    lane = lax.broadcasted_iota(jnp.int32, values.shape, values.ndim - 1)
    step = 1
    while step < width:
        up = pltpu.roll(values, lanes - step, values.ndim - 1)
        down = pltpu.roll(values, step, values.ndim - 1)
        values = values + jnp.where((lane // step) % 2 == 0, up, down)
        step *= 2
    return values


def moments(blocks):
    first = next(blocks)
    pivot = jnp.sum(first, axis=0, keepdims=True) * (1.0 / first.shape[0])
    cells, total, squares = 0, 0.0, 0.0
    for block in itertools.chain([first], blocks):
        away = block - pivot
        cells += block.shape[0]
        total = total + jnp.sum(away, axis=0, keepdims=True)
        squares = squares + jnp.sum(away * away, axis=0, keepdims=True)
    shift = total * (1.0 / cells)
    return jnp.concatenate([(pivot + shift) * cells, squares - total * shift], axis=1)


def affine(stats, cells, scale, shift):
    devices, channels = stats.shape[0], scale.shape[-1]
    width = channels // GROUPS
    totals, centred = stats[:, :channels], stats[:, channels:]
    count = cells * width * devices
    average = group_sum(jnp.sum(totals, axis=0, keepdims=True), width) * (1.0 / count)
    away = totals * (1.0 / cells) - average
    inner = jnp.sum(centred + cells * (away * away), axis=0, keepdims=True)
    spread = group_sum(inner, width) * (1.0 / count)
    slope = 0.5 * scale / jnp.sqrt(spread + epsilon)
    return slope, 0.5 * shift - average * slope


def activate(values, slope, offset):
    half = values.astype(jnp.float32) * slope + offset
    return half + half * jnp.tanh(half)


def pair_conv(field, row, frames, weight_ref):
    columns, channels = field.shape[2], field.shape[3]
    pieces, blocks = [], []
    nothing = jnp.zeros((channels, channels), jnp.bfloat16)
    for frame_tap in range(3):
        for line in range(4):
            piece = field[frame_tap : frame_tap + frames, row + line]
            pieces.append(piece.reshape(frames * columns, channels))
            blocks.append(
                jnp.concatenate(
                    [
                        weight_ref[frame_tap, line - out, col_tap]
                        if 0 <= line - out <= 2
                        else nothing
                        for col_tap in range(3)
                        for out in range(2)
                    ],
                    axis=1,
                )
            )
    product = jnp.dot(
        jnp.concatenate(pieces, axis=1),
        jnp.concatenate(blocks, axis=0),
        preferred_element_type=jnp.float32,
    )
    cells = frames * columns
    column = lax.broadcasted_iota(jnp.int32, (cells, channels), 0) % columns
    results = []
    for out in range(2):
        left, centre, right = (
            product[:, (2 * tap + out) * channels : (2 * tap + out + 1) * channels]
            for tap in range(3)
        )
        left = jnp.where(column == 0, 0.0, pltpu.roll(left, 1, 0))
        right = jnp.where(column == columns - 1, 0.0, pltpu.roll(right, cells - 1, 0))
        results.append(left + centre + right)
    return results


def copy_kernel(sections, own_ref, second_cache_ref, first_cache_ref, copied, halo_ref, sems):
    last = lax.axis_index("section") == sections - 1
    frames = own_ref.shape[0]
    spare = SPAN_HALO - 2
    tail = pltpu.make_async_copy(own_ref.at[frames - SPAN_HALO :], halo_ref, sems.at[0])
    older = pltpu.make_async_copy(second_cache_ref, halo_ref.at[:spare], sems.at[1])
    newer = pltpu.make_async_copy(first_cache_ref, halo_ref.at[spare:], sems.at[2])
    load = pltpu.make_async_copy(own_ref, copied, sems.at[3])

    @pl.when(last)
    def _():
        older.start()
        newer.start()

    @pl.when(jnp.logical_not(last))
    def _():
        tail.start()

    load.start()

    @pl.when(last)
    def _():
        older.wait()
        newer.wait()

    @pl.when(jnp.logical_not(last))
    def _():
        tail.wait()

    load.wait()


def stats_kernel(own_ref, weight_ref, *rest):
    *vector_refs, stats_ref, vectors_ref, weight_copy, sems = rest
    loads = [pltpu.make_async_copy(weight_ref, weight_copy, sems.at[0])]
    loads += [
        pltpu.make_async_copy(vector_ref, vectors_ref.at[index], sems.at[1 + index])
        for index, vector_ref in enumerate(vector_refs)
    ]
    for load in loads:
        load.start()
    channels = own_ref.shape[-1]
    blocks = (own_ref[frame].astype(jnp.float32) for frame in range(own_ref.shape[0]))
    stats_ref[...] = moments(block.reshape(-1, channels) for block in blocks)
    for load in loads:
        load.wait()


def first_kernel(
    row_count, own_ref, near_ref, far_ref, stats_ref, vectors_ref, weight_ref, middle_ref,
    sums_ref, field
):
    section, row_at = lax.axis_index("section"), lax.axis_index("rows")
    frames, lines, columns, channels = own_ref.shape
    inner = frames - SPAN_HALO
    cells = inner * lines * columns
    scale, shift = vectors_ref[0], vectors_ref[1]
    mine, before = stats_ref[:, 0], stats_ref[:, 1]
    slope, offset = affine(mine, cells, scale, shift)
    slope_before, offset_before = affine(before, cells, scale, shift)
    even = row_at % 2 == 0
    at_start = section == 0

    def fill(line):
        side, local = divmod(line, lines)
        if side == 1:
            block = own_ref[:, local]
        else:
            near_side = even if side == 2 else jnp.logical_not(even)
            block = jnp.where(near_side, near_ref[:, local], far_ref[:, local])
        halo, body = block[:SPAN_HALO], block[SPAN_HALO:]
        behind = activate(halo, slope_before, offset_before).astype(jnp.bfloat16)
        behind = jnp.where(at_start, halo, behind)
        ahead = activate(body, slope, offset).astype(jnp.bfloat16)
        if side != 1:
            outside = row_at == 0 if side == 0 else row_at == row_count - 1
            behind = jnp.where(outside, jnp.zeros_like(behind), behind)
            ahead = jnp.where(outside, jnp.zeros_like(ahead), ahead)
        field[:SPAN_HALO, line] = behind
        field[SPAN_HALO:, line] = ahead

    bias = vectors_ref[2]
    kept = []
    spare = SPAN_HALO - 2
    ready = 0
    for pair in range((lines + 2) // 2):
        for line in range(ready, 2 * pair + 4):
            fill(line)
        ready = 2 * pair + 4
        results = pair_conv(field, 2 * pair, inner + 2, weight_ref)
        for out in range(2):
            line = 2 * pair + out
            rounded = (results[out] + bias).astype(jnp.bfloat16)
            rounded = rounded.reshape(inner + 2, columns, channels)
            middle_ref[:2, line] = jnp.where(at_start, field[:spare, line + lines - 1], rounded[:2])
            middle_ref[2:, line] = rounded[2:]
            if 1 <= line <= lines:
                kept.append(rounded[2:].astype(jnp.float32).reshape(-1, channels))
    sums_ref[...] = jnp.broadcast_to(moments(iter(kept))[None], sums_ref.shape)


def second_kernel(
    row_count, middle_ref, stats_ref, vectors_ref, weight_ref, own_ref, out_ref, field
):
    section, row_at = lax.axis_index("section"), lax.axis_index("rows")
    frames, lines, columns, channels = own_ref.shape
    cells = frames * lines * columns
    scale, shift = vectors_ref[3], vectors_ref[4]
    mine = stats_ref[pl.ds(section * row_count, row_count), 0]
    before = stats_ref[pl.ds(jnp.maximum(section - 1, 0) * row_count, row_count), 0]
    slope, offset = affine(mine, cells, scale, shift)
    slope_before, offset_before = affine(before, cells, scale, shift)
    at_start = section == 0
    for line in range(lines + 2):
        halo, body = middle_ref[:2, line], middle_ref[2:, line]
        behind = activate(halo, slope_before, offset_before).astype(jnp.bfloat16)
        behind = jnp.where(at_start, halo, behind)
        ahead = activate(body, slope, offset).astype(jnp.bfloat16)
        if line == 0 or line == lines + 1:
            outside = row_at == 0 if line == 0 else row_at == row_count - 1
            behind = jnp.where(outside, jnp.zeros_like(behind), behind)
            ahead = jnp.where(outside, jnp.zeros_like(ahead), ahead)
        field[:2, line] = behind
        field[2:, line] = ahead
    bias = vectors_ref[5]
    for pair in range(lines // 2):
        results = pair_conv(field, 2 * pair, frames, weight_ref)
        for out in range(2):
            line = 2 * pair + out
            result = (results[out] + bias).reshape(frames, columns, channels)
            out_ref[:, line] = (result + own_ref[:, line].astype(jnp.float32)).astype(jnp.bfloat16)


def call(kernel, out_shape, scratch, operands, in_place=(), flops=0):
    vmem = pl.BlockSpec(memory_space=pltpu.VMEM)
    specs = [vmem] * len(operands)
    for index in in_place:
        specs[index] = pl.BlockSpec(memory_space=pltpu.HBM)
    operands = [
        pltpu.with_memory_space_constraint(operand, pltpu.HBM) if index in in_place else operand
        for index, operand in enumerate(operands)
    ]
    return pl.pallas_call(
        kernel,
        out_shape=out_shape,
        in_specs=specs,
        out_specs=jax.tree.map(lambda _: vmem, out_shape),
        scratch_shapes=scratch,
        compiler_params=pltpu.CompilerParams(vmem_limit_bytes=40 * 2**20),
        cost_estimate=pl.CostEstimate(flops=flops, bytes_accessed=2**20, transcendentals=0),
    )(*operands)


def on_device(
    activations,
    first_cache,
    second_cache,
    norm1_scale,
    norm1_shift,
    conv1_weight,
    conv1_bias,
    norm2_scale,
    norm2_shift,
    conv2_weight,
    conv2_bias,
):
    frames, lines, columns, channels = activations.shape
    sections, row_count = lax.axis_size("section"), lax.axis_size("rows")
    everyone = sections * row_count
    stats_shape = jax.ShapeDtypeStruct((everyone, 1, 2 * channels), jnp.float32)
    vectors = (norm1_scale, norm1_shift, conv1_bias, norm2_scale, norm2_shift, conv2_bias)

    near = [i ^ 1 for i in range(row_count)]
    far = [0] + [i + 1 if i % 2 else i - 1 for i in range(1, row_count - 1)] + [row_count - 1]

    def across(block, partner):
        return lax.ppermute(block, "rows", list(enumerate(partner)))

    ring = [(at, (at + 1) % sections) for at in range(sections)]
    own, halo = call(
        functools.partial(copy_kernel, sections),
        (
            jax.ShapeDtypeStruct(activations.shape, jnp.bfloat16),
            jax.ShapeDtypeStruct((SPAN_HALO, lines, columns, channels), jnp.bfloat16),
        ),
        [pltpu.SemaphoreType.DMA((4,))],
        (activations, second_cache, first_cache),
        in_place=range(3),
    )
    sums, packed, weight = call(
        stats_kernel,
        (
            jax.ShapeDtypeStruct((1, 2 * channels), jnp.float32),
            jax.ShapeDtypeStruct((len(vectors), 1, channels), jnp.float32),
            jax.ShapeDtypeStruct(conv1_weight.shape, jnp.bfloat16),
        ),
        [pltpu.SemaphoreType.DMA((1 + len(vectors),))],
        (own, conv1_weight) + tuple(vector.reshape(1, channels) for vector in vectors),
        in_place=range(1, 2 + len(vectors)),
    )
    received = lax.ppermute(halo, "section", ring)
    passed = lax.ppermute(sums, "section", ring)
    received, sums, passed = lax.optimization_barrier((received, sums, passed))
    joined = jnp.concatenate([received, own], axis=0)
    both = jnp.stack([sums, passed], axis=1)
    both = jnp.broadcast_to(both, (row_count,) + both.shape[1:])
    stats = lax.all_to_all(both, "rows", 0, 0, tiled=True)
    middle, sums_two = call(
        functools.partial(first_kernel, row_count),
        (
            jax.ShapeDtypeStruct((frames + 2, lines + 2, columns, channels), jnp.bfloat16),
            stats_shape,
        ),
        [pltpu.VMEM((frames + SPAN_HALO, 3 * lines, columns, channels), jnp.bfloat16)],
        (joined, across(joined, near), across(joined, far), stats, packed, weight),
        flops=10**9,
    )
    stats_two = lax.all_to_all(sums_two, ("section", "rows"), 0, 0, tiled=True)
    return call(
        functools.partial(second_kernel, row_count),
        jax.ShapeDtypeStruct(activations.shape, jnp.bfloat16),
        [pltpu.VMEM((frames + 2, lines + 2, columns, channels), jnp.bfloat16)],
        (middle, stats_two, packed, conv2_weight, own),
        flops=10**9,
    )


def solution(mesh):
    in_specs = (
        P("section", "rows", None, None),
        P(None, "rows", None, None),
        P(None, "rows", None, None),
        P(),
        P(),
        P(),
        P(),
        P(),
        P(),
        P(),
        P(),
    )
    out_specs = P("section", "rows", None, None)
    return jax.shard_map(
        on_device, mesh=mesh, in_specs=in_specs, out_specs=out_specs, check_vma=False
    )
```

```python
import functools

import functools

import jax
import jax.numpy as jnp
from jax import lax
from jax.experimental import pallas as pl
from jax.experimental.pallas import tpu as pltpu
from jax.sharding import PartitionSpec as P

GROUPS = 32
REACH = 2

epsilon = 1e-06


def moments(blocks):
    pivot = blocks[0][:1]
    cells = sum(block.shape[0] for block in blocks)
    total, squares = 0.0, 0.0
    for block in blocks:
        away = block - pivot
        total = total + jnp.sum(away, axis=0, keepdims=True)
        squares = squares + jnp.sum(away * away, axis=0, keepdims=True)
    shift = total * (1.0 / cells)
    return jnp.concatenate([pivot + shift, squares - total * shift], axis=1)


def affine(stats, cells, scale, shift):
    devices, channels = stats.shape[0], scale.shape[-1]
    means, squares = stats[:, :channels], stats[:, channels:]
    mean = jnp.sum(means, axis=0, keepdims=True) * (1.0 / devices)
    away = means - mean
    square = jnp.sum(squares + cells * (away * away), axis=0, keepdims=True)
    count = cells * devices
    lane = lax.broadcasted_iota(jnp.int32, mean.shape, 1)
    step = 1
    while step < channels // GROUPS:

        def partner(values):
            up = pltpu.roll(values, channels - step, 1)
            return jnp.where((lane // step) % 2 == 0, up, pltpu.roll(values, step, 1))

        away = partner(mean) - mean
        square = square + partner(square) + (0.5 * count) * (away * away)
        mean = mean + 0.5 * away
        count, step = 2 * count, 2 * step
    slope = 0.5 * scale * lax.rsqrt(square * (1.0 / count) + epsilon)
    return slope, 0.5 * shift - mean * slope


def activate(values, slope, offset):
    half = values.astype(jnp.float32) * slope + offset
    return half + half * jnp.tanh(half)


def pair_conv(field, row, frames, weight_ref):
    columns, channels = field.shape[2], field.shape[3]
    pieces, blocks = [], []
    nothing = jnp.zeros((channels, channels), jnp.bfloat16)
    for frame_tap in range(3):
        for line in range(4):
            piece = field[frame_tap : frame_tap + frames, row + line]
            pieces.append(piece.reshape(frames * columns, channels))
            blocks.append(
                jnp.concatenate(
                    [
                        weight_ref[frame_tap, line - out, col_tap]
                        if 0 <= line - out <= 2
                        else nothing
                        for col_tap in range(3)
                        for out in range(2)
                    ],
                    axis=1,
                )
            )
    product = jnp.dot(
        jnp.concatenate(pieces, axis=1),
        jnp.concatenate(blocks, axis=0),
        preferred_element_type=jnp.float32,
    )
    cells = frames * columns
    column = lax.broadcasted_iota(jnp.int32, (cells, channels), 0) % columns
    results = []
    for out in range(2):
        left, centre, right = (
            product[:, (2 * tap + out) * channels : (2 * tap + out + 1) * channels]
            for tap in range(3)
        )
        left = jnp.where(column == 0, 0.0, pltpu.roll(left, 1, 0))
        right = jnp.where(column == columns - 1, 0.0, pltpu.roll(right, cells - 1, 0))
        results.append(left + centre + right)
    return results


def copy_kernel(own_ref, second_cache_ref, first_cache_ref, tail_ref, copied, caches_ref, sems):
    kept = tail_ref.shape[0]
    copies = [
        (own_ref.at[own_ref.shape[0] - kept :], tail_ref),
        (own_ref, copied),
        (second_cache_ref, caches_ref.at[0]),
        (first_cache_ref, caches_ref.at[1]),
    ]
    copies = [
        pltpu.make_async_copy(source, target, sems.at[index])
        for index, (source, target) in enumerate(copies)
    ]
    for copy in copies:
        copy.start()
    for copy in copies:
        copy.wait()


def stats_kernel(own_ref, weight_ref, *rest):
    *vector_refs, stats_ref, vectors_ref, weight_copy, sems = rest
    loads = [pltpu.make_async_copy(weight_ref, weight_copy, sems.at[0])]
    loads += [
        pltpu.make_async_copy(vector_ref, vectors_ref.at[index], sems.at[1 + index])
        for index, vector_ref in enumerate(vector_refs)
    ]
    for load in loads:
        load.start()
    channels = own_ref.shape[-1]
    blocks = [own_ref[frame].astype(jnp.float32) for frame in range(own_ref.shape[0])]
    stats_ref[...] = moments([block.reshape(-1, channels) for block in blocks])
    for load in loads:
        load.wait()


def span_moments(stats_ref, section, row_count):
    chips = row_count // 2
    own = stats_ref[pl.ds(section * chips, chips)]
    return own.reshape(row_count, own.shape[-1])


def first_kernel(
    row_count, own_ref, near_ref, far_ref, stats_ref, vectors_ref, weight_ref, middle_ref,
    tail_ref, cache_ref, sums_ref, field
):
    section, row_at = lax.axis_index("section"), lax.axis_index("rows")
    inner, columns = middle_ref.shape[0], middle_ref.shape[2]
    lines, channels = own_ref.shape[1], own_ref.shape[3]
    cells = inner * lines * columns
    scale, shift = vectors_ref[0], vectors_ref[1]
    mine = span_moments(stats_ref, section, row_count)
    before = span_moments(stats_ref, jnp.maximum(section - 1, 0), row_count)
    slope, offset = affine(mine, cells, scale, shift)
    slope_before, offset_before = affine(before, cells, scale, shift)
    even = row_at % 2 == 0
    at_start = section == 0

    def fill(line):
        side, local = divmod(line, lines)
        if side == 1:
            block = own_ref[:, local]
        else:
            near_side = even if side == 2 else jnp.logical_not(even)
            block = jnp.where(near_side, near_ref[:, local], far_ref[:, local])
        cache, halo, body = block[:REACH], block[REACH : 2 * REACH], block[2 * REACH :]
        behind = activate(halo, slope_before, offset_before).astype(jnp.bfloat16)
        behind = jnp.where(at_start, halo, behind)
        ahead = activate(body, slope, offset).astype(jnp.bfloat16)
        if side != 1:
            outside = row_at == 0 if side == 0 else row_at == row_count - 1
            behind = jnp.where(outside, jnp.zeros_like(behind), behind)
            ahead = jnp.where(outside, jnp.zeros_like(ahead), ahead)
        field[:REACH, line] = behind
        field[REACH:, line] = ahead
        if lines - 1 <= line <= 2 * lines:
            cache_ref[:, line - lines + 1] = cache

    bias = vectors_ref[2]
    kept = []
    ready = 0
    for pair in range((lines + 2) // 2):
        for line in range(ready, 2 * pair + 4):
            fill(line)
        ready = 2 * pair + 4
        results = pair_conv(field, 2 * pair, inner, weight_ref)
        for out in range(2):
            line = 2 * pair + out
            rounded = (results[out] + bias).astype(jnp.bfloat16)
            if 1 <= line <= lines:
                kept.append(rounded.astype(jnp.float32))
            rounded = rounded.reshape(inner, columns, channels)
            middle_ref[:, line] = rounded
            tail_ref[:, line] = rounded[inner - REACH :]
    sums_ref[...] = moments(kept)


def second_kernel(
    row_count, middle_ref, halo_ref, cache_ref, stats_ref, vectors_ref, weight_ref, own_ref,
    out_ref, field
):
    section, row_at = lax.axis_index("section"), lax.axis_index("rows")
    frames, lines, columns, channels = own_ref.shape
    cells = frames * lines * columns
    scale, shift = vectors_ref[3], vectors_ref[4]
    mine = span_moments(stats_ref, section, row_count)
    before = span_moments(stats_ref, jnp.maximum(section - 1, 0), row_count)
    slope, offset = affine(mine, cells, scale, shift)
    slope_before, offset_before = affine(before, cells, scale, shift)
    at_start = section == 0
    for line in range(lines + 2):
        behind = activate(halo_ref[:, line], slope_before, offset_before).astype(jnp.bfloat16)
        behind = jnp.where(at_start, cache_ref[:, line], behind)
        ahead = activate(middle_ref[:, line], slope, offset).astype(jnp.bfloat16)
        if line == 0 or line == lines + 1:
            outside = row_at == 0 if line == 0 else row_at == row_count - 1
            behind = jnp.where(outside, jnp.zeros_like(behind), behind)
            ahead = jnp.where(outside, jnp.zeros_like(ahead), ahead)
        field[:REACH, line] = behind
        field[REACH:, line] = ahead
    bias = vectors_ref[5]
    for pair in range(lines // 2):
        results = pair_conv(field, 2 * pair, frames, weight_ref)
        for out in range(2):
            line = 2 * pair + out
            result = (results[out] + bias).reshape(frames, columns, channels)
            out_ref[:, line] = (result + own_ref[:, line].astype(jnp.float32)).astype(jnp.bfloat16)


def call(kernel, out_shape, scratch, operands, in_place=(), flops=0):
    vmem = pl.BlockSpec(memory_space=pltpu.VMEM)
    specs = [vmem] * len(operands)
    for index in in_place:
        specs[index] = pl.BlockSpec(memory_space=pltpu.HBM)
    operands = [
        pltpu.with_memory_space_constraint(operand, pltpu.HBM) if index in in_place else operand
        for index, operand in enumerate(operands)
    ]
    return pl.pallas_call(
        kernel,
        out_shape=out_shape,
        in_specs=specs,
        out_specs=jax.tree.map(lambda _: vmem, out_shape),
        scratch_shapes=scratch,
        compiler_params=pltpu.CompilerParams(vmem_limit_bytes=40 * 2**20),
        cost_estimate=pl.CostEstimate(flops=flops, bytes_accessed=2**20, transcendentals=0),
    )(*operands)


def on_device(
    activations,
    first_cache,
    second_cache,
    norm1_scale,
    norm1_shift,
    conv1_weight,
    conv1_bias,
    norm2_scale,
    norm2_shift,
    conv2_weight,
    conv2_bias,
):
    frames, lines, columns, channels = activations.shape
    sections, row_count = lax.axis_size("section"), lax.axis_size("rows")
    chips = sections * row_count // 2
    near = [i ^ 1 for i in range(row_count)]
    far = [0] + [i + 1 if i % 2 else i - 1 for i in range(1, row_count - 1)] + [row_count - 1]
    ring = [(at, (at + 1) % sections) for at in range(sections)]
    vectors = (norm1_scale, norm1_shift, conv1_bias, norm2_scale, norm2_shift, conv2_bias)
    wide = (lines + 2, columns, channels)

    def across(block, partner):
        return lax.ppermute(block, "rows", list(enumerate(partner)))

    def with_near(sums):
        return jnp.stack([sums, across(sums, near)], axis=1)

    def exchange(pair):
        same_core = [list(range(core, 2 * chips, 2)) for core in range(2)]
        return lax.all_to_all(
            jnp.broadcast_to(pair, (chips,) + pair.shape[1:]), ("section", "rows"), 0, 0,
            tiled=True, axis_index_groups=same_core,
        )

    def shaped(*shape):
        return jax.ShapeDtypeStruct(shape, jnp.bfloat16)

    sums_shape = jax.ShapeDtypeStruct((1, 2 * channels), jnp.float32)
    tail, own, caches = call(
        copy_kernel,
        (
            shaped(REACH, lines, columns, channels),
            shaped(*activations.shape),
            shaped(2, REACH, lines, columns, channels),
        ),
        [pltpu.SemaphoreType.DMA((4,))],
        (activations, second_cache, first_cache),
        in_place=range(3),
    )
    received = lax.ppermute(tail, "section", ring)
    sums, packed, weight = call(
        stats_kernel,
        (
            sums_shape,
            jax.ShapeDtypeStruct((len(vectors), 1, channels), jnp.float32),
            shaped(*conv1_weight.shape),
        ),
        [pltpu.SemaphoreType.DMA((1 + len(vectors),))],
        (own, conv1_weight) + tuple(vector.reshape(1, channels) for vector in vectors),
        in_place=range(1, 2 + len(vectors)),
    )
    received, pair = lax.optimization_barrier((received, with_near(sums)))
    halo = jnp.where(lax.axis_index("section") == 0, caches[1], received)
    joined = jnp.concatenate([caches[0], halo, own], axis=0)
    middle, tail, cache, sums = call(
        functools.partial(first_kernel, row_count),
        (shaped(frames, *wide), shaped(REACH, *wide), shaped(REACH, *wide), sums_shape),
        [pltpu.VMEM((frames + REACH, 3 * lines, columns, channels), jnp.bfloat16)],
        (joined, across(joined, near), across(joined, far), exchange(pair), packed, weight),
        flops=10**9,
    )
    return call(
        functools.partial(second_kernel, row_count),
        shaped(*activations.shape),
        [pltpu.VMEM((frames + REACH, *wide), jnp.bfloat16)],
        (
            middle, lax.ppermute(tail, "section", ring), cache, exchange(with_near(sums)),
            packed, conv2_weight, own,
        ),
        flops=10**9,
    )


def solution(mesh):
    in_specs = (
        P("section", "rows", None, None),
        P(None, "rows", None, None),
        P(None, "rows", None, None),
        P(),
        P(),
        P(),
        P(),
        P(),
        P(),
        P(),
        P(),
    )
    out_specs = P("section", "rows", None, None)
    return jax.shard_map(
        on_device, mesh=mesh, in_specs=in_specs, out_specs=out_specs, check_vma=False
    )
```

```python
import functools

import functools

import jax
import jax.numpy as jnp
from jax import lax
from jax.experimental import pallas as pl
from jax.experimental.pallas import tpu as pltpu
from jax.sharding import PartitionSpec as P

GROUPS = 32
REACH = 2

epsilon = 1e-06


def moments(blocks):
    pivot = blocks[0][:1]
    cells = sum(block.shape[0] for block in blocks)
    total, squares = 0.0, 0.0
    for block in blocks:
        away = block - pivot
        total = total + jnp.sum(away, axis=0, keepdims=True)
        squares = squares + jnp.sum(away * away, axis=0, keepdims=True)
    shift = total * (1.0 / cells)
    return jnp.concatenate([pivot + shift, squares - total * shift], axis=1)


def affine(stats, cells, scale, shift):
    devices, channels = stats.shape[0], scale.shape[-1]
    means, squares = stats[:, :channels], stats[:, channels:]
    mean = jnp.sum(means, axis=0, keepdims=True) * (1.0 / devices)
    away = means - mean
    square = jnp.sum(squares + cells * (away * away), axis=0, keepdims=True)
    count = cells * devices
    lane = lax.broadcasted_iota(jnp.int32, mean.shape, 1)
    step = 1
    while step < channels // GROUPS:

        def partner(values):
            up = pltpu.roll(values, channels - step, 1)
            return jnp.where((lane // step) % 2 == 0, up, pltpu.roll(values, step, 1))

        away = partner(mean) - mean
        square = square + partner(square) + (0.5 * count) * (away * away)
        mean = mean + 0.5 * away
        count, step = 2 * count, 2 * step
    slope = 0.5 * scale * lax.rsqrt(square * (1.0 / count) + epsilon)
    return slope, 0.5 * shift - mean * slope


def activate(values, slope, offset):
    half = values.astype(jnp.float32) * slope + offset
    return half + half * jnp.tanh(half)


def pair_conv(field, row, frames, weight_ref):
    columns, channels = field.shape[2], field.shape[3]
    pieces, blocks = [], []
    nothing = jnp.zeros((channels, channels), jnp.bfloat16)
    for frame_tap in range(3):
        for line in range(4):
            piece = field[frame_tap : frame_tap + frames, row + line]
            pieces.append(piece.reshape(frames * columns, channels))
            blocks.append(
                jnp.concatenate(
                    [
                        weight_ref[frame_tap, line - out, col_tap]
                        if 0 <= line - out <= 2
                        else nothing
                        for col_tap in range(3)
                        for out in range(2)
                    ],
                    axis=1,
                )
            )
    product = jnp.dot(
        jnp.concatenate(pieces, axis=1),
        jnp.concatenate(blocks, axis=0),
        preferred_element_type=jnp.float32,
    )
    cells = frames * columns
    column = lax.broadcasted_iota(jnp.int32, (cells, channels), 0) % columns
    results = []
    for out in range(2):
        left, centre, right = (
            product[:, (2 * tap + out) * channels : (2 * tap + out + 1) * channels]
            for tap in range(3)
        )
        left = jnp.where(column == 0, 0.0, pltpu.roll(left, 1, 0))
        right = jnp.where(column == columns - 1, 0.0, pltpu.roll(right, cells - 1, 0))
        results.append(left + centre + right)
    return results


def copy_kernel(own_ref, second_cache_ref, first_cache_ref, tail_ref, copied, caches_ref, sems):
    kept = tail_ref.shape[0]
    copies = [
        (own_ref.at[own_ref.shape[0] - kept :], tail_ref),
        (own_ref, copied),
        (second_cache_ref, caches_ref.at[0]),
        (first_cache_ref, caches_ref.at[1]),
    ]
    copies = [
        pltpu.make_async_copy(source, target, sems.at[index])
        for index, (source, target) in enumerate(copies)
    ]
    for copy in copies:
        copy.start()
    for copy in copies:
        copy.wait()


def stats_kernel(own_ref, weight_ref, *rest):
    *vector_refs, stats_ref, vectors_ref, weight_copy, sems = rest
    loads = [pltpu.make_async_copy(weight_ref, weight_copy, sems.at[0])]
    loads += [
        pltpu.make_async_copy(vector_ref, vectors_ref.at[index], sems.at[1 + index])
        for index, vector_ref in enumerate(vector_refs)
    ]
    for load in loads:
        load.start()
    channels = own_ref.shape[-1]
    blocks = [own_ref[frame].astype(jnp.float32) for frame in range(own_ref.shape[0])]
    stats_ref[...] = moments([block.reshape(-1, channels) for block in blocks])
    for load in loads:
        load.wait()


def affine_kernel(row_count, cells, which, stats_ref, vectors_ref, affine_ref):
    section = lax.axis_index("section")
    scale, shift = vectors_ref[which], vectors_ref[which + 1]
    for index, span in enumerate((section, jnp.maximum(section - 1, 0))):
        stats = stats_ref[pl.ds(span * row_count, row_count)]
        slope, offset = affine(stats.reshape(row_count, stats.shape[-1]), cells, scale, shift)
        affine_ref[2 * index] = slope
        affine_ref[2 * index + 1] = offset


def first_kernel(
    row_count, own_ref, near_ref, far_ref, affine_ref, vectors_ref, weight_ref, middle_ref,
    tail_ref, cache_ref, sums_ref, field
):
    section, row_at = lax.axis_index("section"), lax.axis_index("rows")
    inner, columns = middle_ref.shape[0], middle_ref.shape[2]
    lines, channels = own_ref.shape[1], own_ref.shape[3]
    slope, offset, slope_before, offset_before = (affine_ref[row] for row in range(4))
    even = row_at % 2 == 0
    at_start = section == 0

    def fill(line):
        side, local = divmod(line, lines)
        if side == 1:
            block = own_ref[:, local]
        else:
            near_side = even if side == 2 else jnp.logical_not(even)
            block = jnp.where(near_side, near_ref[:, local], far_ref[:, local])
        cache, halo, body = block[:REACH], block[REACH : 2 * REACH], block[2 * REACH :]
        behind = activate(halo, slope_before, offset_before).astype(jnp.bfloat16)
        behind = jnp.where(at_start, halo, behind)
        ahead = activate(body, slope, offset).astype(jnp.bfloat16)
        if side != 1:
            outside = row_at == 0 if side == 0 else row_at == row_count - 1
            behind = jnp.where(outside, jnp.zeros_like(behind), behind)
            ahead = jnp.where(outside, jnp.zeros_like(ahead), ahead)
        field[:REACH, line] = behind
        field[REACH:, line] = ahead
        if lines - 1 <= line <= 2 * lines:
            cache_ref[:, line - lines + 1] = cache

    bias = vectors_ref[2]
    kept = []
    ready = 0
    for pair in range((lines + 2) // 2):
        for line in range(ready, 2 * pair + 4):
            fill(line)
        ready = 2 * pair + 4
        results = pair_conv(field, 2 * pair, inner, weight_ref)
        for out in range(2):
            line = 2 * pair + out
            rounded = (results[out] + bias).astype(jnp.bfloat16)
            if 1 <= line <= lines:
                kept.append(rounded.astype(jnp.float32))
            rounded = rounded.reshape(inner, columns, channels)
            middle_ref[:, line] = rounded
            tail_ref[:, line] = rounded[inner - REACH :]
    sums_ref[...] = moments(kept)


def second_kernel(
    row_count, middle_ref, halo_ref, cache_ref, affine_ref, vectors_ref, weight_ref, own_ref,
    out_ref, field
):
    section, row_at = lax.axis_index("section"), lax.axis_index("rows")
    frames, lines, columns, channels = own_ref.shape
    slope, offset, slope_before, offset_before = (affine_ref[row] for row in range(4))
    at_start = section == 0
    for line in range(lines + 2):
        behind = activate(halo_ref[:, line], slope_before, offset_before).astype(jnp.bfloat16)
        behind = jnp.where(at_start, cache_ref[:, line], behind)
        ahead = activate(middle_ref[:, line], slope, offset).astype(jnp.bfloat16)
        if line == 0 or line == lines + 1:
            outside = row_at == 0 if line == 0 else row_at == row_count - 1
            behind = jnp.where(outside, jnp.zeros_like(behind), behind)
            ahead = jnp.where(outside, jnp.zeros_like(ahead), ahead)
        field[:REACH, line] = behind
        field[REACH:, line] = ahead
    bias = vectors_ref[5]
    for pair in range(lines // 2):
        results = pair_conv(field, 2 * pair, frames, weight_ref)
        for out in range(2):
            line = 2 * pair + out
            result = (results[out] + bias).reshape(frames, columns, channels)
            out_ref[:, line] = (result + own_ref[:, line].astype(jnp.float32)).astype(jnp.bfloat16)


def call(kernel, out_shape, scratch, operands, in_place=(), flops=0):
    vmem = pl.BlockSpec(memory_space=pltpu.VMEM)
    specs = [vmem] * len(operands)
    for index in in_place:
        specs[index] = pl.BlockSpec(memory_space=pltpu.HBM)
    operands = [
        pltpu.with_memory_space_constraint(operand, pltpu.HBM) if index in in_place else operand
        for index, operand in enumerate(operands)
    ]
    return pl.pallas_call(
        kernel,
        out_shape=out_shape,
        in_specs=specs,
        out_specs=jax.tree.map(lambda _: vmem, out_shape),
        scratch_shapes=scratch,
        compiler_params=pltpu.CompilerParams(vmem_limit_bytes=40 * 2**20),
        cost_estimate=pl.CostEstimate(flops=flops, bytes_accessed=2**20, transcendentals=0),
    )(*operands)


def on_device(
    activations,
    first_cache,
    second_cache,
    norm1_scale,
    norm1_shift,
    conv1_weight,
    conv1_bias,
    norm2_scale,
    norm2_shift,
    conv2_weight,
    conv2_bias,
):
    frames, lines, columns, channels = activations.shape
    sections, row_count = lax.axis_size("section"), lax.axis_size("rows")
    near = [i ^ 1 for i in range(row_count)]
    far = [0] + [i + 1 if i % 2 else i - 1 for i in range(1, row_count - 1)] + [row_count - 1]
    ring = [(at, (at + 1) % sections) for at in range(sections)]
    vectors = (norm1_scale, norm1_shift, conv1_bias, norm2_scale, norm2_shift, conv2_bias)
    wide = (lines + 2, columns, channels)

    def across(block, partner):
        return lax.ppermute(block, "rows", list(enumerate(partner)))

    def coefficients(sums, which):
        everyone = jnp.broadcast_to(sums, (sections * row_count,) + sums.shape)
        stats = lax.all_to_all(everyone, ("section", "rows"), 0, 0, tiled=True)
        return call(
            functools.partial(affine_kernel, row_count, frames * lines * columns, which),
            jax.ShapeDtypeStruct((4, 1, channels), jnp.float32),
            [],
            (stats, packed),
            flops=10**11,
        )

    def shaped(*shape):
        return jax.ShapeDtypeStruct(shape, jnp.bfloat16)

    sums_shape = jax.ShapeDtypeStruct((1, 2 * channels), jnp.float32)
    tail, own, caches = call(
        copy_kernel,
        (
            shaped(REACH, lines, columns, channels),
            shaped(*activations.shape),
            shaped(2, REACH, lines, columns, channels),
        ),
        [pltpu.SemaphoreType.DMA((4,))],
        (activations, second_cache, first_cache),
        in_place=range(3),
    )
    received = lax.ppermute(tail, "section", ring)
    sums, packed, weight = call(
        stats_kernel,
        (
            sums_shape,
            jax.ShapeDtypeStruct((len(vectors), 1, channels), jnp.float32),
            shaped(*conv1_weight.shape),
        ),
        [pltpu.SemaphoreType.DMA((1 + len(vectors),))],
        (own, conv1_weight) + tuple(vector.reshape(1, channels) for vector in vectors),
        in_place=range(1, 2 + len(vectors)),
    )
    received, _ = lax.optimization_barrier((received, sums))
    halo = jnp.where(lax.axis_index("section") == 0, caches[1], received)
    joined = jnp.concatenate([caches[0], halo, own], axis=0)
    middle, tail, cache, sums = call(
        functools.partial(first_kernel, row_count),
        (shaped(frames, *wide), shaped(REACH, *wide), shaped(REACH, *wide), sums_shape),
        [pltpu.VMEM((frames + REACH, 3 * lines, columns, channels), jnp.bfloat16)],
        (
            joined, across(joined, near), across(joined, far), coefficients(sums, 0), packed,
            weight,
        ),
        flops=10**9,
    )
    return call(
        functools.partial(second_kernel, row_count),
        shaped(*activations.shape),
        [pltpu.VMEM((frames + REACH, *wide), jnp.bfloat16)],
        (
            middle, lax.ppermute(tail, "section", ring), cache, coefficients(sums, 3),
            packed, conv2_weight, own,
        ),
        flops=10**9,
    )


def solution(mesh):
    in_specs = (
        P("section", "rows", None, None),
        P(None, "rows", None, None),
        P(None, "rows", None, None),
        P(),
        P(),
        P(),
        P(),
        P(),
        P(),
        P(),
        P(),
    )
    out_specs = P("section", "rows", None, None)
    return jax.shard_map(
        on_device, mesh=mesh, in_specs=in_specs, out_specs=out_specs, check_vma=False
    )
```

```python
import functools

import functools

import jax
import jax.numpy as jnp
from jax import lax
from jax.experimental import pallas as pl
from jax.experimental.pallas import tpu as pltpu
from jax.sharding import PartitionSpec as P

GROUPS = 32
SPAN_HALO = 4

epsilon = 1e-06


def moments(blocks):
    pivot = blocks[0][:1]
    cells = sum(block.shape[0] for block in blocks)
    total, squares = 0.0, 0.0
    for block in blocks:
        away = block - pivot
        total = total + jnp.sum(away, axis=0, keepdims=True)
        squares = squares + jnp.sum(away * away, axis=0, keepdims=True)
    shift = total * (1.0 / cells)
    return jnp.concatenate([pivot + shift, squares - total * shift], axis=1)


def affine(stats, cells, scale, shift):
    devices, channels = stats.shape[0], scale.shape[-1]
    means, squares = stats[:, :channels], stats[:, channels:]
    mean = jnp.sum(means, axis=0, keepdims=True) * (1.0 / devices)
    away = means - mean
    square = jnp.sum(squares + cells * (away * away), axis=0, keepdims=True)
    count = cells * devices
    lane = lax.broadcasted_iota(jnp.int32, mean.shape, 1)
    step = 1
    while step < channels // GROUPS:

        def partner(values):
            up = pltpu.roll(values, channels - step, 1)
            return jnp.where((lane // step) % 2 == 0, up, pltpu.roll(values, step, 1))

        away = partner(mean) - mean
        square = square + partner(square) + (0.5 * count) * (away * away)
        mean = mean + 0.5 * away
        count, step = 2 * count, 2 * step
    slope = 0.5 * scale * lax.rsqrt(square * (1.0 / count) + epsilon)
    return slope, 0.5 * shift - mean * slope


def activate(values, slope, offset):
    half = values.astype(jnp.float32) * slope + offset
    return half + half * jnp.tanh(half)


def pair_conv(field, row, frames, weight_ref):
    columns, channels = field.shape[2], field.shape[3]
    pieces, blocks = [], []
    nothing = jnp.zeros((channels, channels), jnp.bfloat16)
    for frame_tap in range(3):
        for line in range(4):
            piece = field[frame_tap : frame_tap + frames, row + line]
            pieces.append(piece.reshape(frames * columns, channels))
            blocks.append(
                jnp.concatenate(
                    [
                        weight_ref[frame_tap, line - out, col_tap]
                        if 0 <= line - out <= 2
                        else nothing
                        for col_tap in range(3)
                        for out in range(2)
                    ],
                    axis=1,
                )
            )
    product = jnp.dot(
        jnp.concatenate(pieces, axis=1),
        jnp.concatenate(blocks, axis=0),
        preferred_element_type=jnp.float32,
    )
    cells = frames * columns
    column = lax.broadcasted_iota(jnp.int32, (cells, channels), 0) % columns
    results = []
    for out in range(2):
        left, centre, right = (
            product[:, (2 * tap + out) * channels : (2 * tap + out + 1) * channels]
            for tap in range(3)
        )
        left = jnp.where(column == 0, 0.0, pltpu.roll(left, 1, 0))
        right = jnp.where(column == columns - 1, 0.0, pltpu.roll(right, cells - 1, 0))
        results.append(left + centre + right)
    return results


def copy_kernel(sections, own_ref, second_cache_ref, first_cache_ref, copied, halo_ref, sems):
    last = lax.axis_index("section") == sections - 1
    frames = own_ref.shape[0]
    spare = SPAN_HALO - 2
    tail = pltpu.make_async_copy(own_ref.at[frames - SPAN_HALO :], halo_ref, sems.at[0])
    older = pltpu.make_async_copy(second_cache_ref, halo_ref.at[:spare], sems.at[1])
    newer = pltpu.make_async_copy(first_cache_ref, halo_ref.at[spare:], sems.at[2])
    load = pltpu.make_async_copy(own_ref, copied, sems.at[3])

    @pl.when(last)
    def _():
        older.start()
        newer.start()

    @pl.when(jnp.logical_not(last))
    def _():
        tail.start()

    load.start()

    @pl.when(last)
    def _():
        older.wait()
        newer.wait()

    @pl.when(jnp.logical_not(last))
    def _():
        tail.wait()

    load.wait()


def stats_kernel(own_ref, weight_ref, *rest):
    *vector_refs, stats_ref, vectors_ref, weight_copy, sems = rest
    loads = [pltpu.make_async_copy(weight_ref, weight_copy, sems.at[0])]
    loads += [
        pltpu.make_async_copy(vector_ref, vectors_ref.at[index], sems.at[1 + index])
        for index, vector_ref in enumerate(vector_refs)
    ]
    for load in loads:
        load.start()
    channels = own_ref.shape[-1]
    blocks = [own_ref[frame].astype(jnp.float32) for frame in range(own_ref.shape[0])]
    packed = moments([block.reshape(-1, channels) for block in blocks])
    stats_ref[...] = jnp.broadcast_to(packed[None], stats_ref.shape)
    for load in loads:
        load.wait()


def affine_kernel(row_count, cells, which, stats_ref, vectors_ref, affine_ref):
    section = lax.axis_index("section")
    scale, shift = vectors_ref[which], vectors_ref[which + 1]
    for index, span in enumerate((section, jnp.maximum(section - 1, 0))):
        stats = stats_ref[pl.ds(span * row_count, row_count)]
        slope, offset = affine(stats.reshape(row_count, stats.shape[-1]), cells, scale, shift)
        affine_ref[2 * index] = slope
        affine_ref[2 * index + 1] = offset


def first_kernel(
    row_count, own_ref, near_ref, far_ref, affine_ref, vectors_ref, weight_ref, middle_ref,
    sums_ref, field
):
    section, row_at = lax.axis_index("section"), lax.axis_index("rows")
    frames, lines, columns, channels = own_ref.shape
    inner = frames - SPAN_HALO
    slope, offset, slope_before, offset_before = (affine_ref[row] for row in range(4))
    even = row_at % 2 == 0
    at_start = section == 0

    def fill(line):
        side, local = divmod(line, lines)
        if side == 1:
            block = own_ref[:, local]
        else:
            near_side = even if side == 2 else jnp.logical_not(even)
            block = jnp.where(near_side, near_ref[:, local], far_ref[:, local])
        halo, body = block[:SPAN_HALO], block[SPAN_HALO:]
        behind = activate(halo, slope_before, offset_before).astype(jnp.bfloat16)
        behind = jnp.where(at_start, halo, behind)
        ahead = activate(body, slope, offset).astype(jnp.bfloat16)
        if side != 1:
            outside = row_at == 0 if side == 0 else row_at == row_count - 1
            behind = jnp.where(outside, jnp.zeros_like(behind), behind)
            ahead = jnp.where(outside, jnp.zeros_like(ahead), ahead)
        field[:SPAN_HALO, line] = behind
        field[SPAN_HALO:, line] = ahead

    bias = vectors_ref[2]
    kept = []
    spare = SPAN_HALO - 2
    ready = 0
    for pair in range((lines + 2) // 2):
        for line in range(ready, 2 * pair + 4):
            fill(line)
        ready = 2 * pair + 4
        results = pair_conv(field, 2 * pair, inner + 2, weight_ref)
        for out in range(2):
            line = 2 * pair + out
            rounded = (results[out] + bias).astype(jnp.bfloat16)
            rounded = rounded.reshape(inner + 2, columns, channels)
            middle_ref[:2, line] = jnp.where(at_start, field[:spare, line + lines - 1], rounded[:2])
            middle_ref[2:, line] = rounded[2:]
            if 1 <= line <= lines:
                kept.append(rounded[2:].astype(jnp.float32).reshape(-1, channels))
    sums_ref[...] = jnp.broadcast_to(moments(kept)[None], sums_ref.shape)


def second_kernel(
    row_count, middle_ref, affine_ref, vectors_ref, weight_ref, own_ref, out_ref, field
):
    section, row_at = lax.axis_index("section"), lax.axis_index("rows")
    frames, lines, columns, channels = own_ref.shape
    slope, offset, slope_before, offset_before = (affine_ref[row] for row in range(4))
    at_start = section == 0
    for line in range(lines + 2):
        halo, body = middle_ref[:2, line], middle_ref[2:, line]
        behind = activate(halo, slope_before, offset_before).astype(jnp.bfloat16)
        behind = jnp.where(at_start, halo, behind)
        ahead = activate(body, slope, offset).astype(jnp.bfloat16)
        if line == 0 or line == lines + 1:
            outside = row_at == 0 if line == 0 else row_at == row_count - 1
            behind = jnp.where(outside, jnp.zeros_like(behind), behind)
            ahead = jnp.where(outside, jnp.zeros_like(ahead), ahead)
        field[:2, line] = behind
        field[2:, line] = ahead
    bias = vectors_ref[5]
    for pair in range(lines // 2):
        results = pair_conv(field, 2 * pair, frames, weight_ref)
        for out in range(2):
            line = 2 * pair + out
            result = (results[out] + bias).reshape(frames, columns, channels)
            out_ref[:, line] = (result + own_ref[:, line].astype(jnp.float32)).astype(jnp.bfloat16)


def call(kernel, out_shape, scratch, operands, in_place=(), flops=0):
    vmem = pl.BlockSpec(memory_space=pltpu.VMEM)
    specs = [vmem] * len(operands)
    for index in in_place:
        specs[index] = pl.BlockSpec(memory_space=pltpu.HBM)
    operands = [
        pltpu.with_memory_space_constraint(operand, pltpu.HBM) if index in in_place else operand
        for index, operand in enumerate(operands)
    ]
    return pl.pallas_call(
        kernel,
        out_shape=out_shape,
        in_specs=specs,
        out_specs=jax.tree.map(lambda _: vmem, out_shape),
        scratch_shapes=scratch,
        compiler_params=pltpu.CompilerParams(vmem_limit_bytes=40 * 2**20),
        cost_estimate=pl.CostEstimate(flops=flops, bytes_accessed=2**20, transcendentals=0),
    )(*operands)


def on_device(
    activations,
    first_cache,
    second_cache,
    norm1_scale,
    norm1_shift,
    conv1_weight,
    conv1_bias,
    norm2_scale,
    norm2_shift,
    conv2_weight,
    conv2_bias,
):
    frames, lines, columns, channels = activations.shape
    sections, row_count = lax.axis_size("section"), lax.axis_size("rows")
    everyone = sections * row_count
    stats_shape = jax.ShapeDtypeStruct((everyone, 1, 2 * channels), jnp.float32)
    vectors = (norm1_scale, norm1_shift, conv1_bias, norm2_scale, norm2_shift, conv2_bias)

    near = [i ^ 1 for i in range(row_count)]
    far = [0] + [i + 1 if i % 2 else i - 1 for i in range(1, row_count - 1)] + [row_count - 1]

    def across(block, partner):
        return lax.ppermute(block, "rows", list(enumerate(partner)))

    ring = [(at, (at + 1) % sections) for at in range(sections)]
    own, halo = call(
        functools.partial(copy_kernel, sections),
        (
            jax.ShapeDtypeStruct(activations.shape, jnp.bfloat16),
            jax.ShapeDtypeStruct((SPAN_HALO, lines, columns, channels), jnp.bfloat16),
        ),
        [pltpu.SemaphoreType.DMA((4,))],
        (activations, second_cache, first_cache),
        in_place=range(3),
    )
    sums, packed, weight = call(
        stats_kernel,
        (
            stats_shape,
            jax.ShapeDtypeStruct((len(vectors), 1, channels), jnp.float32),
            jax.ShapeDtypeStruct(conv1_weight.shape, jnp.bfloat16),
        ),
        [pltpu.SemaphoreType.DMA((1 + len(vectors),))],
        (own, conv1_weight) + tuple(vector.reshape(1, channels) for vector in vectors),
        in_place=range(1, 2 + len(vectors)),
    )
    received = lax.ppermute(halo, "section", ring)
    received, _ = lax.optimization_barrier((received, sums))
    joined = jnp.concatenate([received, own], axis=0)

    def coefficients(sums, which):
        stats = lax.all_to_all(sums, ("section", "rows"), 0, 0, tiled=True)
        return call(
            functools.partial(affine_kernel, row_count, frames * lines * columns, which),
            jax.ShapeDtypeStruct((4, 1, channels), jnp.float32),
            [],
            (stats, packed),
            flops=10**11,
        )

    middle, sums = call(
        functools.partial(first_kernel, row_count),
        (
            jax.ShapeDtypeStruct((frames + 2, lines + 2, columns, channels), jnp.bfloat16),
            stats_shape,
        ),
        [pltpu.VMEM((frames + SPAN_HALO, 3 * lines, columns, channels), jnp.bfloat16)],
        (
            joined, across(joined, near), across(joined, far), coefficients(sums, 0), packed,
            weight,
        ),
        flops=10**9,
    )
    return call(
        functools.partial(second_kernel, row_count),
        jax.ShapeDtypeStruct(activations.shape, jnp.bfloat16),
        [pltpu.VMEM((frames + 2, lines + 2, columns, channels), jnp.bfloat16)],
        (middle, coefficients(sums, 3), packed, conv2_weight, own),
        flops=10**9,
    )


def solution(mesh):
    in_specs = (
        P("section", "rows", None, None),
        P(None, "rows", None, None),
        P(None, "rows", None, None),
        P(),
        P(),
        P(),
        P(),
        P(),
        P(),
        P(),
        P(),
    )
    out_specs = P("section", "rows", None, None)
    return jax.shard_map(
        on_device, mesh=mesh, in_specs=in_specs, out_specs=out_specs, check_vma=False
    )
```

```python
import functools

import functools

import jax
import jax.numpy as jnp
from jax import lax
from jax.experimental import pallas as pl
from jax.experimental.pallas import tpu as pltpu
from jax.sharding import PartitionSpec as P

GROUPS = 32
SPAN_HALO = 4

epsilon = 1e-06


def moments(blocks):
    pivot = blocks[0][:1]
    cells = sum(block.shape[0] for block in blocks)
    total, squares = 0.0, 0.0
    for block in blocks:
        away = block - pivot
        total = total + jnp.sum(away, axis=0, keepdims=True)
        squares = squares + jnp.sum(away * away, axis=0, keepdims=True)
    shift = total * (1.0 / cells)
    return jnp.concatenate([pivot + shift, squares - total * shift], axis=0)


def affine(stats, cells, scale, shift):
    devices, _, channels = stats.shape
    means, squares = stats[:, 0], stats[:, 1]
    mean = jnp.sum(means, axis=0, keepdims=True) * (1.0 / devices)
    away = means - mean
    square = jnp.sum(squares + cells * (away * away), axis=0, keepdims=True)
    count = cells * devices
    lane = lax.broadcasted_iota(jnp.int32, mean.shape, 1)
    step = 1
    while step < channels // GROUPS:

        def partner(values):
            up = pltpu.roll(values, channels - step, 1)
            return jnp.where((lane // step) % 2 == 0, up, pltpu.roll(values, step, 1))

        away = partner(mean) - mean
        square = square + partner(square) + (0.5 * count) * (away * away)
        mean = mean + 0.5 * away
        count, step = 2 * count, 2 * step
    slope = 0.5 * scale * lax.rsqrt(square * (1.0 / count) + epsilon)
    return slope, 0.5 * shift - mean * slope


def activate(values, slope, offset):
    half = values.astype(jnp.float32) * slope + offset
    return half + half * jnp.tanh(half)


def pair_conv(field, row, frames, weight_ref):
    columns, channels = field.shape[2], field.shape[3]
    pieces, blocks = [], []
    nothing = jnp.zeros((channels, channels), jnp.bfloat16)
    for frame_tap in range(3):
        for line in range(4):
            piece = field[frame_tap : frame_tap + frames, row + line]
            pieces.append(piece.reshape(frames * columns, channels))
            blocks.append(
                jnp.concatenate(
                    [
                        weight_ref[frame_tap, line - out, col_tap]
                        if 0 <= line - out <= 2
                        else nothing
                        for col_tap in range(3)
                        for out in range(2)
                    ],
                    axis=1,
                )
            )
    product = jnp.dot(
        jnp.concatenate(pieces, axis=1),
        jnp.concatenate(blocks, axis=0),
        preferred_element_type=jnp.float32,
    )
    cells = frames * columns
    column = lax.broadcasted_iota(jnp.int32, (cells, channels), 0) % columns
    results = []
    for out in range(2):
        left, centre, right = (
            product[:, (2 * tap + out) * channels : (2 * tap + out + 1) * channels]
            for tap in range(3)
        )
        left = jnp.where(column == 0, 0.0, pltpu.roll(left, 1, 0))
        right = jnp.where(column == columns - 1, 0.0, pltpu.roll(right, cells - 1, 0))
        results.append(left + centre + right)
    return results


def copy_kernel(sections, own_ref, second_cache_ref, first_cache_ref, copied, halo_ref, sems):
    last = lax.axis_index("section") == sections - 1
    frames = own_ref.shape[0]
    spare = SPAN_HALO - 2
    tail = pltpu.make_async_copy(own_ref.at[frames - SPAN_HALO :], halo_ref, sems.at[0])
    older = pltpu.make_async_copy(second_cache_ref, halo_ref.at[:spare], sems.at[1])
    newer = pltpu.make_async_copy(first_cache_ref, halo_ref.at[spare:], sems.at[2])
    load = pltpu.make_async_copy(own_ref, copied, sems.at[3])

    @pl.when(last)
    def _():
        older.start()
        newer.start()

    @pl.when(jnp.logical_not(last))
    def _():
        tail.start()

    load.start()

    @pl.when(last)
    def _():
        older.wait()
        newer.wait()

    @pl.when(jnp.logical_not(last))
    def _():
        tail.wait()

    load.wait()


def stats_kernel(own_ref, weight_ref, *rest):
    *vector_refs, stats_ref, vectors_ref, weight_copy, sems = rest
    loads = [pltpu.make_async_copy(weight_ref, weight_copy, sems.at[0])]
    loads += [
        pltpu.make_async_copy(vector_ref, vectors_ref.at[index], sems.at[1 + index])
        for index, vector_ref in enumerate(vector_refs)
    ]
    for load in loads:
        load.start()
    channels = own_ref.shape[-1]
    blocks = [own_ref[frame].astype(jnp.float32) for frame in range(own_ref.shape[0])]
    packed = moments([block.reshape(-1, channels) for block in blocks])
    for device in range(stats_ref.shape[0]):
        stats_ref[device] = packed
    for load in loads:
        load.wait()


def affine_kernel(row_count, cells, which, stats_ref, vectors_ref, affine_ref):
    section = lax.axis_index("section")
    scale, shift = vectors_ref[which], vectors_ref[which + 1]
    for index, span in enumerate((section, jnp.maximum(section - 1, 0))):
        stats = stats_ref[pl.ds(span * row_count, row_count)]
        slope, offset = affine(stats, cells, scale, shift)
        affine_ref[2 * index] = slope
        affine_ref[2 * index + 1] = offset


def first_kernel(
    row_count, own_ref, near_ref, far_ref, affine_ref, vectors_ref, weight_ref, next_ref,
    middle_ref, sums_ref, next_copy, field, sem
):
    load = pltpu.make_async_copy(next_ref, next_copy, sem)
    load.start()
    section, row_at = lax.axis_index("section"), lax.axis_index("rows")
    frames, lines, columns, channels = own_ref.shape
    inner = frames - SPAN_HALO
    slope, offset, slope_before, offset_before = (affine_ref[row] for row in range(4))
    even = row_at % 2 == 0
    at_start = section == 0

    def fill(line):
        side, local = divmod(line, lines)
        if side == 1:
            block = own_ref[:, local]
        else:
            near_side = even if side == 2 else jnp.logical_not(even)
            block = jnp.where(near_side, near_ref[:, local], far_ref[:, local])
        halo, body = block[:SPAN_HALO], block[SPAN_HALO:]
        behind = activate(halo, slope_before, offset_before).astype(jnp.bfloat16)
        behind = jnp.where(at_start, halo, behind)
        ahead = activate(body, slope, offset).astype(jnp.bfloat16)
        if side != 1:
            outside = row_at == 0 if side == 0 else row_at == row_count - 1
            behind = jnp.where(outside, jnp.zeros_like(behind), behind)
            ahead = jnp.where(outside, jnp.zeros_like(ahead), ahead)
        field[:SPAN_HALO, line] = behind
        field[SPAN_HALO:, line] = ahead

    bias = vectors_ref[2]
    kept = []
    spare = SPAN_HALO - 2
    ready = 0
    for pair in range((lines + 2) // 2):
        for line in range(ready, 2 * pair + 4):
            fill(line)
        ready = 2 * pair + 4
        results = pair_conv(field, 2 * pair, inner + 2, weight_ref)
        for out in range(2):
            line = 2 * pair + out
            rounded = (results[out] + bias).astype(jnp.bfloat16)
            rounded = rounded.reshape(inner + 2, columns, channels)
            middle_ref[:2, line] = jnp.where(at_start, field[:spare, line + lines - 1], rounded[:2])
            middle_ref[2:, line] = rounded[2:]
            if 1 <= line <= lines:
                kept.append(rounded[2:].astype(jnp.float32).reshape(-1, channels))
    packed = moments(kept)
    for device in range(sums_ref.shape[0]):
        sums_ref[device] = packed
    load.wait()


def second_kernel(
    row_count, middle_ref, affine_ref, vectors_ref, weight_ref, own_ref, out_ref, field
):
    section, row_at = lax.axis_index("section"), lax.axis_index("rows")
    frames, lines, columns, channels = own_ref.shape
    slope, offset, slope_before, offset_before = (affine_ref[row] for row in range(4))
    at_start = section == 0
    for line in range(lines + 2):
        halo, body = middle_ref[:2, line], middle_ref[2:, line]
        behind = activate(halo, slope_before, offset_before).astype(jnp.bfloat16)
        behind = jnp.where(at_start, halo, behind)
        ahead = activate(body, slope, offset).astype(jnp.bfloat16)
        if line == 0 or line == lines + 1:
            outside = row_at == 0 if line == 0 else row_at == row_count - 1
            behind = jnp.where(outside, jnp.zeros_like(behind), behind)
            ahead = jnp.where(outside, jnp.zeros_like(ahead), ahead)
        field[:2, line] = behind
        field[2:, line] = ahead
    bias = vectors_ref[5]
    for pair in range(lines // 2):
        results = pair_conv(field, 2 * pair, frames, weight_ref)
        for out in range(2):
            line = 2 * pair + out
            result = (results[out] + bias).reshape(frames, columns, channels)
            out_ref[:, line] = (result + own_ref[:, line].astype(jnp.float32)).astype(jnp.bfloat16)


def call(kernel, out_shape, scratch, operands, in_place=(), flops=0):
    vmem = pl.BlockSpec(memory_space=pltpu.VMEM)
    specs = [vmem] * len(operands)
    for index in in_place:
        specs[index] = pl.BlockSpec(memory_space=pltpu.HBM)
    operands = [
        pltpu.with_memory_space_constraint(operand, pltpu.HBM) if index in in_place else operand
        for index, operand in enumerate(operands)
    ]
    return pl.pallas_call(
        kernel,
        out_shape=out_shape,
        in_specs=specs,
        out_specs=jax.tree.map(lambda _: vmem, out_shape),
        scratch_shapes=scratch,
        compiler_params=pltpu.CompilerParams(vmem_limit_bytes=40 * 2**20),
        cost_estimate=pl.CostEstimate(flops=flops, bytes_accessed=2**20, transcendentals=0),
    )(*operands)


def on_device(
    activations,
    first_cache,
    second_cache,
    norm1_scale,
    norm1_shift,
    conv1_weight,
    conv1_bias,
    norm2_scale,
    norm2_shift,
    conv2_weight,
    conv2_bias,
):
    frames, lines, columns, channels = activations.shape
    sections, row_count = lax.axis_size("section"), lax.axis_size("rows")
    everyone = sections * row_count
    stats_shape = jax.ShapeDtypeStruct((everyone, 2, channels), jnp.float32)
    vectors = (norm1_scale, norm1_shift, conv1_bias, norm2_scale, norm2_shift, conv2_bias)

    near = [i ^ 1 for i in range(row_count)]
    far = [0] + [i + 1 if i % 2 else i - 1 for i in range(1, row_count - 1)] + [row_count - 1]

    def across(block, partner):
        return lax.ppermute(block, "rows", list(enumerate(partner)))

    ring = [(at, (at + 1) % sections) for at in range(sections)]
    own, halo = call(
        functools.partial(copy_kernel, sections),
        (
            jax.ShapeDtypeStruct(activations.shape, jnp.bfloat16),
            jax.ShapeDtypeStruct((SPAN_HALO, lines, columns, channels), jnp.bfloat16),
        ),
        [pltpu.SemaphoreType.DMA((4,))],
        (activations, second_cache, first_cache),
        in_place=range(3),
    )
    sums, packed, weight = call(
        stats_kernel,
        (
            stats_shape,
            jax.ShapeDtypeStruct((len(vectors), 1, channels), jnp.float32),
            jax.ShapeDtypeStruct(conv1_weight.shape, jnp.bfloat16),
        ),
        [pltpu.SemaphoreType.DMA((1 + len(vectors),))],
        (own, conv1_weight) + tuple(vector.reshape(1, channels) for vector in vectors),
        in_place=range(1, 2 + len(vectors)),
    )
    received = lax.ppermute(halo, "section", ring)
    received, _ = lax.optimization_barrier((received, sums))
    joined = jnp.concatenate([received, own], axis=0)

    def coefficients(sums, which):
        stats = lax.all_to_all(sums, ("section", "rows"), 0, 0, tiled=True)
        return call(
            functools.partial(affine_kernel, row_count, frames * lines * columns, which),
            jax.ShapeDtypeStruct((4, 1, channels), jnp.float32),
            [],
            (stats, packed),
            flops=10**11,
        )

    middle, sums, weight = call(
        functools.partial(first_kernel, row_count),
        (
            jax.ShapeDtypeStruct((frames + 2, lines + 2, columns, channels), jnp.bfloat16),
            stats_shape,
            jax.ShapeDtypeStruct(conv2_weight.shape, jnp.bfloat16),
        ),
        [
            pltpu.VMEM((frames + SPAN_HALO, 3 * lines, columns, channels), jnp.bfloat16),
            pltpu.SemaphoreType.DMA,
        ],
        (
            joined, across(joined, near), across(joined, far), coefficients(sums, 0), packed,
            weight, conv2_weight,
        ),
        in_place=(6,),
        flops=10**9,
    )
    return call(
        functools.partial(second_kernel, row_count),
        jax.ShapeDtypeStruct(activations.shape, jnp.bfloat16),
        [pltpu.VMEM((frames + 2, lines + 2, columns, channels), jnp.bfloat16)],
        (middle, coefficients(sums, 3), packed, weight, own),
        flops=10**9,
    )


def solution(mesh):
    in_specs = (
        P("section", "rows", None, None),
        P(None, "rows", None, None),
        P(None, "rows", None, None),
        P(),
        P(),
        P(),
        P(),
        P(),
        P(),
        P(),
        P(),
    )
    out_specs = P("section", "rows", None, None)
    return jax.shard_map(
        on_device, mesh=mesh, in_specs=in_specs, out_specs=out_specs, check_vma=False
    )
```

```python
import functools

import functools

import jax
import jax.numpy as jnp
from jax import lax
from jax.experimental import pallas as pl
from jax.experimental.pallas import tpu as pltpu
from jax.sharding import PartitionSpec as P

GROUPS = 32
SPAN_HALO = 4

epsilon = 1e-06


def moments(blocks):
    pivot = blocks[0][:1]
    cells = sum(block.shape[0] for block in blocks)
    total, squares = 0.0, 0.0
    for block in blocks:
        away = block - pivot
        total = total + jnp.sum(away, axis=0, keepdims=True)
        squares = squares + jnp.sum(away * away, axis=0, keepdims=True)
    shift = total * (1.0 / cells)
    return jnp.concatenate([pivot + shift, squares - total * shift], axis=0)


def affine(stats, cells, scale, shift):
    devices, _, channels = stats.shape
    means, squares = stats[:, 0], stats[:, 1]
    mean = jnp.sum(means, axis=0, keepdims=True) * (1.0 / devices)
    away = means - mean
    square = jnp.sum(squares + cells * (away * away), axis=0, keepdims=True)
    count = cells * devices
    lane = lax.broadcasted_iota(jnp.int32, mean.shape, 1)
    step = 1
    while step < channels // GROUPS:

        def partner(values):
            up = pltpu.roll(values, channels - step, 1)
            return jnp.where((lane // step) % 2 == 0, up, pltpu.roll(values, step, 1))

        away = partner(mean) - mean
        square = square + partner(square) + (0.5 * count) * (away * away)
        mean = mean + 0.5 * away
        count, step = 2 * count, 2 * step
    slope = 0.5 * scale * lax.rsqrt(square * (1.0 / count) + epsilon)
    return slope, 0.5 * shift - mean * slope


def activate(values, slope, offset):
    half = values.astype(jnp.float32) * slope + offset
    return half + half * jnp.tanh(half)


def pair_conv(field, row, frames, weight_ref):
    columns, channels = field.shape[2], field.shape[3]
    pieces, blocks = [], []
    nothing = jnp.zeros((channels, channels), jnp.bfloat16)
    for frame_tap in range(3):
        for line in range(4):
            piece = field[frame_tap : frame_tap + frames, row + line]
            pieces.append(piece.reshape(frames * columns, channels))
            blocks.append(
                jnp.concatenate(
                    [
                        weight_ref[frame_tap, line - out, col_tap]
                        if 0 <= line - out <= 2
                        else nothing
                        for col_tap in range(3)
                        for out in range(2)
                    ],
                    axis=1,
                )
            )
    product = jnp.dot(
        jnp.concatenate(pieces, axis=1),
        jnp.concatenate(blocks, axis=0),
        preferred_element_type=jnp.float32,
    )
    cells = frames * columns
    column = lax.broadcasted_iota(jnp.int32, (cells, channels), 0) % columns
    results = []
    for out in range(2):
        left, centre, right = (
            product[:, (2 * tap + out) * channels : (2 * tap + out + 1) * channels]
            for tap in range(3)
        )
        left = jnp.where(column == 0, 0.0, pltpu.roll(left, 1, 0))
        right = jnp.where(column == columns - 1, 0.0, pltpu.roll(right, cells - 1, 0))
        results.append(left + centre + right)
    return results


def copy_kernel(sections, own_ref, second_cache_ref, first_cache_ref, copied, halo_ref, sems):
    last = lax.axis_index("section") == sections - 1
    frames = own_ref.shape[0]
    spare = SPAN_HALO - 2
    tail = pltpu.make_async_copy(own_ref.at[frames - SPAN_HALO :], halo_ref, sems.at[0])
    older = pltpu.make_async_copy(second_cache_ref, halo_ref.at[:spare], sems.at[1])
    newer = pltpu.make_async_copy(first_cache_ref, halo_ref.at[spare:], sems.at[2])
    load = pltpu.make_async_copy(own_ref, copied, sems.at[3])

    @pl.when(last)
    def _():
        older.start()
        newer.start()

    @pl.when(jnp.logical_not(last))
    def _():
        tail.start()

    load.start()

    @pl.when(last)
    def _():
        older.wait()
        newer.wait()

    @pl.when(jnp.logical_not(last))
    def _():
        tail.wait()

    load.wait()


def stats_kernel(own_ref, weight_ref, *rest):
    *vector_refs, stats_ref, vectors_ref, weight_copy, sems = rest
    loads = [pltpu.make_async_copy(weight_ref, weight_copy, sems.at[0])]
    loads += [
        pltpu.make_async_copy(vector_ref, vectors_ref.at[index], sems.at[1 + index])
        for index, vector_ref in enumerate(vector_refs)
    ]
    for load in loads:
        load.start()
    channels = own_ref.shape[-1]
    blocks = [own_ref[frame].astype(jnp.float32) for frame in range(own_ref.shape[0])]
    packed = moments([block.reshape(-1, channels) for block in blocks])
    for device in range(stats_ref.shape[0]):
        stats_ref[device] = packed
    for load in loads:
        load.wait()


def affine_kernel(row_count, cells, which, stats_ref, vectors_ref, *rest):
    affine_ref = rest[-1]
    section = lax.axis_index("section")
    scale, shift = vectors_ref[which], vectors_ref[which + 1]
    for index, span in enumerate((section, jnp.maximum(section - 1, 0))):
        stats = stats_ref[pl.ds(span * row_count, row_count)]
        slope, offset = affine(stats, cells, scale, shift)
        affine_ref[2 * index] = slope
        affine_ref[2 * index + 1] = offset


def first_kernel(
    row_count, own_ref, near_ref, far_ref, halo_ref, halo_near_ref, halo_far_ref, affine_ref,
    vectors_ref, weight_ref, next_ref, middle_ref, sums_ref, next_copy, field, sem
):
    load = pltpu.make_async_copy(next_ref, next_copy, sem)
    load.start()
    section, row_at = lax.axis_index("section"), lax.axis_index("rows")
    inner, lines, columns, channels = own_ref.shape
    slope, offset, slope_before, offset_before = (affine_ref[row] for row in range(4))
    even = row_at % 2 == 0
    at_start = section == 0

    def fill(line):
        side, local = divmod(line, lines)
        if side == 1:
            halo, body = halo_ref[:, local], own_ref[:, local]
        else:
            near_side = even if side == 2 else jnp.logical_not(even)
            halo = jnp.where(near_side, halo_near_ref[:, local], halo_far_ref[:, local])
            body = jnp.where(near_side, near_ref[:, local], far_ref[:, local])
        behind = activate(halo, slope_before, offset_before).astype(jnp.bfloat16)
        behind = jnp.where(at_start, halo, behind)
        ahead = activate(body, slope, offset).astype(jnp.bfloat16)
        if side != 1:
            outside = row_at == 0 if side == 0 else row_at == row_count - 1
            behind = jnp.where(outside, jnp.zeros_like(behind), behind)
            ahead = jnp.where(outside, jnp.zeros_like(ahead), ahead)
        field[:SPAN_HALO, line] = behind
        field[SPAN_HALO:, line] = ahead

    bias = vectors_ref[2]
    kept = []
    spare = SPAN_HALO - 2
    ready = 0
    for pair in range((lines + 2) // 2):
        for line in range(ready, 2 * pair + 4):
            fill(line)
        ready = 2 * pair + 4
        results = pair_conv(field, 2 * pair, inner + 2, weight_ref)
        for out in range(2):
            line = 2 * pair + out
            rounded = (results[out] + bias).astype(jnp.bfloat16)
            rounded = rounded.reshape(inner + 2, columns, channels)
            middle_ref[:2, line] = jnp.where(at_start, field[:spare, line + lines - 1], rounded[:2])
            middle_ref[2:, line] = rounded[2:]
            if 1 <= line <= lines:
                kept.append(rounded[2:].astype(jnp.float32).reshape(-1, channels))
    packed = moments(kept)
    for device in range(sums_ref.shape[0]):
        sums_ref[device] = packed
    load.wait()


def second_kernel(
    row_count, middle_ref, affine_ref, vectors_ref, weight_ref, own_ref, out_ref, field
):
    section, row_at = lax.axis_index("section"), lax.axis_index("rows")
    frames, lines, columns, channels = own_ref.shape
    slope, offset, slope_before, offset_before = (affine_ref[row] for row in range(4))
    at_start = section == 0
    for line in range(lines + 2):
        halo, body = middle_ref[:2, line], middle_ref[2:, line]
        behind = activate(halo, slope_before, offset_before).astype(jnp.bfloat16)
        behind = jnp.where(at_start, halo, behind)
        ahead = activate(body, slope, offset).astype(jnp.bfloat16)
        if line == 0 or line == lines + 1:
            outside = row_at == 0 if line == 0 else row_at == row_count - 1
            behind = jnp.where(outside, jnp.zeros_like(behind), behind)
            ahead = jnp.where(outside, jnp.zeros_like(ahead), ahead)
        field[:2, line] = behind
        field[2:, line] = ahead
    bias = vectors_ref[5]
    for pair in range(lines // 2):
        results = pair_conv(field, 2 * pair, frames, weight_ref)
        for out in range(2):
            line = 2 * pair + out
            result = (results[out] + bias).reshape(frames, columns, channels)
            out_ref[:, line] = (result + own_ref[:, line].astype(jnp.float32)).astype(jnp.bfloat16)


def call(kernel, out_shape, scratch, operands, in_place=(), unread=(), flops=0):
    vmem = pl.BlockSpec(memory_space=pltpu.VMEM)
    specs = [vmem] * len(operands)
    for index in in_place:
        specs[index] = pl.BlockSpec(memory_space=pltpu.HBM)
    for index in unread:
        specs[index] = pl.BlockSpec(memory_space=pl.ANY)
    operands = [
        pltpu.with_memory_space_constraint(operand, pltpu.HBM) if index in in_place else operand
        for index, operand in enumerate(operands)
    ]
    return pl.pallas_call(
        kernel,
        out_shape=out_shape,
        in_specs=specs,
        out_specs=jax.tree.map(lambda _: vmem, out_shape),
        scratch_shapes=scratch,
        compiler_params=pltpu.CompilerParams(vmem_limit_bytes=40 * 2**20),
        cost_estimate=pl.CostEstimate(flops=flops, bytes_accessed=2**20, transcendentals=0),
    )(*operands)


def on_device(
    activations,
    first_cache,
    second_cache,
    norm1_scale,
    norm1_shift,
    conv1_weight,
    conv1_bias,
    norm2_scale,
    norm2_shift,
    conv2_weight,
    conv2_bias,
):
    frames, lines, columns, channels = activations.shape
    sections, row_count = lax.axis_size("section"), lax.axis_size("rows")
    everyone = sections * row_count
    stats_shape = jax.ShapeDtypeStruct((everyone, 2, channels), jnp.float32)
    vectors = (norm1_scale, norm1_shift, conv1_bias, norm2_scale, norm2_shift, conv2_bias)

    near = [i ^ 1 for i in range(row_count)]
    far = [0] + [i + 1 if i % 2 else i - 1 for i in range(1, row_count - 1)] + [row_count - 1]

    def across(block, partner):
        return lax.ppermute(block, "rows", list(enumerate(partner)))

    ring = [(at, (at + 1) % sections) for at in range(sections)]
    own, halo = call(
        functools.partial(copy_kernel, sections),
        (
            jax.ShapeDtypeStruct(activations.shape, jnp.bfloat16),
            jax.ShapeDtypeStruct((SPAN_HALO, lines, columns, channels), jnp.bfloat16),
        ),
        [pltpu.SemaphoreType.DMA((4,))],
        (activations, second_cache, first_cache),
        in_place=range(3),
    )
    sums, packed, weight = call(
        stats_kernel,
        (
            stats_shape,
            jax.ShapeDtypeStruct((len(vectors), 1, channels), jnp.float32),
            jax.ShapeDtypeStruct(conv1_weight.shape, jnp.bfloat16),
        ),
        [pltpu.SemaphoreType.DMA((1 + len(vectors),))],
        (own, conv1_weight) + tuple(vector.reshape(1, channels) for vector in vectors),
        in_place=range(1, 2 + len(vectors)),
        flops=10**11,
    )
    received = lax.ppermute(halo, "section", ring)
    received, _ = lax.optimization_barrier((received, sums))
    beside = [across(activations, near), across(activations, far)]
    behind = [received, across(received, near), across(received, far)]

    def coefficients(sums, which, *after):
        stats = lax.all_to_all(sums, ("section", "rows"), 0, 0, tiled=True)
        return call(
            functools.partial(affine_kernel, row_count, frames * lines * columns, which),
            jax.ShapeDtypeStruct((4, 1, channels), jnp.float32),
            [],
            (stats, packed, *after),
            unread=range(2, 2 + len(after)),
            flops=10**11,
        )

    middle, sums, weight = call(
        functools.partial(first_kernel, row_count),
        (
            jax.ShapeDtypeStruct((frames + 2, lines + 2, columns, channels), jnp.bfloat16),
            stats_shape,
            jax.ShapeDtypeStruct(conv2_weight.shape, jnp.bfloat16),
        ),
        [
            pltpu.VMEM((frames + SPAN_HALO, 3 * lines, columns, channels), jnp.bfloat16),
            pltpu.SemaphoreType.DMA,
        ],
        (
            own, *beside, *behind, coefficients(sums, 0, *beside), packed, weight,
            conv2_weight,
        ),
        in_place=(9,),
        flops=10**9,
    )
    return call(
        functools.partial(second_kernel, row_count),
        jax.ShapeDtypeStruct(activations.shape, jnp.bfloat16),
        [pltpu.VMEM((frames + 2, lines + 2, columns, channels), jnp.bfloat16)],
        (middle, coefficients(sums, 3), packed, weight, own),
        flops=10**9,
    )


def solution(mesh):
    in_specs = (
        P("section", "rows", None, None),
        P(None, "rows", None, None),
        P(None, "rows", None, None),
        P(),
        P(),
        P(),
        P(),
        P(),
        P(),
        P(),
        P(),
    )
    out_specs = P("section", "rows", None, None)
    return jax.shard_map(
        on_device, mesh=mesh, in_specs=in_specs, out_specs=out_specs, check_vma=False
    )
```

```python
import functools

import functools

import jax
import jax.numpy as jnp
from jax import lax
from jax.experimental import pallas as pl
from jax.experimental.pallas import tpu as pltpu
from jax.sharding import PartitionSpec as P

GROUPS = 32
SPAN_HALO = 4

epsilon = 1e-06


def moments(blocks):
    pivot = blocks[0][:1]
    cells = sum(block.shape[0] for block in blocks)
    total, squares = 0.0, 0.0
    for block in blocks:
        away = block - pivot
        total = total + jnp.sum(away, axis=0, keepdims=True)
        squares = squares + jnp.sum(away * away, axis=0, keepdims=True)
    shift = total * (1.0 / cells)
    return jnp.concatenate([pivot + shift, squares - total * shift], axis=0)


def affine(stats, cells, scale, shift):
    devices, _, channels = stats.shape
    means, squares = stats[:, 0], stats[:, 1]
    mean = jnp.sum(means, axis=0, keepdims=True) * (1.0 / devices)
    away = means - mean
    square = jnp.sum(squares + cells * (away * away), axis=0, keepdims=True)
    count = cells * devices
    lane = lax.broadcasted_iota(jnp.int32, mean.shape, 1)
    step = 1
    while step < channels // GROUPS:

        def partner(values):
            up = pltpu.roll(values, channels - step, 1)
            return jnp.where((lane // step) % 2 == 0, up, pltpu.roll(values, step, 1))

        away = partner(mean) - mean
        square = square + partner(square) + (0.5 * count) * (away * away)
        mean = mean + 0.5 * away
        count, step = 2 * count, 2 * step
    slope = 0.5 * scale * lax.rsqrt(square * (1.0 / count) + epsilon)
    return slope, 0.5 * shift - mean * slope


def activate(values, slope, offset):
    half = values.astype(jnp.float32) * slope + offset
    return half + half * jnp.tanh(half)


def pair_conv(field, row, frames, weight_ref):
    columns, channels = field.shape[2], field.shape[3]
    pieces, blocks = [], []
    nothing = jnp.zeros((channels, channels), jnp.bfloat16)
    for frame_tap in range(3):
        for line in range(4):
            piece = field[frame_tap : frame_tap + frames, row + line]
            pieces.append(piece.reshape(frames * columns, channels))
            blocks.append(
                jnp.concatenate(
                    [
                        weight_ref[frame_tap, line - out, col_tap]
                        if 0 <= line - out <= 2
                        else nothing
                        for col_tap in range(3)
                        for out in range(2)
                    ],
                    axis=1,
                )
            )
    product = jnp.dot(
        jnp.concatenate(pieces, axis=1),
        jnp.concatenate(blocks, axis=0),
        preferred_element_type=jnp.float32,
    )
    cells = frames * columns
    column = lax.broadcasted_iota(jnp.int32, (cells, channels), 0) % columns
    results = []
    for out in range(2):
        left, centre, right = (
            product[:, (2 * tap + out) * channels : (2 * tap + out + 1) * channels]
            for tap in range(3)
        )
        left = jnp.where(column == 0, 0.0, pltpu.roll(left, 1, 0))
        right = jnp.where(column == columns - 1, 0.0, pltpu.roll(right, cells - 1, 0))
        results.append(left + centre + right)
    return results


def copy_kernel(sections, own_ref, second_cache_ref, first_cache_ref, copied, halo_ref, sems):
    last = lax.axis_index("section") == sections - 1
    frames = own_ref.shape[0]
    spare = SPAN_HALO - 2
    tail = pltpu.make_async_copy(own_ref.at[frames - SPAN_HALO :], halo_ref, sems.at[0])
    older = pltpu.make_async_copy(second_cache_ref, halo_ref.at[:spare], sems.at[1])
    newer = pltpu.make_async_copy(first_cache_ref, halo_ref.at[spare:], sems.at[2])
    load = pltpu.make_async_copy(own_ref, copied, sems.at[3])

    @pl.when(last)
    def _():
        older.start()
        newer.start()

    @pl.when(jnp.logical_not(last))
    def _():
        tail.start()

    load.start()

    @pl.when(last)
    def _():
        older.wait()
        newer.wait()

    @pl.when(jnp.logical_not(last))
    def _():
        tail.wait()

    load.wait()


def stats_kernel(own_ref, weight_ref, *rest):
    *vector_refs, stats_ref, vectors_ref, weight_copy, sems = rest
    loads = [pltpu.make_async_copy(weight_ref, weight_copy, sems.at[0])]
    loads += [
        pltpu.make_async_copy(vector_ref, vectors_ref.at[index], sems.at[1 + index])
        for index, vector_ref in enumerate(vector_refs)
    ]
    for load in loads:
        load.start()
    channels = own_ref.shape[-1]
    blocks = [own_ref[frame].astype(jnp.float32) for frame in range(own_ref.shape[0])]
    packed = moments([block.reshape(-1, channels) for block in blocks])
    stats_ref[0] = packed
    for load in loads:
        load.wait()


def affine_kernel(row_count, cells, which, stats_ref, vectors_ref, *rest):
    affine_ref = rest[-1]
    section = lax.axis_index("section")
    scale, shift = vectors_ref[which], vectors_ref[which + 1]
    for index, span in enumerate((section, jnp.maximum(section - 1, 0))):
        if stats_ref.shape[1] == 4:
            stats = stats_ref[:, 2 * index : 2 * index + 2]
        else:
            stats = stats_ref[pl.ds(span * row_count, row_count)]
        slope, offset = affine(stats, cells, scale, shift)
        affine_ref[2 * index] = slope
        affine_ref[2 * index + 1] = offset


def first_kernel(
    row_count, own_ref, near_ref, far_ref, halo_ref, halo_near_ref, halo_far_ref, affine_ref,
    vectors_ref, weight_ref, next_ref, middle_ref, sums_ref, next_copy, field, sem
):
    load = pltpu.make_async_copy(next_ref, next_copy, sem)
    load.start()
    section, row_at = lax.axis_index("section"), lax.axis_index("rows")
    inner, lines, columns, channels = own_ref.shape
    slope, offset, slope_before, offset_before = (affine_ref[row] for row in range(4))
    even = row_at % 2 == 0
    at_start = section == 0

    def fill(line):
        side, local = divmod(line, lines)
        if side == 1:
            halo, body = halo_ref[:, local], own_ref[:, local]
        else:
            near_side = even if side == 2 else jnp.logical_not(even)
            halo = jnp.where(near_side, halo_near_ref[:, local], halo_far_ref[:, local])
            body = jnp.where(near_side, near_ref[:, local], far_ref[:, local])
        behind = activate(halo, slope_before, offset_before).astype(jnp.bfloat16)
        behind = jnp.where(at_start, halo, behind)
        ahead = activate(body, slope, offset).astype(jnp.bfloat16)
        if side != 1:
            outside = row_at == 0 if side == 0 else row_at == row_count - 1
            behind = jnp.where(outside, jnp.zeros_like(behind), behind)
            ahead = jnp.where(outside, jnp.zeros_like(ahead), ahead)
        field[:SPAN_HALO, line] = behind
        field[SPAN_HALO:, line] = ahead

    bias = vectors_ref[2]
    kept = []
    spare = SPAN_HALO - 2
    ready = 0
    for pair in range((lines + 2) // 2):
        for line in range(ready, 2 * pair + 4):
            fill(line)
        ready = 2 * pair + 4
        results = pair_conv(field, 2 * pair, inner + 2, weight_ref)
        for out in range(2):
            line = 2 * pair + out
            rounded = (results[out] + bias).astype(jnp.bfloat16)
            rounded = rounded.reshape(inner + 2, columns, channels)
            middle_ref[:2, line] = jnp.where(at_start, field[:spare, line + lines - 1], rounded[:2])
            middle_ref[2:, line] = rounded[2:]
            if 1 <= line <= lines:
                kept.append(rounded[2:].astype(jnp.float32).reshape(-1, channels))
    packed = moments(kept)
    for device in range(sums_ref.shape[0]):
        sums_ref[device] = packed
    load.wait()


def second_kernel(
    row_count, middle_ref, affine_ref, vectors_ref, weight_ref, own_ref, out_ref, field
):
    section, row_at = lax.axis_index("section"), lax.axis_index("rows")
    frames, lines, columns, channels = own_ref.shape
    slope, offset, slope_before, offset_before = (affine_ref[row] for row in range(4))
    at_start = section == 0
    for line in range(lines + 2):
        halo, body = middle_ref[:2, line], middle_ref[2:, line]
        behind = activate(halo, slope_before, offset_before).astype(jnp.bfloat16)
        behind = jnp.where(at_start, halo, behind)
        ahead = activate(body, slope, offset).astype(jnp.bfloat16)
        if line == 0 or line == lines + 1:
            outside = row_at == 0 if line == 0 else row_at == row_count - 1
            behind = jnp.where(outside, jnp.zeros_like(behind), behind)
            ahead = jnp.where(outside, jnp.zeros_like(ahead), ahead)
        field[:2, line] = behind
        field[2:, line] = ahead
    bias = vectors_ref[5]
    for pair in range(lines // 2):
        results = pair_conv(field, 2 * pair, frames, weight_ref)
        for out in range(2):
            line = 2 * pair + out
            result = (results[out] + bias).reshape(frames, columns, channels)
            out_ref[:, line] = (result + own_ref[:, line].astype(jnp.float32)).astype(jnp.bfloat16)


def call(kernel, out_shape, scratch, operands, in_place=(), unread=(), flops=0):
    vmem = pl.BlockSpec(memory_space=pltpu.VMEM)
    specs = [vmem] * len(operands)
    for index in in_place:
        specs[index] = pl.BlockSpec(memory_space=pltpu.HBM)
    for index in unread:
        specs[index] = pl.BlockSpec(memory_space=pl.ANY)
    operands = [
        pltpu.with_memory_space_constraint(operand, pltpu.HBM) if index in in_place else operand
        for index, operand in enumerate(operands)
    ]
    return pl.pallas_call(
        kernel,
        out_shape=out_shape,
        in_specs=specs,
        out_specs=jax.tree.map(lambda _: vmem, out_shape),
        scratch_shapes=scratch,
        compiler_params=pltpu.CompilerParams(vmem_limit_bytes=40 * 2**20),
        cost_estimate=pl.CostEstimate(flops=flops, bytes_accessed=2**20, transcendentals=0),
    )(*operands)


def on_device(
    activations,
    first_cache,
    second_cache,
    norm1_scale,
    norm1_shift,
    conv1_weight,
    conv1_bias,
    norm2_scale,
    norm2_shift,
    conv2_weight,
    conv2_bias,
):
    frames, lines, columns, channels = activations.shape
    sections, row_count = lax.axis_size("section"), lax.axis_size("rows")
    everyone = sections * row_count
    stats_shape = jax.ShapeDtypeStruct((everyone, 2, channels), jnp.float32)
    vectors = (norm1_scale, norm1_shift, conv1_bias, norm2_scale, norm2_shift, conv2_bias)

    near = [i ^ 1 for i in range(row_count)]
    far = [0] + [i + 1 if i % 2 else i - 1 for i in range(1, row_count - 1)] + [row_count - 1]

    def across(block, partner):
        return lax.ppermute(block, "rows", list(enumerate(partner)))

    ring = [(at, (at + 1) % sections) for at in range(sections)]
    own, halo = call(
        functools.partial(copy_kernel, sections),
        (
            jax.ShapeDtypeStruct(activations.shape, jnp.bfloat16),
            jax.ShapeDtypeStruct((SPAN_HALO, lines, columns, channels), jnp.bfloat16),
        ),
        [pltpu.SemaphoreType.DMA((4,))],
        (activations, second_cache, first_cache),
        in_place=range(3),
    )
    sums, packed, weight = call(
        stats_kernel,
        (
            jax.ShapeDtypeStruct((1, 2, channels), jnp.float32),
            jax.ShapeDtypeStruct((len(vectors), 1, channels), jnp.float32),
            jax.ShapeDtypeStruct(conv1_weight.shape, jnp.bfloat16),
        ),
        [pltpu.SemaphoreType.DMA((1 + len(vectors),))],
        (own, conv1_weight) + tuple(vector.reshape(1, channels) for vector in vectors),
        in_place=range(1, 2 + len(vectors)),
        flops=10**11,
    )
    received = lax.ppermute(halo, "section", ring)
    received, _ = lax.optimization_barrier((received, sums))
    beside = [across(activations, near), across(activations, far)]
    behind = [received, across(received, near), across(received, far)]

    both = jnp.concatenate([sums, lax.ppermute(sums, "section", ring)], axis=1)
    both = jnp.broadcast_to(both, (row_count,) + both.shape[1:])

    def coefficients(sums, axes, which, *after):
        stats = lax.all_to_all(sums, axes, 0, 0, tiled=True)
        return call(
            functools.partial(affine_kernel, row_count, frames * lines * columns, which),
            jax.ShapeDtypeStruct((4, 1, channels), jnp.float32),
            [],
            (stats, packed, *after),
            unread=range(2, 2 + len(after)),
            flops=10**11,
        )

    middle, sums, weight = call(
        functools.partial(first_kernel, row_count),
        (
            jax.ShapeDtypeStruct((frames + 2, lines + 2, columns, channels), jnp.bfloat16),
            stats_shape,
            jax.ShapeDtypeStruct(conv2_weight.shape, jnp.bfloat16),
        ),
        [
            pltpu.VMEM((frames + SPAN_HALO, 3 * lines, columns, channels), jnp.bfloat16),
            pltpu.SemaphoreType.DMA,
        ],
        (
            own, *beside, *behind, coefficients(both, "rows", 0, *beside), packed, weight,
            conv2_weight,
        ),
        in_place=(9,),
        flops=10**9,
    )
    return call(
        functools.partial(second_kernel, row_count),
        jax.ShapeDtypeStruct(activations.shape, jnp.bfloat16),
        [pltpu.VMEM((frames + 2, lines + 2, columns, channels), jnp.bfloat16)],
        (middle, coefficients(sums, ("section", "rows"), 3), packed, weight, own),
        flops=10**9,
    )


def solution(mesh):
    in_specs = (
        P("section", "rows", None, None),
        P(None, "rows", None, None),
        P(None, "rows", None, None),
        P(),
        P(),
        P(),
        P(),
        P(),
        P(),
        P(),
        P(),
    )
    out_specs = P("section", "rows", None, None)
    return jax.shard_map(
        on_device, mesh=mesh, in_specs=in_specs, out_specs=out_specs, check_vma=False
    )
```

```python
import functools

import functools

import jax
import jax.numpy as jnp
from jax import lax
from jax.experimental import pallas as pl
from jax.experimental.pallas import tpu as pltpu
from jax.sharding import PartitionSpec as P

GROUPS = 32
SPAN_HALO = 4

epsilon = 1e-06


def moments(blocks):
    pivot = blocks[0][:1]
    cells = sum(block.shape[0] for block in blocks)
    total, squares = 0.0, 0.0
    for block in blocks:
        away = block - pivot
        total = total + jnp.sum(away, axis=0, keepdims=True)
        squares = squares + jnp.sum(away * away, axis=0, keepdims=True)
    shift = total * (1.0 / cells)
    return jnp.concatenate([pivot + shift, squares - total * shift], axis=0)


def affine(stats, cells, scale, shift):
    devices, _, channels = stats.shape
    means, squares = stats[:, 0], stats[:, 1]
    mean = jnp.sum(means, axis=0, keepdims=True) * (1.0 / devices)
    away = means - mean
    square = jnp.sum(squares + cells * (away * away), axis=0, keepdims=True)
    count = cells * devices
    lane = lax.broadcasted_iota(jnp.int32, mean.shape, 1)
    step = 1
    while step < channels // GROUPS:

        def partner(values):
            up = pltpu.roll(values, channels - step, 1)
            return jnp.where((lane // step) % 2 == 0, up, pltpu.roll(values, step, 1))

        away = partner(mean) - mean
        square = square + partner(square) + (0.5 * count) * (away * away)
        mean = mean + 0.5 * away
        count, step = 2 * count, 2 * step
    slope = 0.5 * scale * lax.rsqrt(square * (1.0 / count) + epsilon)
    return slope, 0.5 * shift - mean * slope


def activate(values, slope, offset):
    half = values.astype(jnp.float32) * slope + offset
    return half + half * jnp.tanh(half)


def pair_conv(field, row, frames, weight_ref):
    columns, channels = field.shape[2], field.shape[3]
    cells = frames * columns
    nothing = jnp.zeros((channels, channels), jnp.bfloat16)

    def piece(frame_tap, line):
        return field[frame_tap : frame_tap + frames, row + line].reshape(cells, channels)

    def dot(pieces, blocks):
        return jnp.dot(pieces, blocks, preferred_element_type=jnp.float32)

    taps = [(frame_tap, row_tap) for frame_tap in range(3) for row_tap in range(3)]
    early = dot(
        jnp.concatenate(
            [
                jnp.concatenate([piece(tap, out + row_tap) for tap, row_tap in taps], axis=1)
                for out in range(2)
            ],
            axis=0,
        ),
        jnp.concatenate(
            [
                jnp.concatenate([weight_ref[tap, row_tap, 0], weight_ref[tap, row_tap, 1]], axis=1)
                for tap, row_tap in taps
            ],
            axis=0,
        ),
    )
    lines = [(frame_tap, line) for frame_tap in range(3) for line in range(4)]
    late = dot(
        jnp.concatenate([piece(tap, line) for tap, line in lines], axis=1),
        jnp.concatenate(
            [
                jnp.concatenate(
                    [
                        weight_ref[tap, line - out, 2] if 0 <= line - out <= 2 else nothing
                        for out in range(2)
                    ],
                    axis=1,
                )
                for tap, line in lines
            ],
            axis=0,
        ),
    )
    column = lax.broadcasted_iota(jnp.int32, (cells, channels), 0) % columns
    results = []
    for out in range(2):
        left, centre = (
            early[out * cells : (out + 1) * cells, tap * channels : (tap + 1) * channels]
            for tap in range(2)
        )
        right = late[:, out * channels : (out + 1) * channels]
        left = jnp.where(column == 0, 0.0, pltpu.roll(left, 1, 0))
        right = jnp.where(column == columns - 1, 0.0, pltpu.roll(right, cells - 1, 0))
        results.append(left + centre + right)
    return results


def copy_kernel(sections, own_ref, second_cache_ref, first_cache_ref, copied, halo_ref, sems):
    last = lax.axis_index("section") == sections - 1
    frames = own_ref.shape[0]
    spare = SPAN_HALO - 2
    tail = pltpu.make_async_copy(own_ref.at[frames - SPAN_HALO :], halo_ref, sems.at[0])
    older = pltpu.make_async_copy(second_cache_ref, halo_ref.at[:spare], sems.at[1])
    newer = pltpu.make_async_copy(first_cache_ref, halo_ref.at[spare:], sems.at[2])
    load = pltpu.make_async_copy(own_ref, copied, sems.at[3])

    @pl.when(last)
    def _():
        older.start()
        newer.start()

    @pl.when(jnp.logical_not(last))
    def _():
        tail.start()

    load.start()

    @pl.when(last)
    def _():
        older.wait()
        newer.wait()

    @pl.when(jnp.logical_not(last))
    def _():
        tail.wait()

    load.wait()


def stats_kernel(own_ref, weight_ref, *rest):
    *vector_refs, stats_ref, vectors_ref, weight_copy, sems = rest
    loads = [pltpu.make_async_copy(weight_ref, weight_copy, sems.at[0])]
    loads += [
        pltpu.make_async_copy(vector_ref, vectors_ref.at[index], sems.at[1 + index])
        for index, vector_ref in enumerate(vector_refs)
    ]
    for load in loads:
        load.start()
    channels = own_ref.shape[-1]
    blocks = [own_ref[frame].astype(jnp.float32) for frame in range(own_ref.shape[0])]
    stats_ref[0] = moments([block.reshape(-1, channels) for block in blocks])
    for load in loads:
        load.wait()


def first_kernel(
    row_count, own_ref, near_ref, far_ref, stats_ref, vectors_ref, weight_ref, middle_ref,
    sums_ref, field
):
    section, row_at = lax.axis_index("section"), lax.axis_index("rows")
    frames, lines, columns, channels = own_ref.shape
    inner = frames - SPAN_HALO
    cells = inner * lines * columns
    scale, shift = vectors_ref[0], vectors_ref[1]
    mine, before = stats_ref[:, :2], stats_ref[:, 2:]
    slope, offset = affine(mine, cells, scale, shift)
    slope_before, offset_before = affine(before, cells, scale, shift)
    even = row_at % 2 == 0
    at_start = section == 0

    def fill(line):
        side, local = divmod(line, lines)
        if side == 1:
            block = own_ref[:, local]
        else:
            near_side = even if side == 2 else jnp.logical_not(even)
            block = jnp.where(near_side, near_ref[:, local], far_ref[:, local])
        halo, body = block[:SPAN_HALO], block[SPAN_HALO:]
        behind = activate(halo, slope_before, offset_before).astype(jnp.bfloat16)
        behind = jnp.where(at_start, halo, behind)
        ahead = activate(body, slope, offset).astype(jnp.bfloat16)
        if side != 1:
            outside = row_at == 0 if side == 0 else row_at == row_count - 1
            behind = jnp.where(outside, jnp.zeros_like(behind), behind)
            ahead = jnp.where(outside, jnp.zeros_like(ahead), ahead)
        field[:SPAN_HALO, line] = behind
        field[SPAN_HALO:, line] = ahead

    bias = vectors_ref[2]
    kept = []
    spare = SPAN_HALO - 2
    ready = 0
    for pair in range((lines + 2) // 2):
        for line in range(ready, 2 * pair + 4):
            fill(line)
        ready = 2 * pair + 4
        results = pair_conv(field, 2 * pair, inner + 2, weight_ref)
        for out in range(2):
            line = 2 * pair + out
            rounded = (results[out] + bias).astype(jnp.bfloat16)
            rounded = rounded.reshape(inner + 2, columns, channels)
            middle_ref[:2, line] = jnp.where(at_start, field[:spare, line + lines - 1], rounded[:2])
            middle_ref[2:, line] = rounded[2:]
            if 1 <= line <= lines:
                kept.append(rounded[2:].astype(jnp.float32).reshape(-1, channels))
    packed = moments(kept)
    for device in range(sums_ref.shape[0]):
        sums_ref[device] = packed


def second_kernel(
    row_count, middle_ref, stats_ref, vectors_ref, weight_ref, own_ref, out_ref, field
):
    section, row_at = lax.axis_index("section"), lax.axis_index("rows")
    frames, lines, columns, channels = own_ref.shape
    cells = frames * lines * columns
    scale, shift = vectors_ref[3], vectors_ref[4]
    mine = stats_ref[pl.ds(section * row_count, row_count)]
    before = stats_ref[pl.ds(jnp.maximum(section - 1, 0) * row_count, row_count)]
    slope, offset = affine(mine, cells, scale, shift)
    slope_before, offset_before = affine(before, cells, scale, shift)
    at_start = section == 0
    for line in range(lines + 2):
        halo, body = middle_ref[:2, line], middle_ref[2:, line]
        behind = activate(halo, slope_before, offset_before).astype(jnp.bfloat16)
        behind = jnp.where(at_start, halo, behind)
        ahead = activate(body, slope, offset).astype(jnp.bfloat16)
        if line == 0 or line == lines + 1:
            outside = row_at == 0 if line == 0 else row_at == row_count - 1
            behind = jnp.where(outside, jnp.zeros_like(behind), behind)
            ahead = jnp.where(outside, jnp.zeros_like(ahead), ahead)
        field[:2, line] = behind
        field[2:, line] = ahead
    bias = vectors_ref[5]
    for pair in range(lines // 2):
        results = pair_conv(field, 2 * pair, frames, weight_ref)
        for out in range(2):
            line = 2 * pair + out
            result = (results[out] + bias).reshape(frames, columns, channels)
            out_ref[:, line] = (result + own_ref[:, line].astype(jnp.float32)).astype(jnp.bfloat16)


def call(kernel, out_shape, scratch, operands, in_place=(), flops=0):
    vmem = pl.BlockSpec(memory_space=pltpu.VMEM)
    specs = [vmem] * len(operands)
    for index in in_place:
        specs[index] = pl.BlockSpec(memory_space=pltpu.HBM)
    operands = [
        pltpu.with_memory_space_constraint(operand, pltpu.HBM) if index in in_place else operand
        for index, operand in enumerate(operands)
    ]
    return pl.pallas_call(
        kernel,
        out_shape=out_shape,
        in_specs=specs,
        out_specs=jax.tree.map(lambda _: vmem, out_shape),
        scratch_shapes=scratch,
        compiler_params=pltpu.CompilerParams(vmem_limit_bytes=40 * 2**20),
        cost_estimate=pl.CostEstimate(flops=flops, bytes_accessed=2**20, transcendentals=0),
    )(*operands)


def on_device(
    activations,
    first_cache,
    second_cache,
    norm1_scale,
    norm1_shift,
    conv1_weight,
    conv1_bias,
    norm2_scale,
    norm2_shift,
    conv2_weight,
    conv2_bias,
):
    frames, lines, columns, channels = activations.shape
    sections, row_count = lax.axis_size("section"), lax.axis_size("rows")
    everyone = sections * row_count
    stats_shape = jax.ShapeDtypeStruct((everyone, 2, channels), jnp.float32)
    vectors = (norm1_scale, norm1_shift, conv1_bias, norm2_scale, norm2_shift, conv2_bias)

    near = [i ^ 1 for i in range(row_count)]
    far = [0] + [i + 1 if i % 2 else i - 1 for i in range(1, row_count - 1)] + [row_count - 1]

    def across(block, partner):
        return lax.ppermute(block, "rows", list(enumerate(partner)))

    ring = [(at, (at + 1) % sections) for at in range(sections)]
    own, halo = call(
        functools.partial(copy_kernel, sections),
        (
            jax.ShapeDtypeStruct(activations.shape, jnp.bfloat16),
            jax.ShapeDtypeStruct((SPAN_HALO, lines, columns, channels), jnp.bfloat16),
        ),
        [pltpu.SemaphoreType.DMA((4,))],
        (activations, second_cache, first_cache),
        in_place=range(3),
    )
    sums, packed, weight = call(
        stats_kernel,
        (
            jax.ShapeDtypeStruct((1, 2, channels), jnp.float32),
            jax.ShapeDtypeStruct((len(vectors), 1, channels), jnp.float32),
            jax.ShapeDtypeStruct(conv1_weight.shape, jnp.bfloat16),
        ),
        [pltpu.SemaphoreType.DMA((1 + len(vectors),))],
        (own, conv1_weight) + tuple(vector.reshape(1, channels) for vector in vectors),
        in_place=range(1, 2 + len(vectors)),
    )
    received = lax.ppermute(halo, "section", ring)
    passed = lax.ppermute(sums, "section", ring)
    received, sums, passed = lax.optimization_barrier((received, sums, passed))
    joined = jnp.concatenate([received, own], axis=0)
    both = jnp.concatenate([sums, passed], axis=1)
    both = jnp.broadcast_to(both, (row_count,) + both.shape[1:])
    stats = lax.all_to_all(both, "rows", 0, 0, tiled=True)
    middle, sums_two = call(
        functools.partial(first_kernel, row_count),
        (
            jax.ShapeDtypeStruct((frames + 2, lines + 2, columns, channels), jnp.bfloat16),
            stats_shape,
        ),
        [pltpu.VMEM((frames + SPAN_HALO, 3 * lines, columns, channels), jnp.bfloat16)],
        (joined, across(joined, near), across(joined, far), stats, packed, weight),
        flops=10**9,
    )
    stats_two = lax.all_to_all(sums_two, ("section", "rows"), 0, 0, tiled=True)
    return call(
        functools.partial(second_kernel, row_count),
        jax.ShapeDtypeStruct(activations.shape, jnp.bfloat16),
        [pltpu.VMEM((frames + 2, lines + 2, columns, channels), jnp.bfloat16)],
        (middle, stats_two, packed, conv2_weight, own),
        flops=10**9,
    )


def solution(mesh):
    in_specs = (
        P("section", "rows", None, None),
        P(None, "rows", None, None),
        P(None, "rows", None, None),
        P(),
        P(),
        P(),
        P(),
        P(),
        P(),
        P(),
        P(),
    )
    out_specs = P("section", "rows", None, None)
    return jax.shard_map(
        on_device, mesh=mesh, in_specs=in_specs, out_specs=out_specs, check_vma=False
    )
```

```python
import functools

import functools

import jax
import jax.numpy as jnp
from jax import lax
from jax.experimental import pallas as pl
from jax.experimental.pallas import tpu as pltpu
from jax.sharding import PartitionSpec as P

GROUPS = 32
SPAN_HALO = 4

epsilon = 1e-06


def moments(blocks):
    pivot = blocks[0][:1]
    cells = sum(block.shape[0] for block in blocks)
    total, squares = 0.0, 0.0
    for block in blocks:
        away = block - pivot
        total = total + jnp.sum(away, axis=0, keepdims=True)
        squares = squares + jnp.sum(away * away, axis=0, keepdims=True)
    shift = total * (1.0 / cells)
    return jnp.concatenate([pivot + shift, squares - total * shift], axis=0)


def affine(stats, cells, scale, shift):
    devices, _, channels = stats.shape
    means, squares = stats[:, 0], stats[:, 1]
    mean = jnp.sum(means, axis=0, keepdims=True) * (1.0 / devices)
    away = means - mean
    square = jnp.sum(squares + cells * (away * away), axis=0, keepdims=True)
    count = cells * devices
    lane = lax.broadcasted_iota(jnp.int32, mean.shape, 1)
    step = 1
    while step < channels // GROUPS:

        def partner(values):
            up = pltpu.roll(values, channels - step, 1)
            return jnp.where((lane // step) % 2 == 0, up, pltpu.roll(values, step, 1))

        away = partner(mean) - mean
        square = square + partner(square) + (0.5 * count) * (away * away)
        mean = mean + 0.5 * away
        count, step = 2 * count, 2 * step
    slope = 0.5 * scale * lax.rsqrt(square * (1.0 / count) + epsilon)
    return slope, 0.5 * shift - mean * slope


def activate(values, slope, offset):
    half = values.astype(jnp.float32) * slope + offset
    return half + half * jnp.tanh(half)


def pair_conv(field, row, frames, weight_ref):
    columns, channels = field.shape[2], field.shape[3]
    cells = frames * columns
    nothing = jnp.zeros((channels, channels), jnp.bfloat16)

    def piece(frame_tap, line):
        return field[frame_tap : frame_tap + frames, row + line].reshape(cells, channels)

    def dot(pieces, blocks):
        return jnp.dot(pieces, blocks, preferred_element_type=jnp.float32)

    taps = [(frame_tap, row_tap) for frame_tap in range(3) for row_tap in range(3)]
    early = dot(
        jnp.concatenate(
            [
                jnp.concatenate([piece(tap, out + row_tap) for tap, row_tap in taps], axis=1)
                for out in range(2)
            ],
            axis=0,
        ),
        jnp.concatenate(
            [
                jnp.concatenate([weight_ref[tap, row_tap, 0], weight_ref[tap, row_tap, 1]], axis=1)
                for tap, row_tap in taps
            ],
            axis=0,
        ),
    )
    lines = [(frame_tap, line) for frame_tap in range(3) for line in range(4)]
    late = dot(
        jnp.concatenate([piece(tap, line) for tap, line in lines], axis=1),
        jnp.concatenate(
            [
                jnp.concatenate(
                    [
                        weight_ref[tap, line - out, 2] if 0 <= line - out <= 2 else nothing
                        for out in range(2)
                    ],
                    axis=1,
                )
                for tap, line in lines
            ],
            axis=0,
        ),
    )
    column = lax.broadcasted_iota(jnp.int32, (cells, channels), 0) % columns
    results = []
    for out in range(2):
        left, centre = (
            early[out * cells : (out + 1) * cells, tap * channels : (tap + 1) * channels]
            for tap in range(2)
        )
        right = late[:, out * channels : (out + 1) * channels]
        left = jnp.where(column == 0, 0.0, pltpu.roll(left, 1, 0))
        right = jnp.where(column == columns - 1, 0.0, pltpu.roll(right, cells - 1, 0))
        results.append(left + centre + right)
    return results


def copy_kernel(sections, own_ref, second_cache_ref, first_cache_ref, copied, halo_ref, sems):
    last = lax.axis_index("section") == sections - 1
    frames = own_ref.shape[0]
    spare = SPAN_HALO - 2
    tail = pltpu.make_async_copy(own_ref.at[frames - SPAN_HALO :], halo_ref, sems.at[0])
    older = pltpu.make_async_copy(second_cache_ref, halo_ref.at[:spare], sems.at[1])
    newer = pltpu.make_async_copy(first_cache_ref, halo_ref.at[spare:], sems.at[2])
    load = pltpu.make_async_copy(own_ref, copied, sems.at[3])

    @pl.when(last)
    def _():
        older.start()
        newer.start()

    @pl.when(jnp.logical_not(last))
    def _():
        tail.start()

    load.start()

    @pl.when(last)
    def _():
        older.wait()
        newer.wait()

    @pl.when(jnp.logical_not(last))
    def _():
        tail.wait()

    load.wait()


def stats_kernel(own_ref, weight_ref, *rest):
    *vector_refs, stats_ref, vectors_ref, weight_copy, sems = rest
    loads = [pltpu.make_async_copy(weight_ref, weight_copy, sems.at[0])]
    loads += [
        pltpu.make_async_copy(vector_ref, vectors_ref.at[index], sems.at[1 + index])
        for index, vector_ref in enumerate(vector_refs)
    ]
    for load in loads:
        load.start()
    channels = own_ref.shape[-1]
    blocks = [own_ref[frame].astype(jnp.float32) for frame in range(own_ref.shape[0])]
    stats_ref[0] = moments([block.reshape(-1, channels) for block in blocks])
    for load in loads:
        load.wait()


def first_kernel(
    row_count, own_ref, far_ref, near_ref, stats_ref, vectors_ref, weight_ref, middle_ref,
    sums_ref, field
):
    section, row_at = lax.axis_index("section"), lax.axis_index("rows")
    frames, lines, columns, channels = own_ref.shape
    inner = frames - SPAN_HALO
    cells = inner * lines * columns
    scale, shift = vectors_ref[0], vectors_ref[1]
    mine, before = stats_ref[:, :2], stats_ref[:, 2:]
    slope, offset = affine(mine, cells, scale, shift)
    slope_before, offset_before = affine(before, cells, scale, shift)
    even = row_at % 2 == 0
    at_start = section == 0

    def fill(line):
        side, local = divmod(line, lines)
        if side == 1:
            block = own_ref[:, local]
        else:
            near_side = even if side == 2 else jnp.logical_not(even)
            block = jnp.where(near_side, near_ref[:, local], far_ref[:, local])
        halo, body = block[:SPAN_HALO], block[SPAN_HALO:]
        behind = activate(halo, slope_before, offset_before).astype(jnp.bfloat16)
        behind = jnp.where(at_start, halo, behind)
        ahead = activate(body, slope, offset).astype(jnp.bfloat16)
        if side != 1:
            outside = row_at == 0 if side == 0 else row_at == row_count - 1
            behind = jnp.where(outside, jnp.zeros_like(behind), behind)
            ahead = jnp.where(outside, jnp.zeros_like(ahead), ahead)
        field[:SPAN_HALO, line] = behind
        field[SPAN_HALO:, line] = ahead

    bias = vectors_ref[2]
    kept = []
    spare = SPAN_HALO - 2
    ready = 0
    for pair in range((lines + 2) // 2):
        for line in range(ready, 2 * pair + 4):
            fill(line)
        ready = 2 * pair + 4
        results = pair_conv(field, 2 * pair, inner + 2, weight_ref)
        for out in range(2):
            line = 2 * pair + out
            rounded = (results[out] + bias).astype(jnp.bfloat16)
            rounded = rounded.reshape(inner + 2, columns, channels)
            middle_ref[:2, line] = jnp.where(at_start, field[:spare, line + lines - 1], rounded[:2])
            middle_ref[2:, line] = rounded[2:]
            if 1 <= line <= lines:
                kept.append(rounded[2:].astype(jnp.float32).reshape(-1, channels))
    packed = moments(kept)
    for device in range(sums_ref.shape[0]):
        sums_ref[device] = packed


def second_kernel(
    row_count, middle_ref, stats_ref, vectors_ref, weight_ref, own_ref, out_ref, field
):
    section, row_at = lax.axis_index("section"), lax.axis_index("rows")
    frames, lines, columns, channels = own_ref.shape
    cells = frames * lines * columns
    scale, shift = vectors_ref[3], vectors_ref[4]
    mine = stats_ref[pl.ds(section * row_count, row_count)]
    before = stats_ref[pl.ds(jnp.maximum(section - 1, 0) * row_count, row_count)]
    slope, offset = affine(mine, cells, scale, shift)
    slope_before, offset_before = affine(before, cells, scale, shift)
    at_start = section == 0
    for line in range(lines + 2):
        halo, body = middle_ref[:2, line], middle_ref[2:, line]
        behind = activate(halo, slope_before, offset_before).astype(jnp.bfloat16)
        behind = jnp.where(at_start, halo, behind)
        ahead = activate(body, slope, offset).astype(jnp.bfloat16)
        if line == 0 or line == lines + 1:
            outside = row_at == 0 if line == 0 else row_at == row_count - 1
            behind = jnp.where(outside, jnp.zeros_like(behind), behind)
            ahead = jnp.where(outside, jnp.zeros_like(ahead), ahead)
        field[:2, line] = behind
        field[2:, line] = ahead
    bias = vectors_ref[5]
    for pair in range(lines // 2):
        results = pair_conv(field, 2 * pair, frames, weight_ref)
        for out in range(2):
            line = 2 * pair + out
            result = (results[out] + bias).reshape(frames, columns, channels)
            out_ref[:, line] = (result + own_ref[:, line].astype(jnp.float32)).astype(jnp.bfloat16)


def call(kernel, out_shape, scratch, operands, in_place=(), flops=0):
    vmem = pl.BlockSpec(memory_space=pltpu.VMEM)
    specs = [vmem] * len(operands)
    for index in in_place:
        specs[index] = pl.BlockSpec(memory_space=pltpu.HBM)
    operands = [
        pltpu.with_memory_space_constraint(operand, pltpu.HBM) if index in in_place else operand
        for index, operand in enumerate(operands)
    ]
    return pl.pallas_call(
        kernel,
        out_shape=out_shape,
        in_specs=specs,
        out_specs=jax.tree.map(lambda _: vmem, out_shape),
        scratch_shapes=scratch,
        compiler_params=pltpu.CompilerParams(vmem_limit_bytes=40 * 2**20),
        cost_estimate=pl.CostEstimate(flops=flops, bytes_accessed=2**20, transcendentals=0),
    )(*operands)


def on_device(
    activations,
    first_cache,
    second_cache,
    norm1_scale,
    norm1_shift,
    conv1_weight,
    conv1_bias,
    norm2_scale,
    norm2_shift,
    conv2_weight,
    conv2_bias,
):
    frames, lines, columns, channels = activations.shape
    sections, row_count = lax.axis_size("section"), lax.axis_size("rows")
    everyone = sections * row_count
    stats_shape = jax.ShapeDtypeStruct((everyone, 2, channels), jnp.float32)
    vectors = (norm1_scale, norm1_shift, conv1_bias, norm2_scale, norm2_shift, conv2_bias)

    near = [i ^ 1 for i in range(row_count)]
    far = [0] + [i + 1 if i % 2 else i - 1 for i in range(1, row_count - 1)] + [row_count - 1]

    def across(block, partner):
        return lax.ppermute(block, "rows", list(enumerate(partner)))

    ring = [(at, (at + 1) % sections) for at in range(sections)]
    own, halo = call(
        functools.partial(copy_kernel, sections),
        (
            jax.ShapeDtypeStruct(activations.shape, jnp.bfloat16),
            jax.ShapeDtypeStruct((SPAN_HALO, lines, columns, channels), jnp.bfloat16),
        ),
        [pltpu.SemaphoreType.DMA((4,))],
        (activations, second_cache, first_cache),
        in_place=range(3),
    )
    sums, packed, weight = call(
        stats_kernel,
        (
            jax.ShapeDtypeStruct((1, 2, channels), jnp.float32),
            jax.ShapeDtypeStruct((len(vectors), 1, channels), jnp.float32),
            jax.ShapeDtypeStruct(conv1_weight.shape, jnp.bfloat16),
        ),
        [pltpu.SemaphoreType.DMA((1 + len(vectors),))],
        (own, conv1_weight) + tuple(vector.reshape(1, channels) for vector in vectors),
        in_place=range(1, 2 + len(vectors)),
    )
    received = lax.ppermute(halo, "section", ring)
    passed = lax.ppermute(sums, "section", ring)
    received, sums, passed = lax.optimization_barrier((received, sums, passed))
    joined = jnp.concatenate([received, own], axis=0)
    from_far = across(joined, far)
    from_near = across(joined, near)
    both = jnp.concatenate([sums, passed], axis=1)
    both = jnp.broadcast_to(both, (row_count,) + both.shape[1:])
    stats = lax.all_to_all(both, "rows", 0, 0, tiled=True)
    middle, sums_two = call(
        functools.partial(first_kernel, row_count),
        (
            jax.ShapeDtypeStruct((frames + 2, lines + 2, columns, channels), jnp.bfloat16),
            stats_shape,
        ),
        [pltpu.VMEM((frames + SPAN_HALO, 3 * lines, columns, channels), jnp.bfloat16)],
        (joined, from_far, from_near, stats, packed, weight),
        flops=10**9,
    )
    stats_two = lax.all_to_all(sums_two, ("section", "rows"), 0, 0, tiled=True)
    return call(
        functools.partial(second_kernel, row_count),
        jax.ShapeDtypeStruct(activations.shape, jnp.bfloat16),
        [pltpu.VMEM((frames + 2, lines + 2, columns, channels), jnp.bfloat16)],
        (middle, stats_two, packed, conv2_weight, own),
        flops=10**9,
    )


def solution(mesh):
    in_specs = (
        P("section", "rows", None, None),
        P(None, "rows", None, None),
        P(None, "rows", None, None),
        P(),
        P(),
        P(),
        P(),
        P(),
        P(),
        P(),
        P(),
    )
    out_specs = P("section", "rows", None, None)
    return jax.shard_map(
        on_device, mesh=mesh, in_specs=in_specs, out_specs=out_specs, check_vma=False
    )
```

```python
import functools

import functools

import jax
import jax.numpy as jnp
from jax import lax
from jax.experimental import pallas as pl
from jax.experimental.pallas import tpu as pltpu
from jax.sharding import PartitionSpec as P

GROUPS = 32
SPAN_HALO = 4

epsilon = 1e-06


def moments(blocks):
    pivot = blocks[0][:1]
    cells = sum(block.shape[0] for block in blocks)
    total, squares = 0.0, 0.0
    for block in blocks:
        away = block - pivot
        total = total + jnp.sum(away, axis=0, keepdims=True)
        squares = squares + jnp.sum(away * away, axis=0, keepdims=True)
    shift = total * (1.0 / cells)
    return jnp.concatenate([pivot + shift, squares - total * shift], axis=0)


def affine(stats, cells, scale, shift):
    devices, _, channels = stats.shape
    means, squares = stats[:, 0], stats[:, 1]
    mean = jnp.sum(means, axis=0, keepdims=True) * (1.0 / devices)
    away = means - mean
    square = jnp.sum(squares + cells * (away * away), axis=0, keepdims=True)
    count = cells * devices
    lane = lax.broadcasted_iota(jnp.int32, mean.shape, 1)
    step = 1
    while step < channels // GROUPS:

        def partner(values):
            up = pltpu.roll(values, channels - step, 1)
            return jnp.where((lane // step) % 2 == 0, up, pltpu.roll(values, step, 1))

        away = partner(mean) - mean
        square = square + partner(square) + (0.5 * count) * (away * away)
        mean = mean + 0.5 * away
        count, step = 2 * count, 2 * step
    slope = 0.5 * scale * lax.rsqrt(square * (1.0 / count) + epsilon)
    return slope, 0.5 * shift - mean * slope


def activate(values, slope, offset):
    half = values.astype(jnp.float32) * slope + offset
    return half + half * jnp.tanh(half)


def pair_conv(field, row, begin, frames, weight_ref):
    columns, channels = field.shape[2], field.shape[3]
    cells = frames * columns
    nothing = jnp.zeros((channels, channels), jnp.bfloat16)

    def piece(frame_tap, line):
        first = begin + frame_tap
        return field[first : first + frames, row + line].reshape(cells, channels)

    def dot(pieces, blocks):
        return jnp.dot(pieces, blocks, preferred_element_type=jnp.float32)

    taps = [(frame_tap, row_tap) for frame_tap in range(3) for row_tap in range(3)]
    early = dot(
        jnp.concatenate(
            [
                jnp.concatenate([piece(tap, out + row_tap) for tap, row_tap in taps], axis=1)
                for out in range(2)
            ],
            axis=0,
        ),
        jnp.concatenate(
            [
                jnp.concatenate([weight_ref[tap, row_tap, 0], weight_ref[tap, row_tap, 1]], axis=1)
                for tap, row_tap in taps
            ],
            axis=0,
        ),
    )
    lines = [(frame_tap, line) for frame_tap in range(3) for line in range(4)]
    late = dot(
        jnp.concatenate([piece(tap, line) for tap, line in lines], axis=1),
        jnp.concatenate(
            [
                jnp.concatenate(
                    [
                        weight_ref[tap, line - out, 2] if 0 <= line - out <= 2 else nothing
                        for out in range(2)
                    ],
                    axis=1,
                )
                for tap, line in lines
            ],
            axis=0,
        ),
    )
    column = lax.broadcasted_iota(jnp.int32, (cells, channels), 0) % columns
    results = []
    for out in range(2):
        left, centre = (
            early[out * cells : (out + 1) * cells, tap * channels : (tap + 1) * channels]
            for tap in range(2)
        )
        right = late[:, out * channels : (out + 1) * channels]
        left = jnp.where(column == 0, 0.0, pltpu.roll(left, 1, 0))
        right = jnp.where(column == columns - 1, 0.0, pltpu.roll(right, cells - 1, 0))
        results.append(left + centre + right)
    return results


def copy_kernel(sections, own_ref, second_cache_ref, first_cache_ref, copied, halo_ref, sems):
    last = lax.axis_index("section") == sections - 1
    frames = own_ref.shape[0]
    spare = SPAN_HALO - 2
    tail = pltpu.make_async_copy(own_ref.at[frames - SPAN_HALO :], halo_ref, sems.at[0])
    older = pltpu.make_async_copy(second_cache_ref, halo_ref.at[:spare], sems.at[1])
    newer = pltpu.make_async_copy(first_cache_ref, halo_ref.at[spare:], sems.at[2])
    load = pltpu.make_async_copy(own_ref, copied, sems.at[3])

    @pl.when(last)
    def _():
        older.start()
        newer.start()

    @pl.when(jnp.logical_not(last))
    def _():
        tail.start()

    load.start()

    @pl.when(last)
    def _():
        older.wait()
        newer.wait()

    @pl.when(jnp.logical_not(last))
    def _():
        tail.wait()

    load.wait()


def stats_kernel(own_ref, weight_ref, *rest):
    *vector_refs, stats_ref, vectors_ref, weight_copy, sems = rest
    loads = [pltpu.make_async_copy(weight_ref, weight_copy, sems.at[0])]
    loads += [
        pltpu.make_async_copy(vector_ref, vectors_ref.at[index], sems.at[1 + index])
        for index, vector_ref in enumerate(vector_refs)
    ]
    for load in loads:
        load.start()
    channels = own_ref.shape[-1]
    blocks = [own_ref[frame].astype(jnp.float32) for frame in range(own_ref.shape[0])]
    stats_ref[0] = moments([block.reshape(-1, channels) for block in blocks])
    for load in loads:
        load.wait()


def first_kernel(
    row_count, own_ref, far_ref, near_ref, stats_ref, vectors_ref, weight_ref, middle_ref,
    sums_ref, field
):
    section, row_at = lax.axis_index("section"), lax.axis_index("rows")
    frames, lines, columns, channels = own_ref.shape
    inner = frames - SPAN_HALO
    cells = inner * lines * columns
    scale, shift = vectors_ref[0], vectors_ref[1]
    mine, before = stats_ref[:, :2], stats_ref[:, 2:]
    slope, offset = affine(mine, cells, scale, shift)
    slope_before, offset_before = affine(before, cells, scale, shift)
    even = row_at % 2 == 0
    at_start = section == 0

    def fill(line):
        side, local = divmod(line, lines)
        if side == 1:
            block = own_ref[:, local]
        else:
            near_side = even if side == 2 else jnp.logical_not(even)
            block = jnp.where(near_side, near_ref[:, local], far_ref[:, local])
        halo, body = block[:SPAN_HALO], block[SPAN_HALO:]
        behind = activate(halo, slope_before, offset_before).astype(jnp.bfloat16)
        behind = jnp.where(at_start, halo, behind)
        ahead = activate(body, slope, offset).astype(jnp.bfloat16)
        if side != 1:
            outside = row_at == 0 if side == 0 else row_at == row_count - 1
            behind = jnp.where(outside, jnp.zeros_like(behind), behind)
            ahead = jnp.where(outside, jnp.zeros_like(ahead), ahead)
        field[:SPAN_HALO, line] = behind
        field[SPAN_HALO:, line] = ahead

    bias = vectors_ref[2]
    kept = []
    spare = SPAN_HALO - 2
    ready = 0
    for pair in range((lines + 2) // 2):
        for line in range(ready, 2 * pair + 4):
            fill(line)
        ready = 2 * pair + 4
        results = pair_conv(field, 2 * pair, 0, inner + 2, weight_ref)
        for out in range(2):
            line = 2 * pair + out
            rounded = (results[out] + bias).astype(jnp.bfloat16)
            rounded = rounded.reshape(inner + 2, columns, channels)
            middle_ref[:2, line] = jnp.where(at_start, field[:spare, line + lines - 1], rounded[:2])
            middle_ref[2:, line] = rounded[2:]
            if 1 <= line <= lines:
                kept.append(rounded[2:].astype(jnp.float32).reshape(-1, channels))
    packed = moments(kept)
    for device in range(sums_ref.shape[0]):
        sums_ref[device] = packed


def second_kernel(
    row_count, middle_ref, stats_ref, vectors_ref, weight_ref, own_ref, out_ref, field, ready,
    sems
):
    section, row_at = lax.axis_index("section"), lax.axis_index("rows")
    frames, lines, columns, channels = own_ref.shape
    cells = frames * lines * columns
    scale, shift = vectors_ref[3], vectors_ref[4]
    mine = stats_ref[pl.ds(section * row_count, row_count)]
    before = stats_ref[pl.ds(jnp.maximum(section - 1, 0) * row_count, row_count)]
    slope, offset = affine(mine, cells, scale, shift)
    slope_before, offset_before = affine(before, cells, scale, shift)
    at_start = section == 0
    half = frames // 2
    copies = []
    for begin in range(0, frames, half):
        filled = 0 if begin == 0 else begin + 2
        for line in range(lines + 2):
            ahead = middle_ref[filled : begin + half + 2, line]
            if begin == 0:
                behind = activate(ahead[:2], slope_before, offset_before).astype(jnp.bfloat16)
                behind = jnp.where(at_start, ahead[:2], behind)
                ahead = activate(ahead[2:], slope, offset).astype(jnp.bfloat16)
                ahead = jnp.concatenate([behind, ahead], axis=0)
            else:
                ahead = activate(ahead, slope, offset).astype(jnp.bfloat16)
            if line == 0 or line == lines + 1:
                outside = row_at == 0 if line == 0 else row_at == row_count - 1
                ahead = jnp.where(outside, jnp.zeros_like(ahead), ahead)
            field[filled : begin + half + 2, line] = ahead
        span = slice(begin, begin + half)
        for pair in range(lines // 2):
            results = pair_conv(field, 2 * pair, begin, half, weight_ref)
            for out in range(2):
                line = 2 * pair + out
                result = (results[out] + vectors_ref[5]).reshape(half, columns, channels)
                result = result + own_ref[span, line].astype(jnp.float32)
                ready[span, line] = result.astype(jnp.bfloat16)
        copy = pltpu.make_async_copy(
            ready.at[span], out_ref.at[span], sems.at[begin // half]
        )
        copy.start()
        copies.append(copy)
    for copy in copies:
        copy.wait()


def call(kernel, out_shape, scratch, operands, in_place=(), out_in_place=False, flops=0):
    vmem = pl.BlockSpec(memory_space=pltpu.VMEM)
    out_spec = pl.BlockSpec(memory_space=pltpu.HBM) if out_in_place else vmem
    specs = [vmem] * len(operands)
    for index in in_place:
        specs[index] = pl.BlockSpec(memory_space=pltpu.HBM)
    operands = [
        pltpu.with_memory_space_constraint(operand, pltpu.HBM) if index in in_place else operand
        for index, operand in enumerate(operands)
    ]
    return pl.pallas_call(
        kernel,
        out_shape=out_shape,
        in_specs=specs,
        out_specs=jax.tree.map(lambda _: out_spec, out_shape),
        scratch_shapes=scratch,
        compiler_params=pltpu.CompilerParams(vmem_limit_bytes=40 * 2**20),
        cost_estimate=pl.CostEstimate(flops=flops, bytes_accessed=2**20, transcendentals=0),
    )(*operands)


def on_device(
    activations,
    first_cache,
    second_cache,
    norm1_scale,
    norm1_shift,
    conv1_weight,
    conv1_bias,
    norm2_scale,
    norm2_shift,
    conv2_weight,
    conv2_bias,
):
    frames, lines, columns, channels = activations.shape
    sections, row_count = lax.axis_size("section"), lax.axis_size("rows")
    everyone = sections * row_count
    stats_shape = jax.ShapeDtypeStruct((everyone, 2, channels), jnp.float32)
    vectors = (norm1_scale, norm1_shift, conv1_bias, norm2_scale, norm2_shift, conv2_bias)

    near = [i ^ 1 for i in range(row_count)]
    far = [0] + [i + 1 if i % 2 else i - 1 for i in range(1, row_count - 1)] + [row_count - 1]

    def across(block, partner):
        return lax.ppermute(block, "rows", list(enumerate(partner)))

    ring = [(at, (at + 1) % sections) for at in range(sections)]
    own, halo = call(
        functools.partial(copy_kernel, sections),
        (
            jax.ShapeDtypeStruct(activations.shape, jnp.bfloat16),
            jax.ShapeDtypeStruct((SPAN_HALO, lines, columns, channels), jnp.bfloat16),
        ),
        [pltpu.SemaphoreType.DMA((4,))],
        (activations, second_cache, first_cache),
        in_place=range(3),
    )
    sums, packed, weight = call(
        stats_kernel,
        (
            jax.ShapeDtypeStruct((1, 2, channels), jnp.float32),
            jax.ShapeDtypeStruct((len(vectors), 1, channels), jnp.float32),
            jax.ShapeDtypeStruct(conv1_weight.shape, jnp.bfloat16),
        ),
        [pltpu.SemaphoreType.DMA((1 + len(vectors),))],
        (own, conv1_weight) + tuple(vector.reshape(1, channels) for vector in vectors),
        in_place=range(1, 2 + len(vectors)),
    )
    received = lax.ppermute(halo, "section", ring)
    passed = lax.ppermute(sums, "section", ring)
    received, sums, passed = lax.optimization_barrier((received, sums, passed))
    joined = jnp.concatenate([received, own], axis=0)
    from_far = across(joined, far)
    from_near = across(joined, near)
    both = jnp.concatenate([sums, passed], axis=1)
    both = jnp.broadcast_to(both, (row_count,) + both.shape[1:])
    stats = lax.all_to_all(both, "rows", 0, 0, tiled=True)
    middle, sums_two = call(
        functools.partial(first_kernel, row_count),
        (
            jax.ShapeDtypeStruct((frames + 2, lines + 2, columns, channels), jnp.bfloat16),
            stats_shape,
        ),
        [pltpu.VMEM((frames + SPAN_HALO, 3 * lines, columns, channels), jnp.bfloat16)],
        (joined, from_far, from_near, stats, packed, weight),
        flops=10**9,
    )
    stats_two = lax.all_to_all(sums_two, ("section", "rows"), 0, 0, tiled=True)
    return call(
        functools.partial(second_kernel, row_count),
        jax.ShapeDtypeStruct(activations.shape, jnp.bfloat16),
        [
            pltpu.VMEM((frames + 2, lines + 2, columns, channels), jnp.bfloat16),
            pltpu.VMEM(activations.shape, jnp.bfloat16),
            pltpu.SemaphoreType.DMA((2,)),
        ],
        (middle, stats_two, packed, conv2_weight, own),
        out_in_place=True,
        flops=10**9,
    )


def solution(mesh):
    in_specs = (
        P("section", "rows", None, None),
        P(None, "rows", None, None),
        P(None, "rows", None, None),
        P(),
        P(),
        P(),
        P(),
        P(),
        P(),
        P(),
        P(),
    )
    out_specs = P("section", "rows", None, None)
    return jax.shard_map(
        on_device, mesh=mesh, in_specs=in_specs, out_specs=out_specs, check_vma=False
    )
```

```python
import functools

import functools

import jax
import jax.numpy as jnp
from jax import lax
from jax.experimental import pallas as pl
from jax.experimental.pallas import tpu as pltpu
from jax.sharding import PartitionSpec as P

GROUPS = 32
SPAN_HALO = 4

epsilon = 1e-06


def moments(blocks):
    pivot = blocks[0][:1]
    cells = sum(block.shape[0] for block in blocks)
    total, squares = 0.0, 0.0
    for block in blocks:
        away = block - pivot
        total = total + jnp.sum(away, axis=0, keepdims=True)
        squares = squares + jnp.sum(away * away, axis=0, keepdims=True)
    shift = total * (1.0 / cells)
    return jnp.concatenate([pivot + shift, squares - total * shift], axis=0)


def affine(stats, cells, scale, shift):
    devices, _, channels = stats.shape
    means, squares = stats[:, 0], stats[:, 1]
    mean = jnp.sum(means, axis=0, keepdims=True) * (1.0 / devices)
    away = means - mean
    square = jnp.sum(squares + cells * (away * away), axis=0, keepdims=True)
    count = cells * devices
    lane = lax.broadcasted_iota(jnp.int32, mean.shape, 1)
    step = 1
    while step < channels // GROUPS:

        def partner(values):
            up = pltpu.roll(values, channels - step, 1)
            return jnp.where((lane // step) % 2 == 0, up, pltpu.roll(values, step, 1))

        away = partner(mean) - mean
        square = square + partner(square) + (0.5 * count) * (away * away)
        mean = mean + 0.5 * away
        count, step = 2 * count, 2 * step
    slope = 0.5 * scale * lax.rsqrt(square * (1.0 / count) + epsilon)
    return slope, 0.5 * shift - mean * slope


def activate(values, slope, offset):
    half = values.astype(jnp.float32) * slope + offset
    return half + half * jnp.tanh(half)


def pair_conv(lines, frames, weight_ref):
    columns, channels = lines[0].shape[1:]
    cells = frames * columns
    nothing = jnp.zeros((channels, channels), jnp.bfloat16)

    def piece(frame_tap, line):
        return lines[line][frame_tap : frame_tap + frames].reshape(cells, channels)

    def dot(pieces, blocks):
        return jnp.dot(pieces, blocks, preferred_element_type=jnp.float32)

    taps = [(frame_tap, row_tap) for frame_tap in range(3) for row_tap in range(3)]
    early = dot(
        jnp.concatenate(
            [
                jnp.concatenate([piece(tap, out + row_tap) for tap, row_tap in taps], axis=1)
                for out in range(2)
            ],
            axis=0,
        ),
        jnp.concatenate(
            [
                jnp.concatenate([weight_ref[tap, row_tap, 0], weight_ref[tap, row_tap, 1]], axis=1)
                for tap, row_tap in taps
            ],
            axis=0,
        ),
    )
    spread = [(frame_tap, line) for frame_tap in range(3) for line in range(4)]
    late = dot(
        jnp.concatenate([piece(tap, line) for tap, line in spread], axis=1),
        jnp.concatenate(
            [
                jnp.concatenate(
                    [
                        weight_ref[tap, line - out, 2] if 0 <= line - out <= 2 else nothing
                        for out in range(2)
                    ],
                    axis=1,
                )
                for tap, line in spread
            ],
            axis=0,
        ),
    )
    column = lax.broadcasted_iota(jnp.int32, (cells, channels), 0) % columns
    results = []
    for out in range(2):
        left, centre = (
            early[out * cells : (out + 1) * cells, tap * channels : (tap + 1) * channels]
            for tap in range(2)
        )
        right = late[:, out * channels : (out + 1) * channels]
        left = jnp.where(column == 0, 0.0, pltpu.roll(left, 1, 0))
        right = jnp.where(column == columns - 1, 0.0, pltpu.roll(right, cells - 1, 0))
        results.append(left + centre + right)
    return results


def copy_kernel(sections, own_ref, second_cache_ref, first_cache_ref, copied, halo_ref, sems):
    last = lax.axis_index("section") == sections - 1
    frames = own_ref.shape[0]
    spare = SPAN_HALO - 2
    tail = pltpu.make_async_copy(own_ref.at[frames - SPAN_HALO :], halo_ref, sems.at[0])
    older = pltpu.make_async_copy(second_cache_ref, halo_ref.at[:spare], sems.at[1])
    newer = pltpu.make_async_copy(first_cache_ref, halo_ref.at[spare:], sems.at[2])
    load = pltpu.make_async_copy(own_ref, copied, sems.at[3])

    @pl.when(last)
    def _():
        older.start()
        newer.start()

    @pl.when(jnp.logical_not(last))
    def _():
        tail.start()

    load.start()

    @pl.when(last)
    def _():
        older.wait()
        newer.wait()

    @pl.when(jnp.logical_not(last))
    def _():
        tail.wait()

    load.wait()


def stats_kernel(own_ref, weight_ref, *rest):
    *vector_refs, stats_ref, vectors_ref, weight_copy, sems = rest
    loads = [pltpu.make_async_copy(weight_ref, weight_copy, sems.at[0])]
    loads += [
        pltpu.make_async_copy(vector_ref, vectors_ref.at[index], sems.at[1 + index])
        for index, vector_ref in enumerate(vector_refs)
    ]
    for load in loads:
        load.start()
    channels = own_ref.shape[-1]
    blocks = [own_ref[frame].astype(jnp.float32) for frame in range(own_ref.shape[0])]
    stats_ref[0] = moments([block.reshape(-1, channels) for block in blocks])
    for load in loads:
        load.wait()


def first_kernel(
    row_count, own_ref, far_ref, near_ref, stats_ref, vectors_ref, weight_ref, middle_ref,
    sums_ref, *field
):
    section, row_at = lax.axis_index("section"), lax.axis_index("rows")
    frames, lines, columns, channels = own_ref.shape
    inner = frames - SPAN_HALO
    cells = inner * lines * columns
    scale, shift = vectors_ref[0], vectors_ref[1]
    mine, before = stats_ref[:, :2], stats_ref[:, 2:]
    slope, offset = affine(mine, cells, scale, shift)
    slope_before, offset_before = affine(before, cells, scale, shift)
    even = row_at % 2 == 0
    at_start = section == 0

    def fill(line):
        side, local = divmod(line, lines)
        if side == 1:
            block = own_ref[:, local]
        else:
            near_side = even if side == 2 else jnp.logical_not(even)
            block = jnp.where(near_side, near_ref[:, local], far_ref[:, local])
        halo, body = block[:SPAN_HALO], block[SPAN_HALO:]
        behind = activate(halo, slope_before, offset_before).astype(jnp.bfloat16)
        behind = jnp.where(at_start, halo, behind)
        ahead = activate(body, slope, offset).astype(jnp.bfloat16)
        if side != 1:
            outside = row_at == 0 if side == 0 else row_at == row_count - 1
            behind = jnp.where(outside, jnp.zeros_like(behind), behind)
            ahead = jnp.where(outside, jnp.zeros_like(ahead), ahead)
        field[line][:SPAN_HALO] = behind
        field[line][SPAN_HALO:] = ahead

    bias = vectors_ref[2]
    kept = []
    spare = SPAN_HALO - 2
    ready = 0
    for pair in range((lines + 2) // 2):
        for line in range(ready, 2 * pair + 4):
            fill(line)
        ready = 2 * pair + 4
        results = pair_conv(field[2 * pair : 2 * pair + 4], inner + 2, weight_ref)
        for out in range(2):
            line = 2 * pair + out
            rounded = (results[out] + bias).astype(jnp.bfloat16)
            rounded = rounded.reshape(inner + 2, columns, channels)
            middle_ref[:2, line] = jnp.where(
                at_start, field[line + lines - 1][:spare], rounded[:2]
            )
            middle_ref[2:, line] = rounded[2:]
            if 1 <= line <= lines:
                kept.append(rounded[2:].astype(jnp.float32).reshape(-1, channels))
    packed = moments(kept)
    for device in range(sums_ref.shape[0]):
        sums_ref[device] = packed


def second_kernel(
    row_count, middle_ref, stats_ref, vectors_ref, weight_ref, own_ref, out_ref, ready, sems,
    *field
):
    section, row_at = lax.axis_index("section"), lax.axis_index("rows")
    frames, lines, columns, channels = own_ref.shape
    cells = frames * lines * columns
    scale, shift = vectors_ref[3], vectors_ref[4]
    mine = stats_ref[pl.ds(section * row_count, row_count)]
    before = stats_ref[pl.ds(jnp.maximum(section - 1, 0) * row_count, row_count)]
    slope, offset = affine(mine, cells, scale, shift)
    slope_before, offset_before = affine(before, cells, scale, shift)
    at_start = section == 0
    half = frames // 2
    copies = []
    for begin in range(0, frames, half):
        parts = field[(begin // half) * (lines + 2) :]
        for line in range(lines + 2):
            ahead = middle_ref[begin : begin + half + 2, line]
            if begin == 0:
                behind = activate(ahead[:2], slope_before, offset_before).astype(jnp.bfloat16)
                behind = jnp.where(at_start, ahead[:2], behind)
                ahead = activate(ahead[2:], slope, offset).astype(jnp.bfloat16)
                ahead = jnp.concatenate([behind, ahead], axis=0)
            else:
                ahead = activate(ahead, slope, offset).astype(jnp.bfloat16)
            if line == 0 or line == lines + 1:
                outside = row_at == 0 if line == 0 else row_at == row_count - 1
                ahead = jnp.where(outside, jnp.zeros_like(ahead), ahead)
            parts[line][...] = ahead
        span = slice(begin, begin + half)
        for pair in range(lines // 2):
            results = pair_conv(parts[2 * pair : 2 * pair + 4], half, weight_ref)
            for out in range(2):
                line = 2 * pair + out
                result = (results[out] + vectors_ref[5]).reshape(half, columns, channels)
                result = result + own_ref[span, line].astype(jnp.float32)
                ready[span, line] = result.astype(jnp.bfloat16)
        copy = pltpu.make_async_copy(
            ready.at[span], out_ref.at[span], sems.at[begin // half]
        )
        copy.start()
        copies.append(copy)
    for copy in copies:
        copy.wait()


def call(kernel, out_shape, scratch, operands, in_place=(), out_in_place=False, flops=0):
    vmem = pl.BlockSpec(memory_space=pltpu.VMEM)
    out_spec = pl.BlockSpec(memory_space=pltpu.HBM) if out_in_place else vmem
    specs = [vmem] * len(operands)
    for index in in_place:
        specs[index] = pl.BlockSpec(memory_space=pltpu.HBM)
    operands = [
        pltpu.with_memory_space_constraint(operand, pltpu.HBM) if index in in_place else operand
        for index, operand in enumerate(operands)
    ]
    return pl.pallas_call(
        kernel,
        out_shape=out_shape,
        in_specs=specs,
        out_specs=jax.tree.map(lambda _: out_spec, out_shape),
        scratch_shapes=scratch,
        compiler_params=pltpu.CompilerParams(vmem_limit_bytes=40 * 2**20),
        cost_estimate=pl.CostEstimate(flops=flops, bytes_accessed=2**20, transcendentals=0),
    )(*operands)


def on_device(
    activations,
    first_cache,
    second_cache,
    norm1_scale,
    norm1_shift,
    conv1_weight,
    conv1_bias,
    norm2_scale,
    norm2_shift,
    conv2_weight,
    conv2_bias,
):
    frames, lines, columns, channels = activations.shape
    sections, row_count = lax.axis_size("section"), lax.axis_size("rows")
    everyone = sections * row_count
    stats_shape = jax.ShapeDtypeStruct((everyone, 2, channels), jnp.float32)
    vectors = (norm1_scale, norm1_shift, conv1_bias, norm2_scale, norm2_shift, conv2_bias)

    near = [i ^ 1 for i in range(row_count)]
    far = [0] + [i + 1 if i % 2 else i - 1 for i in range(1, row_count - 1)] + [row_count - 1]

    def across(block, partner):
        return lax.ppermute(block, "rows", list(enumerate(partner)))

    ring = [(at, (at + 1) % sections) for at in range(sections)]
    own, halo = call(
        functools.partial(copy_kernel, sections),
        (
            jax.ShapeDtypeStruct(activations.shape, jnp.bfloat16),
            jax.ShapeDtypeStruct((SPAN_HALO, lines, columns, channels), jnp.bfloat16),
        ),
        [pltpu.SemaphoreType.DMA((4,))],
        (activations, second_cache, first_cache),
        in_place=range(3),
    )
    sums, packed, weight = call(
        stats_kernel,
        (
            jax.ShapeDtypeStruct((1, 2, channels), jnp.float32),
            jax.ShapeDtypeStruct((len(vectors), 1, channels), jnp.float32),
            jax.ShapeDtypeStruct(conv1_weight.shape, jnp.bfloat16),
        ),
        [pltpu.SemaphoreType.DMA((1 + len(vectors),))],
        (own, conv1_weight) + tuple(vector.reshape(1, channels) for vector in vectors),
        in_place=range(1, 2 + len(vectors)),
    )
    received = lax.ppermute(halo, "section", ring)
    passed = lax.ppermute(sums, "section", ring)
    received, sums, passed = lax.optimization_barrier((received, sums, passed))
    joined = jnp.concatenate([received, own], axis=0)
    from_far = across(joined, far)
    from_near = across(joined, near)
    both = jnp.concatenate([sums, passed], axis=1)
    both = jnp.broadcast_to(both, (row_count,) + both.shape[1:])
    stats = lax.all_to_all(both, "rows", 0, 0, tiled=True)
    middle, sums_two = call(
        functools.partial(first_kernel, row_count),
        (
            jax.ShapeDtypeStruct((frames + 2, lines + 2, columns, channels), jnp.bfloat16),
            stats_shape,
        ),
        [pltpu.VMEM((frames + SPAN_HALO, columns, channels), jnp.bfloat16)] * (3 * lines),
        (joined, from_far, from_near, stats, packed, weight),
        flops=10**9,
    )
    stats_two = lax.all_to_all(sums_two, ("section", "rows"), 0, 0, tiled=True)
    return call(
        functools.partial(second_kernel, row_count),
        jax.ShapeDtypeStruct(activations.shape, jnp.bfloat16),
        [
            pltpu.VMEM(activations.shape, jnp.bfloat16),
            pltpu.SemaphoreType.DMA((2,)),
        ]
        + [pltpu.VMEM((frames // 2 + 2, columns, channels), jnp.bfloat16)] * (2 * lines + 4),
        (middle, stats_two, packed, conv2_weight, own),
        out_in_place=True,
        flops=10**9,
    )


def solution(mesh):
    in_specs = (
        P("section", "rows", None, None),
        P(None, "rows", None, None),
        P(None, "rows", None, None),
        P(),
        P(),
        P(),
        P(),
        P(),
        P(),
        P(),
        P(),
    )
    out_specs = P("section", "rows", None, None)
    return jax.shard_map(
        on_device, mesh=mesh, in_specs=in_specs, out_specs=out_specs, check_vma=False
    )
```

```python
import functools

import functools

import jax
import jax.numpy as jnp
from jax import lax
from jax.experimental import pallas as pl
from jax.experimental.pallas import tpu as pltpu
from jax.sharding import PartitionSpec as P

GROUPS = 32
SPAN_HALO = 4

epsilon = 1e-06


def moments(blocks):
    pivot = blocks[0][:1]
    cells = sum(block.shape[0] for block in blocks)
    total, squares = 0.0, 0.0
    for block in blocks:
        away = block - pivot
        total = total + jnp.sum(away, axis=0, keepdims=True)
        squares = squares + jnp.sum(away * away, axis=0, keepdims=True)
    shift = total * (1.0 / cells)
    return jnp.concatenate([pivot + shift, squares - total * shift], axis=0)


def affine(stats, cells, scale, shift):
    devices, _, channels = stats.shape
    means, squares = stats[:, 0], stats[:, 1]
    mean = jnp.sum(means, axis=0, keepdims=True) * (1.0 / devices)
    away = means - mean
    square = jnp.sum(squares + cells * (away * away), axis=0, keepdims=True)
    count = cells * devices
    lane = lax.broadcasted_iota(jnp.int32, mean.shape, 1)
    step = 1
    while step < channels // GROUPS:

        def partner(values):
            up = pltpu.roll(values, channels - step, 1)
            return jnp.where((lane // step) % 2 == 0, up, pltpu.roll(values, step, 1))

        away = partner(mean) - mean
        square = square + partner(square) + (0.5 * count) * (away * away)
        mean = mean + 0.5 * away
        count, step = 2 * count, 2 * step
    slope = 0.5 * scale * lax.rsqrt(square * (1.0 / count) + epsilon)
    return slope, 0.5 * shift - mean * slope


def activate(values, slope, offset):
    half = values.astype(jnp.float32) * slope + offset
    return half + half * jnp.tanh(half)


def pair_conv(field, row, begin, frames, weight_ref):
    columns, channels = field.shape[2], field.shape[3]
    cells = frames * columns
    nothing = jnp.zeros((channels, channels), jnp.bfloat16)

    def piece(frame_tap, line):
        first = begin + frame_tap
        return field[first : first + frames, row + line].reshape(cells, channels)

    def dot(pieces, blocks):
        return jnp.dot(pieces, blocks, preferred_element_type=jnp.float32)

    taps = [(frame_tap, row_tap) for frame_tap in range(3) for row_tap in range(3)]
    early = dot(
        jnp.concatenate(
            [
                jnp.concatenate([piece(tap, out + row_tap) for tap, row_tap in taps], axis=1)
                for out in range(2)
            ],
            axis=0,
        ),
        jnp.concatenate(
            [
                jnp.concatenate([weight_ref[tap, row_tap, 0], weight_ref[tap, row_tap, 1]], axis=1)
                for tap, row_tap in taps
            ],
            axis=0,
        ),
    )
    lines = [(frame_tap, line) for frame_tap in range(3) for line in range(4)]
    late = dot(
        jnp.concatenate([piece(tap, line) for tap, line in lines], axis=1),
        jnp.concatenate(
            [
                jnp.concatenate(
                    [
                        weight_ref[tap, line - out, 2] if 0 <= line - out <= 2 else nothing
                        for out in range(2)
                    ],
                    axis=1,
                )
                for tap, line in lines
            ],
            axis=0,
        ),
    )
    column = lax.broadcasted_iota(jnp.int32, (cells, channels), 0) % columns
    results = []
    for out in range(2):
        left, centre = (
            early[out * cells : (out + 1) * cells, tap * channels : (tap + 1) * channels]
            for tap in range(2)
        )
        right = late[:, out * channels : (out + 1) * channels]
        left = jnp.where(column == 0, 0.0, pltpu.roll(left, 1, 0))
        right = jnp.where(column == columns - 1, 0.0, pltpu.roll(right, cells - 1, 0))
        results.append(left + centre + right)
    return results


def copy_kernel(sections, own_ref, second_cache_ref, first_cache_ref, copied, halo_ref, sems):
    last = lax.axis_index("section") == sections - 1
    frames = own_ref.shape[0]
    spare = SPAN_HALO - 2
    tail = pltpu.make_async_copy(own_ref.at[frames - SPAN_HALO :], halo_ref, sems.at[0])
    older = pltpu.make_async_copy(second_cache_ref, halo_ref.at[:spare], sems.at[1])
    newer = pltpu.make_async_copy(first_cache_ref, halo_ref.at[spare:], sems.at[2])
    load = pltpu.make_async_copy(own_ref, copied, sems.at[3])

    @pl.when(last)
    def _():
        older.start()
        newer.start()

    @pl.when(jnp.logical_not(last))
    def _():
        tail.start()

    load.start()

    @pl.when(last)
    def _():
        older.wait()
        newer.wait()

    @pl.when(jnp.logical_not(last))
    def _():
        tail.wait()

    load.wait()


def stats_kernel(own_ref, weight_ref, *rest):
    *vector_refs, stats_ref, vectors_ref, weight_copy, sems = rest
    loads = [pltpu.make_async_copy(weight_ref, weight_copy, sems.at[0])]
    loads += [
        pltpu.make_async_copy(vector_ref, vectors_ref.at[index], sems.at[1 + index])
        for index, vector_ref in enumerate(vector_refs)
    ]
    for load in loads:
        load.start()
    channels = own_ref.shape[-1]
    blocks = [own_ref[frame].astype(jnp.float32) for frame in range(own_ref.shape[0])]
    stats_ref[0] = moments([block.reshape(-1, channels) for block in blocks])
    for load in loads:
        load.wait()


def first_kernel(
    row_count, halo_ref, own_ref, near_ref, far_ref, stats_ref, vectors_ref, weight_ref,
    middle_ref, sums_ref, field
):
    section, row_at = lax.axis_index("section"), lax.axis_index("rows")
    inner, lines, columns, channels = own_ref.shape
    cells = inner * lines * columns
    scale, shift = vectors_ref[0], vectors_ref[1]
    mine, before = stats_ref[:, :2], stats_ref[:, 2:]
    slope, offset = affine(mine, cells, scale, shift)
    slope_before, offset_before = affine(before, cells, scale, shift)
    even = row_at % 2 == 0
    at_start = section == 0

    def fill(line):
        side, local = divmod(line, lines)
        if side == 1:
            halo, body = halo_ref[:, local], own_ref[:, local]
        else:
            near_side = even if side == 2 else jnp.logical_not(even)
            block = jnp.where(near_side, near_ref[:, local], far_ref[:, local])
            halo, body = block[:SPAN_HALO], block[SPAN_HALO:]
        behind = activate(halo, slope_before, offset_before).astype(jnp.bfloat16)
        behind = jnp.where(at_start, halo, behind)
        ahead = activate(body, slope, offset).astype(jnp.bfloat16)
        if side != 1:
            outside = row_at == 0 if side == 0 else row_at == row_count - 1
            behind = jnp.where(outside, jnp.zeros_like(behind), behind)
            ahead = jnp.where(outside, jnp.zeros_like(ahead), ahead)
        field[:SPAN_HALO, line] = behind
        field[SPAN_HALO:, line] = ahead

    bias = vectors_ref[2]
    kept = []
    spare = SPAN_HALO - 2
    ready = 0
    for pair in range((lines + 2) // 2):
        for line in range(ready, 2 * pair + 4):
            fill(line)
        ready = 2 * pair + 4
        results = pair_conv(field, 2 * pair, 0, inner + 2, weight_ref)
        for out in range(2):
            line = 2 * pair + out
            rounded = (results[out] + bias).astype(jnp.bfloat16)
            rounded = rounded.reshape(inner + 2, columns, channels)
            middle_ref[:2, line] = jnp.where(at_start, field[:spare, line + lines - 1], rounded[:2])
            middle_ref[2:, line] = rounded[2:]
            if 1 <= line <= lines:
                kept.append(rounded[2:].astype(jnp.float32).reshape(-1, channels))
    packed = moments(kept)
    for device in range(sums_ref.shape[0]):
        sums_ref[device] = packed


def second_kernel(
    row_count, middle_ref, stats_ref, vectors_ref, weight_ref, own_ref, out_ref, field, ready,
    sems
):
    section, row_at = lax.axis_index("section"), lax.axis_index("rows")
    frames, lines, columns, channels = own_ref.shape
    cells = frames * lines * columns
    scale, shift = vectors_ref[3], vectors_ref[4]
    mine = stats_ref[pl.ds(section * row_count, row_count)]
    before = stats_ref[pl.ds(jnp.maximum(section - 1, 0) * row_count, row_count)]
    slope, offset = affine(mine, cells, scale, shift)
    slope_before, offset_before = affine(before, cells, scale, shift)
    at_start = section == 0
    half = frames // 2
    copies = []
    for begin in range(0, frames, half):
        filled = 0 if begin == 0 else begin + 2
        for line in range(lines + 2):
            ahead = middle_ref[filled : begin + half + 2, line]
            if begin == 0:
                behind = activate(ahead[:2], slope_before, offset_before).astype(jnp.bfloat16)
                behind = jnp.where(at_start, ahead[:2], behind)
                ahead = activate(ahead[2:], slope, offset).astype(jnp.bfloat16)
                ahead = jnp.concatenate([behind, ahead], axis=0)
            else:
                ahead = activate(ahead, slope, offset).astype(jnp.bfloat16)
            if line == 0 or line == lines + 1:
                outside = row_at == 0 if line == 0 else row_at == row_count - 1
                ahead = jnp.where(outside, jnp.zeros_like(ahead), ahead)
            field[filled : begin + half + 2, line] = ahead
        span = slice(begin, begin + half)
        for pair in range(lines // 2):
            results = pair_conv(field, 2 * pair, begin, half, weight_ref)
            for out in range(2):
                line = 2 * pair + out
                result = (results[out] + vectors_ref[5]).reshape(half, columns, channels)
                result = result + own_ref[span, line].astype(jnp.float32)
                ready[span, line] = result.astype(jnp.bfloat16)
        copy = pltpu.make_async_copy(
            ready.at[span], out_ref.at[span], sems.at[begin // half]
        )
        copy.start()
        copies.append(copy)
    for copy in copies:
        copy.wait()


def call(kernel, out_shape, scratch, operands, in_place=(), out_in_place=False, flops=0):
    vmem = pl.BlockSpec(memory_space=pltpu.VMEM)
    out_spec = pl.BlockSpec(memory_space=pltpu.HBM) if out_in_place else vmem
    specs = [vmem] * len(operands)
    for index in in_place:
        specs[index] = pl.BlockSpec(memory_space=pltpu.HBM)
    operands = [
        pltpu.with_memory_space_constraint(operand, pltpu.HBM) if index in in_place else operand
        for index, operand in enumerate(operands)
    ]
    return pl.pallas_call(
        kernel,
        out_shape=out_shape,
        in_specs=specs,
        out_specs=jax.tree.map(lambda _: out_spec, out_shape),
        scratch_shapes=scratch,
        compiler_params=pltpu.CompilerParams(vmem_limit_bytes=40 * 2**20),
        cost_estimate=pl.CostEstimate(flops=flops, bytes_accessed=2**20, transcendentals=0),
    )(*operands)


def on_device(
    activations,
    first_cache,
    second_cache,
    norm1_scale,
    norm1_shift,
    conv1_weight,
    conv1_bias,
    norm2_scale,
    norm2_shift,
    conv2_weight,
    conv2_bias,
):
    frames, lines, columns, channels = activations.shape
    sections, row_count = lax.axis_size("section"), lax.axis_size("rows")
    everyone = sections * row_count
    stats_shape = jax.ShapeDtypeStruct((everyone, 2, channels), jnp.float32)
    vectors = (norm1_scale, norm1_shift, conv1_bias, norm2_scale, norm2_shift, conv2_bias)

    near = [i ^ 1 for i in range(row_count)]
    far = [i + 2 if i % 2 == 0 else i - 2 for i in range(row_count)]
    far[row_count - 2], far[1] = row_count - 1, 0

    def across(block, partner):
        return lax.ppermute(block, "rows", list(enumerate(partner)))

    ring = [(at, (at + 1) % sections) for at in range(sections)]
    own, halo = call(
        functools.partial(copy_kernel, sections),
        (
            jax.ShapeDtypeStruct(activations.shape, jnp.bfloat16),
            jax.ShapeDtypeStruct((SPAN_HALO, lines, columns, channels), jnp.bfloat16),
        ),
        [pltpu.SemaphoreType.DMA((4,))],
        (activations, second_cache, first_cache),
        in_place=range(3),
    )
    sums, packed, weight = call(
        stats_kernel,
        (
            jax.ShapeDtypeStruct((1, 2, channels), jnp.float32),
            jax.ShapeDtypeStruct((len(vectors), 1, channels), jnp.float32),
            jax.ShapeDtypeStruct(conv1_weight.shape, jnp.bfloat16),
        ),
        [pltpu.SemaphoreType.DMA((1 + len(vectors),))],
        (own, conv1_weight) + tuple(vector.reshape(1, channels) for vector in vectors),
        in_place=range(1, 2 + len(vectors)),
    )
    received = lax.ppermute(halo, "section", ring)
    passed = lax.ppermute(sums, "section", ring)
    received, sums, passed = lax.optimization_barrier((received, sums, passed))
    from_near = jnp.concatenate([across(received, near), across(own, near)], axis=0)
    from_far = across(from_near, far)
    both = jnp.concatenate([sums, passed], axis=1)
    both = jnp.broadcast_to(both, (row_count,) + both.shape[1:])
    stats = lax.all_to_all(both, "rows", 0, 0, tiled=True)
    middle, sums_two = call(
        functools.partial(first_kernel, row_count),
        (
            jax.ShapeDtypeStruct((frames + 2, lines + 2, columns, channels), jnp.bfloat16),
            stats_shape,
        ),
        [pltpu.VMEM((frames + SPAN_HALO, 3 * lines, columns, channels), jnp.bfloat16)],
        (received, own, from_near, from_far, stats, packed, weight),
        flops=10**9,
    )
    stats_two = lax.all_to_all(sums_two, ("section", "rows"), 0, 0, tiled=True)
    return call(
        functools.partial(second_kernel, row_count),
        jax.ShapeDtypeStruct(activations.shape, jnp.bfloat16),
        [
            pltpu.VMEM((frames + 2, lines + 2, columns, channels), jnp.bfloat16),
            pltpu.VMEM(activations.shape, jnp.bfloat16),
            pltpu.SemaphoreType.DMA((2,)),
        ],
        (middle, stats_two, packed, conv2_weight, own),
        out_in_place=True,
        flops=10**9,
    )


def solution(mesh):
    in_specs = (
        P("section", "rows", None, None),
        P(None, "rows", None, None),
        P(None, "rows", None, None),
        P(),
        P(),
        P(),
        P(),
        P(),
        P(),
        P(),
        P(),
    )
    out_specs = P("section", "rows", None, None)
    return jax.shard_map(
        on_device, mesh=mesh, in_specs=in_specs, out_specs=out_specs, check_vma=False
    )
```

```python
import functools

import functools

import jax
import jax.numpy as jnp
from jax import lax
from jax.experimental import pallas as pl
from jax.experimental.pallas import tpu as pltpu
from jax.sharding import PartitionSpec as P

GROUPS = 32
SPAN_HALO = 4

epsilon = 1e-06


def moments(blocks):
    pivot = blocks[0][:1]
    cells = sum(block.shape[0] for block in blocks)
    total, squares = 0.0, 0.0
    for block in blocks:
        away = block - pivot
        total = total + jnp.sum(away, axis=0, keepdims=True)
        squares = squares + jnp.sum(away * away, axis=0, keepdims=True)
    shift = total * (1.0 / cells)
    return jnp.concatenate([pivot + shift, squares - total * shift], axis=0)


def affine(stats, cells, scale, shift):
    devices, _, channels = stats.shape
    means, squares = stats[:, 0], stats[:, 1]
    mean = jnp.sum(means, axis=0, keepdims=True) * (1.0 / devices)
    away = means - mean
    square = jnp.sum(squares + cells * (away * away), axis=0, keepdims=True)
    count = cells * devices
    lane = lax.broadcasted_iota(jnp.int32, mean.shape, 1)
    step = 1
    while step < channels // GROUPS:

        def partner(values):
            up = pltpu.roll(values, channels - step, 1)
            return jnp.where((lane // step) % 2 == 0, up, pltpu.roll(values, step, 1))

        away = partner(mean) - mean
        square = square + partner(square) + (0.5 * count) * (away * away)
        mean = mean + 0.5 * away
        count, step = 2 * count, 2 * step
    slope = 0.5 * scale * lax.rsqrt(square * (1.0 / count) + epsilon)
    return slope, 0.5 * shift - mean * slope


def activate(values, slope, offset):
    half = values.astype(jnp.float32) * slope + offset
    return half + half * jnp.tanh(half)


def pair_conv(field, row, begin, frames, weight_ref):
    columns, channels = field.shape[2], field.shape[3]
    cells = frames * columns
    nothing = jnp.zeros((channels, channels), jnp.bfloat16)

    def piece(frame_tap, line):
        first = begin + frame_tap
        return field[first : first + frames, row + line].reshape(cells, channels)

    def dot(pieces, blocks):
        return jnp.dot(pieces, blocks, preferred_element_type=jnp.float32)

    taps = [(frame_tap, row_tap) for frame_tap in range(3) for row_tap in range(3)]
    early = dot(
        jnp.concatenate(
            [
                jnp.concatenate([piece(tap, out + row_tap) for tap, row_tap in taps], axis=1)
                for out in range(2)
            ],
            axis=0,
        ),
        jnp.concatenate(
            [
                jnp.concatenate([weight_ref[tap, row_tap, 0], weight_ref[tap, row_tap, 1]], axis=1)
                for tap, row_tap in taps
            ],
            axis=0,
        ),
    )
    lines = [(frame_tap, line) for frame_tap in range(3) for line in range(4)]
    late = dot(
        jnp.concatenate([piece(tap, line) for tap, line in lines], axis=1),
        jnp.concatenate(
            [
                jnp.concatenate(
                    [
                        weight_ref[tap, line - out, 2] if 0 <= line - out <= 2 else nothing
                        for out in range(2)
                    ],
                    axis=1,
                )
                for tap, line in lines
            ],
            axis=0,
        ),
    )
    column = lax.broadcasted_iota(jnp.int32, (cells, channels), 0) % columns
    results = []
    for out in range(2):
        left, centre = (
            early[out * cells : (out + 1) * cells, tap * channels : (tap + 1) * channels]
            for tap in range(2)
        )
        right = late[:, out * channels : (out + 1) * channels]
        left = jnp.where(column == 0, 0.0, pltpu.roll(left, 1, 0))
        right = jnp.where(column == columns - 1, 0.0, pltpu.roll(right, cells - 1, 0))
        results.append(left + centre + right)
    return results


def copy_kernel(sections, own_ref, second_cache_ref, first_cache_ref, copied, halo_ref, sems):
    last = lax.axis_index("section") == sections - 1
    frames = own_ref.shape[0]
    spare = SPAN_HALO - 2
    tail = pltpu.make_async_copy(own_ref.at[frames - SPAN_HALO :], halo_ref, sems.at[0])
    older = pltpu.make_async_copy(second_cache_ref, halo_ref.at[:spare], sems.at[1])
    newer = pltpu.make_async_copy(first_cache_ref, halo_ref.at[spare:], sems.at[2])
    load = pltpu.make_async_copy(own_ref, copied, sems.at[3])

    @pl.when(last)
    def _():
        older.start()
        newer.start()

    @pl.when(jnp.logical_not(last))
    def _():
        tail.start()

    load.start()

    @pl.when(last)
    def _():
        older.wait()
        newer.wait()

    @pl.when(jnp.logical_not(last))
    def _():
        tail.wait()

    load.wait()


def stats_kernel(own_ref, weight_ref, *rest):
    *vector_refs, stats_ref, vectors_ref, weight_copy, sems = rest
    loads = [pltpu.make_async_copy(weight_ref, weight_copy, sems.at[0])]
    loads += [
        pltpu.make_async_copy(vector_ref, vectors_ref.at[index], sems.at[1 + index])
        for index, vector_ref in enumerate(vector_refs)
    ]
    for load in loads:
        load.start()
    channels = own_ref.shape[-1]
    blocks = [own_ref[frame].astype(jnp.float32) for frame in range(own_ref.shape[0])]
    stats_ref[0] = moments([block.reshape(-1, channels) for block in blocks])
    for load in loads:
        load.wait()


def first_kernel(
    row_count, own_ref, near_ref, far_ref, halo_ref, halo_near_ref, halo_far_ref, stats_ref,
    vectors_ref, weight_ref, middle_ref, sums_ref, field
):
    section, row_at = lax.axis_index("section"), lax.axis_index("rows")
    inner, lines, columns, channels = own_ref.shape
    cells = inner * lines * columns
    scale, shift = vectors_ref[0], vectors_ref[1]
    mine, before = stats_ref[:, :2], stats_ref[:, 2:]
    slope, offset = affine(mine, cells, scale, shift)
    slope_before, offset_before = affine(before, cells, scale, shift)
    even = row_at % 2 == 0
    at_start = section == 0

    def fill(line):
        side, local = divmod(line, lines)
        if side == 1:
            halo, body = halo_ref[:, local], own_ref[:, local]
        else:
            near_side = even if side == 2 else jnp.logical_not(even)
            halo = jnp.where(near_side, halo_near_ref[:, local], halo_far_ref[:, local])
            body = jnp.where(near_side, near_ref[:, local], far_ref[:, local])
        behind = activate(halo, slope_before, offset_before).astype(jnp.bfloat16)
        behind = jnp.where(at_start, halo, behind)
        ahead = activate(body, slope, offset).astype(jnp.bfloat16)
        if side != 1:
            outside = row_at == 0 if side == 0 else row_at == row_count - 1
            behind = jnp.where(outside, jnp.zeros_like(behind), behind)
            ahead = jnp.where(outside, jnp.zeros_like(ahead), ahead)
        field[:SPAN_HALO, line] = behind
        field[SPAN_HALO:, line] = ahead

    bias = vectors_ref[2]
    kept = []
    spare = SPAN_HALO - 2
    ready = 0
    for pair in range((lines + 2) // 2):
        for line in range(ready, 2 * pair + 4):
            fill(line)
        ready = 2 * pair + 4
        results = pair_conv(field, 2 * pair, 0, inner + 2, weight_ref)
        for out in range(2):
            line = 2 * pair + out
            rounded = (results[out] + bias).astype(jnp.bfloat16)
            rounded = rounded.reshape(inner + 2, columns, channels)
            middle_ref[:2, line] = jnp.where(at_start, field[:spare, line + lines - 1], rounded[:2])
            middle_ref[2:, line] = rounded[2:]
            if 1 <= line <= lines:
                kept.append(rounded[2:].astype(jnp.float32).reshape(-1, channels))
    packed = moments(kept)
    for device in range(sums_ref.shape[0]):
        sums_ref[device] = packed


def second_kernel(
    row_count, middle_ref, stats_ref, vectors_ref, weight_ref, own_ref, out_ref, field, ready,
    sems
):
    section, row_at = lax.axis_index("section"), lax.axis_index("rows")
    frames, lines, columns, channels = own_ref.shape
    cells = frames * lines * columns
    scale, shift = vectors_ref[3], vectors_ref[4]
    mine = stats_ref[pl.ds(section * row_count, row_count)]
    before = stats_ref[pl.ds(jnp.maximum(section - 1, 0) * row_count, row_count)]
    slope, offset = affine(mine, cells, scale, shift)
    slope_before, offset_before = affine(before, cells, scale, shift)
    at_start = section == 0
    half = frames // 2
    copies = []
    for begin in range(0, frames, half):
        filled = 0 if begin == 0 else begin + 2
        for line in range(lines + 2):
            ahead = middle_ref[filled : begin + half + 2, line]
            if begin == 0:
                behind = activate(ahead[:2], slope_before, offset_before).astype(jnp.bfloat16)
                behind = jnp.where(at_start, ahead[:2], behind)
                ahead = activate(ahead[2:], slope, offset).astype(jnp.bfloat16)
                ahead = jnp.concatenate([behind, ahead], axis=0)
            else:
                ahead = activate(ahead, slope, offset).astype(jnp.bfloat16)
            if line == 0 or line == lines + 1:
                outside = row_at == 0 if line == 0 else row_at == row_count - 1
                ahead = jnp.where(outside, jnp.zeros_like(ahead), ahead)
            field[filled : begin + half + 2, line] = ahead
        span = slice(begin, begin + half)
        for pair in range(lines // 2):
            results = pair_conv(field, 2 * pair, begin, half, weight_ref)
            for out in range(2):
                line = 2 * pair + out
                result = (results[out] + vectors_ref[5]).reshape(half, columns, channels)
                result = result + own_ref[span, line].astype(jnp.float32)
                ready[span, line] = result.astype(jnp.bfloat16)
        copy = pltpu.make_async_copy(
            ready.at[span], out_ref.at[span], sems.at[begin // half]
        )
        copy.start()
        copies.append(copy)
    for copy in copies:
        copy.wait()


def call(kernel, out_shape, scratch, operands, in_place=(), out_in_place=False, flops=0):
    vmem = pl.BlockSpec(memory_space=pltpu.VMEM)
    out_spec = pl.BlockSpec(memory_space=pltpu.HBM) if out_in_place else vmem
    specs = [vmem] * len(operands)
    for index in in_place:
        specs[index] = pl.BlockSpec(memory_space=pltpu.HBM)
    operands = [
        pltpu.with_memory_space_constraint(operand, pltpu.HBM) if index in in_place else operand
        for index, operand in enumerate(operands)
    ]
    return pl.pallas_call(
        kernel,
        out_shape=out_shape,
        in_specs=specs,
        out_specs=jax.tree.map(lambda _: out_spec, out_shape),
        scratch_shapes=scratch,
        compiler_params=pltpu.CompilerParams(vmem_limit_bytes=40 * 2**20),
        cost_estimate=pl.CostEstimate(flops=flops, bytes_accessed=2**20, transcendentals=0),
    )(*operands)


def on_device(
    activations,
    first_cache,
    second_cache,
    norm1_scale,
    norm1_shift,
    conv1_weight,
    conv1_bias,
    norm2_scale,
    norm2_shift,
    conv2_weight,
    conv2_bias,
):
    frames, lines, columns, channels = activations.shape
    sections, row_count = lax.axis_size("section"), lax.axis_size("rows")
    everyone = sections * row_count
    stats_shape = jax.ShapeDtypeStruct((everyone, 2, channels), jnp.float32)
    vectors = (norm1_scale, norm1_shift, conv1_bias, norm2_scale, norm2_shift, conv2_bias)

    near = [i ^ 1 for i in range(row_count)]
    far = [i + 2 if i % 2 == 0 else i - 2 for i in range(row_count)]
    far[row_count - 2], far[1] = row_count - 1, 0

    def across(block, partner):
        return lax.ppermute(block, "rows", list(enumerate(partner)))

    ring = [(at, (at + 1) % sections) for at in range(sections)]
    own, halo = call(
        functools.partial(copy_kernel, sections),
        (
            jax.ShapeDtypeStruct(activations.shape, jnp.bfloat16),
            jax.ShapeDtypeStruct((SPAN_HALO, lines, columns, channels), jnp.bfloat16),
        ),
        [pltpu.SemaphoreType.DMA((4,))],
        (activations, second_cache, first_cache),
        in_place=range(3),
    )
    sums, packed, weight = call(
        stats_kernel,
        (
            jax.ShapeDtypeStruct((1, 2, channels), jnp.float32),
            jax.ShapeDtypeStruct((len(vectors), 1, channels), jnp.float32),
            jax.ShapeDtypeStruct(conv1_weight.shape, jnp.bfloat16),
        ),
        [pltpu.SemaphoreType.DMA((1 + len(vectors),))],
        (own, conv1_weight) + tuple(vector.reshape(1, channels) for vector in vectors),
        in_place=range(1, 2 + len(vectors)),
    )
    received = lax.ppermute(halo, "section", ring)
    bodies = [own, across(own, near)]
    bodies.append(across(bodies[1], far))
    passed = lax.ppermute(sums, "section", ring)
    received, sums, passed = lax.optimization_barrier((received, sums, passed))
    halos = [received, across(received, near)]
    halos.append(across(halos[1], far))
    both = jnp.concatenate([sums, passed], axis=1)
    both = jnp.broadcast_to(both, (row_count,) + both.shape[1:])
    stats = lax.all_to_all(both, "rows", 0, 0, tiled=True)
    middle, sums_two = call(
        functools.partial(first_kernel, row_count),
        (
            jax.ShapeDtypeStruct((frames + 2, lines + 2, columns, channels), jnp.bfloat16),
            stats_shape,
        ),
        [pltpu.VMEM((frames + SPAN_HALO, 3 * lines, columns, channels), jnp.bfloat16)],
        (*bodies, *halos, stats, packed, weight),
        flops=10**9,
    )
    stats_two = lax.all_to_all(sums_two, ("section", "rows"), 0, 0, tiled=True)
    return call(
        functools.partial(second_kernel, row_count),
        jax.ShapeDtypeStruct(activations.shape, jnp.bfloat16),
        [
            pltpu.VMEM((frames + 2, lines + 2, columns, channels), jnp.bfloat16),
            pltpu.VMEM(activations.shape, jnp.bfloat16),
            pltpu.SemaphoreType.DMA((2,)),
        ],
        (middle, stats_two, packed, conv2_weight, own),
        out_in_place=True,
        flops=10**9,
    )


def solution(mesh):
    in_specs = (
        P("section", "rows", None, None),
        P(None, "rows", None, None),
        P(None, "rows", None, None),
        P(),
        P(),
        P(),
        P(),
        P(),
        P(),
        P(),
        P(),
    )
    out_specs = P("section", "rows", None, None)
    return jax.shard_map(
        on_device, mesh=mesh, in_specs=in_specs, out_specs=out_specs, check_vma=False
    )
```

```python
import functools

import functools

import jax
import jax.numpy as jnp
from jax import lax
from jax.experimental import pallas as pl
from jax.experimental.pallas import tpu as pltpu
from jax.sharding import PartitionSpec as P

GROUPS = 32
SPAN_HALO = 4

epsilon = 1e-06


def moments(blocks):
    pivot = blocks[0][:1]
    cells = sum(block.shape[0] for block in blocks)
    total, squares = 0.0, 0.0
    for block in blocks:
        away = block - pivot
        total = total + jnp.sum(away, axis=0, keepdims=True)
        squares = squares + jnp.sum(away * away, axis=0, keepdims=True)
    shift = total * (1.0 / cells)
    return jnp.concatenate([pivot + shift, squares - total * shift], axis=0)


def affine(stats, cells, scale, shift):
    devices, _, channels = stats.shape
    means, squares = stats[:, 0], stats[:, 1]
    mean = jnp.sum(means, axis=0, keepdims=True) * (1.0 / devices)
    away = means - mean
    square = jnp.sum(squares + cells * (away * away), axis=0, keepdims=True)
    count = cells * devices
    lane = lax.broadcasted_iota(jnp.int32, mean.shape, 1)
    step = 1
    while step < channels // GROUPS:

        def partner(values):
            up = pltpu.roll(values, channels - step, 1)
            return jnp.where((lane // step) % 2 == 0, up, pltpu.roll(values, step, 1))

        away = partner(mean) - mean
        square = square + partner(square) + (0.5 * count) * (away * away)
        mean = mean + 0.5 * away
        count, step = 2 * count, 2 * step
    slope = 0.5 * scale * lax.rsqrt(square * (1.0 / count) + epsilon)
    return slope, 0.5 * shift - mean * slope


def activate(values, slope, offset):
    half = values.astype(jnp.float32) * slope + offset
    return half + half * jnp.tanh(half)


def pair_conv(field, row, begin, frames, weight_ref):
    columns, channels = field.shape[2], field.shape[3]
    cells = frames * columns
    nothing = jnp.zeros((channels, channels), jnp.bfloat16)

    def piece(frame_tap, line):
        first = begin + frame_tap
        return field[first : first + frames, row + line].reshape(cells, channels)

    def dot(pieces, blocks):
        return jnp.dot(pieces, blocks, preferred_element_type=jnp.float32)

    taps = [(frame_tap, row_tap) for frame_tap in range(3) for row_tap in range(3)]
    early = dot(
        jnp.concatenate(
            [
                jnp.concatenate([piece(tap, out + row_tap) for tap, row_tap in taps], axis=1)
                for out in range(2)
            ],
            axis=0,
        ),
        jnp.concatenate(
            [
                jnp.concatenate([weight_ref[tap, row_tap, 0], weight_ref[tap, row_tap, 1]], axis=1)
                for tap, row_tap in taps
            ],
            axis=0,
        ),
    )
    lines = [(frame_tap, line) for frame_tap in range(3) for line in range(4)]
    late = dot(
        jnp.concatenate([piece(tap, line) for tap, line in lines], axis=1),
        jnp.concatenate(
            [
                jnp.concatenate(
                    [
                        weight_ref[tap, line - out, 2] if 0 <= line - out <= 2 else nothing
                        for out in range(2)
                    ],
                    axis=1,
                )
                for tap, line in lines
            ],
            axis=0,
        ),
    )
    column = lax.broadcasted_iota(jnp.int32, (cells, channels), 0) % columns
    results = []
    for out in range(2):
        left, centre = (
            early[out * cells : (out + 1) * cells, tap * channels : (tap + 1) * channels]
            for tap in range(2)
        )
        right = late[:, out * channels : (out + 1) * channels]
        left = jnp.where(column == 0, 0.0, pltpu.roll(left, 1, 0))
        right = jnp.where(column == columns - 1, 0.0, pltpu.roll(right, cells - 1, 0))
        results.append(left + centre + right)
    return results


def copy_kernel(sections, own_ref, second_cache_ref, first_cache_ref, halo_ref, sems):
    last = lax.axis_index("section") == sections - 1
    frames = own_ref.shape[0]
    spare = SPAN_HALO - 2
    tail = pltpu.make_async_copy(own_ref.at[frames - SPAN_HALO :], halo_ref, sems.at[0])
    older = pltpu.make_async_copy(second_cache_ref, halo_ref.at[:spare], sems.at[1])
    newer = pltpu.make_async_copy(first_cache_ref, halo_ref.at[spare:], sems.at[2])

    @pl.when(last)
    def _():
        older.start()
        newer.start()
        older.wait()
        newer.wait()

    @pl.when(jnp.logical_not(last))
    def _():
        tail.start()
        tail.wait()


def stats_kernel(own_ref, weight_ref, *rest):
    *vector_refs, stats_ref, vectors_ref, copied, weight_copy, sems = rest
    first = pltpu.make_async_copy(own_ref, copied, sems.at[0])
    first.start()
    loads = [pltpu.make_async_copy(weight_ref, weight_copy, sems.at[1])]
    loads += [
        pltpu.make_async_copy(vector_ref, vectors_ref.at[index], sems.at[2 + index])
        for index, vector_ref in enumerate(vector_refs)
    ]
    for load in loads:
        load.start()
    first.wait()
    channels = own_ref.shape[-1]
    blocks = [copied[frame].astype(jnp.float32) for frame in range(own_ref.shape[0])]
    stats_ref[0] = moments([block.reshape(-1, channels) for block in blocks])
    for load in loads:
        load.wait()


def first_kernel(
    row_count, halo_ref, own_ref, near_ref, far_ref, stats_ref, vectors_ref, weight_ref,
    middle_ref, sums_ref, field
):
    section, row_at = lax.axis_index("section"), lax.axis_index("rows")
    inner, lines, columns, channels = own_ref.shape
    cells = inner * lines * columns
    scale, shift = vectors_ref[0], vectors_ref[1]
    mine, before = stats_ref[:, :2], stats_ref[:, 2:]
    slope, offset = affine(mine, cells, scale, shift)
    slope_before, offset_before = affine(before, cells, scale, shift)
    even = row_at % 2 == 0
    at_start = section == 0

    def fill(line):
        side, local = divmod(line, lines)
        if side == 1:
            halo, body = halo_ref[:, local], own_ref[:, local]
        else:
            near_side = even if side == 2 else jnp.logical_not(even)
            block = jnp.where(near_side, near_ref[:, local], far_ref[:, local])
            halo, body = block[:SPAN_HALO], block[SPAN_HALO:]
        behind = activate(halo, slope_before, offset_before).astype(jnp.bfloat16)
        behind = jnp.where(at_start, halo, behind)
        ahead = activate(body, slope, offset).astype(jnp.bfloat16)
        if side != 1:
            outside = row_at == 0 if side == 0 else row_at == row_count - 1
            behind = jnp.where(outside, jnp.zeros_like(behind), behind)
            ahead = jnp.where(outside, jnp.zeros_like(ahead), ahead)
        field[:SPAN_HALO, line] = behind
        field[SPAN_HALO:, line] = ahead

    bias = vectors_ref[2]
    kept = []
    spare = SPAN_HALO - 2
    ready = 0
    for pair in range((lines + 2) // 2):
        for line in range(ready, 2 * pair + 4):
            fill(line)
        ready = 2 * pair + 4
        results = pair_conv(field, 2 * pair, 0, inner + 2, weight_ref)
        for out in range(2):
            line = 2 * pair + out
            rounded = (results[out] + bias).astype(jnp.bfloat16)
            rounded = rounded.reshape(inner + 2, columns, channels)
            middle_ref[:2, line] = jnp.where(at_start, field[:spare, line + lines - 1], rounded[:2])
            middle_ref[2:, line] = rounded[2:]
            if 1 <= line <= lines:
                kept.append(rounded[2:].astype(jnp.float32).reshape(-1, channels))
    packed = moments(kept)
    for device in range(sums_ref.shape[0]):
        sums_ref[device] = packed


def second_kernel(
    row_count, middle_ref, stats_ref, vectors_ref, weight_ref, own_ref, out_ref, field, ready,
    sems
):
    section, row_at = lax.axis_index("section"), lax.axis_index("rows")
    frames, lines, columns, channels = own_ref.shape
    cells = frames * lines * columns
    scale, shift = vectors_ref[3], vectors_ref[4]
    mine = stats_ref[:, section]
    before = stats_ref[:, jnp.maximum(section - 1, 0)]
    slope, offset = affine(mine, cells, scale, shift)
    slope_before, offset_before = affine(before, cells, scale, shift)
    at_start = section == 0
    half = frames // 2
    copies = []
    for begin in range(0, frames, half):
        filled = 0 if begin == 0 else begin + 2
        for line in range(lines + 2):
            ahead = middle_ref[filled : begin + half + 2, line]
            if begin == 0:
                behind = activate(ahead[:2], slope_before, offset_before).astype(jnp.bfloat16)
                behind = jnp.where(at_start, ahead[:2], behind)
                ahead = activate(ahead[2:], slope, offset).astype(jnp.bfloat16)
                ahead = jnp.concatenate([behind, ahead], axis=0)
            else:
                ahead = activate(ahead, slope, offset).astype(jnp.bfloat16)
            if line == 0 or line == lines + 1:
                outside = row_at == 0 if line == 0 else row_at == row_count - 1
                ahead = jnp.where(outside, jnp.zeros_like(ahead), ahead)
            field[filled : begin + half + 2, line] = ahead
        span = slice(begin, begin + half)
        for pair in range(lines // 2):
            results = pair_conv(field, 2 * pair, begin, half, weight_ref)
            for out in range(2):
                line = 2 * pair + out
                result = (results[out] + vectors_ref[5]).reshape(half, columns, channels)
                result = result + own_ref[span, line].astype(jnp.float32)
                ready[span, line] = result.astype(jnp.bfloat16)
        copy = pltpu.make_async_copy(
            ready.at[span], out_ref.at[span], sems.at[begin // half]
        )
        copy.start()
        copies.append(copy)
    for copy in copies:
        copy.wait()


def call(kernel, out_shape, scratch, operands, in_place=(), out_in_place=False, flops=0):
    vmem = pl.BlockSpec(memory_space=pltpu.VMEM)
    out_spec = pl.BlockSpec(memory_space=pltpu.HBM) if out_in_place else vmem
    specs = [vmem] * len(operands)
    for index in in_place:
        specs[index] = pl.BlockSpec(memory_space=pltpu.HBM)
    operands = [
        pltpu.with_memory_space_constraint(operand, pltpu.HBM) if index in in_place else operand
        for index, operand in enumerate(operands)
    ]
    return pl.pallas_call(
        kernel,
        out_shape=out_shape,
        in_specs=specs,
        out_specs=jax.tree.map(lambda _: out_spec, out_shape),
        scratch_shapes=scratch,
        compiler_params=pltpu.CompilerParams(vmem_limit_bytes=40 * 2**20),
        cost_estimate=pl.CostEstimate(flops=flops, bytes_accessed=2**20, transcendentals=0),
    )(*operands)


def on_device(
    activations,
    first_cache,
    second_cache,
    norm1_scale,
    norm1_shift,
    conv1_weight,
    conv1_bias,
    norm2_scale,
    norm2_shift,
    conv2_weight,
    conv2_bias,
):
    frames, lines, columns, channels = activations.shape
    sections, row_count = lax.axis_size("section"), lax.axis_size("rows")
    everyone = sections * row_count
    stats_shape = jax.ShapeDtypeStruct((everyone, 2, channels), jnp.float32)
    vectors = (norm1_scale, norm1_shift, conv1_bias, norm2_scale, norm2_shift, conv2_bias)

    near = [i ^ 1 for i in range(row_count)]
    far = [i + 2 if i % 2 == 0 else i - 2 for i in range(row_count)]
    far[row_count - 2], far[1] = row_count - 1, 0

    def across(block, partner):
        return lax.ppermute(block, "rows", list(enumerate(partner)))

    ring = [(at, (at + 1) % sections) for at in range(sections)]
    halo = call(
        functools.partial(copy_kernel, sections),
        jax.ShapeDtypeStruct((SPAN_HALO, lines, columns, channels), jnp.bfloat16),
        [pltpu.SemaphoreType.DMA((3,))],
        (activations, second_cache, first_cache),
        in_place=range(3),
    )
    sums, packed, own, weight = call(
        stats_kernel,
        (
            jax.ShapeDtypeStruct((1, 2, channels), jnp.float32),
            jax.ShapeDtypeStruct((len(vectors), 1, channels), jnp.float32),
            jax.ShapeDtypeStruct(activations.shape, jnp.bfloat16),
            jax.ShapeDtypeStruct(conv1_weight.shape, jnp.bfloat16),
        ),
        [pltpu.SemaphoreType.DMA((2 + len(vectors),))],
        (activations, conv1_weight) + tuple(vector.reshape(1, channels) for vector in vectors),
        in_place=range(2 + len(vectors)),
    )
    received = lax.ppermute(halo, "section", ring)
    passed = lax.ppermute(sums, "section", ring)
    received, sums, passed = lax.optimization_barrier((received, sums, passed))
    from_near = jnp.concatenate([across(received, near), across(activations, near)], axis=0)
    from_far = across(from_near, far)
    both = jnp.concatenate([sums, passed], axis=1)
    both = jnp.broadcast_to(both, (row_count,) + both.shape[1:])
    stats = lax.all_to_all(both, "rows", 0, 0, tiled=True)
    middle, sums_two = call(
        functools.partial(first_kernel, row_count),
        (
            jax.ShapeDtypeStruct((frames + 2, lines + 2, columns, channels), jnp.bfloat16),
            stats_shape,
        ),
        [pltpu.VMEM((frames + SPAN_HALO, 3 * lines, columns, channels), jnp.bfloat16)],
        (received, own, from_near, from_far, stats, packed, weight),
        flops=10**9,
    )
    stats_two = lax.all_to_all(sums_two, ("rows", "section"), 0, 0, tiled=True)
    stats_two = stats_two.reshape(row_count, sections, 2, channels)
    return call(
        functools.partial(second_kernel, row_count),
        jax.ShapeDtypeStruct(activations.shape, jnp.bfloat16),
        [
            pltpu.VMEM((frames + 2, lines + 2, columns, channels), jnp.bfloat16),
            pltpu.VMEM(activations.shape, jnp.bfloat16),
            pltpu.SemaphoreType.DMA((2,)),
        ],
        (middle, stats_two, packed, conv2_weight, own),
        out_in_place=True,
        flops=10**9,
    )


def solution(mesh):
    in_specs = (
        P("section", "rows", None, None),
        P(None, "rows", None, None),
        P(None, "rows", None, None),
        P(),
        P(),
        P(),
        P(),
        P(),
        P(),
        P(),
        P(),
    )
    out_specs = P("section", "rows", None, None)
    return jax.shard_map(
        on_device, mesh=mesh, in_specs=in_specs, out_specs=out_specs, check_vma=False
    )
```

```python
import functools

import functools

import jax
import jax.numpy as jnp
from jax import lax
from jax.experimental import pallas as pl
from jax.experimental.pallas import tpu as pltpu
from jax.sharding import PartitionSpec as P

GROUPS = 32
SPAN_HALO = 4

epsilon = 1e-06


def moments(blocks):
    pivot = blocks[0][:1]
    cells = sum(block.shape[0] for block in blocks)
    total, squares = 0.0, 0.0
    for block in blocks:
        away = block - pivot
        total = total + jnp.sum(away, axis=0, keepdims=True)
        squares = squares + jnp.sum(away * away, axis=0, keepdims=True)
    shift = total * (1.0 / cells)
    return jnp.concatenate([pivot + shift, squares - total * shift], axis=0)


def affine(stats, cells, scale, shift):
    devices, _, channels = stats.shape
    means, squares = stats[:, 0], stats[:, 1]
    mean = jnp.sum(means, axis=0, keepdims=True) * (1.0 / devices)
    away = means - mean
    square = jnp.sum(squares + cells * (away * away), axis=0, keepdims=True)
    count = cells * devices
    lane = lax.broadcasted_iota(jnp.int32, mean.shape, 1)
    step = 1
    while step < channels // GROUPS:

        def partner(values):
            up = pltpu.roll(values, channels - step, 1)
            return jnp.where((lane // step) % 2 == 0, up, pltpu.roll(values, step, 1))

        away = partner(mean) - mean
        square = square + partner(square) + (0.5 * count) * (away * away)
        mean = mean + 0.5 * away
        count, step = 2 * count, 2 * step
    slope = 0.5 * scale * lax.rsqrt(square * (1.0 / count) + epsilon)
    return slope, 0.5 * shift - mean * slope


def activate(values, slope, offset):
    half = values.astype(jnp.float32) * slope + offset
    return half + half * jnp.tanh(half)


def pair_conv(field, row, begin, frames, weight_ref):
    columns, channels = field.shape[2], field.shape[3]
    cells = frames * columns
    nothing = jnp.zeros((channels, channels), jnp.bfloat16)

    def piece(frame_tap, line):
        first = begin + frame_tap
        return field[first : first + frames, row + line].reshape(cells, channels)

    def dot(pieces, blocks):
        return jnp.dot(pieces, blocks, preferred_element_type=jnp.float32)

    taps = [(frame_tap, row_tap) for frame_tap in range(3) for row_tap in range(3)]
    early = dot(
        jnp.concatenate(
            [
                jnp.concatenate([piece(tap, out + row_tap) for tap, row_tap in taps], axis=1)
                for out in range(2)
            ],
            axis=0,
        ),
        jnp.concatenate(
            [
                jnp.concatenate([weight_ref[tap, row_tap, 0], weight_ref[tap, row_tap, 1]], axis=1)
                for tap, row_tap in taps
            ],
            axis=0,
        ),
    )
    lines = [(frame_tap, line) for frame_tap in range(3) for line in range(4)]
    late = dot(
        jnp.concatenate([piece(tap, line) for tap, line in lines], axis=1),
        jnp.concatenate(
            [
                jnp.concatenate(
                    [
                        weight_ref[tap, line - out, 2] if 0 <= line - out <= 2 else nothing
                        for out in range(2)
                    ],
                    axis=1,
                )
                for tap, line in lines
            ],
            axis=0,
        ),
    )
    column = lax.broadcasted_iota(jnp.int32, (cells, channels), 0) % columns
    results = []
    for out in range(2):
        left, centre = (
            early[out * cells : (out + 1) * cells, tap * channels : (tap + 1) * channels]
            for tap in range(2)
        )
        right = late[:, out * channels : (out + 1) * channels]
        left = jnp.where(column == 0, 0.0, pltpu.roll(left, 1, 0))
        right = jnp.where(column == columns - 1, 0.0, pltpu.roll(right, cells - 1, 0))
        results.append(left + centre + right)
    return results


def copy_kernel(sections, own_ref, second_cache_ref, first_cache_ref, copied, halo_ref, sems):
    last = lax.axis_index("section") == sections - 1
    frames = own_ref.shape[0]
    spare = SPAN_HALO - 2
    tail = pltpu.make_async_copy(own_ref.at[frames - SPAN_HALO :], halo_ref, sems.at[0])
    older = pltpu.make_async_copy(second_cache_ref, halo_ref.at[:spare], sems.at[1])
    newer = pltpu.make_async_copy(first_cache_ref, halo_ref.at[spare:], sems.at[2])
    load = pltpu.make_async_copy(own_ref, copied, sems.at[3])

    @pl.when(last)
    def _():
        older.start()
        newer.start()

    @pl.when(jnp.logical_not(last))
    def _():
        tail.start()

    load.start()

    @pl.when(last)
    def _():
        older.wait()
        newer.wait()

    @pl.when(jnp.logical_not(last))
    def _():
        tail.wait()

    load.wait()


def stats_kernel(own_ref, weight_ref, *rest):
    *vector_refs, stats_ref, vectors_ref, weight_copy, sems = rest
    loads = [pltpu.make_async_copy(weight_ref, weight_copy, sems.at[0])]
    loads += [
        pltpu.make_async_copy(vector_ref, vectors_ref.at[index], sems.at[1 + index])
        for index, vector_ref in enumerate(vector_refs)
    ]
    for load in loads:
        load.start()
    channels = own_ref.shape[-1]
    blocks = [own_ref[frame].astype(jnp.float32) for frame in range(own_ref.shape[0])]
    packed = moments([block.reshape(-1, channels) for block in blocks])
    for device in range(stats_ref.shape[0]):
        stats_ref[device] = packed
    for load in loads:
        load.wait()


def affine_kernel(row_count, cells, which, stats_ref, vectors_ref, affine_ref):
    section = lax.axis_index("section")
    scale, shift = vectors_ref[which], vectors_ref[which + 1]
    for index, span in enumerate((section, jnp.maximum(section - 1, 0))):
        stats = stats_ref[pl.ds(span * row_count, row_count)]
        slope, offset = affine(stats, cells, scale, shift)
        affine_ref[2 * index] = slope
        affine_ref[2 * index + 1] = offset


def first_kernel(
    row_count, own_ref, near_ref, far_ref, halo_ref, halo_near_ref, halo_far_ref, affine_ref,
    vectors_ref, weight_ref, middle_ref, sums_ref, field
):
    section, row_at = lax.axis_index("section"), lax.axis_index("rows")
    inner, lines, columns, channels = own_ref.shape
    slope, offset, slope_before, offset_before = (affine_ref[row] for row in range(4))
    even = row_at % 2 == 0
    at_start = section == 0

    def fill(line):
        side, local = divmod(line, lines)
        if side == 1:
            halo, body = halo_ref[:, local], own_ref[:, local]
        else:
            near_side = even if side == 2 else jnp.logical_not(even)
            halo = jnp.where(near_side, halo_near_ref[:, local], halo_far_ref[:, local])
            body = jnp.where(near_side, near_ref[:, local], far_ref[:, local])
        behind = activate(halo, slope_before, offset_before).astype(jnp.bfloat16)
        behind = jnp.where(at_start, halo, behind)
        ahead = activate(body, slope, offset).astype(jnp.bfloat16)
        if side != 1:
            outside = row_at == 0 if side == 0 else row_at == row_count - 1
            behind = jnp.where(outside, jnp.zeros_like(behind), behind)
            ahead = jnp.where(outside, jnp.zeros_like(ahead), ahead)
        field[:SPAN_HALO, line] = behind
        field[SPAN_HALO:, line] = ahead

    bias = vectors_ref[2]
    kept = []
    spare = SPAN_HALO - 2
    ready = 0
    for pair in range((lines + 2) // 2):
        for line in range(ready, 2 * pair + 4):
            fill(line)
        ready = 2 * pair + 4
        results = pair_conv(field, 2 * pair, 0, inner + 2, weight_ref)
        for out in range(2):
            line = 2 * pair + out
            rounded = (results[out] + bias).astype(jnp.bfloat16)
            rounded = rounded.reshape(inner + 2, columns, channels)
            middle_ref[:2, line] = jnp.where(at_start, field[:spare, line + lines - 1], rounded[:2])
            middle_ref[2:, line] = rounded[2:]
            if 1 <= line <= lines:
                kept.append(rounded[2:].astype(jnp.float32).reshape(-1, channels))
    packed = moments(kept)
    for device in range(sums_ref.shape[0]):
        sums_ref[device] = packed


def second_kernel(
    row_count, middle_ref, stats_ref, vectors_ref, weight_ref, own_ref, out_ref, field, ready,
    sems
):
    section, row_at = lax.axis_index("section"), lax.axis_index("rows")
    frames, lines, columns, channels = own_ref.shape
    cells = frames * lines * columns
    scale, shift = vectors_ref[3], vectors_ref[4]
    mine = stats_ref[pl.ds(section * row_count, row_count)]
    before = stats_ref[pl.ds(jnp.maximum(section - 1, 0) * row_count, row_count)]
    slope, offset = affine(mine, cells, scale, shift)
    slope_before, offset_before = affine(before, cells, scale, shift)
    at_start = section == 0
    half = frames // 2
    copies = []
    for begin in range(0, frames, half):
        filled = 0 if begin == 0 else begin + 2
        for line in range(lines + 2):
            ahead = middle_ref[filled : begin + half + 2, line]
            if begin == 0:
                behind = activate(ahead[:2], slope_before, offset_before).astype(jnp.bfloat16)
                behind = jnp.where(at_start, ahead[:2], behind)
                ahead = activate(ahead[2:], slope, offset).astype(jnp.bfloat16)
                ahead = jnp.concatenate([behind, ahead], axis=0)
            else:
                ahead = activate(ahead, slope, offset).astype(jnp.bfloat16)
            if line == 0 or line == lines + 1:
                outside = row_at == 0 if line == 0 else row_at == row_count - 1
                ahead = jnp.where(outside, jnp.zeros_like(ahead), ahead)
            field[filled : begin + half + 2, line] = ahead
        span = slice(begin, begin + half)
        for pair in range(lines // 2):
            results = pair_conv(field, 2 * pair, begin, half, weight_ref)
            for out in range(2):
                line = 2 * pair + out
                result = (results[out] + vectors_ref[5]).reshape(half, columns, channels)
                result = result + own_ref[span, line].astype(jnp.float32)
                ready[span, line] = result.astype(jnp.bfloat16)
        copy = pltpu.make_async_copy(
            ready.at[span], out_ref.at[span], sems.at[begin // half]
        )
        copy.start()
        copies.append(copy)
    for copy in copies:
        copy.wait()


def call(kernel, out_shape, scratch, operands, in_place=(), out_in_place=False, flops=0):
    vmem = pl.BlockSpec(memory_space=pltpu.VMEM)
    out_spec = pl.BlockSpec(memory_space=pltpu.HBM) if out_in_place else vmem
    specs = [vmem] * len(operands)
    for index in in_place:
        specs[index] = pl.BlockSpec(memory_space=pltpu.HBM)
    operands = [
        pltpu.with_memory_space_constraint(operand, pltpu.HBM) if index in in_place else operand
        for index, operand in enumerate(operands)
    ]
    return pl.pallas_call(
        kernel,
        out_shape=out_shape,
        in_specs=specs,
        out_specs=jax.tree.map(lambda _: out_spec, out_shape),
        scratch_shapes=scratch,
        compiler_params=pltpu.CompilerParams(vmem_limit_bytes=40 * 2**20),
        cost_estimate=pl.CostEstimate(flops=flops, bytes_accessed=2**20, transcendentals=0),
    )(*operands)


def on_device(
    activations,
    first_cache,
    second_cache,
    norm1_scale,
    norm1_shift,
    conv1_weight,
    conv1_bias,
    norm2_scale,
    norm2_shift,
    conv2_weight,
    conv2_bias,
):
    frames, lines, columns, channels = activations.shape
    sections, row_count = lax.axis_size("section"), lax.axis_size("rows")
    everyone = sections * row_count
    stats_shape = jax.ShapeDtypeStruct((everyone, 2, channels), jnp.float32)
    vectors = (norm1_scale, norm1_shift, conv1_bias, norm2_scale, norm2_shift, conv2_bias)

    near = [i ^ 1 for i in range(row_count)]
    far = [i + 2 if i % 2 == 0 else i - 2 for i in range(row_count)]
    far[row_count - 2], far[1] = row_count - 1, 0

    def across(block, partner):
        return lax.ppermute(block, "rows", list(enumerate(partner)))

    ring = [(at, (at + 1) % sections) for at in range(sections)]
    own, halo = call(
        functools.partial(copy_kernel, sections),
        (
            jax.ShapeDtypeStruct(activations.shape, jnp.bfloat16),
            jax.ShapeDtypeStruct((SPAN_HALO, lines, columns, channels), jnp.bfloat16),
        ),
        [pltpu.SemaphoreType.DMA((4,))],
        (activations, second_cache, first_cache),
        in_place=range(3),
    )
    sums, packed, weight = call(
        stats_kernel,
        (
            stats_shape,
            jax.ShapeDtypeStruct((len(vectors), 1, channels), jnp.float32),
            jax.ShapeDtypeStruct(conv1_weight.shape, jnp.bfloat16),
        ),
        [pltpu.SemaphoreType.DMA((1 + len(vectors),))],
        (own, conv1_weight) + tuple(vector.reshape(1, channels) for vector in vectors),
        in_place=range(1, 2 + len(vectors)),
    )
    received = lax.ppermute(halo, "section", ring)
    bodies = [own, across(own, near)]
    bodies.append(across(bodies[1], far))
    received, _ = lax.optimization_barrier((received, sums))
    halos = [received, across(received, near)]
    halos.append(across(halos[1], far))
    stats = lax.all_to_all(sums, ("section", "rows"), 0, 0, tiled=True)
    coefficients = call(
        functools.partial(affine_kernel, row_count, frames * lines * columns, 0),
        jax.ShapeDtypeStruct((4, 1, channels), jnp.float32),
        [],
        (stats, packed),
        flops=10**11,
    )
    middle, sums_two = call(
        functools.partial(first_kernel, row_count),
        (
            jax.ShapeDtypeStruct((frames + 2, lines + 2, columns, channels), jnp.bfloat16),
            stats_shape,
        ),
        [pltpu.VMEM((frames + SPAN_HALO, 3 * lines, columns, channels), jnp.bfloat16)],
        (*bodies, *halos, coefficients, packed, weight),
        flops=10**9,
    )
    stats_two = lax.all_to_all(sums_two, ("section", "rows"), 0, 0, tiled=True)
    return call(
        functools.partial(second_kernel, row_count),
        jax.ShapeDtypeStruct(activations.shape, jnp.bfloat16),
        [
            pltpu.VMEM((frames + 2, lines + 2, columns, channels), jnp.bfloat16),
            pltpu.VMEM(activations.shape, jnp.bfloat16),
            pltpu.SemaphoreType.DMA((2,)),
        ],
        (middle, stats_two, packed, conv2_weight, own),
        out_in_place=True,
        flops=10**9,
    )


def solution(mesh):
    in_specs = (
        P("section", "rows", None, None),
        P(None, "rows", None, None),
        P(None, "rows", None, None),
        P(),
        P(),
        P(),
        P(),
        P(),
        P(),
        P(),
        P(),
    )
    out_specs = P("section", "rows", None, None)
    return jax.shard_map(
        on_device, mesh=mesh, in_specs=in_specs, out_specs=out_specs, check_vma=False
    )
```

```python
import functools

import functools

import jax
import jax.numpy as jnp
from jax import lax
from jax.experimental import pallas as pl
from jax.experimental.pallas import tpu as pltpu
from jax.sharding import PartitionSpec as P

GROUPS = 32
SPAN_HALO = 4

epsilon = 1e-06


def moments(blocks):
    pivot = blocks[0][:1]
    cells = sum(block.shape[0] for block in blocks)
    total, squares = 0.0, 0.0
    for block in blocks:
        away = block - pivot
        total = total + jnp.sum(away, axis=0, keepdims=True)
        squares = squares + jnp.sum(away * away, axis=0, keepdims=True)
    shift = total * (1.0 / cells)
    return jnp.concatenate([pivot + shift, squares - total * shift], axis=0)


def affine(stats, cells, scale, shift):
    devices, _, channels = stats.shape
    means, squares = stats[:, 0], stats[:, 1]
    mean = jnp.sum(means, axis=0, keepdims=True) * (1.0 / devices)
    away = means - mean
    square = jnp.sum(squares + cells * (away * away), axis=0, keepdims=True)
    count = cells * devices
    lane = lax.broadcasted_iota(jnp.int32, mean.shape, 1)
    step = 1
    while step < channels // GROUPS:

        def partner(values):
            up = pltpu.roll(values, channels - step, 1)
            return jnp.where((lane // step) % 2 == 0, up, pltpu.roll(values, step, 1))

        away = partner(mean) - mean
        square = square + partner(square) + (0.5 * count) * (away * away)
        mean = mean + 0.5 * away
        count, step = 2 * count, 2 * step
    slope = 0.5 * scale * lax.rsqrt(square * (1.0 / count) + epsilon)
    return slope, 0.5 * shift - mean * slope


def activate(values, slope, offset):
    half = values.astype(jnp.float32) * slope + offset
    return half + half * jnp.tanh(half)


def pair_conv(field, row, begin, frames, weight_ref):
    columns, channels = field.shape[2], field.shape[3]
    cells = frames * columns
    nothing = jnp.zeros((channels, channels), jnp.bfloat16)

    def piece(frame_tap, line):
        first = begin + frame_tap
        return field[first : first + frames, row + line].reshape(cells, channels)

    def dot(pieces, blocks):
        return jnp.dot(pieces, blocks, preferred_element_type=jnp.float32)

    taps = [(frame_tap, row_tap) for frame_tap in range(3) for row_tap in range(3)]
    early = dot(
        jnp.concatenate(
            [
                jnp.concatenate([piece(tap, out + row_tap) for tap, row_tap in taps], axis=1)
                for out in range(2)
            ],
            axis=0,
        ),
        jnp.concatenate(
            [
                jnp.concatenate([weight_ref[tap, row_tap, 0], weight_ref[tap, row_tap, 1]], axis=1)
                for tap, row_tap in taps
            ],
            axis=0,
        ),
    )
    lines = [(frame_tap, line) for frame_tap in range(3) for line in range(4)]
    late = dot(
        jnp.concatenate([piece(tap, line) for tap, line in lines], axis=1),
        jnp.concatenate(
            [
                jnp.concatenate(
                    [
                        weight_ref[tap, line - out, 2] if 0 <= line - out <= 2 else nothing
                        for out in range(2)
                    ],
                    axis=1,
                )
                for tap, line in lines
            ],
            axis=0,
        ),
    )
    column = lax.broadcasted_iota(jnp.int32, (cells, channels), 0) % columns
    results = []
    for out in range(2):
        left, centre = (
            early[out * cells : (out + 1) * cells, tap * channels : (tap + 1) * channels]
            for tap in range(2)
        )
        right = late[:, out * channels : (out + 1) * channels]
        left = jnp.where(column == 0, 0.0, pltpu.roll(left, 1, 0))
        right = jnp.where(column == columns - 1, 0.0, pltpu.roll(right, cells - 1, 0))
        results.append(left + centre + right)
    return results


def copy_kernel(sections, own_ref, second_cache_ref, first_cache_ref, copied, halo_ref, sems):
    last = lax.axis_index("section") == sections - 1
    frames = own_ref.shape[0]
    spare = SPAN_HALO - 2
    tail = pltpu.make_async_copy(own_ref.at[frames - SPAN_HALO :], halo_ref, sems.at[0])
    older = pltpu.make_async_copy(second_cache_ref, halo_ref.at[:spare], sems.at[1])
    newer = pltpu.make_async_copy(first_cache_ref, halo_ref.at[spare:], sems.at[2])
    load = pltpu.make_async_copy(own_ref, copied, sems.at[3])

    @pl.when(last)
    def _():
        older.start()
        newer.start()

    @pl.when(jnp.logical_not(last))
    def _():
        tail.start()

    load.start()

    @pl.when(last)
    def _():
        older.wait()
        newer.wait()

    @pl.when(jnp.logical_not(last))
    def _():
        tail.wait()

    load.wait()


def stats_kernel(own_ref, weight_ref, *rest):
    *vector_refs, stats_ref, vectors_ref, weight_copy, sems = rest
    loads = [pltpu.make_async_copy(weight_ref, weight_copy, sems.at[0])]
    loads += [
        pltpu.make_async_copy(vector_ref, vectors_ref.at[index], sems.at[1 + index])
        for index, vector_ref in enumerate(vector_refs)
    ]
    for load in loads:
        load.start()
    channels = own_ref.shape[-1]
    blocks = [own_ref[frame].astype(jnp.float32) for frame in range(own_ref.shape[0])]
    stats_ref[0] = moments([block.reshape(-1, channels) for block in blocks])
    for load in loads:
        load.wait()


def first_kernel(
    row_count, own_ref, near_ref, far_ref, halo_ref, halo_near_ref, halo_far_ref, stats_ref,
    vectors_ref, weight_ref, middle_ref, sums_ref, field
):
    section, row_at = lax.axis_index("section"), lax.axis_index("rows")
    inner, lines, columns, channels = own_ref.shape
    cells = inner * lines * columns
    scale, shift = vectors_ref[0], vectors_ref[1]
    mine, before = stats_ref[:, :2], stats_ref[:, 2:]
    slope, offset = affine(mine, cells, scale, shift)
    slope_before, offset_before = affine(before, cells, scale, shift)
    even = row_at % 2 == 0
    at_start = section == 0

    def fill(line):
        side, local = divmod(line, lines)
        if side == 1:
            halo, body = halo_ref[:, local], own_ref[:, local]
        else:
            near_side = even if side == 2 else jnp.logical_not(even)
            halo = jnp.where(near_side, halo_near_ref[:, local], halo_far_ref[:, local])
            body = jnp.where(near_side, near_ref[:, local], far_ref[:, local])
        behind = activate(halo, slope_before, offset_before).astype(jnp.bfloat16)
        behind = jnp.where(at_start, halo, behind)
        ahead = activate(body, slope, offset).astype(jnp.bfloat16)
        if side != 1:
            outside = row_at == 0 if side == 0 else row_at == row_count - 1
            behind = jnp.where(outside, jnp.zeros_like(behind), behind)
            ahead = jnp.where(outside, jnp.zeros_like(ahead), ahead)
        field[:SPAN_HALO, line] = behind
        field[SPAN_HALO:, line] = ahead

    bias = vectors_ref[2]
    kept = []
    spare = SPAN_HALO - 2
    ready = 0
    for pair in range((lines + 2) // 2):
        for line in range(ready, 2 * pair + 4):
            fill(line)
        ready = 2 * pair + 4
        results = pair_conv(field, 2 * pair, 0, inner + 2, weight_ref)
        for out in range(2):
            line = 2 * pair + out
            rounded = (results[out] + bias).astype(jnp.bfloat16)
            rounded = rounded.reshape(inner + 2, columns, channels)
            middle_ref[:2, line] = jnp.where(at_start, field[:spare, line + lines - 1], rounded[:2])
            middle_ref[2:, line] = rounded[2:]
            if 1 <= line <= lines:
                kept.append(rounded[2:].astype(jnp.float32).reshape(-1, channels))
    packed = moments(kept)
    for device in range(sums_ref.shape[0]):
        sums_ref[device] = packed


def second_kernel(
    row_count, middle_ref, stats_ref, vectors_ref, weight_ref, own_ref, out_ref, field, ready,
    sems
):
    section, row_at = lax.axis_index("section"), lax.axis_index("rows")
    frames, lines, columns, channels = own_ref.shape
    cells = frames * lines * columns
    scale, shift = vectors_ref[3], vectors_ref[4]
    mine = stats_ref[pl.ds(section * row_count, row_count)]
    before = stats_ref[pl.ds(jnp.maximum(section - 1, 0) * row_count, row_count)]
    slope, offset = affine(mine, cells, scale, shift)
    slope_before, offset_before = affine(before, cells, scale, shift)
    at_start = section == 0
    half = frames // 2
    copies = []
    for begin in range(0, frames, half):
        filled = 0 if begin == 0 else begin + 2
        for line in range(lines + 2):
            ahead = middle_ref[filled : begin + half + 2, line]
            if begin == 0:
                behind = activate(ahead[:2], slope_before, offset_before).astype(jnp.bfloat16)
                behind = jnp.where(at_start, ahead[:2], behind)
                ahead = activate(ahead[2:], slope, offset).astype(jnp.bfloat16)
                ahead = jnp.concatenate([behind, ahead], axis=0)
            else:
                ahead = activate(ahead, slope, offset).astype(jnp.bfloat16)
            if line == 0 or line == lines + 1:
                outside = row_at == 0 if line == 0 else row_at == row_count - 1
                ahead = jnp.where(outside, jnp.zeros_like(ahead), ahead)
            field[filled : begin + half + 2, line] = ahead
        span = slice(begin, begin + half)
        for pair in range(lines // 2):
            results = pair_conv(field, 2 * pair, begin, half, weight_ref)
            for out in range(2):
                line = 2 * pair + out
                result = (results[out] + vectors_ref[5]).reshape(half, columns, channels)
                result = result + own_ref[span, line].astype(jnp.float32)
                ready[span, line] = result.astype(jnp.bfloat16)
        copy = pltpu.make_async_copy(
            ready.at[span], out_ref.at[span], sems.at[begin // half]
        )
        copy.start()
        copies.append(copy)
    for copy in copies:
        copy.wait()


def call(kernel, out_shape, scratch, operands, in_place=(), out_in_place=False, flops=0):
    vmem = pl.BlockSpec(memory_space=pltpu.VMEM)
    out_spec = pl.BlockSpec(memory_space=pltpu.HBM) if out_in_place else vmem
    specs = [vmem] * len(operands)
    for index in in_place:
        specs[index] = pl.BlockSpec(memory_space=pltpu.HBM)
    operands = [
        pltpu.with_memory_space_constraint(operand, pltpu.HBM) if index in in_place else operand
        for index, operand in enumerate(operands)
    ]
    return pl.pallas_call(
        kernel,
        out_shape=out_shape,
        in_specs=specs,
        out_specs=jax.tree.map(lambda _: out_spec, out_shape),
        scratch_shapes=scratch,
        compiler_params=pltpu.CompilerParams(vmem_limit_bytes=40 * 2**20),
        cost_estimate=pl.CostEstimate(flops=flops, bytes_accessed=2**20, transcendentals=0),
    )(*operands)


def on_device(
    activations,
    first_cache,
    second_cache,
    norm1_scale,
    norm1_shift,
    conv1_weight,
    conv1_bias,
    norm2_scale,
    norm2_shift,
    conv2_weight,
    conv2_bias,
):
    frames, lines, columns, channels = activations.shape
    sections, row_count = lax.axis_size("section"), lax.axis_size("rows")
    everyone = sections * row_count
    stats_shape = jax.ShapeDtypeStruct((everyone, 2, channels), jnp.float32)
    vectors = (norm1_scale, norm1_shift, conv1_bias, norm2_scale, norm2_shift, conv2_bias)

    near = [i ^ 1 for i in range(row_count)]
    far = [i + 2 if i % 2 == 0 else i - 2 for i in range(row_count)]
    far[row_count - 2], far[1] = row_count - 1, 0

    def across(block, partner):
        return lax.ppermute(block, "rows", list(enumerate(partner)))

    ring = [(at, (at + 1) % sections) for at in range(sections)]
    own, halo = call(
        functools.partial(copy_kernel, sections),
        (
            jax.ShapeDtypeStruct(activations.shape, jnp.bfloat16),
            jax.ShapeDtypeStruct((SPAN_HALO, lines, columns, channels), jnp.bfloat16),
        ),
        [pltpu.SemaphoreType.DMA((4,))],
        (activations, second_cache, first_cache),
        in_place=range(3),
    )
    sums, packed, weight = call(
        stats_kernel,
        (
            jax.ShapeDtypeStruct((1, 2, channels), jnp.float32),
            jax.ShapeDtypeStruct((len(vectors), 1, channels), jnp.float32),
            jax.ShapeDtypeStruct(conv1_weight.shape, jnp.bfloat16),
        ),
        [pltpu.SemaphoreType.DMA((1 + len(vectors),))],
        (own, conv1_weight) + tuple(vector.reshape(1, channels) for vector in vectors),
        in_place=range(1, 2 + len(vectors)),
    )
    received = lax.ppermute(halo, "section", ring)
    bodies = [own, across(own, near)]
    bodies.append(across(bodies[1], far))
    passed = lax.ppermute(sums, "section", ring)
    received, _ = lax.optimization_barrier((received, sums))
    halos = [received, across(received, near)]
    halos.append(across(halos[1], far))
    both = jnp.concatenate([sums, passed], axis=1)
    both = jnp.broadcast_to(both, (row_count,) + both.shape[1:])
    stats = lax.all_to_all(both, "rows", 0, 0, tiled=True)
    middle, sums_two = call(
        functools.partial(first_kernel, row_count),
        (
            jax.ShapeDtypeStruct((frames + 2, lines + 2, columns, channels), jnp.bfloat16),
            stats_shape,
        ),
        [pltpu.VMEM((frames + SPAN_HALO, 3 * lines, columns, channels), jnp.bfloat16)],
        (*bodies, *halos, stats, packed, weight),
        flops=10**9,
    )
    stats_two = lax.all_to_all(sums_two, ("section", "rows"), 0, 0, tiled=True)
    return call(
        functools.partial(second_kernel, row_count),
        jax.ShapeDtypeStruct(activations.shape, jnp.bfloat16),
        [
            pltpu.VMEM((frames + 2, lines + 2, columns, channels), jnp.bfloat16),
            pltpu.VMEM(activations.shape, jnp.bfloat16),
            pltpu.SemaphoreType.DMA((2,)),
        ],
        (middle, stats_two, packed, conv2_weight, own),
        out_in_place=True,
        flops=10**9,
    )


def solution(mesh):
    in_specs = (
        P("section", "rows", None, None),
        P(None, "rows", None, None),
        P(None, "rows", None, None),
        P(),
        P(),
        P(),
        P(),
        P(),
        P(),
        P(),
        P(),
    )
    out_specs = P("section", "rows", None, None)
    return jax.shard_map(
        on_device, mesh=mesh, in_specs=in_specs, out_specs=out_specs, check_vma=False
    )
```

```python
import functools

import functools

import jax
import jax.numpy as jnp
from jax import lax
from jax.experimental import pallas as pl
from jax.experimental.pallas import tpu as pltpu
from jax.sharding import PartitionSpec as P

GROUPS = 32
SPAN_HALO = 4

epsilon = 1e-06


def moments(blocks):
    pivot = blocks[0][:1]
    cells = sum(block.shape[0] for block in blocks)
    total, squares = 0.0, 0.0
    for block in blocks:
        away = block - pivot
        total = total + jnp.sum(away, axis=0, keepdims=True)
        squares = squares + jnp.sum(away * away, axis=0, keepdims=True)
    shift = total * (1.0 / cells)
    return jnp.concatenate([pivot + shift, squares - total * shift], axis=0)


def affine(stats, cells, scale, shift):
    devices, _, channels = stats.shape
    means, squares = stats[:, 0], stats[:, 1]
    mean = jnp.sum(means, axis=0, keepdims=True) * (1.0 / devices)
    away = means - mean
    square = jnp.sum(squares + cells * (away * away), axis=0, keepdims=True)
    count = cells * devices
    lane = lax.broadcasted_iota(jnp.int32, mean.shape, 1)
    step = 1
    while step < channels // GROUPS:

        def partner(values):
            up = pltpu.roll(values, channels - step, 1)
            return jnp.where((lane // step) % 2 == 0, up, pltpu.roll(values, step, 1))

        away = partner(mean) - mean
        square = square + partner(square) + (0.5 * count) * (away * away)
        mean = mean + 0.5 * away
        count, step = 2 * count, 2 * step
    slope = 0.5 * scale * lax.rsqrt(square * (1.0 / count) + epsilon)
    return slope, 0.5 * shift - mean * slope


def activate(values, slope, offset):
    half = values.astype(jnp.float32) * slope + offset
    return half + half * jnp.tanh(half)


def pair_conv(field, row, begin, frames, weight_ref):
    columns, channels = field.shape[2], field.shape[3]
    cells = frames * columns
    nothing = jnp.zeros((channels, channels), jnp.bfloat16)

    def piece(frame_tap, line):
        first = begin + frame_tap
        return field[first : first + frames, row + line].reshape(cells, channels)

    def dot(pieces, blocks):
        return jnp.dot(pieces, blocks, preferred_element_type=jnp.float32)

    taps = [(frame_tap, row_tap) for frame_tap in range(3) for row_tap in range(3)]
    early = dot(
        jnp.concatenate(
            [
                jnp.concatenate([piece(tap, out + row_tap) for tap, row_tap in taps], axis=1)
                for out in range(2)
            ],
            axis=0,
        ),
        jnp.concatenate(
            [
                jnp.concatenate([weight_ref[tap, row_tap, 0], weight_ref[tap, row_tap, 1]], axis=1)
                for tap, row_tap in taps
            ],
            axis=0,
        ),
    )
    lines = [(frame_tap, line) for frame_tap in range(3) for line in range(4)]
    late = dot(
        jnp.concatenate([piece(tap, line) for tap, line in lines], axis=1),
        jnp.concatenate(
            [
                jnp.concatenate(
                    [
                        weight_ref[tap, line - out, 2] if 0 <= line - out <= 2 else nothing
                        for out in range(2)
                    ],
                    axis=1,
                )
                for tap, line in lines
            ],
            axis=0,
        ),
    )
    column = lax.broadcasted_iota(jnp.int32, (cells, channels), 0) % columns
    results = []
    for out in range(2):
        left, centre = (
            early[out * cells : (out + 1) * cells, tap * channels : (tap + 1) * channels]
            for tap in range(2)
        )
        right = late[:, out * channels : (out + 1) * channels]
        left = jnp.where(column == 0, 0.0, pltpu.roll(left, 1, 0))
        right = jnp.where(column == columns - 1, 0.0, pltpu.roll(right, cells - 1, 0))
        results.append(left + centre + right)
    return results


def copy_kernel(sections, own_ref, second_cache_ref, first_cache_ref, copied, halo_ref, sems):
    last = lax.axis_index("section") == sections - 1
    frames = own_ref.shape[0]
    spare = SPAN_HALO - 2
    tail = pltpu.make_async_copy(own_ref.at[frames - SPAN_HALO :], halo_ref, sems.at[0])
    older = pltpu.make_async_copy(second_cache_ref, halo_ref.at[:spare], sems.at[1])
    newer = pltpu.make_async_copy(first_cache_ref, halo_ref.at[spare:], sems.at[2])
    load = pltpu.make_async_copy(own_ref, copied, sems.at[3])

    @pl.when(last)
    def _():
        older.start()
        newer.start()

    @pl.when(jnp.logical_not(last))
    def _():
        tail.start()

    load.start()

    @pl.when(last)
    def _():
        older.wait()
        newer.wait()

    @pl.when(jnp.logical_not(last))
    def _():
        tail.wait()

    load.wait()


def stats_kernel(own_ref, weight_ref, *rest):
    *vector_refs, stats_ref, vectors_ref, weight_copy, sems = rest
    loads = [pltpu.make_async_copy(weight_ref, weight_copy, sems.at[0])]
    loads += [
        pltpu.make_async_copy(vector_ref, vectors_ref.at[index], sems.at[1 + index])
        for index, vector_ref in enumerate(vector_refs)
    ]
    for load in loads:
        load.start()
    channels = own_ref.shape[-1]
    blocks = [own_ref[frame].astype(jnp.float32) for frame in range(own_ref.shape[0])]
    stats_ref[0] = moments([block.reshape(-1, channels) for block in blocks])
    for load in loads:
        load.wait()


def first_kernel(
    row_count, own_ref, far_ref, near_ref, stats_ref, vectors_ref, weight_ref, middle_ref,
    sums_ref, field
):
    section, row_at = lax.axis_index("section"), lax.axis_index("rows")
    frames, lines, columns, channels = own_ref.shape
    inner = frames - SPAN_HALO
    cells = inner * lines * columns
    scale, shift = vectors_ref[0], vectors_ref[1]
    mine, before = stats_ref[:, :2], stats_ref[:, 2:]
    slope, offset = affine(mine, cells, scale, shift)
    slope_before, offset_before = affine(before, cells, scale, shift)
    even = row_at % 2 == 0
    at_start = section == 0

    def fill(line):
        side, local = divmod(line, lines)
        if side == 1:
            block = own_ref[:, local]
        else:
            near_side = even if side == 2 else jnp.logical_not(even)
            block = jnp.where(near_side, near_ref[:, local], far_ref[:, local])
        halo, body = block[:SPAN_HALO], block[SPAN_HALO:]
        behind = activate(halo, slope_before, offset_before).astype(jnp.bfloat16)
        behind = jnp.where(at_start, halo, behind)
        ahead = activate(body, slope, offset).astype(jnp.bfloat16)
        if side != 1:
            outside = row_at == 0 if side == 0 else row_at == row_count - 1
            behind = jnp.where(outside, jnp.zeros_like(behind), behind)
            ahead = jnp.where(outside, jnp.zeros_like(ahead), ahead)
        field[:SPAN_HALO, line] = behind
        field[SPAN_HALO:, line] = ahead

    bias = vectors_ref[2]
    kept = []
    spare = SPAN_HALO - 2
    ready = 0
    for pair in range((lines + 2) // 2):
        for line in range(ready, 2 * pair + 4):
            fill(line)
        ready = 2 * pair + 4
        results = pair_conv(field, 2 * pair, 0, inner + 2, weight_ref)
        for out in range(2):
            line = 2 * pair + out
            rounded = (results[out] + bias).astype(jnp.bfloat16)
            rounded = rounded.reshape(inner + 2, columns, channels)
            middle_ref[:2, line] = jnp.where(at_start, field[:spare, line + lines - 1], rounded[:2])
            middle_ref[2:, line] = rounded[2:]
            if 1 <= line <= lines:
                kept.append(rounded[2:].astype(jnp.float32).reshape(-1, channels))
    packed = moments(kept)
    for device in range(sums_ref.shape[0]):
        sums_ref[device] = packed


def second_kernel(
    row_count, middle_ref, stats_ref, vectors_ref, weight_ref, own_ref, out_ref, field, ready,
    sems
):
    section, row_at = lax.axis_index("section"), lax.axis_index("rows")
    frames, lines, columns, channels = own_ref.shape
    cells = frames * lines * columns
    scale, shift = vectors_ref[3], vectors_ref[4]
    mine = stats_ref[pl.ds(section * row_count, row_count)]
    before = stats_ref[pl.ds(jnp.maximum(section - 1, 0) * row_count, row_count)]
    slope, offset = affine(mine, cells, scale, shift)
    slope_before, offset_before = affine(before, cells, scale, shift)
    at_start = section == 0
    half = frames // 2
    copies = []
    for begin in range(0, frames, half):
        filled = 0 if begin == 0 else begin + 2
        for line in range(lines + 2):
            ahead = middle_ref[filled : begin + half + 2, line]
            if begin == 0:
                behind = activate(ahead[:2], slope_before, offset_before).astype(jnp.bfloat16)
                behind = jnp.where(at_start, ahead[:2], behind)
                ahead = activate(ahead[2:], slope, offset).astype(jnp.bfloat16)
                ahead = jnp.concatenate([behind, ahead], axis=0)
            else:
                ahead = activate(ahead, slope, offset).astype(jnp.bfloat16)
            if line == 0 or line == lines + 1:
                outside = row_at == 0 if line == 0 else row_at == row_count - 1
                ahead = jnp.where(outside, jnp.zeros_like(ahead), ahead)
            field[filled : begin + half + 2, line] = ahead
        span = slice(begin, begin + half)
        for pair in range(lines // 2):
            results = pair_conv(field, 2 * pair, begin, half, weight_ref)
            for out in range(2):
                line = 2 * pair + out
                result = (results[out] + vectors_ref[5]).reshape(half, columns, channels)
                result = result + own_ref[span, line].astype(jnp.float32)
                ready[span, line] = result.astype(jnp.bfloat16)
        copy = pltpu.make_async_copy(
            ready.at[span], out_ref.at[span], sems.at[begin // half]
        )
        copy.start()
        copies.append(copy)
    for copy in copies:
        copy.wait()


def call(kernel, out_shape, scratch, operands, in_place=(), out_in_place=False, flops=0):
    vmem = pl.BlockSpec(memory_space=pltpu.VMEM)
    out_spec = pl.BlockSpec(memory_space=pltpu.HBM) if out_in_place else vmem
    specs = [vmem] * len(operands)
    for index in in_place:
        specs[index] = pl.BlockSpec(memory_space=pltpu.HBM)
    operands = [
        pltpu.with_memory_space_constraint(operand, pltpu.HBM) if index in in_place else operand
        for index, operand in enumerate(operands)
    ]
    return pl.pallas_call(
        kernel,
        out_shape=out_shape,
        in_specs=specs,
        out_specs=jax.tree.map(lambda _: out_spec, out_shape),
        scratch_shapes=scratch,
        compiler_params=pltpu.CompilerParams(vmem_limit_bytes=40 * 2**20),
        cost_estimate=pl.CostEstimate(flops=flops, bytes_accessed=2**20, transcendentals=0),
    )(*operands)


def on_device(
    activations,
    first_cache,
    second_cache,
    norm1_scale,
    norm1_shift,
    conv1_weight,
    conv1_bias,
    norm2_scale,
    norm2_shift,
    conv2_weight,
    conv2_bias,
):
    frames, lines, columns, channels = activations.shape
    sections, row_count = lax.axis_size("section"), lax.axis_size("rows")
    everyone = sections * row_count
    stats_shape = jax.ShapeDtypeStruct((everyone, 2, channels), jnp.float32)
    vectors = (norm1_scale, norm1_shift, conv1_bias, norm2_scale, norm2_shift, conv2_bias)

    near = [i ^ 1 for i in range(row_count)]
    far = [0] + [i + 1 if i % 2 else i - 1 for i in range(1, row_count - 1)] + [row_count - 1]

    def across(block, partner):
        return lax.ppermute(block, "rows", list(enumerate(partner)))

    ring = [(at, (at + 1) % sections) for at in range(sections)]
    own, halo = call(
        functools.partial(copy_kernel, sections),
        (
            jax.ShapeDtypeStruct(activations.shape, jnp.bfloat16),
            jax.ShapeDtypeStruct((SPAN_HALO, lines, columns, channels), jnp.bfloat16),
        ),
        [pltpu.SemaphoreType.DMA((4,))],
        (activations, second_cache, first_cache),
        in_place=range(3),
    )
    sums, packed, weight = call(
        stats_kernel,
        (
            jax.ShapeDtypeStruct((1, 2, channels), jnp.float32),
            jax.ShapeDtypeStruct((len(vectors), 1, channels), jnp.float32),
            jax.ShapeDtypeStruct(conv1_weight.shape, jnp.bfloat16),
        ),
        [pltpu.SemaphoreType.DMA((1 + len(vectors),))],
        (own, conv1_weight) + tuple(vector.reshape(1, channels) for vector in vectors),
        in_place=range(1, 2 + len(vectors)),
    )
    received = lax.ppermute(halo, "section", ring)
    passed = lax.ppermute(sums, "section", ring)
    received, _ = lax.optimization_barrier((received, sums))
    joined = jnp.concatenate([received, own], axis=0)
    from_far = across(joined, far)
    from_near = across(joined, near)
    both = jnp.concatenate([sums, passed], axis=1)
    both = jnp.broadcast_to(both, (row_count,) + both.shape[1:])
    stats = lax.all_to_all(both, "rows", 0, 0, tiled=True)
    middle, sums_two = call(
        functools.partial(first_kernel, row_count),
        (
            jax.ShapeDtypeStruct((frames + 2, lines + 2, columns, channels), jnp.bfloat16),
            stats_shape,
        ),
        [pltpu.VMEM((frames + SPAN_HALO, 3 * lines, columns, channels), jnp.bfloat16)],
        (joined, from_far, from_near, stats, packed, weight),
        flops=10**9,
    )
    stats_two = lax.all_to_all(sums_two, ("section", "rows"), 0, 0, tiled=True)
    return call(
        functools.partial(second_kernel, row_count),
        jax.ShapeDtypeStruct(activations.shape, jnp.bfloat16),
        [
            pltpu.VMEM((frames + 2, lines + 2, columns, channels), jnp.bfloat16),
            pltpu.VMEM(activations.shape, jnp.bfloat16),
            pltpu.SemaphoreType.DMA((2,)),
        ],
        (middle, stats_two, packed, conv2_weight, own),
        out_in_place=True,
        flops=10**9,
    )


def solution(mesh):
    in_specs = (
        P("section", "rows", None, None),
        P(None, "rows", None, None),
        P(None, "rows", None, None),
        P(),
        P(),
        P(),
        P(),
        P(),
        P(),
        P(),
        P(),
    )
    out_specs = P("section", "rows", None, None)
    return jax.shard_map(
        on_device, mesh=mesh, in_specs=in_specs, out_specs=out_specs, check_vma=False
    )
```

```python
import functools

import functools

import jax
import jax.numpy as jnp
from jax import lax
from jax.experimental import pallas as pl
from jax.experimental.pallas import tpu as pltpu
from jax.sharding import PartitionSpec as P

GROUPS = 32
SPAN_HALO = 4

epsilon = 1e-06


def moments(blocks):
    pivot = blocks[0][:1]
    cells = sum(block.shape[0] for block in blocks)
    total, squares = 0.0, 0.0
    for block in blocks:
        away = block - pivot
        total = total + jnp.sum(away, axis=0, keepdims=True)
        squares = squares + jnp.sum(away * away, axis=0, keepdims=True)
    shift = total * (1.0 / cells)
    return jnp.concatenate([pivot + shift, squares - total * shift], axis=0)


def affine(stats, cells, scale, shift):
    devices, _, channels = stats.shape
    means, squares = stats[:, 0], stats[:, 1]
    mean = jnp.sum(means, axis=0, keepdims=True) * (1.0 / devices)
    away = means - mean
    square = jnp.sum(squares + cells * (away * away), axis=0, keepdims=True)
    count = cells * devices
    lane = lax.broadcasted_iota(jnp.int32, mean.shape, 1)
    step = 1
    while step < channels // GROUPS:

        def partner(values):
            up = pltpu.roll(values, channels - step, 1)
            return jnp.where((lane // step) % 2 == 0, up, pltpu.roll(values, step, 1))

        away = partner(mean) - mean
        square = square + partner(square) + (0.5 * count) * (away * away)
        mean = mean + 0.5 * away
        count, step = 2 * count, 2 * step
    slope = 0.5 * scale * lax.rsqrt(square * (1.0 / count) + epsilon)
    return slope, 0.5 * shift - mean * slope


def activate(values, slope, offset):
    half = values.astype(jnp.float32) * slope + offset
    return half + half * jnp.tanh(half)


def pair_conv(field, row, begin, frames, weight_ref):
    columns, channels = field.shape[2], field.shape[3]
    cells = frames * columns
    nothing = jnp.zeros((channels, channels), jnp.bfloat16)

    def piece(frame_tap, line):
        first = begin + frame_tap
        return field[first : first + frames, row + line].reshape(cells, channels)

    def dot(pieces, blocks):
        return jnp.dot(pieces, blocks, preferred_element_type=jnp.float32)

    taps = [(frame_tap, row_tap) for frame_tap in range(3) for row_tap in range(3)]
    early = dot(
        jnp.concatenate(
            [
                jnp.concatenate([piece(tap, out + row_tap) for tap, row_tap in taps], axis=1)
                for out in range(2)
            ],
            axis=0,
        ),
        jnp.concatenate(
            [
                jnp.concatenate([weight_ref[tap, row_tap, 0], weight_ref[tap, row_tap, 1]], axis=1)
                for tap, row_tap in taps
            ],
            axis=0,
        ),
    )
    lines = [(frame_tap, line) for frame_tap in range(3) for line in range(4)]
    late = dot(
        jnp.concatenate([piece(tap, line) for tap, line in lines], axis=1),
        jnp.concatenate(
            [
                jnp.concatenate(
                    [
                        weight_ref[tap, line - out, 2] if 0 <= line - out <= 2 else nothing
                        for out in range(2)
                    ],
                    axis=1,
                )
                for tap, line in lines
            ],
            axis=0,
        ),
    )
    column = lax.broadcasted_iota(jnp.int32, (cells, channels), 0) % columns
    results = []
    for out in range(2):
        left, centre = (
            early[out * cells : (out + 1) * cells, tap * channels : (tap + 1) * channels]
            for tap in range(2)
        )
        right = late[:, out * channels : (out + 1) * channels]
        left = jnp.where(column == 0, 0.0, pltpu.roll(left, 1, 0))
        right = jnp.where(column == columns - 1, 0.0, pltpu.roll(right, cells - 1, 0))
        results.append(left + centre + right)
    return results


def copy_kernel(sections, own_ref, second_cache_ref, first_cache_ref, copied, halo_ref, sems):
    last = lax.axis_index("section") == sections - 1
    frames = own_ref.shape[0]
    spare = SPAN_HALO - 2
    tail = pltpu.make_async_copy(own_ref.at[frames - SPAN_HALO :], halo_ref, sems.at[0])
    older = pltpu.make_async_copy(second_cache_ref, halo_ref.at[:spare], sems.at[1])
    newer = pltpu.make_async_copy(first_cache_ref, halo_ref.at[spare:], sems.at[2])
    load = pltpu.make_async_copy(own_ref, copied, sems.at[3])

    @pl.when(last)
    def _():
        older.start()
        newer.start()

    @pl.when(jnp.logical_not(last))
    def _():
        tail.start()

    load.start()

    @pl.when(last)
    def _():
        older.wait()
        newer.wait()

    @pl.when(jnp.logical_not(last))
    def _():
        tail.wait()

    load.wait()


def stats_kernel(own_ref, weight_ref, *rest):
    *vector_refs, stats_ref, vectors_ref, weight_copy, sems = rest
    loads = [pltpu.make_async_copy(weight_ref, weight_copy, sems.at[0])]
    loads += [
        pltpu.make_async_copy(vector_ref, vectors_ref.at[index], sems.at[1 + index])
        for index, vector_ref in enumerate(vector_refs)
    ]
    for load in loads:
        load.start()
    channels = own_ref.shape[-1]
    blocks = [own_ref[frame].astype(jnp.float32) for frame in range(own_ref.shape[0])]
    stats_ref[0] = moments([block.reshape(-1, channels) for block in blocks])
    for load in loads:
        load.wait()


def first_kernel(
    row_count, own_ref, near_ref, far_ref, halo_ref, halo_far_ref, halo_near_ref, stats_ref,
    vectors_ref, weight_ref, middle_ref, sums_ref, field
):
    section, row_at = lax.axis_index("section"), lax.axis_index("rows")
    inner, lines, columns, channels = own_ref.shape
    cells = inner * lines * columns
    scale, shift = vectors_ref[0], vectors_ref[1]
    mine, before = stats_ref[:, :2], stats_ref[:, 2:]
    slope, offset = affine(mine, cells, scale, shift)
    slope_before, offset_before = affine(before, cells, scale, shift)
    even = row_at % 2 == 0
    at_start = section == 0

    def fill(line):
        side, local = divmod(line, lines)
        if side == 1:
            halo, body = halo_ref[:, local], own_ref[:, local]
        else:
            near_side = even if side == 2 else jnp.logical_not(even)
            halo = jnp.where(near_side, halo_near_ref[:, local], halo_far_ref[:, local])
            body = jnp.where(near_side, near_ref[:, local], far_ref[:, local])
        behind = activate(halo, slope_before, offset_before).astype(jnp.bfloat16)
        behind = jnp.where(at_start, halo, behind)
        ahead = activate(body, slope, offset).astype(jnp.bfloat16)
        if side != 1:
            outside = row_at == 0 if side == 0 else row_at == row_count - 1
            behind = jnp.where(outside, jnp.zeros_like(behind), behind)
            ahead = jnp.where(outside, jnp.zeros_like(ahead), ahead)
        field[:SPAN_HALO, line] = behind
        field[SPAN_HALO:, line] = ahead

    bias = vectors_ref[2]
    kept = []
    spare = SPAN_HALO - 2
    ready = 0
    for pair in range((lines + 2) // 2):
        for line in range(ready, 2 * pair + 4):
            fill(line)
        ready = 2 * pair + 4
        results = pair_conv(field, 2 * pair, 0, inner + 2, weight_ref)
        for out in range(2):
            line = 2 * pair + out
            rounded = (results[out] + bias).astype(jnp.bfloat16)
            rounded = rounded.reshape(inner + 2, columns, channels)
            middle_ref[:2, line] = jnp.where(at_start, field[:spare, line + lines - 1], rounded[:2])
            middle_ref[2:, line] = rounded[2:]
            if 1 <= line <= lines:
                kept.append(rounded[2:].astype(jnp.float32).reshape(-1, channels))
    packed = moments(kept)
    for device in range(sums_ref.shape[0]):
        sums_ref[device] = packed


def second_kernel(
    row_count, middle_ref, stats_ref, vectors_ref, weight_ref, own_ref, out_ref, field, ready,
    sems
):
    section, row_at = lax.axis_index("section"), lax.axis_index("rows")
    frames, lines, columns, channels = own_ref.shape
    cells = frames * lines * columns
    scale, shift = vectors_ref[3], vectors_ref[4]
    mine = stats_ref[pl.ds(section * row_count, row_count)]
    before = stats_ref[pl.ds(jnp.maximum(section - 1, 0) * row_count, row_count)]
    slope, offset = affine(mine, cells, scale, shift)
    slope_before, offset_before = affine(before, cells, scale, shift)
    at_start = section == 0
    half = frames // 2
    copies = []
    for begin in range(0, frames, half):
        filled = 0 if begin == 0 else begin + 2
        for line in range(lines + 2):
            ahead = middle_ref[filled : begin + half + 2, line]
            if begin == 0:
                behind = activate(ahead[:2], slope_before, offset_before).astype(jnp.bfloat16)
                behind = jnp.where(at_start, ahead[:2], behind)
                ahead = activate(ahead[2:], slope, offset).astype(jnp.bfloat16)
                ahead = jnp.concatenate([behind, ahead], axis=0)
            else:
                ahead = activate(ahead, slope, offset).astype(jnp.bfloat16)
            if line == 0 or line == lines + 1:
                outside = row_at == 0 if line == 0 else row_at == row_count - 1
                ahead = jnp.where(outside, jnp.zeros_like(ahead), ahead)
            field[filled : begin + half + 2, line] = ahead
        span = slice(begin, begin + half)
        for pair in range(lines // 2):
            results = pair_conv(field, 2 * pair, begin, half, weight_ref)
            for out in range(2):
                line = 2 * pair + out
                result = (results[out] + vectors_ref[5]).reshape(half, columns, channels)
                result = result + own_ref[span, line].astype(jnp.float32)
                ready[span, line] = result.astype(jnp.bfloat16)
        copy = pltpu.make_async_copy(
            ready.at[span], out_ref.at[span], sems.at[begin // half]
        )
        copy.start()
        copies.append(copy)
    for copy in copies:
        copy.wait()


def call(kernel, out_shape, scratch, operands, in_place=(), out_in_place=False, flops=0):
    vmem = pl.BlockSpec(memory_space=pltpu.VMEM)
    out_spec = pl.BlockSpec(memory_space=pltpu.HBM) if out_in_place else vmem
    specs = [vmem] * len(operands)
    for index in in_place:
        specs[index] = pl.BlockSpec(memory_space=pltpu.HBM)
    operands = [
        pltpu.with_memory_space_constraint(operand, pltpu.HBM) if index in in_place else operand
        for index, operand in enumerate(operands)
    ]
    return pl.pallas_call(
        kernel,
        out_shape=out_shape,
        in_specs=specs,
        out_specs=jax.tree.map(lambda _: out_spec, out_shape),
        scratch_shapes=scratch,
        compiler_params=pltpu.CompilerParams(vmem_limit_bytes=40 * 2**20),
        cost_estimate=pl.CostEstimate(flops=flops, bytes_accessed=2**20, transcendentals=0),
    )(*operands)


def on_device(
    activations,
    first_cache,
    second_cache,
    norm1_scale,
    norm1_shift,
    conv1_weight,
    conv1_bias,
    norm2_scale,
    norm2_shift,
    conv2_weight,
    conv2_bias,
):
    frames, lines, columns, channels = activations.shape
    sections, row_count = lax.axis_size("section"), lax.axis_size("rows")
    everyone = sections * row_count
    stats_shape = jax.ShapeDtypeStruct((everyone, 2, channels), jnp.float32)
    vectors = (norm1_scale, norm1_shift, conv1_bias, norm2_scale, norm2_shift, conv2_bias)

    near = [i ^ 1 for i in range(row_count)]
    far = [i + 2 if i % 2 == 0 else i - 2 for i in range(row_count)]
    far[row_count - 2], far[1] = row_count - 1, 0

    def across(block, partner):
        return lax.ppermute(block, "rows", list(enumerate(partner)))

    ring = [(at, (at + 1) % sections) for at in range(sections)]
    own, halo = call(
        functools.partial(copy_kernel, sections),
        (
            jax.ShapeDtypeStruct(activations.shape, jnp.bfloat16),
            jax.ShapeDtypeStruct((SPAN_HALO, lines, columns, channels), jnp.bfloat16),
        ),
        [pltpu.SemaphoreType.DMA((4,))],
        (activations, second_cache, first_cache),
        in_place=range(3),
    )
    sums, packed, weight = call(
        stats_kernel,
        (
            jax.ShapeDtypeStruct((1, 2, channels), jnp.float32),
            jax.ShapeDtypeStruct((len(vectors), 1, channels), jnp.float32),
            jax.ShapeDtypeStruct(conv1_weight.shape, jnp.bfloat16),
        ),
        [pltpu.SemaphoreType.DMA((1 + len(vectors),))],
        (own, conv1_weight) + tuple(vector.reshape(1, channels) for vector in vectors),
        in_place=range(1, 2 + len(vectors)),
    )
    received = lax.ppermute(halo, "section", ring)
    bodies = [own, across(own, near)]
    bodies.append(across(bodies[1], far))
    passed = lax.ppermute(sums, "section", ring)
    pairs = [0] + [i + 1 if i % 2 else i - 1 for i in range(1, row_count - 1)] + [row_count - 1]
    halos = [received, across(received, pairs), across(received, near)]
    both = jnp.concatenate([sums, passed], axis=1)
    both = jnp.broadcast_to(both, (row_count,) + both.shape[1:])
    stats = lax.all_to_all(both, "rows", 0, 0, tiled=True)
    middle, sums_two = call(
        functools.partial(first_kernel, row_count),
        (
            jax.ShapeDtypeStruct((frames + 2, lines + 2, columns, channels), jnp.bfloat16),
            stats_shape,
        ),
        [pltpu.VMEM((frames + SPAN_HALO, 3 * lines, columns, channels), jnp.bfloat16)],
        (*bodies, *halos, stats, packed, weight),
        flops=10**9,
    )
    stats_two = lax.all_to_all(sums_two, ("section", "rows"), 0, 0, tiled=True)
    return call(
        functools.partial(second_kernel, row_count),
        jax.ShapeDtypeStruct(activations.shape, jnp.bfloat16),
        [
            pltpu.VMEM((frames + 2, lines + 2, columns, channels), jnp.bfloat16),
            pltpu.VMEM(activations.shape, jnp.bfloat16),
            pltpu.SemaphoreType.DMA((2,)),
        ],
        (middle, stats_two, packed, conv2_weight, own),
        out_in_place=True,
        flops=10**9,
    )


def solution(mesh):
    in_specs = (
        P("section", "rows", None, None),
        P(None, "rows", None, None),
        P(None, "rows", None, None),
        P(),
        P(),
        P(),
        P(),
        P(),
        P(),
        P(),
        P(),
    )
    out_specs = P("section", "rows", None, None)
    return jax.shard_map(
        on_device, mesh=mesh, in_specs=in_specs, out_specs=out_specs, check_vma=False
    )
```

```python
import functools

import functools

import jax
import jax.numpy as jnp
from jax import lax
from jax.experimental import pallas as pl
from jax.experimental.pallas import tpu as pltpu
from jax.sharding import PartitionSpec as P

GROUPS = 32
SPAN_HALO = 4

epsilon = 1e-06


def moments(blocks):
    pivot = blocks[0][:1]
    cells = sum(block.shape[0] for block in blocks)
    total, squares = 0.0, 0.0
    for block in blocks:
        away = block - pivot
        total = total + jnp.sum(away, axis=0, keepdims=True)
        squares = squares + jnp.sum(away * away, axis=0, keepdims=True)
    shift = total * (1.0 / cells)
    return jnp.concatenate([pivot + shift, squares - total * shift], axis=0)


def affine(stats, cells, scale, shift):
    devices, _, channels = stats.shape
    means, squares = stats[:, 0], stats[:, 1]
    mean = jnp.sum(means, axis=0, keepdims=True) * (1.0 / devices)
    away = means - mean
    square = jnp.sum(squares + cells * (away * away), axis=0, keepdims=True)
    count = cells * devices
    lane = lax.broadcasted_iota(jnp.int32, mean.shape, 1)
    step = 1
    while step < channels // GROUPS:

        def partner(values):
            up = pltpu.roll(values, channels - step, 1)
            return jnp.where((lane // step) % 2 == 0, up, pltpu.roll(values, step, 1))

        away = partner(mean) - mean
        square = square + partner(square) + (0.5 * count) * (away * away)
        mean = mean + 0.5 * away
        count, step = 2 * count, 2 * step
    slope = 0.5 * scale * lax.rsqrt(square * (1.0 / count) + epsilon)
    return slope, 0.5 * shift - mean * slope


def activate(values, slope, offset):
    half = values.astype(jnp.float32) * slope + offset
    return half + half * jnp.tanh(half)


def pair_conv(field, row, begin, frames, weight_ref):
    columns, channels = field.shape[2], field.shape[3]
    cells = frames * columns
    nothing = jnp.zeros((channels, channels), jnp.bfloat16)

    def piece(frame_tap, line):
        first = begin + frame_tap
        return field[first : first + frames, row + line].reshape(cells, channels)

    def dot(pieces, blocks):
        return jnp.dot(pieces, blocks, preferred_element_type=jnp.float32)

    taps = [(frame_tap, row_tap) for frame_tap in range(3) for row_tap in range(3)]
    early = dot(
        jnp.concatenate(
            [
                jnp.concatenate([piece(tap, out + row_tap) for tap, row_tap in taps], axis=1)
                for out in range(2)
            ],
            axis=0,
        ),
        jnp.concatenate(
            [
                jnp.concatenate([weight_ref[tap, row_tap, 0], weight_ref[tap, row_tap, 1]], axis=1)
                for tap, row_tap in taps
            ],
            axis=0,
        ),
    )
    lines = [(frame_tap, line) for frame_tap in range(3) for line in range(4)]
    late = dot(
        jnp.concatenate([piece(tap, line) for tap, line in lines], axis=1),
        jnp.concatenate(
            [
                jnp.concatenate(
                    [
                        weight_ref[tap, line - out, 2] if 0 <= line - out <= 2 else nothing
                        for out in range(2)
                    ],
                    axis=1,
                )
                for tap, line in lines
            ],
            axis=0,
        ),
    )
    column = lax.broadcasted_iota(jnp.int32, (frames, columns, channels), 1)
    column = column.reshape(cells, channels)
    results = []
    for out in range(2):
        left, centre = (
            early[out * cells : (out + 1) * cells, tap * channels : (tap + 1) * channels]
            for tap in range(2)
        )
        right = late[:, out * channels : (out + 1) * channels]
        left = jnp.where(column == 0, 0.0, pltpu.roll(left, 1, 0))
        right = jnp.where(column == columns - 1, 0.0, pltpu.roll(right, cells - 1, 0))
        results.append(left + centre + right)
    return results


def copy_kernel(sections, own_ref, second_cache_ref, first_cache_ref, copied, halo_ref, sems):
    last = lax.axis_index("section") == sections - 1
    frames = own_ref.shape[0]
    spare = SPAN_HALO - 2
    tail = pltpu.make_async_copy(own_ref.at[frames - SPAN_HALO :], halo_ref, sems.at[0])
    older = pltpu.make_async_copy(second_cache_ref, halo_ref.at[:spare], sems.at[1])
    newer = pltpu.make_async_copy(first_cache_ref, halo_ref.at[spare:], sems.at[2])
    load = pltpu.make_async_copy(own_ref, copied, sems.at[3])

    @pl.when(last)
    def _():
        older.start()
        newer.start()

    @pl.when(jnp.logical_not(last))
    def _():
        tail.start()

    load.start()

    @pl.when(last)
    def _():
        older.wait()
        newer.wait()

    @pl.when(jnp.logical_not(last))
    def _():
        tail.wait()

    load.wait()


def stats_kernel(own_ref, weight_ref, *rest):
    *vector_refs, stats_ref, vectors_ref, weight_copy, sems = rest
    loads = [pltpu.make_async_copy(weight_ref, weight_copy, sems.at[0])]
    loads += [
        pltpu.make_async_copy(vector_ref, vectors_ref.at[index], sems.at[1 + index])
        for index, vector_ref in enumerate(vector_refs)
    ]
    for load in loads:
        load.start()
    channels = own_ref.shape[-1]
    blocks = [own_ref[frame].astype(jnp.float32) for frame in range(own_ref.shape[0])]
    stats_ref[0] = moments([block.reshape(-1, channels) for block in blocks])
    for load in loads:
        load.wait()


def first_kernel(
    row_count, halo_ref, own_ref, near_ref, far_ref, stats_ref, vectors_ref, weight_ref,
    middle_ref, sums_ref, field
):
    section, row_at = lax.axis_index("section"), lax.axis_index("rows")
    inner, lines, columns, channels = own_ref.shape
    cells = inner * lines * columns
    scale, shift = vectors_ref[0], vectors_ref[1]
    mine, before = stats_ref[:, :2], stats_ref[:, 2:]
    slope, offset = affine(mine, cells, scale, shift)
    slope_before, offset_before = affine(before, cells, scale, shift)
    even = row_at % 2 == 0
    at_start = section == 0

    def fill(line):
        side, local = divmod(line, lines)
        if side == 1:
            halo, body = halo_ref[:, local], own_ref[:, local]
        else:
            near_side = even if side == 2 else jnp.logical_not(even)
            block = jnp.where(near_side, near_ref[:, local], far_ref[:, local])
            halo, body = block[:SPAN_HALO], block[SPAN_HALO:]
        behind = activate(halo, slope_before, offset_before).astype(jnp.bfloat16)
        behind = jnp.where(at_start, halo, behind)
        ahead = activate(body, slope, offset).astype(jnp.bfloat16)
        if side != 1:
            outside = row_at == 0 if side == 0 else row_at == row_count - 1
            behind = jnp.where(outside, jnp.zeros_like(behind), behind)
            ahead = jnp.where(outside, jnp.zeros_like(ahead), ahead)
        field[:SPAN_HALO, line] = behind
        field[SPAN_HALO:, line] = ahead

    bias = vectors_ref[2]
    kept = []
    spare = SPAN_HALO - 2
    ready = 0
    for pair in range((lines + 2) // 2):
        for line in range(ready, 2 * pair + 4):
            fill(line)
        ready = 2 * pair + 4
        results = pair_conv(field, 2 * pair, 0, inner + 2, weight_ref)
        for out in range(2):
            line = 2 * pair + out
            rounded = (results[out] + bias).astype(jnp.bfloat16)
            rounded = rounded.reshape(inner + 2, columns, channels)
            middle_ref[:2, line] = jnp.where(at_start, field[:spare, line + lines - 1], rounded[:2])
            middle_ref[2:, line] = rounded[2:]
            if 1 <= line <= lines:
                kept.append(rounded[2:].astype(jnp.float32).reshape(-1, channels))
    packed = moments(kept)
    for device in range(sums_ref.shape[0]):
        sums_ref[device] = packed


def second_kernel(
    row_count, middle_ref, stats_ref, vectors_ref, weight_ref, own_ref, out_ref, field, ready,
    sems
):
    section, row_at = lax.axis_index("section"), lax.axis_index("rows")
    frames, lines, columns, channels = own_ref.shape
    cells = frames * lines * columns
    scale, shift = vectors_ref[3], vectors_ref[4]
    mine = stats_ref[pl.ds(section * row_count, row_count)]
    before = stats_ref[pl.ds(jnp.maximum(section - 1, 0) * row_count, row_count)]
    slope, offset = affine(mine, cells, scale, shift)
    slope_before, offset_before = affine(before, cells, scale, shift)
    at_start = section == 0
    half = frames // 2
    copies = []
    for begin in range(0, frames, half):
        filled = 0 if begin == 0 else begin + 2
        for line in range(lines + 2):
            ahead = middle_ref[filled : begin + half + 2, line]
            if begin == 0:
                behind = activate(ahead[:2], slope_before, offset_before).astype(jnp.bfloat16)
                behind = jnp.where(at_start, ahead[:2], behind)
                ahead = activate(ahead[2:], slope, offset).astype(jnp.bfloat16)
                ahead = jnp.concatenate([behind, ahead], axis=0)
            else:
                ahead = activate(ahead, slope, offset).astype(jnp.bfloat16)
            if line == 0 or line == lines + 1:
                outside = row_at == 0 if line == 0 else row_at == row_count - 1
                ahead = jnp.where(outside, jnp.zeros_like(ahead), ahead)
            field[filled : begin + half + 2, line] = ahead
        span = slice(begin, begin + half)
        for pair in range(lines // 2):
            results = pair_conv(field, 2 * pair, begin, half, weight_ref)
            for out in range(2):
                line = 2 * pair + out
                result = (results[out] + vectors_ref[5]).reshape(half, columns, channels)
                result = result + own_ref[span, line].astype(jnp.float32)
                ready[span, line] = result.astype(jnp.bfloat16)
        copy = pltpu.make_async_copy(
            ready.at[span], out_ref.at[span], sems.at[begin // half]
        )
        copy.start()
        copies.append(copy)
    for copy in copies:
        copy.wait()


def call(kernel, out_shape, scratch, operands, in_place=(), out_in_place=False, flops=0):
    vmem = pl.BlockSpec(memory_space=pltpu.VMEM)
    out_spec = pl.BlockSpec(memory_space=pltpu.HBM) if out_in_place else vmem
    specs = [vmem] * len(operands)
    for index in in_place:
        specs[index] = pl.BlockSpec(memory_space=pltpu.HBM)
    operands = [
        pltpu.with_memory_space_constraint(operand, pltpu.HBM) if index in in_place else operand
        for index, operand in enumerate(operands)
    ]
    return pl.pallas_call(
        kernel,
        out_shape=out_shape,
        in_specs=specs,
        out_specs=jax.tree.map(lambda _: out_spec, out_shape),
        scratch_shapes=scratch,
        compiler_params=pltpu.CompilerParams(vmem_limit_bytes=40 * 2**20),
        cost_estimate=pl.CostEstimate(flops=flops, bytes_accessed=2**20, transcendentals=0),
    )(*operands)


def on_device(
    activations,
    first_cache,
    second_cache,
    norm1_scale,
    norm1_shift,
    conv1_weight,
    conv1_bias,
    norm2_scale,
    norm2_shift,
    conv2_weight,
    conv2_bias,
):
    frames, lines, columns, channels = activations.shape
    sections, row_count = lax.axis_size("section"), lax.axis_size("rows")
    everyone = sections * row_count
    stats_shape = jax.ShapeDtypeStruct((everyone, 2, channels), jnp.float32)
    vectors = (norm1_scale, norm1_shift, conv1_bias, norm2_scale, norm2_shift, conv2_bias)

    near = [i ^ 1 for i in range(row_count)]
    far = [i + 2 if i % 2 == 0 else i - 2 for i in range(row_count)]
    far[row_count - 2], far[1] = row_count - 1, 0

    def across(block, partner):
        return lax.ppermute(block, "rows", list(enumerate(partner)))

    ring = [(at, (at + 1) % sections) for at in range(sections)]
    own, halo = call(
        functools.partial(copy_kernel, sections),
        (
            jax.ShapeDtypeStruct(activations.shape, jnp.bfloat16),
            jax.ShapeDtypeStruct((SPAN_HALO, lines, columns, channels), jnp.bfloat16),
        ),
        [pltpu.SemaphoreType.DMA((4,))],
        (activations, second_cache, first_cache),
        in_place=range(3),
    )
    sums, packed, weight = call(
        stats_kernel,
        (
            jax.ShapeDtypeStruct((1, 2, channels), jnp.float32),
            jax.ShapeDtypeStruct((len(vectors), 1, channels), jnp.float32),
            jax.ShapeDtypeStruct(conv1_weight.shape, jnp.bfloat16),
        ),
        [pltpu.SemaphoreType.DMA((1 + len(vectors),))],
        (own, conv1_weight) + tuple(vector.reshape(1, channels) for vector in vectors),
        in_place=range(1, 2 + len(vectors)),
    )
    received = lax.ppermute(halo, "section", ring)
    passed = lax.ppermute(sums, "section", ring)
    received, sums, passed = lax.optimization_barrier((received, sums, passed))
    from_near = jnp.concatenate([across(received, near), across(own, near)], axis=0)
    from_far = across(from_near, far)
    both = jnp.concatenate([sums, passed], axis=1)
    both = jnp.broadcast_to(both, (row_count,) + both.shape[1:])
    stats = lax.all_to_all(both, "rows", 0, 0, tiled=True)
    middle, sums_two = call(
        functools.partial(first_kernel, row_count),
        (
            jax.ShapeDtypeStruct((frames + 2, lines + 2, columns, channels), jnp.bfloat16),
            stats_shape,
        ),
        [pltpu.VMEM((frames + SPAN_HALO, 3 * lines, columns, channels), jnp.bfloat16)],
        (received, own, from_near, from_far, stats, packed, weight),
        flops=10**9,
    )
    stats_two = lax.all_to_all(sums_two, ("section", "rows"), 0, 0, tiled=True)
    return call(
        functools.partial(second_kernel, row_count),
        jax.ShapeDtypeStruct(activations.shape, jnp.bfloat16),
        [
            pltpu.VMEM((frames + 2, lines + 2, columns, channels), jnp.bfloat16),
            pltpu.VMEM(activations.shape, jnp.bfloat16),
            pltpu.SemaphoreType.DMA((2,)),
        ],
        (middle, stats_two, packed, conv2_weight, own),
        out_in_place=True,
        flops=10**9,
    )


def solution(mesh):
    in_specs = (
        P("section", "rows", None, None),
        P(None, "rows", None, None),
        P(None, "rows", None, None),
        P(),
        P(),
        P(),
        P(),
        P(),
        P(),
        P(),
        P(),
    )
    out_specs = P("section", "rows", None, None)
    return jax.shard_map(
        on_device, mesh=mesh, in_specs=in_specs, out_specs=out_specs, check_vma=False
    )
```

```python
import functools

import functools

import jax
import jax.numpy as jnp
from jax import lax
from jax.experimental import pallas as pl
from jax.experimental.pallas import tpu as pltpu
from jax.sharding import PartitionSpec as P

GROUPS = 32
SPAN_HALO = 4

epsilon = 1e-06


def moments(blocks):
    pivot = blocks[0][:1]
    cells = sum(block.shape[0] for block in blocks)
    total, squares = 0.0, 0.0
    for block in blocks:
        away = block - pivot
        total = total + jnp.sum(away, axis=0, keepdims=True)
        squares = squares + jnp.sum(away * away, axis=0, keepdims=True)
    shift = total * (1.0 / cells)
    return jnp.concatenate([pivot + shift, squares - total * shift], axis=0)


def affine(stats, cells, scale, shift):
    devices, _, channels = stats.shape
    means, squares = stats[:, 0], stats[:, 1]
    mean = jnp.sum(means, axis=0, keepdims=True) * (1.0 / devices)
    away = means - mean
    square = jnp.sum(squares + cells * (away * away), axis=0, keepdims=True)
    count = cells * devices
    lane = lax.broadcasted_iota(jnp.int32, mean.shape, 1)
    step = 1
    while step < channels // GROUPS:

        def partner(values):
            up = pltpu.roll(values, channels - step, 1)
            return jnp.where((lane // step) % 2 == 0, up, pltpu.roll(values, step, 1))

        away = partner(mean) - mean
        square = square + partner(square) + (0.5 * count) * (away * away)
        mean = mean + 0.5 * away
        count, step = 2 * count, 2 * step
    slope = 0.5 * scale * lax.rsqrt(square * (1.0 / count) + epsilon)
    return slope, 0.5 * shift - mean * slope


def activate(values, slope, offset):
    half = values.astype(jnp.float32) * slope + offset
    return half + half * jnp.tanh(half)


def pair_conv(field, row, begin, frames, weight_ref, prepare):
    columns, channels = field.shape[2], field.shape[3]
    cells = frames * columns
    nothing = jnp.zeros((channels, channels), jnp.bfloat16)

    def piece(frame_tap, line):
        first = begin + frame_tap
        return field[first : first + frames, row + line].reshape(cells, channels)

    def dot(pieces, blocks):
        return jnp.dot(pieces, blocks, preferred_element_type=jnp.float32)

    taps = [(frame_tap, row_tap) for frame_tap in range(3) for row_tap in range(3)]
    early_weight = jnp.concatenate(
        [
            jnp.concatenate([weight_ref[tap, row_tap, 0], weight_ref[tap, row_tap, 1]], axis=1)
            for tap, row_tap in taps
        ],
        axis=0,
    )
    early = []
    for out in range(2):
        prepare(row + out + 2)
        pieces = [piece(tap, out + row_tap) for tap, row_tap in taps]
        early.append(dot(jnp.concatenate(pieces, axis=1), early_weight))
    lines = [(frame_tap, line) for frame_tap in range(3) for line in range(4)]
    late = dot(
        jnp.concatenate([piece(tap, line) for tap, line in lines], axis=1),
        jnp.concatenate(
            [
                jnp.concatenate(
                    [
                        weight_ref[tap, line - out, 2] if 0 <= line - out <= 2 else nothing
                        for out in range(2)
                    ],
                    axis=1,
                )
                for tap, line in lines
            ],
            axis=0,
        ),
    )
    column = lax.broadcasted_iota(jnp.int32, (frames, columns, channels), 1)
    column = column.reshape(cells, channels)
    results = []
    for out in range(2):
        left, centre = (
            early[out][:, tap * channels : (tap + 1) * channels] for tap in range(2)
        )
        right = late[:, out * channels : (out + 1) * channels]
        left = jnp.where(column == 0, 0.0, pltpu.roll(left, 1, 0))
        right = jnp.where(column == columns - 1, 0.0, pltpu.roll(right, cells - 1, 0))
        results.append(left + centre + right)
    return results


def copy_kernel(sections, own_ref, second_cache_ref, first_cache_ref, copied, halo_ref, sems):
    last = lax.axis_index("section") == sections - 1
    frames = own_ref.shape[0]
    spare = SPAN_HALO - 2
    tail = pltpu.make_async_copy(own_ref.at[frames - SPAN_HALO :], halo_ref, sems.at[0])
    older = pltpu.make_async_copy(second_cache_ref, halo_ref.at[:spare], sems.at[1])
    newer = pltpu.make_async_copy(first_cache_ref, halo_ref.at[spare:], sems.at[2])
    load = pltpu.make_async_copy(own_ref, copied, sems.at[3])

    @pl.when(last)
    def _():
        older.start()
        newer.start()

    @pl.when(jnp.logical_not(last))
    def _():
        tail.start()

    load.start()

    @pl.when(last)
    def _():
        older.wait()
        newer.wait()

    @pl.when(jnp.logical_not(last))
    def _():
        tail.wait()

    load.wait()


def stats_kernel(own_ref, weight_ref, *rest):
    *vector_refs, stats_ref, vectors_ref, weight_copy, sems = rest
    loads = [pltpu.make_async_copy(weight_ref, weight_copy, sems.at[0])]
    loads += [
        pltpu.make_async_copy(vector_ref, vectors_ref.at[index], sems.at[1 + index])
        for index, vector_ref in enumerate(vector_refs)
    ]
    for load in loads:
        load.start()
    channels = own_ref.shape[-1]
    blocks = [own_ref[frame].astype(jnp.float32) for frame in range(own_ref.shape[0])]
    stats_ref[0] = moments([block.reshape(-1, channels) for block in blocks])
    for load in loads:
        load.wait()


def first_kernel(
    row_count, halo_ref, own_ref, near_ref, far_ref, stats_ref, vectors_ref, weight_ref,
    middle_ref, sums_ref, field
):
    section, row_at = lax.axis_index("section"), lax.axis_index("rows")
    inner, lines, columns, channels = own_ref.shape
    cells = inner * lines * columns
    scale, shift = vectors_ref[0], vectors_ref[1]
    mine, before = stats_ref[:, :2], stats_ref[:, 2:]
    slope, offset = affine(mine, cells, scale, shift)
    slope_before, offset_before = affine(before, cells, scale, shift)
    even = row_at % 2 == 0
    at_start = section == 0

    def fill(line):
        side, local = divmod(line, lines)
        if side == 1:
            halo, body = halo_ref[:, local], own_ref[:, local]
        else:
            near_side = even if side == 2 else jnp.logical_not(even)
            block = jnp.where(near_side, near_ref[:, local], far_ref[:, local])
            halo, body = block[:SPAN_HALO], block[SPAN_HALO:]
        behind = activate(halo, slope_before, offset_before).astype(jnp.bfloat16)
        behind = jnp.where(at_start, halo, behind)
        ahead = activate(body, slope, offset).astype(jnp.bfloat16)
        if side != 1:
            outside = row_at == 0 if side == 0 else row_at == row_count - 1
            behind = jnp.where(outside, jnp.zeros_like(behind), behind)
            ahead = jnp.where(outside, jnp.zeros_like(ahead), ahead)
        field[:SPAN_HALO, line] = behind
        field[SPAN_HALO:, line] = ahead

    bias = vectors_ref[2]
    kept = []
    spare = SPAN_HALO - 2
    filled = []

    def prepare(last):
        while len(filled) <= last:
            fill(len(filled))
            filled.append(last)

    for pair in range((lines + 2) // 2):
        results = pair_conv(field, 2 * pair, 0, inner + 2, weight_ref, prepare)
        for out in range(2):
            line = 2 * pair + out
            rounded = (results[out] + bias).astype(jnp.bfloat16)
            rounded = rounded.reshape(inner + 2, columns, channels)
            middle_ref[:2, line] = jnp.where(at_start, field[:spare, line + lines - 1], rounded[:2])
            middle_ref[2:, line] = rounded[2:]
            if 1 <= line <= lines:
                kept.append(rounded[2:].astype(jnp.float32).reshape(-1, channels))
    packed = moments(kept)
    for device in range(sums_ref.shape[0]):
        sums_ref[device] = packed


def second_kernel(
    row_count, middle_ref, stats_ref, vectors_ref, weight_ref, own_ref, out_ref, field, ready,
    sems
):
    section, row_at = lax.axis_index("section"), lax.axis_index("rows")
    frames, lines, columns, channels = own_ref.shape
    cells = frames * lines * columns
    scale, shift = vectors_ref[3], vectors_ref[4]
    mine = stats_ref[pl.ds(section * row_count, row_count)]
    before = stats_ref[pl.ds(jnp.maximum(section - 1, 0) * row_count, row_count)]
    slope, offset = affine(mine, cells, scale, shift)
    slope_before, offset_before = affine(before, cells, scale, shift)
    at_start = section == 0
    half = frames // 2
    copies = []
    for begin in range(0, frames, half):
        start = 0 if begin == 0 else begin + 2

        def fill(line):
            ahead = middle_ref[start : begin + half + 2, line]
            if begin == 0:
                behind = activate(ahead[:2], slope_before, offset_before).astype(jnp.bfloat16)
                behind = jnp.where(at_start, ahead[:2], behind)
                ahead = activate(ahead[2:], slope, offset).astype(jnp.bfloat16)
                ahead = jnp.concatenate([behind, ahead], axis=0)
            else:
                ahead = activate(ahead, slope, offset).astype(jnp.bfloat16)
            if line == 0 or line == lines + 1:
                outside = row_at == 0 if line == 0 else row_at == row_count - 1
                ahead = jnp.where(outside, jnp.zeros_like(ahead), ahead)
            field[start : begin + half + 2, line] = ahead

        filled = []

        def prepare(last):
            while len(filled) <= last:
                fill(len(filled))
                filled.append(last)

        span = slice(begin, begin + half)
        for pair in range(lines // 2):
            results = pair_conv(field, 2 * pair, begin, half, weight_ref, prepare)
            for out in range(2):
                line = 2 * pair + out
                result = (results[out] + vectors_ref[5]).reshape(half, columns, channels)
                result = result + own_ref[span, line].astype(jnp.float32)
                ready[span, line] = result.astype(jnp.bfloat16)
        copy = pltpu.make_async_copy(
            ready.at[span], out_ref.at[span], sems.at[begin // half]
        )
        copy.start()
        copies.append(copy)
    for copy in copies:
        copy.wait()


def call(kernel, out_shape, scratch, operands, in_place=(), out_in_place=False, flops=0):
    vmem = pl.BlockSpec(memory_space=pltpu.VMEM)
    out_spec = pl.BlockSpec(memory_space=pltpu.HBM) if out_in_place else vmem
    specs = [vmem] * len(operands)
    for index in in_place:
        specs[index] = pl.BlockSpec(memory_space=pltpu.HBM)
    operands = [
        pltpu.with_memory_space_constraint(operand, pltpu.HBM) if index in in_place else operand
        for index, operand in enumerate(operands)
    ]
    return pl.pallas_call(
        kernel,
        out_shape=out_shape,
        in_specs=specs,
        out_specs=jax.tree.map(lambda _: out_spec, out_shape),
        scratch_shapes=scratch,
        compiler_params=pltpu.CompilerParams(vmem_limit_bytes=40 * 2**20),
        cost_estimate=pl.CostEstimate(flops=flops, bytes_accessed=2**20, transcendentals=0),
    )(*operands)


def on_device(
    activations,
    first_cache,
    second_cache,
    norm1_scale,
    norm1_shift,
    conv1_weight,
    conv1_bias,
    norm2_scale,
    norm2_shift,
    conv2_weight,
    conv2_bias,
):
    frames, lines, columns, channels = activations.shape
    sections, row_count = lax.axis_size("section"), lax.axis_size("rows")
    everyone = sections * row_count
    stats_shape = jax.ShapeDtypeStruct((everyone, 2, channels), jnp.float32)
    vectors = (norm1_scale, norm1_shift, conv1_bias, norm2_scale, norm2_shift, conv2_bias)

    near = [i ^ 1 for i in range(row_count)]
    far = [i + 2 if i % 2 == 0 else i - 2 for i in range(row_count)]
    far[row_count - 2], far[1] = row_count - 1, 0

    def across(block, partner):
        return lax.ppermute(block, "rows", list(enumerate(partner)))

    ring = [(at, (at + 1) % sections) for at in range(sections)]
    own, halo = call(
        functools.partial(copy_kernel, sections),
        (
            jax.ShapeDtypeStruct(activations.shape, jnp.bfloat16),
            jax.ShapeDtypeStruct((SPAN_HALO, lines, columns, channels), jnp.bfloat16),
        ),
        [pltpu.SemaphoreType.DMA((4,))],
        (activations, second_cache, first_cache),
        in_place=range(3),
    )
    sums, packed, weight = call(
        stats_kernel,
        (
            jax.ShapeDtypeStruct((1, 2, channels), jnp.float32),
            jax.ShapeDtypeStruct((len(vectors), 1, channels), jnp.float32),
            jax.ShapeDtypeStruct(conv1_weight.shape, jnp.bfloat16),
        ),
        [pltpu.SemaphoreType.DMA((1 + len(vectors),))],
        (own, conv1_weight) + tuple(vector.reshape(1, channels) for vector in vectors),
        in_place=range(1, 2 + len(vectors)),
    )
    received = lax.ppermute(halo, "section", ring)
    passed = lax.ppermute(sums, "section", ring)
    received, sums, passed = lax.optimization_barrier((received, sums, passed))
    from_near = jnp.concatenate([across(received, near), across(own, near)], axis=0)
    from_far = across(from_near, far)
    both = jnp.concatenate([sums, passed], axis=1)
    both = jnp.broadcast_to(both, (row_count,) + both.shape[1:])
    stats = lax.all_to_all(both, "rows", 0, 0, tiled=True)
    middle, sums_two = call(
        functools.partial(first_kernel, row_count),
        (
            jax.ShapeDtypeStruct((frames + 2, lines + 2, columns, channels), jnp.bfloat16),
            stats_shape,
        ),
        [pltpu.VMEM((frames + SPAN_HALO, 3 * lines, columns, channels), jnp.bfloat16)],
        (received, own, from_near, from_far, stats, packed, weight),
        flops=10**9,
    )
    stats_two = lax.all_to_all(sums_two, ("section", "rows"), 0, 0, tiled=True)
    return call(
        functools.partial(second_kernel, row_count),
        jax.ShapeDtypeStruct(activations.shape, jnp.bfloat16),
        [
            pltpu.VMEM((frames + 2, lines + 2, columns, channels), jnp.bfloat16),
            pltpu.VMEM(activations.shape, jnp.bfloat16),
            pltpu.SemaphoreType.DMA((2,)),
        ],
        (middle, stats_two, packed, conv2_weight, own),
        out_in_place=True,
        flops=10**9,
    )


def solution(mesh):
    in_specs = (
        P("section", "rows", None, None),
        P(None, "rows", None, None),
        P(None, "rows", None, None),
        P(),
        P(),
        P(),
        P(),
        P(),
        P(),
        P(),
        P(),
    )
    out_specs = P("section", "rows", None, None)
    return jax.shard_map(
        on_device, mesh=mesh, in_specs=in_specs, out_specs=out_specs, check_vma=False
    )
```

```python
import functools

import jax
import jax.numpy as jnp
from jax import lax
from jax.experimental import pallas as pl
from jax.experimental.pallas import tpu as pltpu
from jax.sharding import PartitionSpec as P

GROUPS = 32
SPAN_HALO = 4

epsilon = 1e-06


def moments(blocks):
    pivot = blocks[0][:1]
    cells = sum(block.shape[0] for block in blocks)
    total, squares = 0.0, 0.0
    for block in blocks:
        away = block - pivot
        total = total + jnp.sum(away, axis=0, keepdims=True)
        squares = squares + jnp.sum(away * away, axis=0, keepdims=True)
    shift = total * (1.0 / cells)
    return jnp.concatenate([pivot + shift, squares - total * shift], axis=0)


def affine(stats, cells, scale, shift):
    devices, _, channels = stats.shape
    means, squares = stats[:, 0], stats[:, 1]
    mean = jnp.sum(means, axis=0, keepdims=True) * (1.0 / devices)
    away = means - mean
    square = jnp.sum(squares + cells * (away * away), axis=0, keepdims=True)
    count = cells * devices
    lane = lax.broadcasted_iota(jnp.int32, mean.shape, 1)
    step = 1
    while step < channels // GROUPS:

        def partner(values):
            up = pltpu.roll(values, channels - step, 1)
            return jnp.where((lane // step) % 2 == 0, up, pltpu.roll(values, step, 1))

        away = partner(mean) - mean
        square = square + partner(square) + (0.5 * count) * (away * away)
        mean = mean + 0.5 * away
        count, step = 2 * count, 2 * step
    slope = 0.5 * scale * lax.rsqrt(square * (1.0 / count) + epsilon)
    return slope, 0.5 * shift - mean * slope


def activate(values, slope, offset):
    half = values.astype(jnp.float32) * slope + offset
    return half + half * jnp.tanh(half)


def pair_conv(field, row, begin, frames, weight_ref):
    columns, channels = field.shape[2], field.shape[3]
    cells = frames * columns
    nothing = jnp.zeros((channels, channels), jnp.bfloat16)

    def piece(frame_tap, line):
        first = begin + frame_tap
        return field[first : first + frames, row + line].reshape(cells, channels)

    def dot(pieces, blocks):
        return jnp.dot(pieces, blocks, preferred_element_type=jnp.float32)

    taps = [(frame_tap, row_tap) for frame_tap in range(3) for row_tap in range(3)]
    early = dot(
        jnp.concatenate(
            [
                jnp.concatenate([piece(tap, out + row_tap) for tap, row_tap in taps], axis=1)
                for out in range(2)
            ],
            axis=0,
        ),
        jnp.concatenate(
            [
                jnp.concatenate([weight_ref[tap, row_tap, 0], weight_ref[tap, row_tap, 1]], axis=1)
                for tap, row_tap in taps
            ],
            axis=0,
        ),
    )
    lines = [(frame_tap, line) for frame_tap in range(3) for line in range(4)]
    late = dot(
        jnp.concatenate([piece(tap, line) for tap, line in lines], axis=1),
        jnp.concatenate(
            [
                jnp.concatenate(
                    [
                        weight_ref[tap, line - out, 2] if 0 <= line - out <= 2 else nothing
                        for out in range(2)
                    ],
                    axis=1,
                )
                for tap, line in lines
            ],
            axis=0,
        ),
    )
    column = lax.broadcasted_iota(jnp.int32, (frames, columns, channels), 1)
    column = column.reshape(cells, channels)
    results = []
    for out in range(2):
        left, centre = (
            early[out * cells : (out + 1) * cells, tap * channels : (tap + 1) * channels]
            for tap in range(2)
        )
        right = late[:, out * channels : (out + 1) * channels]
        left = jnp.where(column == 0, 0.0, pltpu.roll(left, 1, 0))
        right = jnp.where(column == columns - 1, 0.0, pltpu.roll(right, cells - 1, 0))
        results.append(left + centre + right)
    return results


def copy_kernel(sections, own_ref, second_cache_ref, first_cache_ref, copied, halo_ref, sems):
    last = lax.axis_index("section") == sections - 1
    frames = own_ref.shape[0]
    spare = SPAN_HALO - 2
    tail = pltpu.make_async_copy(own_ref.at[frames - SPAN_HALO :], halo_ref, sems.at[0])
    older = pltpu.make_async_copy(second_cache_ref, halo_ref.at[:spare], sems.at[1])
    newer = pltpu.make_async_copy(first_cache_ref, halo_ref.at[spare:], sems.at[2])
    load = pltpu.make_async_copy(own_ref, copied, sems.at[3])

    @pl.when(last)
    def _():
        older.start()
        newer.start()

    @pl.when(jnp.logical_not(last))
    def _():
        tail.start()

    load.start()

    @pl.when(last)
    def _():
        older.wait()
        newer.wait()

    @pl.when(jnp.logical_not(last))
    def _():
        tail.wait()

    load.wait()


def stats_kernel(own_ref, weight_ref, *rest):
    *vector_refs, stats_ref, vectors_ref, weight_copy, sems = rest
    loads = [pltpu.make_async_copy(weight_ref, weight_copy, sems.at[0])]
    loads += [
        pltpu.make_async_copy(vector_ref, vectors_ref.at[index], sems.at[1 + index])
        for index, vector_ref in enumerate(vector_refs)
    ]
    for load in loads:
        load.start()
    channels = own_ref.shape[-1]
    blocks = [own_ref[frame].astype(jnp.float32) for frame in range(own_ref.shape[0])]
    stats_ref[0] = moments([block.reshape(-1, channels) for block in blocks])
    for load in loads:
        load.wait()


def first_kernel(
    row_count, halo_ref, own_ref, near_ref, far_ref, stats_ref, vectors_ref, weight_ref,
    middle_ref, sums_ref, field
):
    section, row_at = lax.axis_index("section"), lax.axis_index("rows")
    inner, lines, columns, channels = own_ref.shape
    cells = inner * lines * columns
    scale, shift = vectors_ref[0], vectors_ref[1]
    mine, before = stats_ref[:, :2], stats_ref[:, 2:]
    slope, offset = affine(mine, cells, scale, shift)
    slope_before, offset_before = affine(before, cells, scale, shift)
    even = row_at % 2 == 0
    at_start = section == 0

    def fill(line):
        side, local = divmod(line, lines)
        if side == 1:
            halo, body = halo_ref[:, local], own_ref[:, local]
        else:
            near_side = even if side == 2 else jnp.logical_not(even)
            block = jnp.where(near_side, near_ref[:, local], far_ref[:, local])
            halo, body = block[:SPAN_HALO], block[SPAN_HALO:]
        behind = activate(halo, slope_before, offset_before).astype(jnp.bfloat16)
        behind = jnp.where(at_start, halo, behind)
        ahead = activate(body, slope, offset).astype(jnp.bfloat16)
        if side != 1:
            outside = row_at == 0 if side == 0 else row_at == row_count - 1
            behind = jnp.where(outside, jnp.zeros_like(behind), behind)
            ahead = jnp.where(outside, jnp.zeros_like(ahead), ahead)
        field[:SPAN_HALO, line] = behind
        field[SPAN_HALO:, line] = ahead

    bias = vectors_ref[2]
    kept = []
    spare = SPAN_HALO - 2
    ready = 0
    for pair in range((lines + 2) // 2):
        for line in range(ready, 2 * pair + 4):
            fill(line)
        ready = 2 * pair + 4
        results = pair_conv(field, 2 * pair, 0, inner + 2, weight_ref)
        for out in range(2):
            line = 2 * pair + out
            rounded = (results[out] + bias).astype(jnp.bfloat16)
            rounded = rounded.reshape(inner + 2, columns, channels)
            middle_ref[:2, line] = jnp.where(at_start, field[:spare, line + lines - 1], rounded[:2])
            middle_ref[2:, line] = rounded[2:]
            if 1 <= line <= lines:
                kept.append(rounded[2:].astype(jnp.float32).reshape(-1, channels))
    packed = moments(kept)
    for device in range(sums_ref.shape[0]):
        sums_ref[device] = packed


def second_kernel(
    row_count, middle_ref, stats_ref, vectors_ref, weight_ref, own_ref, out_ref, field, ready,
    sems
):
    section, row_at = lax.axis_index("section"), lax.axis_index("rows")
    frames, lines, columns, channels = own_ref.shape
    cells = frames * lines * columns
    scale, shift = vectors_ref[3], vectors_ref[4]
    mine = stats_ref[pl.ds(section * row_count, row_count)]
    before = stats_ref[pl.ds(jnp.maximum(section - 1, 0) * row_count, row_count)]
    slope, offset = affine(mine, cells, scale, shift)
    slope_before, offset_before = affine(before, cells, scale, shift)
    at_start = section == 0
    half = frames
    copies = []
    for begin in range(0, frames, half):
        filled = 0 if begin == 0 else begin + 2
        for line in range(lines + 2):
            ahead = middle_ref[filled : begin + half + 2, line]
            if begin == 0:
                behind = activate(ahead[:2], slope_before, offset_before).astype(jnp.bfloat16)
                behind = jnp.where(at_start, ahead[:2], behind)
                ahead = activate(ahead[2:], slope, offset).astype(jnp.bfloat16)
                ahead = jnp.concatenate([behind, ahead], axis=0)
            else:
                ahead = activate(ahead, slope, offset).astype(jnp.bfloat16)
            if line == 0 or line == lines + 1:
                outside = row_at == 0 if line == 0 else row_at == row_count - 1
                ahead = jnp.where(outside, jnp.zeros_like(ahead), ahead)
            field[filled : begin + half + 2, line] = ahead
        span = slice(begin, begin + half)
        for pair in range(lines // 2):
            results = pair_conv(field, 2 * pair, begin, half, weight_ref)
            for out in range(2):
                line = 2 * pair + out
                result = (results[out] + vectors_ref[5]).reshape(half, columns, channels)
                result = result + own_ref[span, line].astype(jnp.float32)
                ready[line] = result.astype(jnp.bfloat16)
                copy = pltpu.make_async_copy(ready.at[line], out_ref.at[:, line], sems.at[line])
                copy.start()
                copies.append(copy)
    for copy in copies:
        copy.wait()


def call(kernel, out_shape, scratch, operands, in_place=(), out_in_place=False, flops=0):
    vmem = pl.BlockSpec(memory_space=pltpu.VMEM)
    out_spec = pl.BlockSpec(memory_space=pltpu.HBM) if out_in_place else vmem
    specs = [vmem] * len(operands)
    for index in in_place:
        specs[index] = pl.BlockSpec(memory_space=pltpu.HBM)
    operands = [
        pltpu.with_memory_space_constraint(operand, pltpu.HBM) if index in in_place else operand
        for index, operand in enumerate(operands)
    ]
    return pl.pallas_call(
        kernel,
        out_shape=out_shape,
        in_specs=specs,
        out_specs=jax.tree.map(lambda _: out_spec, out_shape),
        scratch_shapes=scratch,
        compiler_params=pltpu.CompilerParams(vmem_limit_bytes=40 * 2**20),
        cost_estimate=pl.CostEstimate(flops=flops, bytes_accessed=2**20, transcendentals=0),
    )(*operands)


def on_device(
    activations,
    first_cache,
    second_cache,
    norm1_scale,
    norm1_shift,
    conv1_weight,
    conv1_bias,
    norm2_scale,
    norm2_shift,
    conv2_weight,
    conv2_bias,
):
    frames, lines, columns, channels = activations.shape
    sections, row_count = lax.axis_size("section"), lax.axis_size("rows")
    everyone = sections * row_count
    stats_shape = jax.ShapeDtypeStruct((everyone, 2, channels), jnp.float32)
    vectors = (norm1_scale, norm1_shift, conv1_bias, norm2_scale, norm2_shift, conv2_bias)

    near = [i ^ 1 for i in range(row_count)]
    far = [i + 2 if i % 2 == 0 else i - 2 for i in range(row_count)]
    far[row_count - 2], far[1] = row_count - 1, 0

    def across(block, partner):
        return lax.ppermute(block, "rows", list(enumerate(partner)))

    ring = [(at, (at + 1) % sections) for at in range(sections)]
    own, halo = call(
        functools.partial(copy_kernel, sections),
        (
            jax.ShapeDtypeStruct(activations.shape, jnp.bfloat16),
            jax.ShapeDtypeStruct((SPAN_HALO, lines, columns, channels), jnp.bfloat16),
        ),
        [pltpu.SemaphoreType.DMA((4,))],
        (activations, second_cache, first_cache),
        in_place=range(3),
    )
    sums, packed, weight = call(
        stats_kernel,
        (
            jax.ShapeDtypeStruct((1, 2, channels), jnp.float32),
            jax.ShapeDtypeStruct((len(vectors), 1, channels), jnp.float32),
            jax.ShapeDtypeStruct(conv1_weight.shape, jnp.bfloat16),
        ),
        [pltpu.SemaphoreType.DMA((1 + len(vectors),))],
        (own, conv1_weight) + tuple(vector.reshape(1, channels) for vector in vectors),
        in_place=range(1, 2 + len(vectors)),
    )
    received = lax.ppermute(halo, "section", ring)
    passed = lax.ppermute(sums, "section", ring)
    received, sums, passed = lax.optimization_barrier((received, sums, passed))
    from_near = jnp.concatenate([across(received, near), across(own, near)], axis=0)
    from_far = across(from_near, far)
    both = jnp.concatenate([sums, passed], axis=1)
    both = jnp.broadcast_to(both, (row_count,) + both.shape[1:])
    stats = lax.all_to_all(both, "rows", 0, 0, tiled=True)
    middle, sums_two = call(
        functools.partial(first_kernel, row_count),
        (
            jax.ShapeDtypeStruct((frames + 2, lines + 2, columns, channels), jnp.bfloat16),
            stats_shape,
        ),
        [pltpu.VMEM((frames + SPAN_HALO, 3 * lines, columns, channels), jnp.bfloat16)],
        (received, own, from_near, from_far, stats, packed, weight),
        flops=10**9,
    )
    stats_two = lax.all_to_all(sums_two, ("section", "rows"), 0, 0, tiled=True)
    return call(
        functools.partial(second_kernel, row_count),
        jax.ShapeDtypeStruct(activations.shape, jnp.bfloat16),
        [
            pltpu.VMEM((frames + 2, lines + 2, columns, channels), jnp.bfloat16),
            pltpu.VMEM((lines, frames, columns, channels), jnp.bfloat16),
            pltpu.SemaphoreType.DMA((lines,)),
        ],
        (middle, stats_two, packed, conv2_weight, own),
        out_in_place=True,
        flops=10**9,
    )


def solution(mesh):
    in_specs = (
        P("section", "rows", None, None),
        P(None, "rows", None, None),
        P(None, "rows", None, None),
        P(),
        P(),
        P(),
        P(),
        P(),
        P(),
        P(),
        P(),
    )
    out_specs = P("section", "rows", None, None)
    return jax.shard_map(
        on_device, mesh=mesh, in_specs=in_specs, out_specs=out_specs, check_vma=False
    )
```

```python
import functools

import jax
import jax.numpy as jnp
from jax import lax
from jax.experimental import pallas as pl
from jax.experimental.pallas import tpu as pltpu
from jax.sharding import PartitionSpec as P

GROUPS = 32
SPAN_HALO = 4

epsilon = 1e-06


def moments(blocks):
    pivot = blocks[0][:1]
    cells = sum(block.shape[0] for block in blocks)
    total, squares = 0.0, 0.0
    for block in blocks:
        away = block - pivot
        total = total + jnp.sum(away, axis=0, keepdims=True)
        squares = squares + jnp.sum(away * away, axis=0, keepdims=True)
    shift = total * (1.0 / cells)
    return jnp.concatenate([pivot + shift, squares - total * shift], axis=0)


def affine(stats, cells, scale, shift):
    devices, _, channels = stats.shape
    means, squares = stats[:, 0], stats[:, 1]
    mean = jnp.sum(means, axis=0, keepdims=True) * (1.0 / devices)
    away = means - mean
    square = jnp.sum(squares + cells * (away * away), axis=0, keepdims=True)
    count = cells * devices
    lane = lax.broadcasted_iota(jnp.int32, mean.shape, 1)
    step = 1
    while step < channels // GROUPS:

        def partner(values):
            up = pltpu.roll(values, channels - step, 1)
            return jnp.where((lane // step) % 2 == 0, up, pltpu.roll(values, step, 1))

        away = partner(mean) - mean
        square = square + partner(square) + (0.5 * count) * (away * away)
        mean = mean + 0.5 * away
        count, step = 2 * count, 2 * step
    slope = 0.5 * scale * lax.rsqrt(square * (1.0 / count) + epsilon)
    return slope, 0.5 * shift - mean * slope


def activate(values, slope, offset):
    half = values.astype(jnp.float32) * slope + offset
    return half + half * jnp.tanh(half)


def pair_conv(field, row, begin, frames, weight_ref):
    columns, channels = field.shape[2], field.shape[3]
    cells = frames * columns
    nothing = jnp.zeros((channels, channels), jnp.bfloat16)

    def piece(frame_tap, line):
        first = begin + frame_tap
        return field[first : first + frames, row + line].reshape(cells, channels)

    def dot(pieces, blocks):
        return jnp.dot(pieces, blocks, preferred_element_type=jnp.float32)

    taps = [(frame_tap, row_tap) for frame_tap in range(3) for row_tap in range(3)]
    early = dot(
        jnp.concatenate(
            [
                jnp.concatenate([piece(tap, out + row_tap) for tap, row_tap in taps], axis=1)
                for out in range(2)
            ],
            axis=0,
        ),
        jnp.concatenate(
            [
                jnp.concatenate([weight_ref[tap, row_tap, 0], weight_ref[tap, row_tap, 1]], axis=1)
                for tap, row_tap in taps
            ],
            axis=0,
        ),
    )
    lines = [(frame_tap, line) for frame_tap in range(3) for line in range(4)]
    late = dot(
        jnp.concatenate([piece(tap, line) for tap, line in lines], axis=1),
        jnp.concatenate(
            [
                jnp.concatenate(
                    [
                        weight_ref[tap, line - out, 2] if 0 <= line - out <= 2 else nothing
                        for out in range(2)
                    ],
                    axis=1,
                )
                for tap, line in lines
            ],
            axis=0,
        ),
    )
    column = lax.broadcasted_iota(jnp.int32, (frames, columns, channels), 1)
    column = column.reshape(cells, channels)
    results = []
    for out in range(2):
        left, centre = (
            early[out * cells : (out + 1) * cells, tap * channels : (tap + 1) * channels]
            for tap in range(2)
        )
        right = late[:, out * channels : (out + 1) * channels]
        left = jnp.where(column == 0, 0.0, pltpu.roll(left, 1, 0))
        right = jnp.where(column == columns - 1, 0.0, pltpu.roll(right, cells - 1, 0))
        results.append(left + centre + right)
    return results


def copy_kernel(sections, own_ref, second_cache_ref, first_cache_ref, copied, halo_ref, sems):
    last = lax.axis_index("section") == sections - 1
    frames = own_ref.shape[0]
    spare = SPAN_HALO - 2
    tail = pltpu.make_async_copy(own_ref.at[frames - SPAN_HALO :], halo_ref, sems.at[0])
    older = pltpu.make_async_copy(second_cache_ref, halo_ref.at[:spare], sems.at[1])
    newer = pltpu.make_async_copy(first_cache_ref, halo_ref.at[spare:], sems.at[2])
    load = pltpu.make_async_copy(own_ref, copied, sems.at[3])

    @pl.when(last)
    def _():
        older.start()
        newer.start()

    @pl.when(jnp.logical_not(last))
    def _():
        tail.start()

    load.start()

    @pl.when(last)
    def _():
        older.wait()
        newer.wait()

    @pl.when(jnp.logical_not(last))
    def _():
        tail.wait()

    load.wait()


def stats_kernel(own_ref, weight_ref, *rest):
    *vector_refs, stats_ref, vectors_ref, weight_copy, sems = rest
    loads = [pltpu.make_async_copy(weight_ref, weight_copy, sems.at[0])]
    loads += [
        pltpu.make_async_copy(vector_ref, vectors_ref.at[index], sems.at[1 + index])
        for index, vector_ref in enumerate(vector_refs)
    ]
    for load in loads:
        load.start()
    channels = own_ref.shape[-1]
    blocks = [own_ref[frame].astype(jnp.float32) for frame in range(own_ref.shape[0])]
    stats_ref[0] = moments([block.reshape(-1, channels) for block in blocks])
    for load in loads:
        load.wait()


def first_kernel(
    row_count, halo_ref, own_ref, near_ref, far_ref, stats_ref, vectors_ref, weight_ref,
    middle_ref, sums_ref, field
):
    section, row_at = lax.axis_index("section"), lax.axis_index("rows")
    inner, lines, columns, channels = own_ref.shape
    cells = inner * lines * columns
    scale, shift = vectors_ref[0], vectors_ref[1]
    mine, before = stats_ref[:, :2], stats_ref[:, 2:]
    slope, offset = affine(mine, cells, scale, shift)
    slope_before, offset_before = affine(before, cells, scale, shift)
    even = row_at % 2 == 0
    at_start = section == 0

    def fill(line):
        side, local = divmod(line, lines)
        if side == 1:
            halo, body = halo_ref[:, local], own_ref[:, local]
        else:
            near_side = even if side == 2 else jnp.logical_not(even)
            block = jnp.where(near_side, near_ref[:, local], far_ref[:, local])
            halo, body = block[:SPAN_HALO], block[SPAN_HALO:]
        behind = activate(halo, slope_before, offset_before).astype(jnp.bfloat16)
        behind = jnp.where(at_start, halo, behind)
        ahead = activate(body, slope, offset).astype(jnp.bfloat16)
        if side != 1:
            outside = row_at == 0 if side == 0 else row_at == row_count - 1
            behind = jnp.where(outside, jnp.zeros_like(behind), behind)
            ahead = jnp.where(outside, jnp.zeros_like(ahead), ahead)
        field[:SPAN_HALO, line] = behind
        field[SPAN_HALO:, line] = ahead

    bias = vectors_ref[2]
    kept = []
    spare = SPAN_HALO - 2
    ready = 0
    for pair in range((lines + 2) // 2):
        for line in range(ready, 2 * pair + 4):
            fill(line)
        ready = 2 * pair + 4
        half = (inner + 2) // 2
        for begin, out in ((begin, out) for begin in (0, half) for out in range(2)):
            if out == 0:
                results = pair_conv(field, 2 * pair, begin, half, weight_ref)
            line = 2 * pair + out
            rounded = (results[out] + bias).astype(jnp.bfloat16)
            rounded = rounded.reshape(half, columns, channels)
            skip = 2 if begin == 0 else 0
            if begin == 0:
                middle_ref[:2, line] = jnp.where(
                    at_start, field[:spare, line + lines - 1], rounded[:2]
                )
            middle_ref[begin + skip : begin + half, line] = rounded[skip:]
            if 1 <= line <= lines:
                kept.append(rounded[skip:].astype(jnp.float32).reshape(-1, channels))
    packed = moments(kept)
    for device in range(sums_ref.shape[0]):
        sums_ref[device] = packed


def second_kernel(
    row_count, middle_ref, stats_ref, vectors_ref, weight_ref, own_ref, out_ref, field, ready,
    sems
):
    section, row_at = lax.axis_index("section"), lax.axis_index("rows")
    frames, lines, columns, channels = own_ref.shape
    cells = frames * lines * columns
    scale, shift = vectors_ref[3], vectors_ref[4]
    mine = stats_ref[pl.ds(section * row_count, row_count)]
    before = stats_ref[pl.ds(jnp.maximum(section - 1, 0) * row_count, row_count)]
    slope, offset = affine(mine, cells, scale, shift)
    slope_before, offset_before = affine(before, cells, scale, shift)
    at_start = section == 0
    half = frames // 2
    copies = []
    for begin in range(0, frames, half):
        filled = 0 if begin == 0 else begin + 2
        for line in range(lines + 2):
            ahead = middle_ref[filled : begin + half + 2, line]
            if begin == 0:
                behind = activate(ahead[:2], slope_before, offset_before).astype(jnp.bfloat16)
                behind = jnp.where(at_start, ahead[:2], behind)
                ahead = activate(ahead[2:], slope, offset).astype(jnp.bfloat16)
                ahead = jnp.concatenate([behind, ahead], axis=0)
            else:
                ahead = activate(ahead, slope, offset).astype(jnp.bfloat16)
            if line == 0 or line == lines + 1:
                outside = row_at == 0 if line == 0 else row_at == row_count - 1
                ahead = jnp.where(outside, jnp.zeros_like(ahead), ahead)
            field[filled : begin + half + 2, line] = ahead
        span = slice(begin, begin + half)
        for pair in range(lines // 2):
            results = pair_conv(field, 2 * pair, begin, half, weight_ref)
            for out in range(2):
                line = 2 * pair + out
                result = (results[out] + vectors_ref[5]).reshape(half, columns, channels)
                result = result + own_ref[span, line].astype(jnp.float32)
                ready[span, line] = result.astype(jnp.bfloat16)
        copy = pltpu.make_async_copy(
            ready.at[span], out_ref.at[span], sems.at[begin // half]
        )
        copy.start()
        copies.append(copy)
    for copy in copies:
        copy.wait()


def call(kernel, out_shape, scratch, operands, in_place=(), out_in_place=False, flops=0):
    vmem = pl.BlockSpec(memory_space=pltpu.VMEM)
    out_spec = pl.BlockSpec(memory_space=pltpu.HBM) if out_in_place else vmem
    specs = [vmem] * len(operands)
    for index in in_place:
        specs[index] = pl.BlockSpec(memory_space=pltpu.HBM)
    operands = [
        pltpu.with_memory_space_constraint(operand, pltpu.HBM) if index in in_place else operand
        for index, operand in enumerate(operands)
    ]
    return pl.pallas_call(
        kernel,
        out_shape=out_shape,
        in_specs=specs,
        out_specs=jax.tree.map(lambda _: out_spec, out_shape),
        scratch_shapes=scratch,
        compiler_params=pltpu.CompilerParams(vmem_limit_bytes=40 * 2**20),
        cost_estimate=pl.CostEstimate(flops=flops, bytes_accessed=2**20, transcendentals=0),
    )(*operands)


def on_device(
    activations,
    first_cache,
    second_cache,
    norm1_scale,
    norm1_shift,
    conv1_weight,
    conv1_bias,
    norm2_scale,
    norm2_shift,
    conv2_weight,
    conv2_bias,
):
    frames, lines, columns, channels = activations.shape
    sections, row_count = lax.axis_size("section"), lax.axis_size("rows")
    everyone = sections * row_count
    stats_shape = jax.ShapeDtypeStruct((everyone, 2, channels), jnp.float32)
    vectors = (norm1_scale, norm1_shift, conv1_bias, norm2_scale, norm2_shift, conv2_bias)

    near = [i ^ 1 for i in range(row_count)]
    far = [i + 2 if i % 2 == 0 else i - 2 for i in range(row_count)]
    far[row_count - 2], far[1] = row_count - 1, 0

    def across(block, partner):
        return lax.ppermute(block, "rows", list(enumerate(partner)))

    ring = [(at, (at + 1) % sections) for at in range(sections)]
    own, halo = call(
        functools.partial(copy_kernel, sections),
        (
            jax.ShapeDtypeStruct(activations.shape, jnp.bfloat16),
            jax.ShapeDtypeStruct((SPAN_HALO, lines, columns, channels), jnp.bfloat16),
        ),
        [pltpu.SemaphoreType.DMA((4,))],
        (activations, second_cache, first_cache),
        in_place=range(3),
    )
    sums, packed, weight = call(
        stats_kernel,
        (
            jax.ShapeDtypeStruct((1, 2, channels), jnp.float32),
            jax.ShapeDtypeStruct((len(vectors), 1, channels), jnp.float32),
            jax.ShapeDtypeStruct(conv1_weight.shape, jnp.bfloat16),
        ),
        [pltpu.SemaphoreType.DMA((1 + len(vectors),))],
        (own, conv1_weight) + tuple(vector.reshape(1, channels) for vector in vectors),
        in_place=range(1, 2 + len(vectors)),
    )
    received = lax.ppermute(halo, "section", ring)
    passed = lax.ppermute(sums, "section", ring)
    received, sums, passed = lax.optimization_barrier((received, sums, passed))
    from_near = jnp.concatenate([across(received, near), across(own, near)], axis=0)
    from_far = across(from_near, far)
    both = jnp.concatenate([sums, passed], axis=1)
    both = jnp.broadcast_to(both, (row_count,) + both.shape[1:])
    stats = lax.all_to_all(both, "rows", 0, 0, tiled=True)
    middle, sums_two = call(
        functools.partial(first_kernel, row_count),
        (
            jax.ShapeDtypeStruct((frames + 2, lines + 2, columns, channels), jnp.bfloat16),
            stats_shape,
        ),
        [pltpu.VMEM((frames + SPAN_HALO, 3 * lines, columns, channels), jnp.bfloat16)],
        (received, own, from_near, from_far, stats, packed, weight),
        flops=10**9,
    )
    stats_two = lax.all_to_all(sums_two, ("section", "rows"), 0, 0, tiled=True)
    return call(
        functools.partial(second_kernel, row_count),
        jax.ShapeDtypeStruct(activations.shape, jnp.bfloat16),
        [
            pltpu.VMEM((frames + 2, lines + 2, columns, channels), jnp.bfloat16),
            pltpu.VMEM(activations.shape, jnp.bfloat16),
            pltpu.SemaphoreType.DMA((2,)),
        ],
        (middle, stats_two, packed, conv2_weight, own),
        out_in_place=True,
        flops=10**9,
    )


def solution(mesh):
    in_specs = (
        P("section", "rows", None, None),
        P(None, "rows", None, None),
        P(None, "rows", None, None),
        P(),
        P(),
        P(),
        P(),
        P(),
        P(),
        P(),
        P(),
    )
    out_specs = P("section", "rows", None, None)
    return jax.shard_map(
        on_device, mesh=mesh, in_specs=in_specs, out_specs=out_specs, check_vma=False
    )
```
